32 devices in a mesh: gx: 8 (over z, core), gy: 4 (over y, x).
Axes of the slice: x: 2, y: 2, z: 4, core: 2. Of those that a mesh axis runs over, the one named last changes fastest.
Arguments:
- features: bfloat16 [128, 64, 1, 1024], P('gx', 'gy'), may hold values from -6 to 6
- slot_map: int32 [8, 4, 2], replicated, may hold values from -1 to 0, as said below
- tap_weights: float32 [27, 64], replicated, may hold values from -1.25 to 1.25
- gain: float32 [64], replicated, may hold values from 0.5 to 1.5
- mix_weight: bfloat16 [64, 64], replicated, may hold values from -0.75 to 0.75
- cotangent: bfloat16 [128, 64, 1, 1024], P('gx', 'gy'), may hold values from -6 to 6
Outputs:
- mixed: bfloat16 [128, 64, 1, 1024], P('gx', 'gy')
- grad_features: bfloat16 [128, 64, 1, 1024], P('gx', 'gy')
- grad_taps: float32 [27, 64], replicated
- grad_gain: float32 [64], replicated
- grad_mix: float32 [64, 64], replicated
The draws below stay inside these ranges and needn't reach their ends.
Inputs may be any that keep to these rules, and one draw needn't show every extreme that they name: `slot_map`: in each block column the active levels carry slot numbers 0, 1, 2, ... in increasing level order and the others carry -1; every block column has exactly 1 active block.
All inputs are finite; a program needn't handle non-finite values.
Results may differ from the reference program's by a relative error of at most 0.0039.
Values may be sent and summed in bfloat16 or wider, within the bound.
No kernel may reach another device: no remote copies, remote signals or barrier semaphores. Data moves between devices by JAX's collectives and lax.ppermute only.
A program may use at most 128 MiB of HBM per device.

```python
import jax
import jax.numpy as jnp
from jax import lax

BS = 16
CH = 64
BZ = 2
B_DEV = 1
NX = 128
NY = 64
LANES = 1024
N_GX = 8
N_GY = 4


def column_order(perm_key):
    return jax.random.permutation(perm_key, BZ)


def draw_slot_map(key, part):
    tile_total = N_GX * N_GY
    key_count, key_full, key_perm = jax.random.split(jax.random.fold_in(key, 7), 3)
    counts = jax.random.randint(key_count, (tile_total,), 1, B_DEV + 1)
    fullest = jax.random.randint(key_full, (), 0, tile_total)
    counts = jnp.where(jnp.arange(tile_total, dtype=jnp.int32) == fullest, B_DEV, counts)
    orders = jax.vmap(column_order)(jax.random.split(key_perm, tile_total)).astype(jnp.int32)
    ranks = jnp.argsort(orders, axis=1, stable=True).astype(jnp.int32)
    active = ranks < counts[:, None]
    slot_index = jnp.cumsum(active.astype(jnp.int32), axis=1) - 1
    result = jnp.where(active, slot_index, -1).astype(jnp.int32)
    return result.reshape(N_GX, N_GY, BZ)


def level_of(stream_key, dims, pieces, smallest, largest):
    factor_of = 1.0
    for dim, blocks in pieces:
        steps = jax.random.uniform(jax.random.fold_in(jax.random.fold_in(stream_key, 6), dim), (blocks,), jnp.float32, smallest / len(pieces), largest / len(pieces))
        factor_of = factor_of * jnp.repeat(jnp.exp(steps), dims[dim] // blocks).reshape((-1,) + (1,) * (len(dims) - 1 - dim))
    return factor_of


def centred(own_key, dims, width, bound, pieces=(), kind=jnp.bfloat16):
    values = width * jax.random.normal(own_key, dims, jnp.float32)
    if pieces:
        values = values * level_of(own_key, dims, pieces, -0.22, 0.18)
    return jnp.clip(values, -bound, bound).astype(kind)


def setup_inputs(seed: int = 0) -> dict:
    key_of = jax.random.split(jax.random.key(seed), 7)
    features = centred(key_of[0], (NX, NY, B_DEV, LANES), 1.0, 6.0, ((0, 8), (1, 4)))
    slot_map = draw_slot_map(jax.random.fold_in(key_of[6], 71), 0)
    tap_weights = centred(key_of[2], (27, CH), 27 ** -0.5, 1.25, (), jnp.float32)
    gain = jnp.clip(1.0 + 0.1 * jax.random.normal(key_of[3], (CH,), jnp.float32), 0.5, 1.5)
    mix_weight = centred(key_of[4], (CH, CH), CH ** -0.5, 0.75)
    cotangent = centred(key_of[5], (NX, NY, B_DEV, LANES), 1.0, 6.0, ((0, 8), (1, 4)))
    return {"features": features, "slot_map": slot_map, "tap_weights": tap_weights, "gain": gain, "mix_weight": mix_weight, "cotangent": cotangent}


EPS = 1e-05

def one_hot_map(level_slots, slot_count):
    slot_ids = jnp.arange(slot_count, dtype=jnp.int32)
    return (level_slots[..., None] == slot_ids).astype(jnp.float32)

def slot_lookup(center, slot_count):
    slot_ids = jnp.arange(slot_count, dtype=jnp.int32)
    matches = center[:, None] == slot_ids[None, :]
    level_ids = jnp.arange(center.shape[0], dtype=jnp.int32)[:, None]
    position = lax.optimization_barrier(jnp.sum(jnp.where(matches, level_ids, 0), axis=0)).astype(jnp.int32)
    active = jnp.any(matches, axis=0)
    return (position, active)

def spread_edges(table, inner, axis):
    first = lax.slice_in_dim(table, 0, 1, axis=axis)
    middle = jnp.repeat(lax.slice_in_dim(table, 1, 2, axis=axis), inner, axis=axis)
    last = lax.slice_in_dim(table, 2, 3, axis=axis)
    return jnp.concatenate([first, middle, last], axis=axis)

def extend_cells(block, near_maps):
    inner = block.shape[0] - 2
    table = one_hot_map(near_maps, block.shape[2])
    table = spread_edges(spread_edges(table, inner, 0), inner, 1)
    dense_cells = jnp.einsum('xysf,xyps->xypf', block.astype(jnp.float32), table, precision=lax.Precision.HIGHEST)
    return dense_cells.astype(jnp.bfloat16)

def widen(extended, channels):
    grid = extended.shape[0]
    flat = extended.reshape(grid, grid, -1)
    return jnp.pad(flat, ((0, 0), (0, 0), (channels, channels)))

def stencil(padded, taps):
    channels = taps.shape[1]
    inner = padded.shape[0] - 2
    length = padded.shape[2] - 2 * channels
    accum_sum = jnp.zeros((inner, inner, length), jnp.float32)
    for tap_index in range(27):
        off_x = tap_index // 9
        off_y = tap_index // 3 % 3
        off_z = tap_index % 3
        shifted = padded[off_x:off_x + inner, off_y:off_y + inner, channels * off_z:channels * off_z + length].astype(jnp.float32)
        accum_sum = accum_sum + shifted * jnp.tile(taps[tap_index], length // channels)
    return accum_sum

def tap_grads(padded, grads, channels):
    inner = padded.shape[0] - 2
    length = padded.shape[2] - 2 * channels
    rows_out = []
    for tap_index in range(27):
        off_x = tap_index // 9
        off_y = tap_index // 3 % 3
        off_z = tap_index % 3
        shifted = padded[off_x:off_x + inner, off_y:off_y + inner, channels * off_z:channels * off_z + length].astype(jnp.float32)
        rows_out.append(lax.optimization_barrier(jnp.sum((shifted * grads).reshape(-1, channels), axis=0)))
    return jnp.stack(rows_out)

def norm_forward(depth_slots):
    mean_square = lax.optimization_barrier(jnp.mean(depth_slots * depth_slots, axis=-1, keepdims=True))
    inv_rms = lax.rsqrt(mean_square + EPS)
    return (depth_slots * inv_rms, inv_rms)

def norm_backward(grad_norm, normed, inv_rms, gain):
    grad_scaled = grad_norm * gain
    return inv_rms * (grad_scaled - normed * lax.optimization_barrier(jnp.mean(grad_scaled * normed, axis=-1, keepdims=True)))

def reference(features, slot_map, tap_weights, gain, mix_weight, cotangent):
    lane_width = BS * CH
    cell_shape = (BS, BS, B_DEV, BS, CH)
    padded_feat = jnp.pad(features, ((1, 1), (1, 1), (0, 0), (0, 0)))
    padded_map = jnp.pad(slot_map, ((1, 1), (1, 1), (0, 0)), constant_values=-1)
    tile_ids = jnp.arange(N_GX * N_GY, dtype=jnp.int32)

    def locate(tile):
        grid_row = tile // N_GY
        grid_col = tile % N_GY
        near_maps = lax.dynamic_slice(padded_map, (grid_row, grid_col, jnp.int32(0)), (3, 3, BZ))
        start = (grid_row * BS, grid_col * BS, jnp.int32(0), jnp.int32(0))
        return (near_maps, start)

    def forward_tile(tile):
        near_maps, start = locate(tile)
        slab = lax.dynamic_slice(padded_feat, start, (BS + 2, BS + 2, B_DEV, lane_width))
        own_grad = lax.dynamic_slice(cotangent, start, (BS, BS, B_DEV, lane_width))
        position, active = slot_lookup(near_maps[1, 1], B_DEV)
        keep_mask = active.astype(jnp.float32)[None, None, :, None, None]
        padded_in = widen(extend_cells(slab, near_maps), CH)
        depth_field = stencil(padded_in, tap_weights).reshape(BS, BS, BZ, lane_width)
        depth_slots = jnp.take(depth_field, position, axis=2).reshape(cell_shape)
        normed, inv_rms = norm_forward(depth_slots)
        norm_bf = (normed * gain).astype(jnp.bfloat16)
        branch = jnp.einsum('xyszc,cd->xyszd', norm_bf.astype(jnp.float32), mix_weight.astype(jnp.float32), precision=lax.Precision.HIGHEST)
        inputs_f = slab[1:-1, 1:-1].reshape(cell_shape).astype(jnp.float32)
        mixed = ((inputs_f + branch) * keep_mask).astype(jnp.bfloat16).reshape(BS, BS, B_DEV, lane_width)
        grad_out = own_grad.reshape(cell_shape) * keep_mask.astype(jnp.bfloat16)
        grad_mix_part = jnp.einsum('xyszc,xyszd->cd', norm_bf.astype(jnp.float32), grad_out.astype(jnp.float32), precision=lax.Precision.HIGHEST)
        grad_norm = jnp.einsum('xyszd,cd->xyszc', grad_out.astype(jnp.float32), mix_weight.astype(jnp.float32), precision=lax.Precision.HIGHEST)
        grad_gain_part = lax.optimization_barrier(jnp.sum(grad_norm * normed, axis=(0, 1, 2, 3)))
        grad_depth = (norm_backward(grad_norm, normed, inv_rms, gain) * keep_mask).astype(jnp.bfloat16)
        return (mixed, grad_depth.reshape(BS, BS, B_DEV, lane_width), grad_mix_part, grad_gain_part)

    def assemble(tiles):
        shaped = tiles.reshape(N_GX, N_GY, BS, BS, B_DEV, lane_width).transpose(0, 2, 1, 3, 4, 5)
        return shaped.reshape(N_GX * BS, N_GY * BS, B_DEV, lane_width)
    mixed_tiles, depth_tiles, mix_parts, gain_parts = lax.map(forward_tile, tile_ids)
    padded_depth = jnp.pad(assemble(depth_tiles), ((1, 1), (1, 1), (0, 0), (0, 0)))

    def backward_tile(tile):
        near_maps, start = locate(tile)
        slab = lax.dynamic_slice(padded_feat, start, (BS + 2, BS + 2, B_DEV, lane_width))
        slab_grad = lax.dynamic_slice(padded_depth, start, (BS + 2, BS + 2, B_DEV, lane_width))
        own_grad = lax.dynamic_slice(cotangent, start, (BS, BS, B_DEV, lane_width))
        position, active = slot_lookup(near_maps[1, 1], B_DEV)
        keep_mask = active.astype(jnp.float32)[None, None, :, None, None]
        padded_in = widen(extend_cells(slab, near_maps), CH)
        padded_grad = widen(extend_cells(slab_grad, near_maps), CH)
        back_field = stencil(padded_grad, tap_weights[::-1]).reshape(BS, BS, BZ, lane_width)
        back_slots = jnp.take(back_field, position, axis=2)
        grad_feat = ((own_grad.astype(jnp.float32) + back_slots).reshape(cell_shape) * keep_mask).astype(jnp.bfloat16)
        grad_center = padded_grad[1:-1, 1:-1, CH:-CH].astype(jnp.float32)
        taps_part = tap_grads(padded_in, grad_center, CH)
        return (grad_feat.reshape(BS, BS, B_DEV, lane_width), taps_part)
    grad_tiles, taps_parts = lax.map(backward_tile, tile_ids)
    return (assemble(mixed_tiles), assemble(grad_tiles), lax.optimization_barrier(jnp.sum(taps_parts, axis=0)), lax.optimization_barrier(jnp.sum(gain_parts, axis=0)), lax.optimization_barrier(jnp.sum(mix_parts, axis=0)))
```

```python
import functools

import jax
import jax.numpy as jnp
from jax import lax
from jax.experimental import pallas as pl
from jax.experimental.pallas import tpu as pltpu
from jax.sharding import PartitionSpec as P

EPS = 1e-05
LANE = 128
F32 = jnp.float32
BF16 = jnp.bfloat16


def level_masks(delta_ref, index):
    d = delta_ref[index]
    return tuple(jnp.where(d == want, 1.0, 0.0).astype(F32) for want in (0, -1, 1))


def plane_tiles(tiles, masks):
    same, below, above = masks
    count = len(tiles)
    half = tiles[0].shape[-1] // 2
    rolled = [pltpu.roll(t, half, 1) for t in tiles]
    low = lax.broadcasted_iota(jnp.int32, tiles[0].shape, 1) < half
    if same is None:
        zero = jnp.zeros_like(tiles[0])
        offset = [jnp.where(low, zero, rolled[0])]
        offset += [jnp.where(low, rolled[j - 1], rolled[j]) for j in range(1, count)]
        offset += [jnp.where(low, rolled[-1], zero)]
        return tiles, offset
    offset = [jnp.where(low, rolled[-1] * below, rolled[0] * same)]
    offset += [jnp.where(low, rolled[j - 1], rolled[j]) * same for j in range(1, count)]
    offset += [jnp.where(low, rolled[-1] * same, rolled[0] * above)]
    return [t * same for t in tiles], offset


def fill_field(field, own_ref, xlo_ref, xhi_ref, ylo_ref, yhi_ref, delta_ref):
    side = own_ref.shape[0]
    tiles = own_ref.shape[2] // LANE
    pitch = side + 8

    def put(planes, store):
        aligned, offset = planes
        for j, t in enumerate(aligned + offset):
            store(j, t)

    def columns(ref, x=None):
        rows = ref[...] if x is None else ref[x]
        return [rows[:, k * LANE:(k + 1) * LANE].astype(F32) for k in range(tiles)]

    def own_plane(x, _):
        base = pl.multiple_of((x + 1) * pitch + 8, 8)

        def store(j, t):
            field[j, pl.ds(base, side), :] = t

        put(plane_tiles(columns(own_ref, x), (None, None, None)), store)
        return 0

    lax.fori_loop(0, side, own_plane, 0)

    for ref, plane, index in ((xlo_ref, 0, 1), (xhi_ref, side + 1, 7)):

        def store(j, t, base=plane * pitch + 8):
            field[j, base:base + side, :] = t

        put(plane_tiles(columns(ref), level_masks(delta_ref, index)), store)

    for ref, shift, first in ((ylo_ref, 7, 0), (yhi_ref, pitch, 2)):
        rows = ref.shape[0]
        row_id = lax.broadcasted_iota(jnp.int32, (rows, LANE), 0)
        corners = [level_masks(delta_ref, first + 3 * i) for i in range(3)]
        masks = tuple(
            jnp.where(row_id == 0, a, jnp.where(row_id == rows - 1, c, b)) for a, b, c in zip(*corners)
        )

        def store(j, t, shift=shift, rows=rows):
            for start in range(0, rows, 8):
                size = min(8, rows - start)
                field[j, pl.ds(start * pitch + shift, size, stride=pitch), :] = t[start:start + size]

        put(plane_tiles(columns(ref), masks), store)


def shifted(field, tiles, k, plane, half, pitch):
    found = {}
    for off_y in range(3):
        row = plane * pitch + 8 + 8 * half + off_y - 1
        for off_z in range(3):
            j = (tiles + k, k, tiles + k + 1)[off_z]
            found[off_y, off_z] = field[j, row:row + 8, :]
    return found


def stencil_tile(field, weights, tiles, side, k, half, flip, emit):
    pitch = side + 8
    sums = {}
    for plane in range(side + 2):
        near = shifted(field, tiles, k, plane, half, pitch)
        for off_x in range(3):
            x = plane - off_x
            if not 0 <= x < side:
                continue
            for (off_y, off_z), value in near.items():
                tap = 9 * off_x + 3 * off_y + off_z
                term = value * weights[26 - tap if flip else tap]
                sums[x] = sums[x] + term if x in sums else term
        done = plane - 2
        if done >= 0:
            emit(done, sums.pop(done))


def spread_taps(taps_ref, weights):
    wide = jnp.concatenate([taps_ref[...], taps_ref[...]], axis=1)
    for tap in range(27):
        weights[tap] = jnp.broadcast_to(wide[tap:tap + 1], (8, LANE))


def forward_kernel(
    delta_ref, own_ref, xlo_ref, xhi_ref, ylo_ref, yhi_ref, cot_ref, taps_ref, gain_ref, mix_ref,
    mixed_ref, grad_ref, packed_ref,
    field, weights, depth, normed_bf, grads,
):
    side = own_ref.shape[0]
    lanes = own_ref.shape[2]
    tiles = lanes // LANE
    channels = gain_ref.shape[1]
    pitch = side + 8
    fill_field(field, own_ref, xlo_ref, xhi_ref, ylo_ref, yhi_ref, delta_ref)
    spread_taps(taps_ref, weights)

    def depth_tile(k, _):
        lane0 = pl.multiple_of(k * LANE, LANE)
        for half in range(side // 8):

            def emit(x, value, half=half):
                row = x * side + 8 * half
                depth[row:row + 8, pl.ds(lane0, LANE)] = value

            stencil_tile(field, weights, tiles, side, k, half, False, emit)
        return 0

    lax.fori_loop(0, tiles, depth_tile, 0)

    wide = 256
    copies = wide // channels
    row_id = lax.broadcasted_iota(jnp.int32, (wide, wide), 0) // channels
    col_id = lax.broadcasted_iota(jnp.int32, (wide, wide), 1) // channels
    block = row_id == col_id
    mean_mat = jnp.where(block, 1.0 / channels, 0.0).astype(BF16)
    mix = mix_ref[...].astype(F32)
    mix_row = jnp.concatenate([mix] * copies, axis=1)
    mix_mat = jnp.where(block, jnp.concatenate([mix_row] * copies, axis=0), 0.0).astype(BF16)
    gain = jnp.concatenate([gain_ref[...]] * copies, axis=1)
    rows = 128
    xs = rows // side
    cells = side * side
    gain_sum = jnp.zeros((8, wide), F32)
    for part in range(lanes // wide):
        cols = slice(part * wide, (part + 1) * wide)
        for chunk in range(cells // rows):
            at = slice(chunk * rows, (chunk + 1) * rows)
            planes = slice(chunk * xs, (chunk + 1) * xs)
            dep = depth[at, cols]
            cot = cot_ref[planes, :, cols].reshape(rows, wide)
            mean_sq = jnp.dot((dep * dep).astype(BF16), mean_mat, preferred_element_type=F32)
            inv = lax.rsqrt(mean_sq + EPS)
            normed = dep * inv
            norm_bf = (normed * gain).astype(BF16)
            normed_bf[at, cols] = norm_bf
            branch = jnp.dot(norm_bf, mix_mat, preferred_element_type=F32)
            feat = own_ref[planes, :, cols].reshape(rows, wide).astype(F32)
            mixed_ref[planes, :, cols] = (feat + branch).astype(BF16).reshape(xs, side, wide)
            grad_norm = lax.dot_general(
                cot, mix_mat, (((1,), (1,)), ((), ())), preferred_element_type=F32
            )
            gain_sum = gain_sum + jnp.sum((grad_norm * normed).reshape(rows // 8, 8, wide), axis=0)
            scaled = grad_norm * gain
            mean = jnp.dot((scaled * normed).astype(BF16), mean_mat, preferred_element_type=F32)
            grad = (inv * (scaled - normed * mean)).astype(BF16)
            grad_ref[planes, :, cols] = grad.reshape(xs, side, wide)
            grads[at, cols] = grad.astype(F32)

    mix_sum = jnp.zeros((wide, wide), F32)
    for part in range(lanes // wide):
        cols = slice(part * wide, (part + 1) * wide)
        mix_sum = mix_sum + lax.dot_general(
            normed_bf[:, cols],
            cot_ref[:, :, cols].reshape(cells, wide),
            (((0,), (0,)), ((), ())),
            preferred_element_type=F32,
        )
    grad_mix = mix_sum[:channels, :channels]
    for i in range(1, copies):
        span = slice(i * channels, (i + 1) * channels)
        grad_mix = grad_mix + mix_sum[span, span]
    packed_ref[0:32, :] = jnp.concatenate([grad_mix[:32], grad_mix[32:]], axis=1)

    def tap_tile(k, sums):
        lane0 = pl.multiple_of(k * LANE, LANE)
        sums = list(sums)
        for half in range(side // 8):
            near_grads = {}
            for plane in range(side + 2):
                if plane < side:
                    row = plane * side + 8 * half
                    near_grads[plane] = grads[row:row + 8, pl.ds(lane0, LANE)]
                near = shifted(field, tiles, k, plane, half, pitch)
                for (off_y, off_z), value in near.items():
                    for off_x in range(3):
                        x = plane - off_x
                        if 0 <= x < side:
                            tap = 9 * off_x + 3 * off_y + off_z
                            sums[tap] = sums[tap] + value * near_grads[x]
                near_grads.pop(plane - 2, None)
        return tuple(sums)

    sums = lax.fori_loop(0, tiles, tap_tile, tuple(jnp.zeros((8, LANE), F32) for _ in range(27)))
    for tap in range(27):
        packed_ref[32 + tap:33 + tap, :] = jnp.sum(sums[tap], axis=0, keepdims=True)
    gain_row = jnp.sum(gain_sum, axis=0, keepdims=True)
    packed_ref[59:60, :] = gain_row[:, :LANE] + gain_row[:, LANE:]
    packed_ref[60:64, :] = jnp.zeros((4, LANE), F32)


def backward_kernel(
    delta_ref, own_ref, xlo_ref, xhi_ref, ylo_ref, yhi_ref, cot_ref, taps_ref, out_ref, field, weights
):
    side = own_ref.shape[0]
    tiles = own_ref.shape[2] // LANE
    fill_field(field, own_ref, xlo_ref, xhi_ref, ylo_ref, yhi_ref, delta_ref)
    spread_taps(taps_ref, weights)

    def grad_tile(k, _):
        lane0 = pl.multiple_of(k * LANE, LANE)
        kept = {}

        for half in range(side // 8):

            def emit(x, value, half=half):
                kept[x, half] = value
                if half == 1:
                    both = jnp.concatenate([depth_half[x], value], axis=0)
                    cot = cot_ref[x, :, pl.ds(lane0, LANE)].astype(F32)
                    out_ref[x, :, pl.ds(lane0, LANE)] = (cot + both).astype(BF16)

            depth_half = {x: v for (x, h), v in kept.items() if h == 0}
            stencil_tile(field, weights, tiles, side, k, half, True, emit)
        return 0

    lax.fori_loop(0, tiles, grad_tile, 0)


def edge_exchange(cells):
    def swap(low, high, axis):
        count = lax.axis_size(axis)
        up = [(i, i + 1) for i in range(count - 1)]
        down = [(i + 1, i) for i in range(count - 1)]
        return lax.ppermute(high, axis, up), lax.ppermute(low, axis, down)

    xlo, xhi = swap(cells[0], cells[-1], "gx")
    left = jnp.concatenate([xlo[:1], cells[:, 0], xhi[:1]], axis=0)
    right = jnp.concatenate([xlo[-1:], cells[:, -1], xhi[-1:]], axis=0)
    ylo, yhi = swap(left, right, "gy")
    return xlo, xhi, ylo, yhi


def level_deltas(slot_map):
    levels = slot_map.shape[2]
    position = jnp.sum(jnp.where(slot_map >= 0, jnp.arange(levels, dtype=jnp.int32), 0), axis=2)
    padded = jnp.pad(position, 1, constant_values=99)
    near = lax.dynamic_slice(padded, (lax.axis_index("gx"), lax.axis_index("gy")), (3, 3))
    return (near - near[1, 1]).reshape(9)


def shards(features, slot_map, tap_weights, gain, mix_weight, cotangent):
    side, _, _, lanes = features.shape
    channels = gain.shape[0]
    tiles = lanes // LANE
    cells = features.reshape(side, side, lanes)
    cot = cotangent.reshape(side, side, lanes)
    deltas = level_deltas(slot_map)
    field = pltpu.VMEM((2 * tiles + 1, (side + 2) * (side + 8) + 8, LANE), F32)
    weights = pltpu.VMEM((27, 8, LANE), F32)
    smem = pl.BlockSpec(memory_space=pltpu.SMEM)
    vmem = pl.BlockSpec(memory_space=pltpu.VMEM)
    params = pltpu.CompilerParams(vmem_limit_bytes=40 * 1024 * 1024)
    block = jax.ShapeDtypeStruct((side, side, lanes), BF16)

    edges = edge_exchange(cells)
    mixed, grad_depth, packed = pl.pallas_call(
        forward_kernel,
        out_shape=(block, block, jax.ShapeDtypeStruct((64, LANE), F32)),
        in_specs=[smem] + [vmem] * 9,
        out_specs=(vmem, vmem, vmem),
        scratch_shapes=[
            field,
            weights,
            pltpu.VMEM((side * side, lanes), F32),
            pltpu.VMEM((side * side, lanes), BF16),
            pltpu.VMEM((side * side, lanes), F32),
        ],
        compiler_params=params,
        name="forward",
    )(deltas, cells, *edges, cot, tap_weights, gain.reshape(1, channels), mix_weight)

    total = jnp.sum(lax.all_gather(packed, ("gx", "gy")), axis=0)
    grad_mix = jnp.concatenate([total[:32, :channels], total[:32, channels:]], axis=0)
    rest = total[32:60, :channels] + total[32:60, channels:]

    grad_edges = edge_exchange(grad_depth)
    grad_features = pl.pallas_call(
        backward_kernel,
        out_shape=block,
        in_specs=[smem] + [vmem] * 7,
        out_specs=vmem,
        scratch_shapes=[field, weights],
        compiler_params=params,
        name="backward",
    )(deltas, grad_depth, *grad_edges, cot, tap_weights)
    shape = features.shape
    return (mixed.reshape(shape), grad_features.reshape(shape), rest[:27], rest[27], grad_mix)


def solution(mesh):
    return jax.shard_map(
        shards,
        mesh=mesh,
        in_specs=(P("gx", "gy", None, None), P(), P(), P(), P(), P("gx", "gy", None, None)),
        out_specs=(P("gx", "gy", None, None), P("gx", "gy", None, None), P(), P(), P()),
        check_vma=False,
    )
```

```python
import jax
import jax.numpy as jnp
from jax import lax
from jax.experimental import pallas as pl
from jax.experimental.pallas import tpu as pltpu
from jax.sharding import PartitionSpec as P

EPS = 1e-05
LANE = 128
F32 = jnp.float32
BF16 = jnp.bfloat16


def level_masks(place_ref, off_x, off_y):
    count_x, count_y = place_ref.shape
    x, y = lax.axis_index("gx"), lax.axis_index("gy")
    near_x = jnp.clip(x + off_x, 0, count_x - 1)
    near_y = jnp.clip(y + off_y, 0, count_y - 1)
    d = place_ref[near_x, near_y] - place_ref[x, y]
    return tuple(jnp.where(d == want, 1.0, 0.0).astype(F32) for want in (0, -1, 1))


def plane_tiles(tiles, masks):
    same, below, above = masks
    count = len(tiles)
    half = tiles[0].shape[-1] // 2
    rolled = [pltpu.roll(t, half, 1) for t in tiles]
    low = lax.broadcasted_iota(jnp.int32, tiles[0].shape, 1) < half
    if same is None:
        zero = jnp.zeros_like(tiles[0])
        offset = [jnp.where(low, zero, rolled[0])]
        offset += [jnp.where(low, rolled[j - 1], rolled[j]) for j in range(1, count)]
        offset += [jnp.where(low, rolled[-1], zero)]
        return tiles, offset
    offset = [jnp.where(low, rolled[-1] * below, rolled[0] * same)]
    offset += [jnp.where(low, rolled[j - 1], rolled[j]) * same for j in range(1, count)]
    offset += [jnp.where(low, rolled[-1] * same, rolled[0] * above)]
    return [t * same for t in tiles], offset


def fill_field(field, place_ref, own_ref, xa_ref, xb_ref, ya_ref, yb_ref):
    side = own_ref.shape[0]
    tiles = own_ref.shape[2] // LANE
    pitch = side + 8

    def put(planes, store):
        aligned, offset = planes
        for j, t in enumerate(aligned + offset):
            store(j, t)

    def columns(rows):
        return [rows[:, k * LANE:(k + 1) * LANE].astype(F32) for k in range(tiles)]

    def own_plane(x, _):
        base = pl.multiple_of((x + 1) * pitch + 8, 8)

        def store(j, t):
            field[j, pl.ds(base, side), :] = t

        put(plane_tiles(columns(own_ref[x]), (None, None, None)), store)
        return 0

    lax.fori_loop(0, side, own_plane, 0)

    odd = lax.axis_index("gx") % 2
    for ref, low_side in ((xa_ref, odd == 1), (xb_ref, odd == 0)):
        lower = level_masks(place_ref, -1, 0)
        upper = level_masks(place_ref, 1, 0)
        masks = tuple(jnp.where(low_side, a, b) for a, b in zip(lower, upper))
        base = pl.multiple_of(jnp.where(low_side, 8, (side + 1) * pitch + 8), 8)

        def store(j, t, base=base):
            field[j, pl.ds(base, side), :] = t

        put(plane_tiles(columns(ref[...]), masks), store)

    odd = lax.axis_index("gy") % 2
    for low_side in (True, False):
        from_a = odd == (1 if low_side else 0)
        edge = jnp.where(from_a, ya_ref[...].astype(F32), yb_ref[...].astype(F32))
        rows = edge.shape[0]
        shift = 7 if low_side else pitch
        row_id = lax.broadcasted_iota(jnp.int32, (rows, LANE), 0)
        corners = [level_masks(place_ref, off, -1 if low_side else 1) for off in (-1, 0, 1)]
        masks = tuple(
            jnp.where(row_id == 0, a, jnp.where(row_id == rows - 1, c, b)) for a, b, c in zip(*corners)
        )

        def store(j, t, shift=shift, rows=rows):
            for start in range(0, rows, 8):
                size = min(8, rows - start)
                field[j, pl.ds(start * pitch + shift, size, stride=pitch), :] = t[start:start + size]

        put(plane_tiles(columns(edge), masks), store)


def shifted(field, tiles, k, plane, half, pitch):
    found = {}
    for off_y in range(3):
        row = plane * pitch + 8 + 8 * half + off_y - 1
        for off_z in range(3):
            j = (tiles + k, k, tiles + k + 1)[off_z]
            found[off_y, off_z] = field[j, row:row + 8, :]
    return found


def stencil_tile(field, weights, tiles, side, k, half, flip, emit):
    pitch = side + 8
    taps = [weights[t] for t in range(27)]
    sums = {}
    for plane in range(side + 2):
        near = shifted(field, tiles, k, plane, half, pitch)
        for off_x in range(3):
            x = plane - off_x
            if not 0 <= x < side:
                continue
            for (off_y, off_z), value in near.items():
                tap = 9 * off_x + 3 * off_y + off_z
                term = value * taps[26 - tap if flip else tap]
                sums[x] = sums[x] + term if x in sums else term
        done = plane - 2
        if done >= 0:
            emit(done, sums.pop(done))


def spread_taps(params_ref, weights):
    wide = jnp.concatenate([params_ref[...], params_ref[...]], axis=1)
    for tap in range(27):
        weights[tap] = jnp.broadcast_to(wide[tap:tap + 1], (8, LANE))


def forward_kernel(
    place_ref, own_ref, xa_ref, xb_ref, ya_ref, yb_ref, cot_ref, params_ref, mix_ref,
    mixed_ref, grad_ref, packed_ref,
    field, weights, depth, normed_bf, grads,
):
    side = own_ref.shape[0]
    lanes = own_ref.shape[2]
    tiles = lanes // LANE
    channels = mix_ref.shape[0]
    pitch = side + 8
    fill_field(field, place_ref, own_ref, xa_ref, xb_ref, ya_ref, yb_ref)
    spread_taps(params_ref, weights)

    def depth_tile(k, _):
        lane0 = pl.multiple_of(k * LANE, LANE)
        for half in range(side // 8):

            def emit(x, value, half=half):
                row = x * side + 8 * half
                depth[row:row + 8, pl.ds(lane0, LANE)] = value

            stencil_tile(field, weights, tiles, side, k, half, False, emit)
        return 0

    lax.fori_loop(0, tiles, depth_tile, 0)

    wide = 256
    copies = wide // channels
    row_id = lax.broadcasted_iota(jnp.int32, (wide, wide), 0) // channels
    col_id = lax.broadcasted_iota(jnp.int32, (wide, wide), 1) // channels
    block = row_id == col_id
    mean_mat = jnp.where(block, 1.0 / channels, 0.0).astype(BF16)
    mix = mix_ref[...].astype(F32)
    mix_row = jnp.concatenate([mix] * copies, axis=1)
    mix_mat = jnp.where(block, jnp.concatenate([mix_row] * copies, axis=0), 0.0).astype(BF16)
    gain = jnp.concatenate([params_ref[27:28, :]] * copies, axis=1)
    rows = 128
    xs = rows // side
    cells = side * side
    gain_sum = jnp.zeros((8, wide), F32)
    for part in range(lanes // wide):
        cols = slice(part * wide, (part + 1) * wide)
        for chunk in range(cells // rows):
            at = slice(chunk * rows, (chunk + 1) * rows)
            planes = slice(chunk * xs, (chunk + 1) * xs)
            dep = depth[at, cols]
            cot = cot_ref[planes, :, cols].reshape(rows, wide)
            mean_sq = jnp.dot((dep * dep).astype(BF16), mean_mat, preferred_element_type=F32)
            inv = lax.rsqrt(mean_sq + EPS)
            normed = dep * inv
            norm_bf = (normed * gain).astype(BF16)
            normed_bf[at, cols] = norm_bf
            branch = jnp.dot(norm_bf, mix_mat, preferred_element_type=F32)
            feat = own_ref[planes, :, cols].reshape(rows, wide).astype(F32)
            mixed_ref[planes, :, cols] = (feat + branch).astype(BF16).reshape(xs, side, wide)
            grad_norm = lax.dot_general(
                cot, mix_mat, (((1,), (1,)), ((), ())), preferred_element_type=F32
            )
            gain_sum = gain_sum + jnp.sum((grad_norm * normed).reshape(rows // 8, 8, wide), axis=0)
            scaled = grad_norm * gain
            mean = jnp.dot((scaled * normed).astype(BF16), mean_mat, preferred_element_type=F32)
            grad = (inv * (scaled - normed * mean)).astype(BF16)
            grad_ref[planes, :, cols] = grad.reshape(xs, side, wide)
            grads[at, cols] = grad.astype(F32)

    mix_sum = jnp.zeros((wide, wide), F32)
    for part in range(lanes // wide):
        cols = slice(part * wide, (part + 1) * wide)
        mix_sum = mix_sum + lax.dot_general(
            normed_bf[:, cols],
            cot_ref[:, :, cols].reshape(cells, wide),
            (((0,), (0,)), ((), ())),
            preferred_element_type=F32,
        )
    grad_mix = mix_sum[:channels, :channels]
    for i in range(1, copies):
        span = slice(i * channels, (i + 1) * channels)
        grad_mix = grad_mix + mix_sum[span, span]
    packed_ref[0:32, :] = jnp.concatenate([grad_mix[:32], grad_mix[32:]], axis=1)

    def tap_tile(k, sums):
        lane0 = pl.multiple_of(k * LANE, LANE)
        sums = list(sums)
        for half in range(side // 8):
            near_grads = {}
            for plane in range(side + 2):
                if plane < side:
                    row = plane * side + 8 * half
                    near_grads[plane] = grads[row:row + 8, pl.ds(lane0, LANE)]
                near = shifted(field, tiles, k, plane, half, pitch)
                for (off_y, off_z), value in near.items():
                    for off_x in range(3):
                        x = plane - off_x
                        if 0 <= x < side:
                            tap = 9 * off_x + 3 * off_y + off_z
                            sums[tap] = sums[tap] + value * near_grads[x]
                near_grads.pop(plane - 2, None)
        return tuple(sums)

    sums = lax.fori_loop(0, tiles, tap_tile, tuple(jnp.zeros((8, LANE), F32) for _ in range(27)))
    gain_row = jnp.sum(gain_sum, axis=0, keepdims=True)
    rows = [jnp.sum(t, axis=0, keepdims=True) for t in sums] + [gain_row[:, :LANE] + gain_row[:, LANE:]]
    rows = jnp.concatenate(rows + [jnp.zeros((4, LANE), F32)], axis=0)
    rows = rows[:, :channels] + rows[:, channels:]
    packed_ref[32:48, :] = jnp.concatenate([rows[:16], rows[16:]], axis=1)


def unpack_kernel(mine_ref, theirs_ref, taps_ref, gain_ref, mix_ref):
    total = mine_ref[...] + theirs_ref[...]
    channels = mix_ref.shape[0]
    mix_ref[0:32, :] = total[:32, :channels]
    mix_ref[32:64, :] = total[:32, channels:]
    taps_ref[0:16, :] = total[32:48, :channels]
    taps_ref[16:27, :] = total[32:43, channels:]
    gain_ref[...] = total[43:44, channels:]


def backward_kernel(
    place_ref, own_ref, xa_ref, xb_ref, ya_ref, yb_ref, cot_ref, params_ref, out_ref, field, weights
):
    side = own_ref.shape[0]
    tiles = own_ref.shape[2] // LANE
    fill_field(field, place_ref, own_ref, xa_ref, xb_ref, ya_ref, yb_ref)
    spread_taps(params_ref, weights)

    def grad_tile(k, _):
        lane0 = pl.multiple_of(k * LANE, LANE)
        first = {}
        for half in range(side // 8):

            def emit(x, value, half=half):
                if half == 0:
                    first[x] = value
                    return
                both = jnp.concatenate([first.pop(x), value], axis=0)
                cot = cot_ref[x, :, pl.ds(lane0, LANE)].astype(F32)
                out_ref[x, :, pl.ds(lane0, LANE)] = (cot + both).astype(BF16)

            stencil_tile(field, weights, tiles, side, k, half, True, emit)
        return 0

    lax.fori_loop(0, tiles, grad_tile, 0)


def swap(low, high, axis):
    count = lax.axis_size(axis)
    odd = lax.axis_index(axis) % 2 == 1
    first = [(i, i ^ 1) for i in range(count) if i ^ 1 < count]
    second = [(i, j) for i in range(count) for j in [((i + 1) ^ 1) - 1] if 0 <= j < count]
    from_first = lax.ppermute(jnp.where(odd, low, high), axis, first)
    from_second = lax.ppermute(jnp.where(odd, high, low), axis, second)
    return from_first, from_second


def edge_exchange(cells):
    xa, xb = swap(cells[0], cells[-1], "gx")
    odd = lax.axis_index("gx") % 2 == 1

    def column(y):
        before = jnp.where(odd, xa[y], xb[y])[None]
        after = jnp.where(odd, xb[y], xa[y])[None]
        return jnp.concatenate([before, cells[:, y], after], axis=0)

    ya, yb = swap(column(0), column(-1), "gy")
    return xa, xb, ya, yb


def sum_over_devices(part, finish):
    steps = []
    for axis in ("gx", "gy"):
        count = lax.axis_size(axis)
        bit = 1
        while bit < count:
            steps.append((axis, [(i, i ^ bit) for i in range(count)]))
            bit *= 2
    for axis, pairs in steps[:-1]:
        part = part + lax.ppermute(part, axis, pairs)
    axis, pairs = steps[-1]
    return finish(part, lax.ppermute(part, axis, pairs))


def shards(features, slot_map, tap_weights, gain, mix_weight, cotangent):
    side, _, _, lanes = features.shape
    channels = gain.shape[0]
    levels = slot_map.shape[2]
    tiles = lanes // LANE
    cells = features.reshape(side, side, lanes)
    cot = cotangent.reshape(side, side, lanes)
    place = jnp.sum(jnp.where(slot_map >= 0, jnp.arange(levels, dtype=jnp.int32), 0), axis=2)
    params = jnp.concatenate([tap_weights, gain[None], jnp.zeros((4, channels), F32)], axis=0)
    field = pltpu.VMEM((2 * tiles + 1, (side + 2) * (side + 8) + 8, LANE), F32)
    weights = pltpu.VMEM((27, 8, LANE), F32)
    smem = pl.BlockSpec(memory_space=pltpu.SMEM)
    vmem = pl.BlockSpec(memory_space=pltpu.VMEM)
    compiler_params = pltpu.CompilerParams(vmem_limit_bytes=40 * 1024 * 1024)
    block = jax.ShapeDtypeStruct((side, side, lanes), BF16)

    edges = edge_exchange(cells)
    mixed, grad_depth, packed = pl.pallas_call(
        forward_kernel,
        out_shape=(block, block, jax.ShapeDtypeStruct((48, LANE), F32)),
        in_specs=[smem] + [vmem] * 8,
        out_specs=(vmem, vmem, vmem),
        scratch_shapes=[
            field,
            weights,
            pltpu.VMEM((side * side, lanes), F32),
            pltpu.VMEM((side * side, lanes), BF16),
            pltpu.VMEM((side * side, lanes), F32),
        ],
        compiler_params=compiler_params,
        cost_estimate=pl.CostEstimate(flops=20_000_000, bytes_accessed=2_000_000, transcendentals=0),
        name="forward",
    )(place, cells, *edges, cot, params, mix_weight)

    grad_edges = edge_exchange(grad_depth)
    grad_features = pl.pallas_call(
        backward_kernel,
        out_shape=block,
        in_specs=[smem] + [vmem] * 7,
        out_specs=vmem,
        scratch_shapes=[field, weights],
        compiler_params=compiler_params,
        cost_estimate=pl.CostEstimate(flops=20_000_000, bytes_accessed=2_000_000, transcendentals=0),
        name="backward",
    )(place, grad_depth, *grad_edges, cot, params)

    def finish(mine, theirs):
        return pl.pallas_call(
            unpack_kernel,
            out_shape=(
                jax.ShapeDtypeStruct((27, channels), F32),
                jax.ShapeDtypeStruct((1, channels), F32),
                jax.ShapeDtypeStruct((channels, channels), F32),
            ),
            in_specs=[vmem, vmem],
            out_specs=(vmem, vmem, vmem),
            name="unpack",
        )(mine, theirs)

    grad_taps, grad_gain, grad_mix = sum_over_devices(packed, finish)
    shape = features.shape
    return (mixed.reshape(shape), grad_features.reshape(shape), grad_taps, grad_gain.reshape(channels), grad_mix)


def solution(mesh):
    return jax.shard_map(
        shards,
        mesh=mesh,
        in_specs=(P("gx", "gy", None, None), P(), P(), P(), P(), P("gx", "gy", None, None)),
        out_specs=(P("gx", "gy", None, None), P("gx", "gy", None, None), P(), P(), P()),
        check_vma=False,
    )
```

```python
import jax
import jax.numpy as jnp
from jax import lax
from jax.experimental import pallas as pl
from jax.experimental.pallas import tpu as pltpu
from jax.sharding import PartitionSpec as P

EPS = 1e-05
LANE = 128
WIDE = 256
PARTS = 4
F32 = jnp.float32
BF16 = jnp.bfloat16


def level_masks(place_ref, off_x, off_y):
    count_x, count_y = place_ref.shape
    x, y = lax.axis_index("gx"), lax.axis_index("gy")
    near_x = jnp.clip(x + off_x, 0, count_x - 1)
    near_y = jnp.clip(y + off_y, 0, count_y - 1)
    d = place_ref[near_x, near_y] - place_ref[x, y]
    return tuple(jnp.where(d == want, 1.0, 0.0).astype(F32) for want in (0, -1, 1))


def plane_tiles(load, total, first, count, masks):
    rolled = {}

    def turned(k):
        if k not in rolled:
            rolled[k] = pltpu.roll(load(k), LANE // 2, 1)
        return rolled[k]

    shape = load(first).shape
    low = lax.broadcasted_iota(jnp.int32, shape, 1) < LANE // 2
    zero = jnp.zeros(shape, F32)
    offset = []
    for j in range(first, first + count + 1):
        if masks is None:
            offset.append(jnp.where(low, turned(j - 1) if j else zero, turned(j) if j < total else zero))
        elif j == 0:
            offset.append(jnp.where(low, turned(total - 1) * masks[1], turned(0) * masks[0]))
        elif j == total:
            offset.append(jnp.where(low, turned(total - 1) * masks[0], turned(0) * masks[2]))
        else:
            offset.append(jnp.where(low, turned(j - 1), turned(j)) * masks[0])
    aligned = [load(k) for k in range(first, first + count)]
    if masks is not None:
        aligned = [t * masks[0] for t in aligned]
    return aligned + offset


def fill_field(field, first, count, place_ref, own_ref, xa_ref, xb_ref, ya_ref, yb_ref):
    side = own_ref.shape[0]
    total = own_ref.shape[2] // LANE
    pitch = side + 8

    def loader(rows):
        return lambda k: rows[:, k * LANE:(k + 1) * LANE].astype(F32)

    def own_plane(x, _):
        base = pl.multiple_of((x + 1) * pitch + 8, 8)
        for i, t in enumerate(plane_tiles(loader(own_ref[x]), total, first, count, None)):
            field[i, pl.ds(base, side), :] = t
        return 0

    lax.fori_loop(0, side, own_plane, 0)

    odd = lax.axis_index("gx") % 2
    lower = level_masks(place_ref, -1, 0)
    upper = level_masks(place_ref, 1, 0)
    for ref, low_side in ((xa_ref, odd == 1), (xb_ref, odd == 0)):
        masks = tuple(jnp.where(low_side, a, b) for a, b in zip(lower, upper))
        base = pl.multiple_of(jnp.where(low_side, 8, (side + 1) * pitch + 8), 8)
        for i, t in enumerate(plane_tiles(loader(ref[...]), total, first, count, masks)):
            field[i, pl.ds(base, side), :] = t

    odd = lax.axis_index("gy") % 2
    for low_side in (True, False):
        from_a = odd == (1 if low_side else 0)
        edge = jnp.where(from_a, ya_ref[...].astype(F32), yb_ref[...].astype(F32))
        rows = edge.shape[0]
        shift = 7 if low_side else pitch
        row_id = lax.broadcasted_iota(jnp.int32, (rows, LANE), 0)
        corners = [level_masks(place_ref, off, -1 if low_side else 1) for off in (-1, 0, 1)]
        masks = tuple(
            jnp.where(row_id == 0, a, jnp.where(row_id == rows - 1, c, b)) for a, b, c in zip(*corners)
        )
        for i, t in enumerate(plane_tiles(loader(edge), total, first, count, masks)):
            for start in range(0, rows, 8):
                size = min(8, rows - start)
                field[i, pl.ds(start * pitch + shift, size, stride=pitch), :] = t[start:start + size]


def shifted(field, count, k, plane, half, pitch):
    found = {}
    for off_y in range(3):
        row = 8 * half + (plane * pitch + 7 + off_y)
        for off_z in range(3):
            i = (count + k, k, count + k + 1)[off_z]
            found[off_y, off_z] = field[i, pl.ds(row, 8), :]
    return found


def stencil(field, weights, count, side, flip, emit):
    pitch = side + 8
    halves = side // 8

    def body(step, _):
        k, half = step // halves, step % halves
        taps = [weights[26 - t if flip else t] for t in range(27)]
        sums = {}
        for plane in range(side + 2):
            near = shifted(field, count, k, plane, half, pitch)
            for off_x in range(3):
                x = plane - off_x
                if not 0 <= x < side:
                    continue
                for (off_y, off_z), value in near.items():
                    term = value * taps[9 * off_x + 3 * off_y + off_z]
                    sums[x] = sums[x] + term if x in sums else term
            done = plane - 2
            if done >= 0:
                emit(k, pl.multiple_of(8 * half + done * side, 8), sums.pop(done))
        return 0

    lax.fori_loop(0, count * halves, body, 0)


def spread_taps(taps_ref, weights):
    wide = jnp.concatenate([taps_ref[...], taps_ref[...]], axis=1)
    for tap in range(27):
        weights[tap] = jnp.broadcast_to(wide[tap:tap + 1], (8, LANE))


def y_edges_kernel(cells_ref, ylo_ref, yhi_ref):
    side, _, lanes = cells_ref.shape
    row = lax.broadcasted_iota(jnp.int32, (2 * side, side * side), 0)
    col = lax.broadcasted_iota(jnp.int32, (2 * side, side * side), 1)
    wanted = jnp.where(row < side, row * side, (row - side) * side + side - 1)
    pick = jnp.where(col == wanted, 1.0, 0.0).astype(BF16)
    flat = cells_ref[...].reshape(side * side, lanes)
    found = jnp.dot(pick, flat, preferred_element_type=F32).astype(BF16)
    ylo_ref[...] = found[:side]
    yhi_ref[...] = found[side:]


def x_edges(cells):
    odd = lax.axis_index("gx") % 2 == 1
    return jnp.where(odd, cells[0], cells[-1]), jnp.where(odd, cells[-1], cells[0])


def forward_kernel(
    place_ref, own_ref, xa_ref, xb_ref, ya_ref, yb_ref, cot_ref, taps_hbm, gain_hbm, mix_hbm,
    mixed_ref, grad_ref, packed_ref, gxa_ref, gxb_ref, gylo_ref, gyhi_ref, weights,
    field, depth, normed_bf, grads, taps_ref, gain_ref, mix_ref, arrived,
):
    side = own_ref.shape[0]
    lanes = own_ref.shape[2]
    tiles = lanes // LANE
    channels = mix_ref.shape[0]
    pitch = side + 8
    halves = side // 8
    cells = side * side
    copies = [
        pltpu.make_async_copy(src, dst, arrived.at[i])
        for i, (src, dst) in enumerate(((taps_hbm, taps_ref), (gain_hbm, gain_ref), (mix_hbm, mix_ref)))
    ]
    for copy in copies:
        copy.start()
    fill_field(field, 0, tiles, place_ref, own_ref, xa_ref, xb_ref, ya_ref, yb_ref)
    for copy in copies:
        copy.wait()
    spread_taps(taps_ref, weights)

    def emit(k, row, value):
        depth[k, pl.ds(row, 8), :] = value

    stencil(field, weights, tiles, side, False, emit)

    copies = WIDE // channels
    row_id = lax.broadcasted_iota(jnp.int32, (WIDE, WIDE), 0) // channels
    col_id = lax.broadcasted_iota(jnp.int32, (WIDE, WIDE), 1) // channels
    block = row_id == col_id
    mean_mat = jnp.where(block, 1.0 / channels, 0.0).astype(BF16)
    mix = mix_ref[...].astype(F32)
    mix_row = jnp.concatenate([mix] * copies, axis=1)
    mix_mat = jnp.where(block, jnp.concatenate([mix_row] * copies, axis=0), 0.0).astype(BF16)
    gain = jnp.concatenate([gain_ref[...]] * copies, axis=1)
    rows = 128
    xs = rows // side
    gain_sum = jnp.zeros((8, WIDE), F32)
    for part in range(lanes // WIDE):
        cols = slice(part * WIDE, (part + 1) * WIDE)
        for chunk in range(cells // rows):
            at = slice(chunk * rows, (chunk + 1) * rows)
            planes = slice(chunk * xs, (chunk + 1) * xs)
            dep = jnp.concatenate([depth[2 * part, at, :], depth[2 * part + 1, at, :]], axis=1)
            cot = cot_ref[planes, :, cols].reshape(rows, WIDE)
            mean_sq = jnp.dot((dep * dep).astype(BF16), mean_mat, preferred_element_type=F32)
            inv = lax.rsqrt(mean_sq + EPS)
            normed = dep * inv
            norm_bf = (normed * gain).astype(BF16)
            normed_bf[at, cols] = norm_bf
            branch = jnp.dot(norm_bf, mix_mat, preferred_element_type=F32)
            feat = own_ref[planes, :, cols].reshape(rows, WIDE).astype(F32)
            mixed_ref[planes, :, cols] = (feat + branch).astype(BF16).reshape(xs, side, WIDE)
            grad_norm = lax.dot_general(
                cot, mix_mat, (((1,), (1,)), ((), ())), preferred_element_type=F32
            )
            gain_sum = gain_sum + jnp.sum((grad_norm * normed).reshape(rows // 8, 8, WIDE), axis=0)
            scaled = grad_norm * gain
            mean = jnp.dot((scaled * normed).astype(BF16), mean_mat, preferred_element_type=F32)
            grad = (inv * (scaled - normed * mean)).astype(BF16)
            grad_ref[planes, :, cols] = grad.reshape(xs, side, WIDE)
            wide_grad = grad.astype(F32)
            grads[2 * part, at, :] = wide_grad[:, :LANE]
            grads[2 * part + 1, at, :] = wide_grad[:, LANE:]
    odd = lax.axis_index("gx") % 2
    gxa_ref[...] = grad_ref[jnp.where(odd == 1, 0, side - 1)]
    gxb_ref[...] = grad_ref[jnp.where(odd == 1, side - 1, 0)]
    y_edges_kernel(grad_ref, gylo_ref, gyhi_ref)

    mix_sum = jnp.zeros((WIDE, WIDE), F32)
    for part in range(lanes // WIDE):
        cols = slice(part * WIDE, (part + 1) * WIDE)
        mix_sum = mix_sum + lax.dot_general(
            normed_bf[:, cols],
            cot_ref[:, :, cols].reshape(cells, WIDE),
            (((0,), (0,)), ((), ())),
            preferred_element_type=F32,
        )
    grad_mix = mix_sum[:channels, :channels]
    for i in range(1, copies):
        span = slice(i * channels, (i + 1) * channels)
        grad_mix = grad_mix + mix_sum[span, span]
    packed_ref[0:32, :] = jnp.concatenate([grad_mix[:32], grad_mix[32:]], axis=1)

    def tap_tile(step, sums):
        k, half = step // halves, step % halves
        sums = list(sums)
        near_grads = {}
        for plane in range(side + 2):
            if plane < side:
                near_grads[plane] = grads[k, pl.ds(pl.multiple_of(8 * half + plane * side, 8), 8), :]
            near = shifted(field, tiles, k, plane, half, pitch)
            for (off_y, off_z), value in near.items():
                for off_x in range(3):
                    x = plane - off_x
                    if 0 <= x < side:
                        tap = 9 * off_x + 3 * off_y + off_z
                        sums[tap] = sums[tap] + value * near_grads[x]
            near_grads.pop(plane - 2, None)
        return tuple(sums)

    sums = lax.fori_loop(
        0, tiles * halves, tap_tile, tuple(jnp.zeros((8, LANE), F32) for _ in range(27))
    )
    gain_row = jnp.sum(gain_sum, axis=0, keepdims=True)
    rows = [jnp.sum(t, axis=0, keepdims=True) for t in sums] + [gain_row[:, :LANE] + gain_row[:, LANE:]]
    rows = jnp.concatenate(rows + [jnp.zeros((4, LANE), F32)], axis=0)
    rows = rows[:, :channels] + rows[:, channels:]
    packed_ref[32:48, :] = jnp.concatenate([rows[:16], rows[16:]], axis=1)


def backward_kernel(
    first, count,
    place_ref, own_ref, xa_ref, xb_ref, ya_ref, yb_ref, cot_ref, weights, *rest,
):
    out_ref, field, sums = rest[-3:]
    side = own_ref.shape[0]
    fill_field(field, first, count, place_ref, own_ref, xa_ref, xb_ref, ya_ref, yb_ref)

    def emit(k, row, value):
        sums[k, pl.ds(row, 8), :] = value

    stencil(field, weights, count, side, True, emit)
    for x in range(side):
        at = slice(x * side, (x + 1) * side)
        for k in range(count):
            cols = slice(k * LANE, (k + 1) * LANE)
            cot = cot_ref[x, :, (first + k) * LANE:(first + k + 1) * LANE].astype(F32)
            out_ref[x, :, cols] = (cot + sums[k, at, :]).astype(BF16)


def unpack_kernel(mine_ref, theirs_ref, taps_ref, gain_ref, mix_ref):
    total = mine_ref[...] + theirs_ref[...]
    channels = mix_ref.shape[0]
    mix_ref[0:32, :] = total[:32, :channels]
    mix_ref[32:64, :] = total[:32, channels:]
    taps_ref[0:16, :] = total[32:48, :channels]
    taps_ref[16:27, :] = total[32:43, channels:]
    gain_ref[...] = total[43:44, channels:]


def swap(to_first, to_second, axis):
    count = lax.axis_size(axis)
    first = [(i, i ^ 1) for i in range(count) if i ^ 1 < count]
    second = [(i, j) for i in range(count) for j in [((i + 1) ^ 1) - 1] if 0 <= j < count]
    return lax.ppermute(to_first, axis, first), lax.ppermute(to_second, axis, second)


def y_messages(xa, xb, ylo, yhi):
    odd_x = lax.axis_index("gx") % 2 == 1
    odd_y = lax.axis_index("gy") % 2 == 1

    def column(edge, y):
        before = jnp.where(odd_x, xa[y], xb[y])[None]
        after = jnp.where(odd_x, xb[y], xa[y])[None]
        return jnp.concatenate([before, edge, after], axis=0)

    low, high = column(ylo, 0), column(yhi, -1)
    return jnp.where(odd_y, low, high), jnp.where(odd_y, high, low)


def sum_steps():
    steps = []
    for axis in ("gx", "gy"):
        count = lax.axis_size(axis)
        bit = 1
        while bit < count:
            steps.append((axis, [(i, i ^ bit) for i in range(count)]))
            bit *= 2
    return steps


def shards(features, slot_map, tap_weights, gain, mix_weight, cotangent):
    side, _, _, lanes = features.shape
    channels = gain.shape[0]
    levels = slot_map.shape[2]
    tiles = lanes // LANE
    count = tiles // PARTS
    field_rows = (side + 2) * (side + 8) + 8
    cells = features.reshape(side, side, lanes)
    cot = cotangent.reshape(side, side, lanes)
    place = jnp.sum(jnp.where(slot_map >= 0, jnp.arange(levels, dtype=jnp.int32), 0), axis=2)
    smem = pl.BlockSpec(memory_space=pltpu.SMEM)
    vmem = pl.BlockSpec(memory_space=pltpu.VMEM)
    compiler_params = pltpu.CompilerParams(vmem_limit_bytes=40 * 1024 * 1024)
    block = jax.ShapeDtypeStruct((side, side, lanes), BF16)
    edge = jax.ShapeDtypeStruct((side, lanes), BF16)
    taps_type = jax.ShapeDtypeStruct((27, channels), F32)
    weights_type = jax.ShapeDtypeStruct((27, 8, LANE), F32)
    gain_type = jax.ShapeDtypeStruct((1, channels), F32)

    xa, xb = swap(*x_edges(cells), "gx")
    ylo, yhi = pl.pallas_call(
        y_edges_kernel,
        out_shape=(edge, edge),
        in_specs=[vmem],
        out_specs=(vmem, vmem),
        compiler_params=compiler_params,
        name="y_edges",
    )(cells)
    ya, yb = swap(*y_messages(xa, xb, ylo, yhi), "gy")

    mixed, grad_depth, part, gxa, gxb, gylo, gyhi, weights = pl.pallas_call(
        forward_kernel,
        out_shape=(block, block, jax.ShapeDtypeStruct((48, LANE), F32), edge, edge, edge, edge, weights_type),
        in_specs=[smem] + [vmem] * 6 + [pl.BlockSpec(memory_space=pltpu.HBM)] * 3,
        out_specs=(vmem,) * 8,
        scratch_shapes=[
            pltpu.VMEM((2 * tiles + 1, field_rows, LANE), F32),
            pltpu.VMEM((tiles, side * side, LANE), F32),
            pltpu.VMEM((side * side, lanes), BF16),
            pltpu.VMEM((tiles, side * side, LANE), F32),
            pltpu.VMEM(taps_type.shape, F32),
            pltpu.VMEM(gain_type.shape, F32),
            pltpu.VMEM(mix_weight.shape, BF16),
            pltpu.SemaphoreType.DMA((3,)),
        ],
        compiler_params=compiler_params,
        cost_estimate=pl.CostEstimate(flops=20_000_000, bytes_accessed=2_000_000, transcendentals=0),
        name="forward",
    )(place, cells, xa, xb, ya, yb, cot, tap_weights, gain.reshape(1, channels), mix_weight)

    def backward_part(index, edges, so_far):
        block_spec = pl.BlockSpec((side, side, lanes // PARTS), lambda i: (0, 0, index))

        def kernel(*refs):
            backward_kernel(index * count, count, *refs)

        operands = (place, grad_depth, *edges, cot, weights) + (() if so_far is None else (so_far,))
        return pl.pallas_call(
            kernel,
            grid=(1,),
            out_shape=block,
            in_specs=[smem] + [vmem] * 7 + ([] if so_far is None else [pl.BlockSpec(memory_space=pl.ANY)]),
            out_specs=block_spec,
            scratch_shapes=[
                pltpu.VMEM((2 * count + 1, field_rows, LANE), F32),
                pltpu.VMEM((count, side * side, LANE), F32),
            ],
            input_output_aliases={} if so_far is None else {8: 0},
            compiler_params=compiler_params,
            cost_estimate=pl.CostEstimate(flops=5_000_000, bytes_accessed=500_000, transcendentals=0),
            name="backward" + str(index),
        )(*operands)

    steps = sum_steps()
    gxa, gxb = swap(gxa, gxb, "gx")
    part = part + lax.ppermute(part, *steps[0])
    part, to_a, to_b = lax.optimization_barrier((part, *y_messages(gxa, gxb, gylo, gyhi)))
    gya, gyb = swap(to_a, to_b, "gy")
    part = part + lax.ppermute(part, *steps[1])
    part, gya, gyb = lax.optimization_barrier((part, gya, gyb))
    edges = (gxa, gxb, gya, gyb)
    grad_features = None
    index = 0
    for step in steps[2:-1]:
        theirs = lax.ppermute(part, *step)
        if index < PARTS:
            grad_features = backward_part(index, edges, grad_features)
            index += 1
            part, grad_features = lax.optimization_barrier((part + theirs, grad_features))
        else:
            part = part + theirs
    theirs = lax.ppermute(part, *steps[-1])
    while index < PARTS:
        grad_features = backward_part(index, edges, grad_features)
        index += 1

    grad_taps, grad_gain, grad_mix = pl.pallas_call(
        unpack_kernel,
        out_shape=(taps_type, gain_type, jax.ShapeDtypeStruct((channels, channels), F32)),
        in_specs=[vmem, vmem],
        out_specs=(vmem, vmem, vmem),
        name="unpack",
    )(part, theirs)
    shape = features.shape
    return (mixed.reshape(shape), grad_features.reshape(shape), grad_taps, grad_gain.reshape(channels), grad_mix)


def solution(mesh):
    return jax.shard_map(
        shards,
        mesh=mesh,
        in_specs=(P("gx", "gy", None, None), P(), P(), P(), P(), P("gx", "gy", None, None)),
        out_specs=(P("gx", "gy", None, None), P("gx", "gy", None, None), P(), P(), P()),
        check_vma=False,
    )
```

```python
import jax
import jax.numpy as jnp
from jax import lax
from jax.experimental import pallas as pl
from jax.experimental.pallas import tpu as pltpu
from jax.sharding import PartitionSpec as P

EPS = 1e-05
LANE = 128
WIDE = 256
F32 = jnp.float32
BF16 = jnp.bfloat16


def level_masks(slot_map, side):
    levels = slot_map.shape[2]
    rows = side + 8
    row = jnp.arange(rows, dtype=jnp.int32)[None, :, None, None]
    edge = jnp.arange(4, dtype=jnp.int32)[:, None, None, None]
    along = jnp.where(row == 0, -1, jnp.where(row == side + 1, 1, 0))
    off_x = jnp.where(edge == 0, -1, jnp.where(edge == 1, 1, along))
    off_y = jnp.where(edge == 2, -1, jnp.where(edge == 3, 1, 0))
    place = jnp.sum(jnp.where(slot_map >= 0, jnp.arange(levels, dtype=jnp.int32), 0), axis=2)
    from_x = jnp.arange(slot_map.shape[0], dtype=jnp.int32)[:, None] - lax.axis_index("gx")
    from_y = jnp.arange(slot_map.shape[1], dtype=jnp.int32)[None, :] - lax.axis_index("gy")
    near = jnp.where((from_x == off_x) & (from_y == off_y), place, 0)
    own = jnp.where((from_x == 0) & (from_y == 0), place, 0)
    d = jnp.sum(near - own, axis=(2, 3))
    masks = jnp.stack([d == 0, d == -1, d == 1], axis=1).astype(F32)
    return jnp.broadcast_to(masks.reshape(12, rows, 1), (12, rows, LANE))


def plane_tiles(load, total, masks):
    low = lax.broadcasted_iota(jnp.int32, load(0).shape, 1) < LANE // 2
    zero = jnp.zeros(load(0).shape, F32)
    aligned = [load(k) for k in range(total)]
    turned = [pltpu.roll(t, LANE // 2, 1) for t in aligned]
    between = [jnp.where(low, turned[j - 1], turned[j]) for j in range(1, total)]
    if masks is None:
        return aligned + [jnp.where(low, zero, turned[0])] + between + [jnp.where(low, turned[-1], zero)]
    same, below, above = masks
    first = jnp.where(low, turned[-1] * below, turned[0] * same)
    last = jnp.where(low, turned[-1] * same, turned[0] * above)
    return [t * same for t in aligned] + [first] + [t * same for t in between] + [last]


def loader(rows):
    return lambda k: rows[:, k * LANE:(k + 1) * LANE].astype(F32)


def column_starts(side, shift):
    pitch = side + 8
    for start in range(0, side + 2, 8):
        size = min(8, side + 2 - start)
        yield start, size, pl.ds(start * pitch + shift, size, stride=pitch)


def own_part(own_ref, field, weights, sums, flip):
    side = own_ref.shape[0]
    tiles = own_ref.shape[2] // LANE
    pitch = side + 8

    def own_plane(x, _):
        base = pl.multiple_of((x + 1) * pitch + 8, 8)
        for i, t in enumerate(plane_tiles(loader(own_ref[x]), tiles, None)):
            field[i, pl.ds(base, side), :] = t
        return 0

    lax.fori_loop(0, side, own_plane, 0)
    for i in range(2 * tiles + 1):
        for shift in (7, pitch):
            for _, size, at in column_starts(side, shift):
                field[i, at, :] = jnp.zeros((size, LANE), F32)

    def tile(k, _):
        taps = [weights[26 - t if flip else t] for t in range(27)]
        for half in range(side // 8):
            part = {}
            for plane in range(1, side + 1):
                near = shifted(field, tiles, k, plane, half, pitch)
                for off_x in range(3):
                    x = plane - off_x
                    if not 0 <= x < side:
                        continue
                    for (off_y, off_z), value in near.items():
                        term = value * taps[9 * off_x + 3 * off_y + off_z]
                        part[x] = part[x] + term if x in part else term
                done = plane - 2
                for x in [done, done + 1] if plane == side else [done]:
                    if x >= 0:
                        sums[k, x * side + 8 * half:x * side + 8 * half + 8, :] = part.pop(x)
        return 0

    lax.fori_loop(0, tiles, tile, 0)


def halo_part(xlo_ref, xhi_ref, ylo_ref, yhi_ref, masks_ref, field, weights, sums, flip):
    side, lanes = xlo_ref.shape
    tiles = lanes // LANE
    pitch = side + 8

    def place(i, ref):
        rows = ref.shape[0]
        masks = tuple(masks_ref[3 * i + m, :rows, :] for m in range(3))
        return plane_tiles(loader(ref[...]), tiles, masks)

    for i, ref, plane in ((0, xlo_ref, 0), (1, xhi_ref, side + 1)):
        for j, t in enumerate(place(i, ref)):
            field[j, plane * pitch + 8:plane * pitch + 8 + side, :] = t

    def x_tile(k, _):
        for plane, off_x, x in ((0, 0, 0), (side + 1, 2, side - 1)):
            for half in range(side // 8):
                row = x * side + 8 * half
                total = sums[k, row:row + 8, :]
                for (off_y, off_z), value in shifted(field, tiles, k, plane, half, pitch).items():
                    tap = 9 * off_x + 3 * off_y + off_z
                    total = total + value * weights[26 - tap if flip else tap]
                sums[k, row:row + 8, :] = total
        return 0

    lax.fori_loop(0, tiles, x_tile, 0)

    for i, ref, shift in ((2, ylo_ref, 7), (3, yhi_ref, pitch)):
        for j, t in enumerate(place(i, ref)):
            for start, size, at in column_starts(side, shift):
                field[j, at, :] = t[start:start + size]

    def y_tile(k, _):
        for shift, off_y, y in ((7, 0, 0), (pitch, 2, side - 1)):
            for x in range(0, side, 8):
                at = pl.ds(x * side + y, 8, stride=side)
                total = sums[k, at, :]
                for off_x in range(3):
                    for off_z in range(3):
                        i = (tiles + k, k, tiles + k + 1)[off_z]
                        tap = 9 * off_x + 3 * off_y + off_z
                        value = field[i, pl.ds((x + off_x) * pitch + shift, 8, stride=pitch), :]
                        total = total + value * weights[26 - tap if flip else tap]
                sums[k, at, :] = total
        return 0

    lax.fori_loop(0, tiles, y_tile, 0)


def shifted(field, tiles, k, plane, half, pitch):
    found = {}
    for off_y in range(3):
        row = plane * pitch + 7 + 8 * half + off_y
        for off_z in range(3):
            i = (tiles + k, k, tiles + k + 1)[off_z]
            found[off_y, off_z] = field[i, row:row + 8, :]
    return found


def y_edges_kernel(cells_ref, ylo_ref, yhi_ref):
    side, _, lanes = cells_ref.shape
    row = lax.broadcasted_iota(jnp.int32, (2 * side, side * side), 0)
    col = lax.broadcasted_iota(jnp.int32, (2 * side, side * side), 1)
    wanted = jnp.where(row < side, row * side, (row - side) * side + side - 1)
    pick = jnp.where(col == wanted, 1.0, 0.0).astype(BF16)
    flat = cells_ref[...].reshape(side * side, lanes)
    found = jnp.dot(pick, flat, preferred_element_type=F32).astype(BF16)
    ylo_ref[...] = found[:side]
    yhi_ref[...] = found[side:]


def x_edges(cells):
    odd = lax.axis_index("gx") % 2 == 1
    return jnp.where(odd, cells[0], cells[-1]), jnp.where(odd, cells[-1], cells[0])


def own_forward_kernel(
    own_ref, cot_ref, params_ref,
    field, depth, grad_norm, weights, mean_mat_ref, mix_mat_ref, gain_wide_ref,
):
    channels = params_ref.shape[1]
    side, _, lanes = own_ref.shape
    wide = jnp.concatenate([params_ref[channels:, :], params_ref[channels:, :]], axis=1)
    for tap in range(27):
        weights[tap] = jnp.broadcast_to(wide[tap:tap + 1], (8, LANE))
    own_part(own_ref, field, weights, depth, False)
    copies = WIDE // channels
    row_id = lax.broadcasted_iota(jnp.int32, (WIDE, WIDE), 0) // channels
    col_id = lax.broadcasted_iota(jnp.int32, (WIDE, WIDE), 1) // channels
    block = row_id == col_id
    mean_mat_ref[...] = jnp.where(block, 1.0 / channels, 0.0).astype(BF16)
    mix = params_ref[:channels, :]
    mix_row = jnp.concatenate([mix] * copies, axis=1)
    mix_mat = jnp.where(block, jnp.concatenate([mix_row] * copies, axis=0), 0.0).astype(BF16)
    mix_mat_ref[...] = mix_mat
    gain_wide_ref[...] = jnp.concatenate([params_ref[channels + 27:channels + 28, :]] * copies, axis=1)
    for part in range(lanes // WIDE):
        cols = slice(part * WIDE, (part + 1) * WIDE)
        grad_norm[:, cols] = lax.dot_general(
            cot_ref[:, :, cols].reshape(side * side, WIDE), mix_mat,
            (((1,), (1,)), ((), ())), preferred_element_type=F32,
        )


def forward_kernel(
    field, depth, grad_norm_ref, weights, mean_mat_ref, mix_mat_ref, gain_wide_ref,
    xlo_ref, xhi_ref, ylo_ref, yhi_ref, masks_ref, own_ref, cot_ref,
    field_out_ref, depth_out_ref, mixed_ref, grad_ref, packed_ref, gxa_ref, gxb_ref, gylo_ref, gyhi_ref,
    normed_bf, grads,
):
    side = own_ref.shape[0]
    lanes = own_ref.shape[2]
    tiles = lanes // LANE
    channels = packed_ref.shape[1] // 2
    pitch = side + 8
    cells = side * side
    halo_part(xlo_ref, xhi_ref, ylo_ref, yhi_ref, masks_ref, field, weights, depth, False)

    copies = WIDE // channels
    mean_mat = mean_mat_ref[...]
    mix_mat = mix_mat_ref[...]
    gain = gain_wide_ref[...]
    rows = 128
    xs = rows // side
    gain_sum = jnp.zeros((8, WIDE), F32)
    for part in range(lanes // WIDE):
        cols = slice(part * WIDE, (part + 1) * WIDE)
        for chunk in range(cells // rows):
            at = slice(chunk * rows, (chunk + 1) * rows)
            planes = slice(chunk * xs, (chunk + 1) * xs)
            dep = jnp.concatenate([depth[2 * part, at, :], depth[2 * part + 1, at, :]], axis=1)
            mean_sq = jnp.dot((dep * dep).astype(BF16), mean_mat, preferred_element_type=F32)
            inv = lax.rsqrt(mean_sq + EPS)
            normed = dep * inv
            norm_bf = (normed * gain).astype(BF16)
            normed_bf[at, cols] = norm_bf
            branch = jnp.dot(norm_bf, mix_mat, preferred_element_type=F32)
            feat = own_ref[planes, :, cols].reshape(rows, WIDE).astype(F32)
            mixed_ref[planes, :, cols] = (feat + branch).astype(BF16).reshape(xs, side, WIDE)
            grad_norm = grad_norm_ref[at, cols]
            gain_sum = gain_sum + jnp.sum((grad_norm * normed).reshape(rows // 8, 8, WIDE), axis=0)
            scaled = grad_norm * gain
            mean = jnp.dot((scaled * normed).astype(BF16), mean_mat, preferred_element_type=F32)
            grad = (inv * (scaled - normed * mean)).astype(BF16)
            grad_ref[planes, :, cols] = grad.reshape(xs, side, WIDE)
            wide_grad = grad.astype(F32)
            grads[2 * part, at, :] = wide_grad[:, :LANE]
            grads[2 * part + 1, at, :] = wide_grad[:, LANE:]
    odd = lax.axis_index("gx") % 2
    gxa_ref[...] = grad_ref[jnp.where(odd == 1, 0, side - 1)]
    gxb_ref[...] = grad_ref[jnp.where(odd == 1, side - 1, 0)]
    y_edges_kernel(grad_ref, gylo_ref, gyhi_ref)

    mix_sum = jnp.zeros((WIDE, WIDE), F32)
    for part in range(lanes // WIDE):
        cols = slice(part * WIDE, (part + 1) * WIDE)
        mix_sum = mix_sum + lax.dot_general(
            normed_bf[:, cols],
            cot_ref[:, :, cols].reshape(cells, WIDE),
            (((0,), (0,)), ((), ())),
            preferred_element_type=F32,
        )
    grad_mix = mix_sum[:channels, :channels]
    for i in range(1, copies):
        span = slice(i * channels, (i + 1) * channels)
        grad_mix = grad_mix + mix_sum[span, span]
    packed_ref[0:32, :] = jnp.concatenate([grad_mix[:32], grad_mix[32:]], axis=1)

    def tap_tile(k, sums):
        sums = list(sums)
        for half in range(side // 8):
            near_grads = {}
            for plane in range(side + 2):
                if plane < side:
                    row = plane * side + 8 * half
                    near_grads[plane] = grads[k, row:row + 8, :]
                near = shifted(field, tiles, k, plane, half, pitch)
                for (off_y, off_z), value in near.items():
                    for off_x in range(3):
                        x = plane - off_x
                        if 0 <= x < side:
                            tap = 9 * off_x + 3 * off_y + off_z
                            sums[tap] = sums[tap] + value * near_grads[x]
                near_grads.pop(plane - 2, None)
        return tuple(sums)

    sums = lax.fori_loop(0, tiles, tap_tile, tuple(jnp.zeros((8, LANE), F32) for _ in range(27)))
    gain_row = jnp.sum(gain_sum, axis=0, keepdims=True)
    rows = [jnp.sum(t, axis=0, keepdims=True) for t in sums] + [gain_row[:, :LANE] + gain_row[:, LANE:]]
    rows = jnp.concatenate(rows + [jnp.zeros((4, LANE), F32)], axis=0)
    rows = rows[:, :channels] + rows[:, channels:]
    packed_ref[32:48, :] = jnp.concatenate([rows[:16], rows[16:]], axis=1)


def own_backward_kernel(own_ref, weights, field, sums):
    own_part(own_ref, field, weights, sums, True)


def backward_kernel(
    field, sums, weights, xlo_ref, xhi_ref, ylo_ref, yhi_ref, masks_ref, cot_ref,
    field_out_ref, sums_out_ref, out_ref,
):
    side = cot_ref.shape[0]
    halo_part(xlo_ref, xhi_ref, ylo_ref, yhi_ref, masks_ref, field, weights, sums, True)
    for x in range(side):
        for k in range(sums.shape[0]):
            cols = slice(k * LANE, (k + 1) * LANE)
            cot = cot_ref[x, :, cols].astype(F32)
            out_ref[x, :, cols] = (cot + sums[k, x * side:(x + 1) * side, :]).astype(BF16)


def unpack_kernel(mine_ref, theirs_ref, taps_hbm, gain_hbm, mix_hbm, taps_ref, gain_ref, mix_ref, done):
    total = mine_ref[...] + theirs_ref[...]
    channels = mix_ref.shape[0]
    mix_ref[0:32, :] = total[:32, :channels]
    mix_ref[32:64, :] = total[:32, channels:]
    taps_ref[0:16, :] = total[32:48, :channels]
    taps_ref[16:27, :] = total[32:43, channels:]
    gain_ref[...] = total[43:44, channels:]
    copies = [
        pltpu.make_async_copy(src, dst, done.at[i])
        for i, (src, dst) in enumerate(((taps_ref, taps_hbm), (gain_ref, gain_hbm), (mix_ref, mix_hbm)))
    ]
    for copy in copies:
        copy.start()
    for copy in copies:
        copy.wait()


def swap(to_first, to_second, axis):
    count = lax.axis_size(axis)
    first = [(i, i ^ 1) for i in range(count) if i ^ 1 < count]
    second = [(i, j) for i in range(count) for j in [((i + 1) ^ 1) - 1] if 0 <= j < count]
    return lax.ppermute(to_first, axis, first), lax.ppermute(to_second, axis, second)


def low_high(from_first, from_second, axis):
    odd = lax.axis_index(axis) % 2 == 1
    return jnp.where(odd, from_first, from_second), jnp.where(odd, from_second, from_first)


def y_messages(xlo, xhi, ylo, yhi):
    low = jnp.concatenate([xlo[:1], ylo, xhi[:1]], axis=0)
    high = jnp.concatenate([xlo[-1:], yhi, xhi[-1:]], axis=0)
    return low_high(low, high, "gy")


def sum_steps():
    steps = []
    for axis in ("gx", "gy"):
        count = lax.axis_size(axis)
        bit = 1
        while bit < count:
            steps.append((axis, [(i, i ^ bit) for i in range(count)]))
            bit *= 2
    return steps


def shards(features, slot_map, tap_weights, gain, mix_weight, cotangent):
    side, _, _, lanes = features.shape
    channels = gain.shape[0]
    tiles = lanes // LANE
    cells = features.reshape(side, side, lanes)
    cot = cotangent.reshape(side, side, lanes)
    vmem = pl.BlockSpec(memory_space=pltpu.VMEM)
    hbm = pl.BlockSpec(memory_space=pltpu.HBM)
    compiler_params = pltpu.CompilerParams(vmem_limit_bytes=40 * 1024 * 1024)
    block = jax.ShapeDtypeStruct((side, side, lanes), BF16)
    edge = jax.ShapeDtypeStruct((side, lanes), BF16)
    field_type = jax.ShapeDtypeStruct((2 * tiles + 1, (side + 2) * (side + 8) + 8, LANE), F32)
    sums_type = jax.ShapeDtypeStruct((tiles, side * side, LANE), F32)
    weights_type = jax.ShapeDtypeStruct((27, 8, LANE), F32)
    mat_type = jax.ShapeDtypeStruct((WIDE, WIDE), BF16)

    def call(kernel, name, operands, outs, scratch=(), aliases={}, flops=0, in_specs=None, out_specs=None):
        return pl.pallas_call(
            kernel,
            out_shape=outs,
            in_specs=in_specs or [vmem] * len(operands),
            out_specs=out_specs or (vmem,) * len(outs),
            scratch_shapes=list(scratch),
            input_output_aliases=aliases,
            compiler_params=compiler_params,
            cost_estimate=pl.CostEstimate(flops=flops, bytes_accessed=500_000, transcendentals=0),
            name=name,
        )(*operands)

    masks = level_masks(slot_map, side)
    params = jnp.concatenate([mix_weight.astype(F32), tap_weights, gain[None], jnp.zeros((4, channels), F32)], axis=0)
    xlo, xhi = low_high(*swap(*x_edges(cells), "gx"), "gx")
    to_a, to_b = y_messages(xlo, xhi, *call(y_edges_kernel, "y_edges", (cells,), (edge, edge)))
    to_a, to_b, cells = lax.optimization_barrier((to_a, to_b, cells))
    ylo, yhi = low_high(*swap(to_a, to_b, "gy"), "gy")
    own = call(
        own_forward_kernel,
        "own_forward",
        (cells, cot, params),
        (
            field_type,
            sums_type,
            jax.ShapeDtypeStruct((side * side, lanes), F32),
            weights_type,
            mat_type,
            mat_type,
            jax.ShapeDtypeStruct((1, WIDE), F32),
        ),
        flops=10_000_000,
    )
    weights = own[3]
    _, _, mixed, grad_depth, part, gxa, gxb, gylo, gyhi = call(
        forward_kernel,
        "forward",
        (*own, xlo, xhi, ylo, yhi, masks, cells, cot),
        (
            field_type, sums_type, block, block, jax.ShapeDtypeStruct((48, LANE), F32),
            edge, edge, edge, edge,
        ),
        scratch=(pltpu.VMEM((side * side, lanes), BF16), pltpu.VMEM(sums_type.shape, F32)),
        aliases={0: 0, 1: 1},
        flops=20_000_000,
    )

    steps = sum_steps()
    gxlo, gxhi = low_high(*swap(gxa, gxb, "gx"), "gx")
    theirs = lax.ppermute(part, *steps[0])
    own_field, own_sums = call(
        own_backward_kernel, "own_backward", (grad_depth, weights), (field_type, sums_type), flops=10_000_000
    )
    part, to_a, to_b, own_field, own_sums = lax.optimization_barrier(
        (part + theirs, *y_messages(gxlo, gxhi, gylo, gyhi), own_field, own_sums)
    )
    gylo, gyhi = low_high(*swap(to_a, to_b, "gy"), "gy")
    part = part + lax.ppermute(part, *steps[1])
    _, _, grad_features = call(
        backward_kernel,
        "backward",
        (own_field, own_sums, weights, gxlo, gxhi, gylo, gyhi, masks, cot),
        (field_type, sums_type, block),
        aliases={0: 0, 1: 1},
        flops=2_000_000,
    )
    for step in steps[2:-1]:
        part = part + lax.ppermute(part, *step)
    part, grad_features = lax.optimization_barrier((part, grad_features))
    theirs = lax.ppermute(part, *steps[-1])

    outs = (
        jax.ShapeDtypeStruct((27, channels), F32),
        jax.ShapeDtypeStruct((1, channels), F32),
        jax.ShapeDtypeStruct((channels, channels), F32),
    )
    grad_taps, grad_gain, grad_mix = call(
        unpack_kernel,
        "unpack",
        (part, theirs),
        outs,
        scratch=[pltpu.VMEM(t.shape, F32) for t in outs] + [pltpu.SemaphoreType.DMA((3,))],
        out_specs=(hbm,) * 3,
    )
    shape = features.shape
    return (mixed.reshape(shape), grad_features.reshape(shape), grad_taps, grad_gain.reshape(channels), grad_mix)


def solution(mesh):
    return jax.shard_map(
        shards,
        mesh=mesh,
        in_specs=(P("gx", "gy", None, None), P(), P(), P(), P(), P("gx", "gy", None, None)),
        out_specs=(P("gx", "gy", None, None), P("gx", "gy", None, None), P(), P(), P()),
        check_vma=False,
    )
```

```python
import functools

import jax
import jax.numpy as jnp
from jax import lax
from jax.experimental import pallas as pl
from jax.experimental.pallas import tpu as pltpu
from jax.sharding import PartitionSpec as P

EPS = 1e-05
LANE = 128
WIDE = 256
F32 = jnp.float32
BF16 = jnp.bfloat16


def level_masks(slots, side, masks_ref):
    level = lax.broadcasted_iota(jnp.int32, slots.shape, 1)
    at_x = lax.broadcasted_iota(jnp.int32, slots.shape, 2) - lax.axis_index("gx")
    at_y = lax.broadcasted_iota(jnp.int32, slots.shape, 0) - lax.axis_index("gy")
    place = jnp.where(slots >= 0, level, 0).astype(F32)

    def near(off_x, off_y):
        found = jnp.where((at_x == off_x) & (at_y == off_y), place, 0.0)
        found = jnp.sum(jnp.sum(found, axis=0), axis=0, keepdims=True)
        return jnp.sum(found, axis=1, keepdims=True)

    own = near(0, 0)
    rows = masks_ref.shape[1]
    row = lax.broadcasted_iota(jnp.int32, (rows, LANE), 0)
    for edge in range(4):
        high = 1 if edge % 2 else -1
        if edge < 2:
            d = jnp.broadcast_to(near(high, 0) - own, (rows, LANE))
        else:
            corner, middle, other = (near(off, high) - own for off in (-1, 0, 1))
            d = jnp.where(row == 0, corner, jnp.where(row == side + 1, other, middle))
        for i, want in enumerate((0.0, -1.0, 1.0)):
            masks_ref[3 * edge + i] = jnp.where(d == want, 1.0, 0.0)


def plane_tiles(load, total, masks):
    low = lax.broadcasted_iota(jnp.int32, load(0).shape, 1) < LANE // 2
    zero = jnp.zeros(load(0).shape, F32)
    aligned = [load(k) for k in range(total)]
    turned = [pltpu.roll(t, LANE // 2, 1) for t in aligned]
    between = [jnp.where(low, turned[j - 1], turned[j]) for j in range(1, total)]
    if masks is None:
        return aligned + [jnp.where(low, zero, turned[0])] + between + [jnp.where(low, turned[-1], zero)]
    same, below, above = masks
    first = jnp.where(low, turned[-1] * below, turned[0] * same)
    last = jnp.where(low, turned[-1] * same, turned[0] * above)
    return [t * same for t in aligned] + [first] + [t * same for t in between] + [last]


def loader(rows):
    return lambda k: rows[:, k * LANE:(k + 1) * LANE].astype(F32)


def column_starts(side, shift):
    pitch = side + 8
    for start in range(0, side + 2, 8):
        size = min(8, side + 2 - start)
        yield start, size, pl.ds(start * pitch + shift, size, stride=pitch)


def own_part(own_ref, field, weights, sums, flip):
    side = own_ref.shape[0]
    tiles = own_ref.shape[2] // LANE
    pitch = side + 8

    def own_plane(x, _):
        base = pl.multiple_of((x + 1) * pitch + 8, 8)
        for i, t in enumerate(plane_tiles(loader(own_ref[x]), tiles, None)):
            field[i, pl.ds(base, side), :] = t
        return 0

    lax.fori_loop(0, side, own_plane, 0)
    for i in range(2 * tiles + 1):
        for shift in (7, pitch):
            for _, size, at in column_starts(side, shift):
                field[i, at, :] = jnp.zeros((size, LANE), F32)

    def tile(k, _):
        taps = [weights[26 - t if flip else t] for t in range(27)]
        for half in range(side // 8):
            part = {}
            for plane in range(1, side + 1):
                near = shifted(field, tiles, k, plane, half, pitch)
                for off_x in range(3):
                    x = plane - off_x
                    if not 0 <= x < side:
                        continue
                    for (off_y, off_z), value in near.items():
                        term = value * taps[9 * off_x + 3 * off_y + off_z]
                        part[x] = part[x] + term if x in part else term
                done = plane - 2
                for x in [done, done + 1] if plane == side else [done]:
                    if x >= 0:
                        sums[k, x * side + 8 * half:x * side + 8 * half + 8, :] = part.pop(x)
        return 0

    lax.fori_loop(0, tiles, tile, 0)


def halo_part(xlo_ref, xhi_ref, ylo_ref, yhi_ref, masks_ref, field, weights, sums, flip):
    side, lanes = xlo_ref.shape
    tiles = lanes // LANE
    pitch = side + 8

    def place(i, ref):
        rows = ref.shape[0]
        masks = tuple(masks_ref[3 * i + m, :rows, :] for m in range(3))
        return plane_tiles(loader(ref[...]), tiles, masks)

    for i, ref, plane in ((0, xlo_ref, 0), (1, xhi_ref, side + 1)):
        for j, t in enumerate(place(i, ref)):
            field[j, plane * pitch + 8:plane * pitch + 8 + side, :] = t

    def x_tile(k, _):
        for plane, off_x, x in ((0, 0, 0), (side + 1, 2, side - 1)):
            for half in range(side // 8):
                row = x * side + 8 * half
                total = sums[k, row:row + 8, :]
                for (off_y, off_z), value in shifted(field, tiles, k, plane, half, pitch).items():
                    tap = 9 * off_x + 3 * off_y + off_z
                    total = total + value * weights[26 - tap if flip else tap]
                sums[k, row:row + 8, :] = total
        return 0

    lax.fori_loop(0, tiles, x_tile, 0)

    for i, ref, shift in ((2, ylo_ref, 7), (3, yhi_ref, pitch)):
        for j, t in enumerate(place(i, ref)):
            for start, size, at in column_starts(side, shift):
                field[j, at, :] = t[start:start + size]

    def y_tile(k, _):
        for shift, off_y, y in ((7, 0, 0), (pitch, 2, side - 1)):
            for x in range(0, side, 8):
                at = pl.ds(x * side + y, 8, stride=side)
                total = sums[k, at, :]
                for off_x in range(3):
                    for off_z in range(3):
                        i = (tiles + k, k, tiles + k + 1)[off_z]
                        tap = 9 * off_x + 3 * off_y + off_z
                        value = field[i, pl.ds((x + off_x) * pitch + shift, 8, stride=pitch), :]
                        total = total + value * weights[26 - tap if flip else tap]
                sums[k, at, :] = total
        return 0

    lax.fori_loop(0, tiles, y_tile, 0)


def shifted(field, tiles, k, plane, half, pitch):
    found = {}
    for off_y in range(3):
        row = plane * pitch + 7 + 8 * half + off_y
        for off_z in range(3):
            i = (tiles + k, k, tiles + k + 1)[off_z]
            found[off_y, off_z] = field[i, row:row + 8, :]
    return found


def edges_of(cells_ref, xa_ref, xb_ref, ylo_ref, yhi_ref):
    side, _, lanes = cells_ref.shape
    odd = lax.axis_index("gx") % 2
    xa_ref[...] = cells_ref[jnp.where(odd == 1, 0, side - 1)]
    xb_ref[...] = cells_ref[jnp.where(odd == 1, side - 1, 0)]
    row = lax.broadcasted_iota(jnp.int32, (2 * side, side * side), 0)
    col = lax.broadcasted_iota(jnp.int32, (2 * side, side * side), 1)
    wanted = jnp.where(row < side, row * side, (row - side) * side + side - 1)
    pick = jnp.where(col == wanted, 1.0, 0.0).astype(BF16)
    flat = cells_ref[...].reshape(side * side, lanes)
    found = jnp.dot(pick, flat, preferred_element_type=F32).astype(BF16)
    ylo_ref[...] = found[:side]
    yhi_ref[...] = found[side:]


def params_kernel(
    slots_ref, mix_ref, taps_ref, gain_ref, masks_ref, weights, mean_mat_ref, mix_mat_ref, gain_wide_ref
):
    channels = mix_ref.shape[0]
    level_masks(slots_ref[...], masks_ref.shape[1] - 8, masks_ref)
    wide = jnp.concatenate([taps_ref[...], taps_ref[...]], axis=1)
    for tap in range(27):
        weights[tap] = jnp.broadcast_to(wide[tap:tap + 1], (8, LANE))
    copies = WIDE // channels
    row_id = lax.broadcasted_iota(jnp.int32, (WIDE, WIDE), 0) // channels
    col_id = lax.broadcasted_iota(jnp.int32, (WIDE, WIDE), 1) // channels
    block = row_id == col_id
    mean_mat_ref[...] = jnp.where(block, 1.0 / channels, 0.0).astype(BF16)
    mix = mix_ref[...].astype(F32)
    mix_row = jnp.concatenate([mix] * copies, axis=1)
    mix_mat_ref[...] = jnp.where(block, jnp.concatenate([mix_row] * copies, axis=0), 0.0).astype(BF16)
    gain_wide_ref[...] = jnp.concatenate([gain_ref[...]] * copies, axis=1)


def own_kernel(flip, own_ref, weights, field, sums):
    own_part(own_ref, field, weights, sums, flip)


def forward_kernel(
    field, depth, weights, mean_mat_ref, mix_mat_ref, gain_wide_ref,
    xlo_ref, xhi_ref, ylo_ref, yhi_ref, masks_ref, own_ref, cot_ref,
    field_out_ref, depth_out_ref, mixed_ref, grad_ref, packed_ref, gxa_ref, gxb_ref, gylo_ref, gyhi_ref,
    normed_bf, grads,
):
    side = own_ref.shape[0]
    lanes = own_ref.shape[2]
    tiles = lanes // LANE
    channels = packed_ref.shape[1] // 2
    pitch = side + 8
    cells = side * side
    halo_part(xlo_ref, xhi_ref, ylo_ref, yhi_ref, masks_ref, field, weights, depth, False)

    copies = WIDE // channels
    mean_mat = mean_mat_ref[...]
    mix_mat = mix_mat_ref[...]
    gain = gain_wide_ref[...]
    rows = 128
    xs = rows // side
    gain_sum = jnp.zeros((8, WIDE), F32)
    for part in range(lanes // WIDE):
        cols = slice(part * WIDE, (part + 1) * WIDE)
        for chunk in range(cells // rows):
            at = slice(chunk * rows, (chunk + 1) * rows)
            planes = slice(chunk * xs, (chunk + 1) * xs)
            dep = jnp.concatenate([depth[2 * part, at, :], depth[2 * part + 1, at, :]], axis=1)
            mean_sq = jnp.dot((dep * dep).astype(BF16), mean_mat, preferred_element_type=F32)
            inv = lax.rsqrt(mean_sq + EPS)
            normed = dep * inv
            norm_bf = (normed * gain).astype(BF16)
            normed_bf[at, cols] = norm_bf
            branch = jnp.dot(norm_bf, mix_mat, preferred_element_type=F32)
            feat = own_ref[planes, :, cols].reshape(rows, WIDE).astype(F32)
            mixed_ref[planes, :, cols] = (feat + branch).astype(BF16).reshape(xs, side, WIDE)
            grad_norm = lax.dot_general(
                cot_ref[planes, :, cols].reshape(rows, WIDE), mix_mat,
                (((1,), (1,)), ((), ())), preferred_element_type=F32,
            )
            gain_sum = gain_sum + jnp.sum((grad_norm * normed).reshape(rows // 8, 8, WIDE), axis=0)
            scaled = grad_norm * gain
            mean = jnp.dot((scaled * normed).astype(BF16), mean_mat, preferred_element_type=F32)
            grad = (inv * (scaled - normed * mean)).astype(BF16)
            grad_ref[planes, :, cols] = grad.reshape(xs, side, WIDE)
            wide_grad = grad.astype(F32)
            grads[2 * part, at, :] = wide_grad[:, :LANE]
            grads[2 * part + 1, at, :] = wide_grad[:, LANE:]
    edges_of(grad_ref, gxa_ref, gxb_ref, gylo_ref, gyhi_ref)

    mix_sum = jnp.zeros((WIDE, WIDE), F32)
    for part in range(lanes // WIDE):
        cols = slice(part * WIDE, (part + 1) * WIDE)
        mix_sum = mix_sum + lax.dot_general(
            normed_bf[:, cols],
            cot_ref[:, :, cols].reshape(cells, WIDE),
            (((0,), (0,)), ((), ())),
            preferred_element_type=F32,
        )
    grad_mix = mix_sum[:channels, :channels]
    for i in range(1, copies):
        span = slice(i * channels, (i + 1) * channels)
        grad_mix = grad_mix + mix_sum[span, span]
    packed_ref[0:32, :] = jnp.concatenate([grad_mix[:32], grad_mix[32:]], axis=1)

    def tap_tile(k, sums):
        sums = list(sums)
        for half in range(side // 8):
            near_grads = {}
            for plane in range(side + 2):
                if plane < side:
                    row = plane * side + 8 * half
                    near_grads[plane] = grads[k, row:row + 8, :]
                near = shifted(field, tiles, k, plane, half, pitch)
                for (off_y, off_z), value in near.items():
                    for off_x in range(3):
                        x = plane - off_x
                        if 0 <= x < side:
                            tap = 9 * off_x + 3 * off_y + off_z
                            sums[tap] = sums[tap] + value * near_grads[x]
                near_grads.pop(plane - 2, None)
        return tuple(sums)

    sums = lax.fori_loop(0, tiles, tap_tile, tuple(jnp.zeros((8, LANE), F32) for _ in range(27)))
    gain_row = jnp.sum(gain_sum, axis=0, keepdims=True)
    rows = [jnp.sum(t, axis=0, keepdims=True) for t in sums] + [gain_row[:, :LANE] + gain_row[:, LANE:]]
    rows = jnp.concatenate(rows + [jnp.zeros((4, LANE), F32)], axis=0)
    rows = rows[:, :channels] + rows[:, channels:]
    packed_ref[32:48, :] = jnp.concatenate([rows[:16], rows[16:]], axis=1)


def backward_kernel(
    field, sums, weights, xlo_ref, xhi_ref, ylo_ref, yhi_ref, masks_ref, cot_ref,
    field_out_ref, sums_out_ref, out_ref,
):
    side = cot_ref.shape[0]
    halo_part(xlo_ref, xhi_ref, ylo_ref, yhi_ref, masks_ref, field, weights, sums, True)
    for x in range(side):
        for k in range(sums.shape[0]):
            cols = slice(k * LANE, (k + 1) * LANE)
            cot = cot_ref[x, :, cols].astype(F32)
            out_ref[x, :, cols] = (cot + sums[k, x * side:(x + 1) * side, :]).astype(BF16)


def unpack_kernel(mine_ref, theirs_ref, taps_hbm, gain_hbm, mix_hbm, taps_ref, gain_ref, mix_ref, done):
    total = mine_ref[...] + theirs_ref[...]
    channels = mix_ref.shape[0]
    mix_ref[0:32, :] = total[:32, :channels]
    mix_ref[32:64, :] = total[:32, channels:]
    taps_ref[0:16, :] = total[32:48, :channels]
    taps_ref[16:27, :] = total[32:43, channels:]
    gain_ref[...] = total[43:44, channels:]
    copies = [
        pltpu.make_async_copy(src, dst, done.at[i])
        for i, (src, dst) in enumerate(((taps_ref, taps_hbm), (gain_ref, gain_hbm), (mix_ref, mix_hbm)))
    ]
    for copy in copies:
        copy.start()
    for copy in copies:
        copy.wait()


def swap(to_first, to_second, axis):
    count = lax.axis_size(axis)
    first = [(i, i ^ 1) for i in range(count) if i ^ 1 < count]
    second = [(i, j) for i in range(count) for j in [((i + 1) ^ 1) - 1] if 0 <= j < count]
    return lax.ppermute(to_first, axis, first), lax.ppermute(to_second, axis, second)


def low_high(from_first, from_second, axis):
    odd = lax.axis_index(axis) % 2 == 1
    return jnp.where(odd, from_first, from_second), jnp.where(odd, from_second, from_first)


def y_messages(xlo, xhi, ylo, yhi):
    low = jnp.concatenate([xlo[:1], ylo, xhi[:1]], axis=0)
    high = jnp.concatenate([xlo[-1:], yhi, xhi[-1:]], axis=0)
    return low_high(low, high, "gy")


def sum_steps():
    steps = []
    for axis in ("gx", "gy"):
        count = lax.axis_size(axis)
        bit = 1
        while bit < count:
            steps.append((axis, [(i, i ^ bit) for i in range(count)]))
            bit *= 2
    return steps


def shards(features, slot_map, tap_weights, gain, mix_weight, cotangent):
    side, _, _, lanes = features.shape
    channels = gain.shape[0]
    tiles = lanes // LANE
    cells = features.reshape(side, side, lanes)
    cot = cotangent.reshape(side, side, lanes)
    vmem = pl.BlockSpec(memory_space=pltpu.VMEM)
    hbm = pl.BlockSpec(memory_space=pltpu.HBM)
    block = jax.ShapeDtypeStruct((side, side, lanes), BF16)
    edge = jax.ShapeDtypeStruct((side, lanes), BF16)
    field_type = jax.ShapeDtypeStruct((2 * tiles + 1, (side + 2) * (side + 8) + 8, LANE), F32)
    sums_type = jax.ShapeDtypeStruct((tiles, side * side, LANE), F32)
    weights_type = jax.ShapeDtypeStruct((27, 8, LANE), F32)
    mat_type = jax.ShapeDtypeStruct((WIDE, WIDE), BF16)

    def call(kernel, name, operands, outs, scratch=(), aliases={}, flops=0, in_specs=None, out_specs=None):
        return pl.pallas_call(
            kernel,
            out_shape=tuple(jax.ShapeDtypeStruct(t.shape, t.dtype) for t in outs),
            in_specs=in_specs or [vmem] * len(operands),
            out_specs=out_specs or (vmem,) * len(outs),
            scratch_shapes=list(scratch),
            input_output_aliases=aliases,
            compiler_params=pltpu.CompilerParams(vmem_limit_bytes=40 * 1024 * 1024),
            cost_estimate=pl.CostEstimate(flops=flops, bytes_accessed=500_000, transcendentals=0),
            name=name,
        )(*operands)

    xa, xb, ylo, yhi = call(edges_of, "edges", (cells,), (edge, edge, edge, edge), flops=100_000_000_000)
    masks, weights, mean_mat, mix_mat, gain_wide = call(
        params_kernel,
        "params",
        (jnp.transpose(slot_map, (1, 2, 0)), mix_weight, tap_weights, gain.reshape(1, channels)),
        (
            jax.ShapeDtypeStruct((12, side + 8, LANE), F32),
            weights_type,
            mat_type,
            mat_type,
            jax.ShapeDtypeStruct((1, WIDE), F32),
        ),
    )
    xlo, xhi = low_high(*swap(xa, xb, "gx"), "gx")
    to_a, to_b = y_messages(xlo, xhi, ylo, yhi)
    to_a, to_b, weights = lax.optimization_barrier((to_a, to_b, weights))
    ylo, yhi = low_high(*swap(to_a, to_b, "gy"), "gy")
    own_field, own_sums = call(
        functools.partial(own_kernel, False), "own_forward", (cells, weights), (field_type, sums_type),
        flops=10_000_000,
    )
    _, _, mixed, grad_depth, part, gxa, gxb, gylo, gyhi = call(
        forward_kernel,
        "forward",
        (own_field, own_sums, weights, mean_mat, mix_mat, gain_wide, xlo, xhi, ylo, yhi, masks, cells, cot),
        (
            field_type, sums_type, block, block, jax.ShapeDtypeStruct((48, LANE), F32),
            edge, edge, edge, edge,
        ),
        scratch=(pltpu.VMEM((side * side, lanes), BF16), pltpu.VMEM(sums_type.shape, F32)),
        aliases={0: 0, 1: 1},
        flops=20_000_000,
    )

    steps = sum_steps()
    gxlo, gxhi = low_high(*swap(gxa, gxb, "gx"), "gx")
    theirs = lax.ppermute(part, *steps[0])
    part, to_a, to_b = lax.optimization_barrier((part + theirs, *y_messages(gxlo, gxhi, gylo, gyhi)))
    gylo, gyhi = low_high(*swap(to_a, to_b, "gy"), "gy")
    part = part + lax.ppermute(part, *steps[1])
    part, gylo, gyhi, grad_depth = lax.optimization_barrier((part, gylo, gyhi, grad_depth))
    own_field, own_sums = call(
        functools.partial(own_kernel, True), "own_backward", (grad_depth, weights), (field_type, sums_type),
        flops=10_000_000,
    )
    for index, step in enumerate(steps[2:-1]):
        part = part + lax.ppermute(part, *step)
        if index == 0:
            part, own_field, own_sums = lax.optimization_barrier((part, own_field, own_sums))
            _, _, grad_features = call(
                backward_kernel,
                "backward",
                (own_field, own_sums, weights, gxlo, gxhi, gylo, gyhi, masks, cot),
                (field_type, sums_type, block),
                aliases={0: 0, 1: 1},
                flops=2_000_000,
            )
    part, grad_features = lax.optimization_barrier((part, grad_features))
    theirs = lax.ppermute(part, *steps[-1])

    outs = (
        jax.ShapeDtypeStruct((27, channels), F32),
        jax.ShapeDtypeStruct((1, channels), F32),
        jax.ShapeDtypeStruct((channels, channels), F32),
    )
    grad_taps, grad_gain, grad_mix = call(
        unpack_kernel,
        "unpack",
        (part, theirs),
        outs,
        scratch=[pltpu.VMEM(t.shape, F32) for t in outs] + [pltpu.SemaphoreType.DMA((3,))],
        out_specs=(hbm,) * 3,
    )
    shape = features.shape
    return (mixed.reshape(shape), grad_features.reshape(shape), grad_taps, grad_gain.reshape(channels), grad_mix)


def solution(mesh):
    return jax.shard_map(
        shards,
        mesh=mesh,
        in_specs=(P("gx", "gy", None, None), P(), P(), P(), P(), P("gx", "gy", None, None)),
        out_specs=(P("gx", "gy", None, None), P("gx", "gy", None, None), P(), P(), P()),
        check_vma=False,
    )
```

```python
import functools

import jax
import jax.numpy as jnp
from jax import lax
from jax.experimental import pallas as pl
from jax.experimental.pallas import tpu as pltpu
from jax.sharding import PartitionSpec as P

EPS = 1e-05
LANE = 128
WIDE = 256
F32 = jnp.float32
BF16 = jnp.bfloat16


def level_masks(slots, side, masks_ref):
    level = lax.broadcasted_iota(jnp.int32, slots.shape, 1)
    at_x = lax.broadcasted_iota(jnp.int32, slots.shape, 2) - lax.axis_index("gx")
    at_y = lax.broadcasted_iota(jnp.int32, slots.shape, 0) - lax.axis_index("gy")
    place = jnp.where(slots >= 0, level + 1, 0).astype(F32)

    def near(off_x, off_y):
        found = jnp.where((at_x == off_x) & (at_y == off_y), place, 0.0)
        found = jnp.sum(jnp.sum(found, axis=0), axis=0, keepdims=True)
        return jnp.sum(found, axis=1, keepdims=True)

    own = near(0, 0)

    def difference(off_x, off_y):
        found = near(off_x, off_y)
        return jnp.where(found > 0.0, found - own, 9.0)

    rows = masks_ref.shape[1]
    row = lax.broadcasted_iota(jnp.int32, (rows, LANE), 0)
    for edge in range(4):
        high = 1 if edge % 2 else -1
        if edge < 2:
            d = jnp.broadcast_to(difference(high, 0), (rows, LANE))
        else:
            corner, middle, other = (difference(off, high) for off in (-1, 0, 1))
            d = jnp.where(row == 0, corner, jnp.where(row == side + 1, other, middle))
        for i, want in enumerate((0.0, -1.0, 1.0)):
            masks_ref[3 * edge + i] = jnp.where(d == want, 1.0, 0.0)


def plane_tiles(load, total, masks):
    low = lax.broadcasted_iota(jnp.int32, load(0).shape, 1) < LANE // 2
    zero = jnp.zeros(load(0).shape, F32)
    aligned = [load(k) for k in range(total)]
    turned = [pltpu.roll(t, LANE // 2, 1) for t in aligned]
    between = [jnp.where(low, turned[j - 1], turned[j]) for j in range(1, total)]
    if masks is None:
        return aligned + [jnp.where(low, zero, turned[0])] + between + [jnp.where(low, turned[-1], zero)]
    same, below, above = masks
    first = jnp.where(low, turned[-1] * below, turned[0] * same)
    last = jnp.where(low, turned[-1] * same, turned[0] * above)
    return [t * same for t in aligned] + [first] + [t * same for t in between] + [last]


def loader(rows):
    return lambda k: rows[:, k * LANE:(k + 1) * LANE].astype(F32)


def column_starts(side, shift):
    pitch = side + 8
    for start in range(0, side + 2, 8):
        size = min(8, side + 2 - start)
        yield start, size, pl.ds(start * pitch + shift, size, stride=pitch)


def own_part(own_ref, field, weights, sums, flip):
    side = own_ref.shape[0]
    tiles = own_ref.shape[2] // LANE
    pitch = side + 8

    def own_plane(x, _):
        base = pl.multiple_of((x + 1) * pitch + 8, 8)
        for i, t in enumerate(plane_tiles(loader(own_ref[x]), tiles, None)):
            field[i, pl.ds(base, side), :] = t
        return 0

    lax.fori_loop(0, side, own_plane, 0)
    for i in range(2 * tiles + 1):
        for shift in (7, pitch):
            for _, size, at in column_starts(side, shift):
                field[i, at, :] = jnp.zeros((size, LANE), F32)

    def tile(k, _):
        taps = [weights[26 - t if flip else t] for t in range(27)]
        for half in range(side // 8):
            part = {}
            for plane in range(1, side + 1):
                near = shifted(field, tiles, k, plane, half, pitch)
                for off_x in range(3):
                    x = plane - off_x
                    if not 0 <= x < side:
                        continue
                    for (off_y, off_z), value in near.items():
                        term = value * taps[9 * off_x + 3 * off_y + off_z]
                        part[x] = part[x] + term if x in part else term
                done = plane - 2
                for x in [done, done + 1] if plane == side else [done]:
                    if x >= 0:
                        sums[k, x * side + 8 * half:x * side + 8 * half + 8, :] = part.pop(x)
        return 0

    lax.fori_loop(0, tiles, tile, 0)


def halo_part(xlo_ref, xhi_ref, ylo_ref, yhi_ref, masks_ref, field, weights, sums, flip):
    side, lanes = xlo_ref.shape
    tiles = lanes // LANE
    pitch = side + 8

    def place(i, ref):
        rows = ref.shape[0]
        masks = tuple(masks_ref[3 * i + m, :rows, :] for m in range(3))
        return plane_tiles(loader(ref[...]), tiles, masks)

    for i, ref, plane in ((0, xlo_ref, 0), (1, xhi_ref, side + 1)):
        for j, t in enumerate(place(i, ref)):
            field[j, plane * pitch + 8:plane * pitch + 8 + side, :] = t

    def x_tile(k, _):
        for plane, off_x, x in ((0, 0, 0), (side + 1, 2, side - 1)):
            for half in range(side // 8):
                row = x * side + 8 * half
                total = sums[k, row:row + 8, :]
                for (off_y, off_z), value in shifted(field, tiles, k, plane, half, pitch).items():
                    tap = 9 * off_x + 3 * off_y + off_z
                    total = total + value * weights[26 - tap if flip else tap]
                sums[k, row:row + 8, :] = total
        return 0

    lax.fori_loop(0, tiles, x_tile, 0)

    for i, ref, shift in ((2, ylo_ref, 7), (3, yhi_ref, pitch)):
        for j, t in enumerate(place(i, ref)):
            for start, size, at in column_starts(side, shift):
                field[j, at, :] = t[start:start + size]

    def y_tile(k, _):
        for shift, off_y, y in ((7, 0, 0), (pitch, 2, side - 1)):
            for x in range(0, side, 8):
                at = pl.ds(x * side + y, 8, stride=side)
                total = sums[k, at, :]
                for off_x in range(3):
                    for off_z in range(3):
                        i = (tiles + k, k, tiles + k + 1)[off_z]
                        tap = 9 * off_x + 3 * off_y + off_z
                        value = field[i, pl.ds((x + off_x) * pitch + shift, 8, stride=pitch), :]
                        total = total + value * weights[26 - tap if flip else tap]
                sums[k, at, :] = total
        return 0

    lax.fori_loop(0, tiles, y_tile, 0)


def shifted(field, tiles, k, plane, half, pitch):
    found = {}
    for off_y in range(3):
        row = plane * pitch + 7 + 8 * half + off_y
        for off_z in range(3):
            i = (tiles + k, k, tiles + k + 1)[off_z]
            found[off_y, off_z] = field[i, row:row + 8, :]
    return found


def edges_of(cells_ref, xa_ref, xb_ref, ylo_ref, yhi_ref):
    side, _, lanes = cells_ref.shape
    odd = lax.axis_index("gx") % 2
    xa_ref[...] = cells_ref[jnp.where(odd == 1, 0, side - 1)]
    xb_ref[...] = cells_ref[jnp.where(odd == 1, side - 1, 0)]
    row = lax.broadcasted_iota(jnp.int32, (2 * side, side * side), 0)
    col = lax.broadcasted_iota(jnp.int32, (2 * side, side * side), 1)
    wanted = jnp.where(row < side, row * side, (row - side) * side + side - 1)
    pick = jnp.where(col == wanted, 1.0, 0.0).astype(BF16)
    flat = cells_ref[...].reshape(side * side, lanes)
    found = jnp.dot(pick, flat, preferred_element_type=F32).astype(BF16)
    ylo_ref[...] = found[:side]
    yhi_ref[...] = found[side:]


def params_kernel(
    slots_ref, mix_ref, taps_ref, gain_ref, masks_ref, weights, mean_mat_ref, mix_mat_ref, gain_wide_ref
):
    channels = mix_ref.shape[0]
    level_masks(slots_ref[...], masks_ref.shape[1] - 8, masks_ref)
    wide = jnp.concatenate([taps_ref[...], taps_ref[...]], axis=1)
    for tap in range(27):
        weights[tap] = jnp.broadcast_to(wide[tap:tap + 1], (8, LANE))
    copies = WIDE // channels
    row_id = lax.broadcasted_iota(jnp.int32, (WIDE, WIDE), 0) // channels
    col_id = lax.broadcasted_iota(jnp.int32, (WIDE, WIDE), 1) // channels
    block = row_id == col_id
    mean_mat_ref[...] = jnp.where(block, 1.0 / channels, 0.0).astype(BF16)
    mix = mix_ref[...].astype(F32)
    mix_row = jnp.concatenate([mix] * copies, axis=1)
    mix_mat_ref[...] = jnp.where(block, jnp.concatenate([mix_row] * copies, axis=0), 0.0).astype(BF16)
    gain_wide_ref[...] = jnp.concatenate([gain_ref[...]] * copies, axis=1)


def own_kernel(flip, own_ref, weights, field, sums):
    own_part(own_ref, field, weights, sums, flip)


def forward_kernel(
    field, depth, weights, mean_mat_ref, mix_mat_ref, gain_wide_ref,
    xlo_ref, xhi_ref, ylo_ref, yhi_ref, masks_ref, own_ref, cot_ref,
    field_out_ref, depth_out_ref, mixed_ref, grad_ref, gxa_ref, gxb_ref, gylo_ref, gyhi_ref,
    normed_bf, grads, gain_sum_ref,
):
    side = own_ref.shape[0]
    lanes = own_ref.shape[2]
    cells = side * side
    halo_part(xlo_ref, xhi_ref, ylo_ref, yhi_ref, masks_ref, field, weights, depth, False)

    mean_mat = mean_mat_ref[...]
    mix_mat = mix_mat_ref[...]
    gain = gain_wide_ref[...]
    rows = 128
    xs = rows // side
    gain_sum = jnp.zeros((8, WIDE), F32)
    for part in range(lanes // WIDE):
        cols = slice(part * WIDE, (part + 1) * WIDE)
        for chunk in range(cells // rows):
            at = slice(chunk * rows, (chunk + 1) * rows)
            planes = slice(chunk * xs, (chunk + 1) * xs)
            dep = jnp.concatenate([depth[2 * part, at, :], depth[2 * part + 1, at, :]], axis=1)
            mean_sq = jnp.dot((dep * dep).astype(BF16), mean_mat, preferred_element_type=F32)
            inv = lax.rsqrt(mean_sq + EPS)
            normed = dep * inv
            norm_bf = (normed * gain).astype(BF16)
            normed_bf[at, cols] = norm_bf
            branch = jnp.dot(norm_bf, mix_mat, preferred_element_type=F32)
            feat = own_ref[planes, :, cols].reshape(rows, WIDE).astype(F32)
            mixed_ref[planes, :, cols] = (feat + branch).astype(BF16).reshape(xs, side, WIDE)
            grad_norm = lax.dot_general(
                cot_ref[planes, :, cols].reshape(rows, WIDE), mix_mat,
                (((1,), (1,)), ((), ())), preferred_element_type=F32,
            )
            gain_sum = gain_sum + jnp.sum((grad_norm * normed).reshape(rows // 8, 8, WIDE), axis=0)
            scaled = grad_norm * gain
            mean = jnp.dot((scaled * normed).astype(BF16), mean_mat, preferred_element_type=F32)
            grad = (inv * (scaled - normed * mean)).astype(BF16)
            grad_ref[planes, :, cols] = grad.reshape(xs, side, WIDE)
            wide_grad = grad.astype(F32)
            grads[2 * part, at, :] = wide_grad[:, :LANE]
            grads[2 * part + 1, at, :] = wide_grad[:, LANE:]
    gain_sum_ref[...] = gain_sum
    edges_of(grad_ref, gxa_ref, gxb_ref, gylo_ref, gyhi_ref)


def sums_kernel(field, normed_bf, grads, gain_sum_ref, cot_ref, packed_ref):
    side, _, lanes = cot_ref.shape
    tiles = lanes // LANE
    channels = packed_ref.shape[1] // 2
    pitch = side + 8
    cells = side * side
    copies = WIDE // channels
    mix_sum = jnp.zeros((WIDE, WIDE), F32)
    for part in range(lanes // WIDE):
        cols = slice(part * WIDE, (part + 1) * WIDE)
        mix_sum = mix_sum + lax.dot_general(
            normed_bf[:, cols],
            cot_ref[:, :, cols].reshape(cells, WIDE),
            (((0,), (0,)), ((), ())),
            preferred_element_type=F32,
        )
    grad_mix = mix_sum[:channels, :channels]
    for i in range(1, copies):
        span = slice(i * channels, (i + 1) * channels)
        grad_mix = grad_mix + mix_sum[span, span]
    packed_ref[0:32, :] = jnp.concatenate([grad_mix[:32], grad_mix[32:]], axis=1)

    def tap_tile(k, sums):
        sums = list(sums)
        for half in range(side // 8):
            near_grads = {}
            for plane in range(side + 2):
                if plane < side:
                    row = plane * side + 8 * half
                    near_grads[plane] = grads[k, row:row + 8, :]
                near = shifted(field, tiles, k, plane, half, pitch)
                for (off_y, off_z), value in near.items():
                    for off_x in range(3):
                        x = plane - off_x
                        if 0 <= x < side:
                            tap = 9 * off_x + 3 * off_y + off_z
                            sums[tap] = sums[tap] + value * near_grads[x]
                near_grads.pop(plane - 2, None)
        return tuple(sums)

    sums = lax.fori_loop(0, tiles, tap_tile, tuple(jnp.zeros((8, LANE), F32) for _ in range(27)))
    gain_row = jnp.sum(gain_sum_ref[...], axis=0, keepdims=True)
    rows = [jnp.sum(t, axis=0, keepdims=True) for t in sums] + [gain_row[:, :LANE] + gain_row[:, LANE:]]
    rows = jnp.concatenate(rows + [jnp.zeros((4, LANE), F32)], axis=0)
    rows = rows[:, :channels] + rows[:, channels:]
    packed_ref[32:48, :] = jnp.concatenate([rows[:16], rows[16:]], axis=1)


def backward_kernel(
    field, sums, weights, xlo_ref, xhi_ref, ylo_ref, yhi_ref, masks_ref, cot_ref,
    field_out_ref, sums_out_ref, out_ref,
):
    side = cot_ref.shape[0]
    halo_part(xlo_ref, xhi_ref, ylo_ref, yhi_ref, masks_ref, field, weights, sums, True)
    for x in range(side):
        for k in range(sums.shape[0]):
            cols = slice(k * LANE, (k + 1) * LANE)
            cot = cot_ref[x, :, cols].astype(F32)
            out_ref[x, :, cols] = (cot + sums[k, x * side:(x + 1) * side, :]).astype(BF16)


def unpack_kernel(mine_ref, theirs_ref, taps_hbm, gain_hbm, mix_hbm, taps_ref, gain_ref, mix_ref, done):
    total = mine_ref[...] + theirs_ref[...]
    channels = mix_ref.shape[0]
    mix_ref[0:32, :] = total[:32, :channels]
    mix_ref[32:64, :] = total[:32, channels:]
    taps_ref[0:16, :] = total[32:48, :channels]
    taps_ref[16:27, :] = total[32:43, channels:]
    gain_ref[...] = total[43:44, channels:]
    copies = [
        pltpu.make_async_copy(src, dst, done.at[i])
        for i, (src, dst) in enumerate(((taps_ref, taps_hbm), (gain_ref, gain_hbm), (mix_ref, mix_hbm)))
    ]
    for copy in copies:
        copy.start()
    for copy in copies:
        copy.wait()


def swap(to_first, to_second, axis):
    count = lax.axis_size(axis)
    first = [(i, i ^ 1 if i ^ 1 < count else i) for i in range(count)]
    second = [(i, min(max(((i + 1) ^ 1) - 1, 0), count - 1)) for i in range(count)]
    return lax.ppermute(to_first, axis, first), lax.ppermute(to_second, axis, second)


def low_high(from_first, from_second, axis):
    odd = lax.axis_index(axis) % 2 == 1
    return jnp.where(odd, from_first, from_second), jnp.where(odd, from_second, from_first)


def y_messages(xlo, xhi, ylo, yhi):
    low = jnp.concatenate([xlo[:1], ylo, xhi[:1]], axis=0)
    high = jnp.concatenate([xlo[-1:], yhi, xhi[-1:]], axis=0)
    return low_high(low, high, "gy")


def sum_steps():
    steps = []
    for axis in ("gx", "gy"):
        count = lax.axis_size(axis)
        bit = 1
        while bit < count:
            steps.append((axis, [(i, i ^ bit) for i in range(count)]))
            bit *= 2
    return steps


def shards(features, slot_map, tap_weights, gain, mix_weight, cotangent):
    side, _, _, lanes = features.shape
    channels = gain.shape[0]
    tiles = lanes // LANE
    cells = features.reshape(side, side, lanes)
    cot = cotangent.reshape(side, side, lanes)
    vmem = pl.BlockSpec(memory_space=pltpu.VMEM)
    hbm = pl.BlockSpec(memory_space=pltpu.HBM)
    block = jax.ShapeDtypeStruct((side, side, lanes), BF16)
    edge = jax.ShapeDtypeStruct((side, lanes), BF16)
    field_type = jax.ShapeDtypeStruct((2 * tiles + 1, (side + 2) * (side + 8) + 8, LANE), F32)
    sums_type = jax.ShapeDtypeStruct((tiles, side * side, LANE), F32)
    weights_type = jax.ShapeDtypeStruct((27, 8, LANE), F32)
    mat_type = jax.ShapeDtypeStruct((WIDE, WIDE), BF16)

    def call(kernel, name, operands, outs, scratch=(), aliases={}, flops=0, in_specs=None, out_specs=None):
        return pl.pallas_call(
            kernel,
            out_shape=tuple(jax.ShapeDtypeStruct(t.shape, t.dtype) for t in outs),
            in_specs=in_specs or [vmem] * len(operands),
            out_specs=out_specs or (vmem,) * len(outs),
            scratch_shapes=list(scratch),
            input_output_aliases=aliases,
            compiler_params=pltpu.CompilerParams(vmem_limit_bytes=40 * 1024 * 1024),
            cost_estimate=pl.CostEstimate(flops=flops, bytes_accessed=500_000, transcendentals=0),
            name=name,
        )(*operands)

    xa, xb, ylo, yhi = call(edges_of, "edges", (cells,), (edge, edge, edge, edge), flops=100_000_000_000)
    masks, weights, mean_mat, mix_mat, gain_wide = call(
        params_kernel,
        "params",
        (jnp.transpose(slot_map, (1, 2, 0)), mix_weight, tap_weights, gain.reshape(1, channels)),
        (
            jax.ShapeDtypeStruct((12, side + 8, LANE), F32),
            weights_type,
            mat_type,
            mat_type,
            jax.ShapeDtypeStruct((1, WIDE), F32),
        ),
    )
    xlo, xhi = low_high(*swap(xa, xb, "gx"), "gx")
    to_a, to_b = y_messages(xlo, xhi, ylo, yhi)
    to_a, to_b, weights = lax.optimization_barrier((to_a, to_b, weights))
    ylo, yhi = low_high(*swap(to_a, to_b, "gy"), "gy")
    own_field, own_sums = call(
        functools.partial(own_kernel, False), "own_forward", (cells, weights), (field_type, sums_type),
        flops=10_000_000,
    )
    field, _, mixed, grad_depth, gxa, gxb, gylo, gyhi, normed_bf, grads, gain_sum = call(
        forward_kernel,
        "forward",
        (own_field, own_sums, weights, mean_mat, mix_mat, gain_wide, xlo, xhi, ylo, yhi, masks, cells, cot),
        (
            field_type, sums_type, block, block, edge, edge, edge, edge,
            jax.ShapeDtypeStruct((side * side, lanes), BF16), sums_type, jax.ShapeDtypeStruct((8, WIDE), F32),
        ),
        aliases={0: 0, 1: 1},
        flops=10_000_000,
    )
    gxlo, gxhi = low_high(*swap(gxa, gxb, "gx"), "gx")
    (part,) = call(
        sums_kernel,
        "sums",
        (field, normed_bf, grads, gain_sum, cot),
        (jax.ShapeDtypeStruct((48, LANE), F32),),
        flops=10_000_000,
    )

    steps = sum_steps()
    part, to_a, to_b = lax.optimization_barrier((part, *y_messages(gxlo, gxhi, gylo, gyhi)))
    gylo, gyhi = low_high(*swap(to_a, to_b, "gy"), "gy")
    part = part + lax.ppermute(part, *steps[0])
    part, grad_depth = lax.optimization_barrier((part, grad_depth))
    theirs = lax.ppermute(part, *steps[1])
    own_field, own_sums = call(
        functools.partial(own_kernel, True), "own_backward", (grad_depth, weights), (field_type, sums_type),
        flops=10_000_000,
    )
    part, gylo, gyhi, own_field, own_sums = lax.optimization_barrier(
        (part + theirs, gylo, gyhi, own_field, own_sums)
    )
    _, _, grad_features = call(
        backward_kernel,
        "backward",
        (own_field, own_sums, weights, gxlo, gxhi, gylo, gyhi, masks, cot),
        (field_type, sums_type, block),
        aliases={0: 0, 1: 1},
        flops=2_000_000,
    )
    for index, step in enumerate(steps[2:-1]):
        part = part + lax.ppermute(part, *step)
        if index == 0:
            part, grad_features = lax.optimization_barrier((part, grad_features))
    theirs = lax.ppermute(part, *steps[-1])

    outs = (
        jax.ShapeDtypeStruct((27, channels), F32),
        jax.ShapeDtypeStruct((1, channels), F32),
        jax.ShapeDtypeStruct((channels, channels), F32),
    )
    grad_taps, grad_gain, grad_mix = call(
        unpack_kernel,
        "unpack",
        (part, theirs),
        outs,
        scratch=[pltpu.VMEM(t.shape, F32) for t in outs] + [pltpu.SemaphoreType.DMA((3,))],
        out_specs=(hbm,) * 3,
    )
    shape = features.shape
    return (mixed.reshape(shape), grad_features.reshape(shape), grad_taps, grad_gain.reshape(channels), grad_mix)


def solution(mesh):
    return jax.shard_map(
        shards,
        mesh=mesh,
        in_specs=(P("gx", "gy", None, None), P(), P(), P(), P(), P("gx", "gy", None, None)),
        out_specs=(P("gx", "gy", None, None), P("gx", "gy", None, None), P(), P(), P()),
        check_vma=False,
    )
```

```python
import functools
import math

import jax
import jax.numpy as jnp
from jax import lax
from jax.experimental import pallas as pl
from jax.experimental.pallas import tpu as pltpu
from jax.sharding import PartitionSpec as P

EPS = 1e-05
LANE = 128
WIDE = 256
F32 = jnp.float32
BF16 = jnp.bfloat16


def level_masks(slots, side, masks_ref):
    level = lax.broadcasted_iota(jnp.int32, slots.shape, 1)
    at_x = lax.broadcasted_iota(jnp.int32, slots.shape, 2) - lax.axis_index("gx")
    at_y = lax.broadcasted_iota(jnp.int32, slots.shape, 0) - lax.axis_index("gy")
    place = jnp.where(slots >= 0, level + 1, 0).astype(F32)

    def near(off_x, off_y):
        found = jnp.where((at_x == off_x) & (at_y == off_y), place, 0.0)
        found = jnp.sum(jnp.sum(found, axis=0), axis=0, keepdims=True)
        return jnp.sum(found, axis=1, keepdims=True)

    own = near(0, 0)

    def difference(off_x, off_y):
        found = near(off_x, off_y)
        return jnp.where(found > 0.0, found - own, 9.0)

    rows = masks_ref.shape[1]
    row = lax.broadcasted_iota(jnp.int32, (rows, LANE), 0)
    for edge in range(4):
        high = 1 if edge % 2 else -1
        if edge < 2:
            d = jnp.broadcast_to(difference(high, 0), (rows, LANE))
        else:
            corner, middle, other = (difference(off, high) for off in (-1, 0, 1))
            d = jnp.where(row == 0, corner, jnp.where(row == side + 1, other, middle))
        for i, want in enumerate((0.0, -1.0, 1.0)):
            masks_ref[3 * edge + i] = jnp.where(d == want, 1.0, 0.0)


def plane_tiles(load, total, masks, first, count):
    shape = load(first).shape
    low = lax.broadcasted_iota(jnp.int32, shape, 1) < LANE // 2
    zero = jnp.zeros(shape, F32)
    kept = {}

    def turned(k):
        if k not in kept:
            kept[k] = pltpu.roll(load(k), LANE // 2, 1)
        return kept[k]

    for k in range(first, first + count):
        yield k, load(k) if masks is None else load(k) * masks[0]
    for j in range(first + 1 if first else 0, first + count + 1):
        if 0 < j < total:
            tile = jnp.where(low, turned(j - 1), turned(j))
            yield total + j, tile if masks is None else tile * masks[0]
        elif masks is None:
            yield total + j, jnp.where(low, zero, turned(0)) if j == 0 else jnp.where(low, turned(total - 1), zero)
        elif j == 0:
            yield total + j, jnp.where(low, turned(total - 1) * masks[1], turned(0) * masks[0])
        else:
            yield total + j, jnp.where(low, turned(total - 1) * masks[0], turned(0) * masks[2])


def loader(rows):
    return lambda k: rows[:, k * LANE:(k + 1) * LANE].astype(F32)


def column_starts(side, shift):
    pitch = side + 8
    for start in range(0, side + 2, 8):
        size = min(8, side + 2 - start)
        yield start, size, pl.ds(start * pitch + shift, size, stride=pitch)


def own_part(own_ref, field, weights, sums, flip, first, count):
    side = own_ref.shape[0]
    tiles = own_ref.shape[2] // LANE
    pitch = side + 8

    def own_plane(x, _):
        base = pl.multiple_of((x + 1) * pitch + 8, 8)
        for i, t in plane_tiles(loader(own_ref[x]), tiles, None, first, count):
            field[i, pl.ds(base, side), :] = t
        return 0

    lax.fori_loop(0, side, own_plane, 0)
    mine = list(range(first, first + count)) + [tiles + j for j in range(first + 1 if first else 0, first + count + 1)]
    for i in mine:
        for shift in (7, pitch):
            for _, size, at in column_starts(side, shift):
                field[i, at, :] = jnp.zeros((size, LANE), F32)

    def tile(k, _):
        taps = [weights[26 - t if flip else t] for t in range(27)]
        for half in range(side // 8):
            part = {}
            for plane in range(1, side + 1):
                near = shifted(field, tiles, k, plane, half, pitch)
                for off_x in range(3):
                    x = plane - off_x
                    if not 0 <= x < side:
                        continue
                    for (off_y, off_z), value in near.items():
                        term = value * taps[9 * off_x + 3 * off_y + off_z]
                        part[x] = part[x] + term if x in part else term
                done = plane - 2
                for x in [done, done + 1] if plane == side else [done]:
                    if x >= 0:
                        sums[k, x * side + 8 * half:x * side + 8 * half + 8, :] = part.pop(x)
        return 0

    lax.fori_loop(first, first + count, tile, 0)


def halo_part(xlo_ref, xhi_ref, ylo_ref, yhi_ref, masks_ref, field, weights, sums, flip):
    side, lanes = xlo_ref.shape
    tiles = lanes // LANE
    pitch = side + 8

    def place(i, ref):
        rows = ref.shape[0]
        masks = tuple(masks_ref[3 * i + m, :rows, :] for m in range(3))
        return plane_tiles(loader(ref[...]), tiles, masks, 0, tiles)

    for i, ref, plane in ((0, xlo_ref, 0), (1, xhi_ref, side + 1)):
        for j, t in place(i, ref):
            field[j, plane * pitch + 8:plane * pitch + 8 + side, :] = t

    def x_tile(k, _):
        for plane, off_x, x in ((0, 0, 0), (side + 1, 2, side - 1)):
            for half in range(side // 8):
                row = x * side + 8 * half
                total = sums[k, row:row + 8, :]
                for (off_y, off_z), value in shifted(field, tiles, k, plane, half, pitch).items():
                    tap = 9 * off_x + 3 * off_y + off_z
                    total = total + value * weights[26 - tap if flip else tap]
                sums[k, row:row + 8, :] = total
        return 0

    lax.fori_loop(0, tiles, x_tile, 0)

    for i, ref, shift in ((2, ylo_ref, 7), (3, yhi_ref, pitch)):
        for j, t in place(i, ref):
            for start, size, at in column_starts(side, shift):
                field[j, at, :] = t[start:start + size]

    def y_tile(k, _):
        for shift, off_y, y in ((7, 0, 0), (pitch, 2, side - 1)):
            for x in range(0, side, 8):
                at = pl.ds(x * side + y, 8, stride=side)
                total = sums[k, at, :]
                for off_x in range(3):
                    for off_z in range(3):
                        i = (tiles + k, k, tiles + k + 1)[off_z]
                        tap = 9 * off_x + 3 * off_y + off_z
                        value = field[i, pl.ds((x + off_x) * pitch + shift, 8, stride=pitch), :]
                        total = total + value * weights[26 - tap if flip else tap]
                sums[k, at, :] = total
        return 0

    lax.fori_loop(0, tiles, y_tile, 0)


def shifted(field, tiles, k, plane, half, pitch):
    found = {}
    for off_y in range(3):
        row = plane * pitch + 7 + 8 * half + off_y
        for off_z in range(3):
            i = (tiles + k, k, tiles + k + 1)[off_z]
            found[off_y, off_z] = field[i, row:row + 8, :]
    return found


def edges_of(cells_ref, rows_ref, ylo_ref, yhi_ref):
    side, _, lanes = cells_ref.shape
    odd = lax.axis_index("gx") % 2
    rows_ref[:side] = cells_ref[jnp.where(odd == 1, 0, side - 1)]
    rows_ref[side:] = cells_ref[jnp.where(odd == 1, side - 1, 0)]
    row = lax.broadcasted_iota(jnp.int32, (2 * side, side * side), 0)
    col = lax.broadcasted_iota(jnp.int32, (2 * side, side * side), 1)
    wanted = jnp.where(row < side, row * side, (row - side) * side + side - 1)
    pick = jnp.where(col == wanted, 1.0, 0.0).astype(BF16)
    flat = cells_ref[...].reshape(side * side, lanes)
    found = jnp.dot(pick, flat, preferred_element_type=F32).astype(BF16)
    ylo_ref[...] = found[:side]
    yhi_ref[...] = found[side:]


def params_kernel(
    slots_ref, mix_ref, taps_ref, gain_ref, masks_ref, weights, mean_mat_ref, mix_mat_ref, gain_wide_ref
):
    channels = mix_ref.shape[0]
    level_masks(slots_ref[...], masks_ref.shape[1] - 8, masks_ref)
    wide = jnp.concatenate([taps_ref[...], taps_ref[...]], axis=1)
    for tap in range(27):
        weights[tap] = jnp.broadcast_to(wide[tap:tap + 1], (8, LANE))
    copies = WIDE // channels
    row_id = lax.broadcasted_iota(jnp.int32, (WIDE, WIDE), 0) // channels
    col_id = lax.broadcasted_iota(jnp.int32, (WIDE, WIDE), 1) // channels
    block = row_id == col_id
    mean_mat_ref[...] = jnp.where(block, 1.0 / channels, 0.0).astype(BF16)
    mix = mix_ref[...].astype(F32)
    mix_row = jnp.concatenate([mix] * copies, axis=1)
    mix_mat_ref[...] = jnp.where(block, jnp.concatenate([mix_row] * copies, axis=0), 0.0).astype(BF16)
    gain_wide_ref[...] = jnp.concatenate([gain_ref[...]] * copies, axis=1)


def own_first_kernel(flip, count, own_ref, weights, field, sums):
    own_part(own_ref, field, weights, sums, flip, 0, count)


def own_rest_kernel(flip, first, count, own_ref, weights, field, sums, field_out_ref, sums_out_ref):
    own_part(own_ref, field, weights, sums, flip, first, count)


def forward_kernel(
    field, depth, weights, mean_mat_ref, mix_mat_ref, gain_wide_ref,
    xlo_ref, xhi_ref, ylo_ref, yhi_ref, masks_ref, own_ref, cot_ref,
    field_out_ref, depth_out_ref, mixed_ref, grad_ref, grows_ref, gylo_ref, gyhi_ref,
    normed_bf, grads, gain_sum_ref,
):
    side = own_ref.shape[0]
    lanes = own_ref.shape[2]
    cells = side * side
    halo_part(xlo_ref, xhi_ref, ylo_ref, yhi_ref, masks_ref, field, weights, depth, False)

    mean_mat = mean_mat_ref[...]
    mix_mat = mix_mat_ref[...]
    gain = gain_wide_ref[...]
    rows = 128
    xs = rows // side
    gain_sum = jnp.zeros((8, WIDE), F32)
    for part in range(lanes // WIDE):
        cols = slice(part * WIDE, (part + 1) * WIDE)
        for chunk in range(cells // rows):
            at = slice(chunk * rows, (chunk + 1) * rows)
            planes = slice(chunk * xs, (chunk + 1) * xs)
            dep = jnp.concatenate([depth[2 * part, at, :], depth[2 * part + 1, at, :]], axis=1)
            mean_sq = jnp.dot((dep * dep).astype(BF16), mean_mat, preferred_element_type=F32)
            inv = lax.rsqrt(mean_sq + EPS)
            normed = dep * inv
            norm_bf = (normed * gain).astype(BF16)
            normed_bf[at, cols] = norm_bf
            branch = jnp.dot(norm_bf, mix_mat, preferred_element_type=F32)
            feat = own_ref[planes, :, cols].reshape(rows, WIDE).astype(F32)
            mixed_ref[planes, :, cols] = (feat + branch).astype(BF16).reshape(xs, side, WIDE)
            grad_norm = lax.dot_general(
                cot_ref[planes, :, cols].reshape(rows, WIDE), mix_mat,
                (((1,), (1,)), ((), ())), preferred_element_type=F32,
            )
            gain_sum = gain_sum + jnp.sum((grad_norm * normed).reshape(rows // 8, 8, WIDE), axis=0)
            scaled = grad_norm * gain
            mean = jnp.dot((scaled * normed).astype(BF16), mean_mat, preferred_element_type=F32)
            grad = (inv * (scaled - normed * mean)).astype(BF16)
            grad_ref[planes, :, cols] = grad.reshape(xs, side, WIDE)
            wide_grad = grad.astype(F32)
            grads[2 * part, at, :] = wide_grad[:, :LANE]
            grads[2 * part + 1, at, :] = wide_grad[:, LANE:]
    gain_sum_ref[...] = gain_sum
    edges_of(grad_ref, grows_ref, gylo_ref, gyhi_ref)


def tap_sums(field, grads, sums, first, count):
    tiles, cells, _ = grads.shape
    side = math.isqrt(cells)
    pitch = side + 8

    def tap_tile(k, sums):
        sums = list(sums)
        for half in range(side // 8):
            near_grads = {}
            for plane in range(side + 2):
                if plane < side:
                    row = plane * side + 8 * half
                    near_grads[plane] = grads[k, row:row + 8, :]
                near = shifted(field, tiles, k, plane, half, pitch)
                for (off_y, off_z), value in near.items():
                    for off_x in range(3):
                        x = plane - off_x
                        if 0 <= x < side:
                            tap = 9 * off_x + 3 * off_y + off_z
                            sums[tap] = sums[tap] + value * near_grads[x]
                near_grads.pop(plane - 2, None)
        return tuple(sums)

    return lax.fori_loop(first, first + count, tap_tile, sums)


def first_sums_kernel(count, field, grads, tap_sums_ref):
    sums = tap_sums(field, grads, tuple(jnp.zeros((8, LANE), F32) for _ in range(27)), 0, count)
    for tap in range(27):
        tap_sums_ref[tap] = sums[tap]


def sums_kernel(first, field, normed_bf, grads, gain_sum_ref, cot_ref, tap_sums_ref, packed_ref):
    side, _, lanes = cot_ref.shape
    channels = packed_ref.shape[1] // 2
    cells = side * side
    copies = WIDE // channels
    mix_sum = jnp.zeros((WIDE, WIDE), F32)
    for part in range(lanes // WIDE):
        cols = slice(part * WIDE, (part + 1) * WIDE)
        mix_sum = mix_sum + lax.dot_general(
            normed_bf[:, cols],
            cot_ref[:, :, cols].reshape(cells, WIDE),
            (((0,), (0,)), ((), ())),
            preferred_element_type=F32,
        )
    grad_mix = mix_sum[:channels, :channels]
    for i in range(1, copies):
        span = slice(i * channels, (i + 1) * channels)
        grad_mix = grad_mix + mix_sum[span, span]
    packed_ref[0:32, :] = jnp.concatenate([grad_mix[:32], grad_mix[32:]], axis=1)

    sums = tap_sums(field, grads, tuple(tap_sums_ref[tap] for tap in range(27)), first, lanes // LANE - first)
    gain_row = jnp.sum(gain_sum_ref[...], axis=0, keepdims=True)
    rows = [jnp.sum(t, axis=0, keepdims=True) for t in sums] + [gain_row[:, :LANE] + gain_row[:, LANE:]]
    rows = jnp.concatenate(rows + [jnp.zeros((4, LANE), F32)], axis=0)
    rows = rows[:, :channels] + rows[:, channels:]
    packed_ref[32:48, :] = jnp.concatenate([rows[:16], rows[16:]], axis=1)


def backward_kernel(
    field, sums, weights, xlo_ref, xhi_ref, ylo_ref, yhi_ref, masks_ref, cot_ref,
    field_out_ref, sums_out_ref, out_ref,
):
    side = cot_ref.shape[0]
    halo_part(xlo_ref, xhi_ref, ylo_ref, yhi_ref, masks_ref, field, weights, sums, True)
    for x in range(side):
        for k in range(sums.shape[0]):
            cols = slice(k * LANE, (k + 1) * LANE)
            cot = cot_ref[x, :, cols].astype(F32)
            out_ref[x, :, cols] = (cot + sums[k, x * side:(x + 1) * side, :]).astype(BF16)


def unpack_kernel(mine_ref, theirs_ref, taps_hbm, gain_hbm, mix_hbm, taps_ref, gain_ref, mix_ref, done):
    total = mine_ref[...] + theirs_ref[...]
    channels = mix_ref.shape[0]
    mix_ref[0:32, :] = total[:32, :channels]
    mix_ref[32:64, :] = total[:32, channels:]
    taps_ref[0:16, :] = total[32:48, :channels]
    taps_ref[16:27, :] = total[32:43, channels:]
    gain_ref[...] = total[43:44, channels:]
    copies = [
        pltpu.make_async_copy(src, dst, done.at[i])
        for i, (src, dst) in enumerate(((taps_ref, taps_hbm), (gain_ref, gain_hbm), (mix_ref, mix_hbm)))
    ]
    for copy in copies:
        copy.start()
    for copy in copies:
        copy.wait()


def swap(message, axis):
    count = lax.axis_size(axis)
    return lax.ppermute(message, axis, [(i, i ^ 1) for i in range(count) if i ^ 1 < count])


def pass_on(message, axis):
    count = lax.axis_size(axis)
    pairs = [(i, i + 2) for i in range(0, count - 2, 2)] + [(i, i - 2) for i in range(3, count, 2)]
    return lax.ppermute(message, axis, pairs)


def low_high(near, far, axis):
    odd = lax.axis_index(axis) % 2 == 1
    return jnp.where(odd, near, far), jnp.where(odd, far, near)


def y_message(xlo, xhi, ylo, yhi):
    low = jnp.concatenate([xlo[:1], ylo, xhi[:1]], axis=0)
    high = jnp.concatenate([xlo[-1:], yhi, xhi[-1:]], axis=0)
    odd = lax.axis_index("gy") % 2 == 1
    return jnp.concatenate([jnp.where(odd, low, high), jnp.where(odd, high, low)], axis=0)


def sum_steps():
    steps = []
    for axis in ("gx", "gy"):
        count = lax.axis_size(axis)
        bit = 1
        while bit < count:
            steps.append((axis, [(i, i ^ bit) for i in range(count)]))
            bit *= 2
    return steps


def shards(features, slot_map, tap_weights, gain, mix_weight, cotangent):
    side, _, _, lanes = features.shape
    channels = gain.shape[0]
    tiles = lanes // LANE
    cells = features.reshape(side, side, lanes)
    cot = cotangent.reshape(side, side, lanes)
    vmem = pl.BlockSpec(memory_space=pltpu.VMEM)
    hbm = pl.BlockSpec(memory_space=pltpu.HBM)
    block = jax.ShapeDtypeStruct((side, side, lanes), BF16)
    edge = jax.ShapeDtypeStruct((side, lanes), BF16)
    two_rows = jax.ShapeDtypeStruct((2 * side, lanes), BF16)
    field_type = jax.ShapeDtypeStruct((2 * tiles + 1, (side + 2) * (side + 8) + 8, LANE), F32)
    sums_type = jax.ShapeDtypeStruct((tiles, side * side, LANE), F32)
    weights_type = jax.ShapeDtypeStruct((27, 8, LANE), F32)
    mat_type = jax.ShapeDtypeStruct((WIDE, WIDE), BF16)

    def call(kernel, name, operands, outs, scratch=(), aliases={}, flops=0, in_specs=None, out_specs=None):
        return pl.pallas_call(
            kernel,
            out_shape=tuple(jax.ShapeDtypeStruct(t.shape, t.dtype) for t in outs),
            in_specs=in_specs or [vmem] * len(operands),
            out_specs=out_specs or (vmem,) * len(outs),
            scratch_shapes=list(scratch),
            input_output_aliases=aliases,
            compiler_params=pltpu.CompilerParams(vmem_limit_bytes=40 * 1024 * 1024),
            cost_estimate=pl.CostEstimate(flops=flops, bytes_accessed=500_000, transcendentals=0),
            name=name,
        )(*operands)

    half = tiles // 2

    def own_first(flip, block_cells, weights, name):
        kernel = functools.partial(own_first_kernel, flip, half)
        return call(kernel, name, (block_cells, weights), (field_type, sums_type), flops=10_000_000)

    def own_rest(flip, block_cells, weights, field, sums, name):
        kernel = functools.partial(own_rest_kernel, flip, half, tiles - half)
        return call(
            kernel, name, (block_cells, weights, field, sums), (field_type, sums_type),
            aliases={2: 0, 3: 1}, flops=10_000_000,
        )

    rows, ylo, yhi = call(edges_of, "edges", (cells,), (two_rows, edge, edge), flops=100_000_000_000)
    masks, weights, mean_mat, mix_mat, gain_wide = call(
        params_kernel,
        "params",
        (jnp.transpose(slot_map, (1, 2, 0)), mix_weight, tap_weights, gain.reshape(1, channels)),
        (
            jax.ShapeDtypeStruct((12, side + 8, LANE), F32),
            weights_type,
            mat_type,
            mat_type,
            jax.ShapeDtypeStruct((1, WIDE), F32),
        ),
    )
    rows = swap(rows, "gx")
    rows, weights = lax.optimization_barrier((rows, weights))
    far = pass_on(rows[side:], "gx")
    field, sums = own_first(False, cells, weights, "own_forward_a")
    far, field, sums = lax.optimization_barrier((far, field, sums))
    xlo, xhi = low_high(rows[:side], far, "gx")
    columns = swap(y_message(xlo, xhi, ylo, yhi), "gy")
    field, sums = own_rest(False, cells, weights, field, sums, "own_forward_b")
    columns, field, sums = lax.optimization_barrier((columns, field, sums))
    ylo, yhi = low_high(columns[:side + 2], pass_on(columns[side + 2:], "gy"), "gy")
    field, _, mixed, grad_depth, rows, gylo, gyhi, normed_bf, grads, gain_sum = call(
        forward_kernel,
        "forward",
        (field, sums, weights, mean_mat, mix_mat, gain_wide, xlo, xhi, ylo, yhi, masks, cells, cot),
        (
            field_type, sums_type, block, block, two_rows, edge, edge,
            jax.ShapeDtypeStruct((side * side, lanes), BF16), sums_type, jax.ShapeDtypeStruct((8, WIDE), F32),
        ),
        aliases={0: 0, 1: 1},
        flops=10_000_000,
    )

    steps = sum_steps()
    rows = swap(rows, "gx")
    (tap_part,) = call(
        functools.partial(first_sums_kernel, half), "sums_a", (field, grads), (weights_type,), flops=5_000_000
    )
    rows, tap_part = lax.optimization_barrier((rows, tap_part))
    far = pass_on(rows[side:], "gx")
    (part,) = call(
        functools.partial(sums_kernel, half),
        "sums_b",
        (field, normed_bf, grads, gain_sum, cot, tap_part),
        (jax.ShapeDtypeStruct((48, LANE), F32),),
        flops=5_000_000,
    )
    theirs = lax.ppermute(part, *steps[0])
    part, near, far = lax.optimization_barrier((part + theirs, rows[:side], far))
    theirs = lax.ppermute(part, *steps[1])
    gxlo, gxhi = low_high(near, far, "gx")
    columns, grad_depth = lax.optimization_barrier((y_message(gxlo, gxhi, gylo, gyhi), grad_depth))
    columns = swap(columns, "gy")
    field, sums = own_first(True, grad_depth, weights, "own_backward_a")
    part, columns, field, sums = lax.optimization_barrier((part + theirs, columns, field, sums))
    theirs = lax.ppermute(part, *steps[2])
    gylo, gyhi = low_high(columns[:side + 2], pass_on(columns[side + 2:], "gy"), "gy")
    field, sums = own_rest(True, grad_depth, weights, field, sums, "own_backward_b")
    part, field, sums = lax.optimization_barrier((part + theirs, field, sums))
    _, _, grad_features = call(
        backward_kernel,
        "backward",
        (field, sums, weights, gxlo, gxhi, gylo, gyhi, masks, cot),
        (field_type, sums_type, block),
        aliases={0: 0, 1: 1},
        flops=2_000_000,
    )
    for index, step in enumerate(steps[3:-1]):
        part = part + lax.ppermute(part, *step)
        if index == 0:
            part, grad_features = lax.optimization_barrier((part, grad_features))
    theirs = lax.ppermute(part, *steps[-1])

    outs = (
        jax.ShapeDtypeStruct((27, channels), F32),
        jax.ShapeDtypeStruct((1, channels), F32),
        jax.ShapeDtypeStruct((channels, channels), F32),
    )
    grad_taps, grad_gain, grad_mix = call(
        unpack_kernel,
        "unpack",
        (part, theirs),
        outs,
        scratch=[pltpu.VMEM(t.shape, F32) for t in outs] + [pltpu.SemaphoreType.DMA((3,))],
        out_specs=(hbm,) * 3,
    )
    shape = features.shape
    return (mixed.reshape(shape), grad_features.reshape(shape), grad_taps, grad_gain.reshape(channels), grad_mix)


def solution(mesh):
    return jax.shard_map(
        shards,
        mesh=mesh,
        in_specs=(P("gx", "gy", None, None), P(), P(), P(), P(), P("gx", "gy", None, None)),
        out_specs=(P("gx", "gy", None, None), P("gx", "gy", None, None), P(), P(), P()),
        check_vma=False,
    )
```

```python
import functools

import jax
import jax.numpy as jnp
from jax import lax
from jax.experimental import pallas as pl
from jax.experimental.pallas import tpu as pltpu
from jax.sharding import PartitionSpec as P

EPS = 1e-05
LANE = 128
WIDE = 256
F32 = jnp.float32
BF16 = jnp.bfloat16


def level_masks(slots, side, masks_ref):
    level = lax.broadcasted_iota(jnp.int32, slots.shape, 1)
    at_x = lax.broadcasted_iota(jnp.int32, slots.shape, 2) - lax.axis_index("gx")
    at_y = lax.broadcasted_iota(jnp.int32, slots.shape, 0) - lax.axis_index("gy")
    place = jnp.where(slots >= 0, level + 1, 0).astype(F32)

    def near(off_x, off_y):
        found = jnp.where((at_x == off_x) & (at_y == off_y), place, 0.0)
        found = jnp.sum(jnp.sum(found, axis=0), axis=0, keepdims=True)
        return jnp.sum(found, axis=1, keepdims=True)

    own = near(0, 0)

    def difference(off_x, off_y):
        found = near(off_x, off_y)
        return jnp.where(found > 0.0, found - own, 9.0)

    rows = masks_ref.shape[1]
    row = lax.broadcasted_iota(jnp.int32, (rows, LANE), 0)
    for edge in range(4):
        high = 1 if edge % 2 else -1
        if edge < 2:
            d = jnp.broadcast_to(difference(high, 0), (rows, LANE))
        else:
            corner, middle, other = (difference(off, high) for off in (-1, 0, 1))
            d = jnp.where(row == 0, corner, jnp.where(row == side + 1, other, middle))
        for i, want in enumerate((0.0, -1.0, 1.0)):
            masks_ref[3 * edge + i] = jnp.where(d == want, 1.0, 0.0)


def plane_tiles(load, total, masks):
    low = lax.broadcasted_iota(jnp.int32, load(0).shape, 1) < LANE // 2
    zero = jnp.zeros(load(0).shape, F32)
    aligned = [load(k) for k in range(total)]
    turned = [pltpu.roll(t, LANE // 2, 1) for t in aligned]
    between = [jnp.where(low, turned[j - 1], turned[j]) for j in range(1, total)]
    if masks is None:
        return aligned + [jnp.where(low, zero, turned[0])] + between + [jnp.where(low, turned[-1], zero)]
    same, below, above = masks
    first = jnp.where(low, turned[-1] * below, turned[0] * same)
    last = jnp.where(low, turned[-1] * same, turned[0] * above)
    return [t * same for t in aligned] + [first] + [t * same for t in between] + [last]


def loader(rows):
    return lambda k: rows[:, k * LANE:(k + 1) * LANE].astype(F32)


def column_starts(side, shift):
    pitch = side + 8
    for start in range(0, side + 2, 8):
        size = min(8, side + 2 - start)
        yield start, size, pl.ds(start * pitch + shift, size, stride=pitch)


def own_part(own_ref, field, weights, sums, flip):
    side = own_ref.shape[0]
    tiles = own_ref.shape[2] // LANE
    pitch = side + 8

    def own_plane(x, _):
        base = pl.multiple_of((x + 1) * pitch + 8, 8)
        for i, t in enumerate(plane_tiles(loader(own_ref[x]), tiles, None)):
            field[i, pl.ds(base, side), :] = t
        return 0

    lax.fori_loop(0, side, own_plane, 0)
    for i in range(2 * tiles + 1):
        for shift in (7, pitch):
            for _, size, at in column_starts(side, shift):
                field[i, at, :] = jnp.zeros((size, LANE), F32)

    def tile(k, _):
        taps = [weights[26 - t if flip else t] for t in range(27)]
        for half in range(side // 8):
            part = {}
            for plane in range(1, side + 1):
                near = shifted(field, tiles, k, plane, half, pitch)
                for off_x in range(3):
                    x = plane - off_x
                    if not 0 <= x < side:
                        continue
                    for (off_y, off_z), value in near.items():
                        term = value * taps[9 * off_x + 3 * off_y + off_z]
                        part[x] = part[x] + term if x in part else term
                done = plane - 2
                for x in [done, done + 1] if plane == side else [done]:
                    if x >= 0:
                        sums[k, x * side + 8 * half:x * side + 8 * half + 8, :] = part.pop(x)
        return 0

    lax.fori_loop(0, tiles, tile, 0)


def halo_part(xlo_ref, xhi_ref, ylo_ref, yhi_ref, masks_ref, field, weights, sums, flip):
    side, lanes = xlo_ref.shape
    tiles = lanes // LANE
    pitch = side + 8

    def place(i, ref):
        rows = ref.shape[0]
        masks = tuple(masks_ref[3 * i + m, :rows, :] for m in range(3))
        return plane_tiles(loader(ref[...]), tiles, masks)

    for i, ref, plane in ((0, xlo_ref, 0), (1, xhi_ref, side + 1)):
        for j, t in enumerate(place(i, ref)):
            field[j, plane * pitch + 8:plane * pitch + 8 + side, :] = t

    def x_tile(k, _):
        for plane, off_x, x in ((0, 0, 0), (side + 1, 2, side - 1)):
            for half in range(side // 8):
                row = x * side + 8 * half
                total = sums[k, row:row + 8, :]
                for (off_y, off_z), value in shifted(field, tiles, k, plane, half, pitch).items():
                    tap = 9 * off_x + 3 * off_y + off_z
                    total = total + value * weights[26 - tap if flip else tap]
                sums[k, row:row + 8, :] = total
        return 0

    lax.fori_loop(0, tiles, x_tile, 0)

    for i, ref, shift in ((2, ylo_ref, 7), (3, yhi_ref, pitch)):
        for j, t in enumerate(place(i, ref)):
            for start, size, at in column_starts(side, shift):
                field[j, at, :] = t[start:start + size]

    def y_tile(k, _):
        for shift, off_y, y in ((7, 0, 0), (pitch, 2, side - 1)):
            for x in range(0, side, 8):
                at = pl.ds(x * side + y, 8, stride=side)
                total = sums[k, at, :]
                for off_x in range(3):
                    for off_z in range(3):
                        i = (tiles + k, k, tiles + k + 1)[off_z]
                        tap = 9 * off_x + 3 * off_y + off_z
                        value = field[i, pl.ds((x + off_x) * pitch + shift, 8, stride=pitch), :]
                        total = total + value * weights[26 - tap if flip else tap]
                sums[k, at, :] = total
        return 0

    lax.fori_loop(0, tiles, y_tile, 0)


def shifted(field, tiles, k, plane, half, pitch):
    found = {}
    for off_y in range(3):
        row = plane * pitch + 7 + 8 * half + off_y
        for off_z in range(3):
            i = (tiles + k, k, tiles + k + 1)[off_z]
            found[off_y, off_z] = field[i, row:row + 8, :]
    return found


def edges_of(cells_ref, xa_ref, xb_ref, ylo_ref, yhi_ref):
    side, _, lanes = cells_ref.shape
    odd = lax.axis_index("gx") % 2
    xa_ref[...] = cells_ref[jnp.where(odd == 1, 0, side - 1)]
    xb_ref[...] = cells_ref[jnp.where(odd == 1, side - 1, 0)]
    row = lax.broadcasted_iota(jnp.int32, (2 * side, side * side), 0)
    col = lax.broadcasted_iota(jnp.int32, (2 * side, side * side), 1)
    wanted = jnp.where(row < side, row * side, (row - side) * side + side - 1)
    pick = jnp.where(col == wanted, 1.0, 0.0).astype(BF16)
    flat = cells_ref[...].reshape(side * side, lanes)
    found = jnp.dot(pick, flat, preferred_element_type=F32).astype(BF16)
    ylo_ref[...] = found[:side]
    yhi_ref[...] = found[side:]


def params_kernel(
    slots_ref, mix_ref, taps_ref, gain_ref, masks_ref, weights, mean_mat_ref, mix_mat_ref, gain_wide_ref
):
    channels = mix_ref.shape[0]
    level_masks(slots_ref[...], masks_ref.shape[1] - 8, masks_ref)
    wide = jnp.concatenate([taps_ref[...], taps_ref[...]], axis=1)
    for tap in range(27):
        weights[tap] = jnp.broadcast_to(wide[tap:tap + 1], (8, LANE))
    copies = WIDE // channels
    row_id = lax.broadcasted_iota(jnp.int32, (WIDE, WIDE), 0) // channels
    col_id = lax.broadcasted_iota(jnp.int32, (WIDE, WIDE), 1) // channels
    block = row_id == col_id
    mean_mat_ref[...] = jnp.where(block, 1.0 / channels, 0.0).astype(BF16)
    mix = mix_ref[...].astype(F32)
    mix_row = jnp.concatenate([mix] * copies, axis=1)
    mix_mat_ref[...] = jnp.where(block, jnp.concatenate([mix_row] * copies, axis=0), 0.0).astype(BF16)
    gain_wide_ref[...] = jnp.concatenate([gain_ref[...]] * copies, axis=1)


def own_kernel(flip, own_ref, weights, field, sums):
    own_part(own_ref, field, weights, sums, flip)


def forward_kernel(
    field, depth, weights, mean_mat_ref, mix_mat_ref, gain_wide_ref,
    xlo_ref, xhi_ref, ylo_ref, yhi_ref, masks_ref, own_ref, cot_ref,
    field_out_ref, depth_out_ref, mixed_ref, grad_ref, gxa_ref, gxb_ref, gylo_ref, gyhi_ref,
    normed_bf, grads, gain_sum_ref,
):
    side = own_ref.shape[0]
    lanes = own_ref.shape[2]
    cells = side * side
    halo_part(xlo_ref, xhi_ref, ylo_ref, yhi_ref, masks_ref, field, weights, depth, False)

    mean_mat = mean_mat_ref[...]
    mix_mat = mix_mat_ref[...]
    gain = gain_wide_ref[...]
    rows = 128
    xs = rows // side
    gain_sum = jnp.zeros((8, WIDE), F32)
    for part in range(lanes // WIDE):
        cols = slice(part * WIDE, (part + 1) * WIDE)
        for chunk in range(cells // rows):
            at = slice(chunk * rows, (chunk + 1) * rows)
            planes = slice(chunk * xs, (chunk + 1) * xs)
            dep = jnp.concatenate([depth[2 * part, at, :], depth[2 * part + 1, at, :]], axis=1)
            mean_sq = jnp.dot((dep * dep).astype(BF16), mean_mat, preferred_element_type=F32)
            inv = lax.rsqrt(mean_sq + EPS)
            normed = dep * inv
            norm_bf = (normed * gain).astype(BF16)
            normed_bf[at, cols] = norm_bf
            branch = jnp.dot(norm_bf, mix_mat, preferred_element_type=F32)
            feat = own_ref[planes, :, cols].reshape(rows, WIDE).astype(F32)
            mixed_ref[planes, :, cols] = (feat + branch).astype(BF16).reshape(xs, side, WIDE)
            grad_norm = lax.dot_general(
                cot_ref[planes, :, cols].reshape(rows, WIDE), mix_mat,
                (((1,), (1,)), ((), ())), preferred_element_type=F32,
            )
            gain_sum = gain_sum + jnp.sum((grad_norm * normed).reshape(rows // 8, 8, WIDE), axis=0)
            scaled = grad_norm * gain
            mean = jnp.dot((scaled * normed).astype(BF16), mean_mat, preferred_element_type=F32)
            grad = (inv * (scaled - normed * mean)).astype(BF16)
            grad_ref[planes, :, cols] = grad.reshape(xs, side, WIDE)
            wide_grad = grad.astype(F32)
            grads[2 * part, at, :] = wide_grad[:, :LANE]
            grads[2 * part + 1, at, :] = wide_grad[:, LANE:]
    gain_sum_ref[...] = gain_sum
    edges_of(grad_ref, gxa_ref, gxb_ref, gylo_ref, gyhi_ref)


def sums_kernel(field, normed_bf, grads, gain_sum_ref, cot_ref, packed_ref):
    side, _, lanes = cot_ref.shape
    tiles = lanes // LANE
    channels = packed_ref.shape[1] // 2
    pitch = side + 8
    cells = side * side
    copies = WIDE // channels
    mix_sum = jnp.zeros((WIDE, WIDE), F32)
    for part in range(lanes // WIDE):
        cols = slice(part * WIDE, (part + 1) * WIDE)
        mix_sum = mix_sum + lax.dot_general(
            normed_bf[:, cols],
            cot_ref[:, :, cols].reshape(cells, WIDE),
            (((0,), (0,)), ((), ())),
            preferred_element_type=F32,
        )
    grad_mix = mix_sum[:channels, :channels]
    for i in range(1, copies):
        span = slice(i * channels, (i + 1) * channels)
        grad_mix = grad_mix + mix_sum[span, span]
    packed_ref[0:32, :] = jnp.concatenate([grad_mix[:32], grad_mix[32:]], axis=1)

    def tap_tile(k, sums):
        sums = list(sums)
        for half in range(side // 8):
            near_grads = {}
            for plane in range(side + 2):
                if plane < side:
                    row = plane * side + 8 * half
                    near_grads[plane] = grads[k, row:row + 8, :]
                near = shifted(field, tiles, k, plane, half, pitch)
                for (off_y, off_z), value in near.items():
                    for off_x in range(3):
                        x = plane - off_x
                        if 0 <= x < side:
                            tap = 9 * off_x + 3 * off_y + off_z
                            sums[tap] = sums[tap] + value * near_grads[x]
                near_grads.pop(plane - 2, None)
        return tuple(sums)

    sums = lax.fori_loop(0, tiles, tap_tile, tuple(jnp.zeros((8, LANE), F32) for _ in range(27)))
    gain_row = jnp.sum(gain_sum_ref[...], axis=0, keepdims=True)
    rows = [jnp.sum(t, axis=0, keepdims=True) for t in sums] + [gain_row[:, :LANE] + gain_row[:, LANE:]]
    rows = jnp.concatenate(rows + [jnp.zeros((4, LANE), F32)], axis=0)
    rows = rows[:, :channels] + rows[:, channels:]
    packed_ref[32:48, :] = jnp.concatenate([rows[:16], rows[16:]], axis=1)


def backward_kernel(
    field, sums, weights, xlo_ref, xhi_ref, ylo_ref, yhi_ref, masks_ref, cot_ref,
    field_out_ref, sums_out_ref, out_ref,
):
    side = cot_ref.shape[0]
    halo_part(xlo_ref, xhi_ref, ylo_ref, yhi_ref, masks_ref, field, weights, sums, True)
    for x in range(side):
        for k in range(sums.shape[0]):
            cols = slice(k * LANE, (k + 1) * LANE)
            cot = cot_ref[x, :, cols].astype(F32)
            out_ref[x, :, cols] = (cot + sums[k, x * side:(x + 1) * side, :]).astype(BF16)


def unpack_kernel(mine_ref, theirs_ref, taps_hbm, gain_hbm, mix_hbm, taps_ref, gain_ref, mix_ref, done):
    total = mine_ref[...] + theirs_ref[...]
    channels = mix_ref.shape[0]
    mix_ref[0:32, :] = total[:32, :channels]
    mix_ref[32:64, :] = total[:32, channels:]
    taps_ref[0:16, :] = total[32:48, :channels]
    taps_ref[16:27, :] = total[32:43, channels:]
    gain_ref[...] = total[43:44, channels:]
    copies = [
        pltpu.make_async_copy(src, dst, done.at[i])
        for i, (src, dst) in enumerate(((taps_ref, taps_hbm), (gain_ref, gain_hbm), (mix_ref, mix_hbm)))
    ]
    for copy in copies:
        copy.start()
    for copy in copies:
        copy.wait()


def swap(to_first, to_second, axis):
    count = lax.axis_size(axis)
    first = [(i, i ^ 1) for i in range(count)]
    second = [(i, (((i + 1) ^ 1) - 1) % count) for i in range(count)]
    return lax.ppermute(to_first, axis, first), lax.ppermute(to_second, axis, second)


def low_high(from_first, from_second, axis):
    odd = lax.axis_index(axis) % 2 == 1
    return jnp.where(odd, from_first, from_second), jnp.where(odd, from_second, from_first)


def y_messages(xlo, xhi, ylo, yhi):
    low = jnp.concatenate([xlo[:1], ylo, xhi[:1]], axis=0)
    high = jnp.concatenate([xlo[-1:], yhi, xhi[-1:]], axis=0)
    return low_high(low, high, "gy")


def sum_steps():
    steps = []
    for axis in ("gx", "gy"):
        count = lax.axis_size(axis)
        bit = 1
        while bit < count:
            steps.append((axis, [(i, i ^ bit) for i in range(count)]))
            bit *= 2
    return steps


def shards(features, slot_map, tap_weights, gain, mix_weight, cotangent):
    side, _, _, lanes = features.shape
    channels = gain.shape[0]
    tiles = lanes // LANE
    cells = features.reshape(side, side, lanes)
    cot = cotangent.reshape(side, side, lanes)
    vmem = pl.BlockSpec(memory_space=pltpu.VMEM)
    hbm = pl.BlockSpec(memory_space=pltpu.HBM)
    block = jax.ShapeDtypeStruct((side, side, lanes), BF16)
    edge = jax.ShapeDtypeStruct((side, lanes), BF16)
    field_type = jax.ShapeDtypeStruct((2 * tiles + 1, (side + 2) * (side + 8) + 8, LANE), F32)
    sums_type = jax.ShapeDtypeStruct((tiles, side * side, LANE), F32)
    weights_type = jax.ShapeDtypeStruct((27, 8, LANE), F32)
    mat_type = jax.ShapeDtypeStruct((WIDE, WIDE), BF16)

    def call(kernel, name, operands, outs, scratch=(), aliases={}, flops=0, in_specs=None, out_specs=None):
        return pl.pallas_call(
            kernel,
            out_shape=tuple(jax.ShapeDtypeStruct(t.shape, t.dtype) for t in outs),
            in_specs=in_specs or [vmem] * len(operands),
            out_specs=out_specs or (vmem,) * len(outs),
            scratch_shapes=list(scratch),
            input_output_aliases=aliases,
            compiler_params=pltpu.CompilerParams(vmem_limit_bytes=40 * 1024 * 1024),
            cost_estimate=pl.CostEstimate(flops=flops, bytes_accessed=500_000, transcendentals=0),
            name=name,
        )(*operands)

    xa, xb, ylo, yhi = call(edges_of, "edges", (cells,), (edge, edge, edge, edge), flops=100_000_000_000)
    masks, weights, mean_mat, mix_mat, gain_wide = call(
        params_kernel,
        "params",
        (jnp.transpose(slot_map, (1, 2, 0)), mix_weight, tap_weights, gain.reshape(1, channels)),
        (
            jax.ShapeDtypeStruct((12, side + 8, LANE), F32),
            weights_type,
            mat_type,
            mat_type,
            jax.ShapeDtypeStruct((1, WIDE), F32),
        ),
    )
    xlo, xhi = low_high(*swap(xa, xb, "gx"), "gx")
    to_a, to_b = y_messages(xlo, xhi, ylo, yhi)
    to_a, to_b, weights = lax.optimization_barrier((to_a, to_b, weights))
    ylo, yhi = low_high(*swap(to_a, to_b, "gy"), "gy")
    own_field, own_sums = call(
        functools.partial(own_kernel, False), "own_forward", (cells, weights), (field_type, sums_type),
        flops=10_000_000,
    )
    field, _, mixed, grad_depth, gxa, gxb, gylo, gyhi, normed_bf, grads, gain_sum = call(
        forward_kernel,
        "forward",
        (own_field, own_sums, weights, mean_mat, mix_mat, gain_wide, xlo, xhi, ylo, yhi, masks, cells, cot),
        (
            field_type, sums_type, block, block, edge, edge, edge, edge,
            jax.ShapeDtypeStruct((side * side, lanes), BF16), sums_type, jax.ShapeDtypeStruct((8, WIDE), F32),
        ),
        aliases={0: 0, 1: 1},
        flops=10_000_000,
    )
    gxlo, gxhi = low_high(*swap(gxa, gxb, "gx"), "gx")
    (part,) = call(
        sums_kernel,
        "sums",
        (field, normed_bf, grads, gain_sum, cot),
        (jax.ShapeDtypeStruct((48, LANE), F32),),
        flops=10_000_000,
    )

    steps = sum_steps()
    part, to_a, to_b = lax.optimization_barrier((part, *y_messages(gxlo, gxhi, gylo, gyhi)))
    gylo, gyhi = low_high(*swap(to_a, to_b, "gy"), "gy")
    part = part + lax.ppermute(part, *steps[0])
    part, grad_depth = lax.optimization_barrier((part, grad_depth))
    theirs = lax.ppermute(part, *steps[1])
    own_field, own_sums = call(
        functools.partial(own_kernel, True), "own_backward", (grad_depth, weights), (field_type, sums_type),
        flops=10_000_000,
    )
    part, gylo, gyhi, own_field, own_sums = lax.optimization_barrier(
        (part + theirs, gylo, gyhi, own_field, own_sums)
    )
    _, _, grad_features = call(
        backward_kernel,
        "backward",
        (own_field, own_sums, weights, gxlo, gxhi, gylo, gyhi, masks, cot),
        (field_type, sums_type, block),
        aliases={0: 0, 1: 1},
        flops=2_000_000,
    )
    for index, step in enumerate(steps[2:-1]):
        part = part + lax.ppermute(part, *step)
        if index == 0:
            part, grad_features = lax.optimization_barrier((part, grad_features))
    theirs = lax.ppermute(part, *steps[-1])

    outs = (
        jax.ShapeDtypeStruct((27, channels), F32),
        jax.ShapeDtypeStruct((1, channels), F32),
        jax.ShapeDtypeStruct((channels, channels), F32),
    )
    grad_taps, grad_gain, grad_mix = call(
        unpack_kernel,
        "unpack",
        (part, theirs),
        outs,
        scratch=[pltpu.VMEM(t.shape, F32) for t in outs] + [pltpu.SemaphoreType.DMA((3,))],
        out_specs=(hbm,) * 3,
    )
    shape = features.shape
    return (mixed.reshape(shape), grad_features.reshape(shape), grad_taps, grad_gain.reshape(channels), grad_mix)


def solution(mesh):
    return jax.shard_map(
        shards,
        mesh=mesh,
        in_specs=(P("gx", "gy", None, None), P(), P(), P(), P(), P("gx", "gy", None, None)),
        out_specs=(P("gx", "gy", None, None), P("gx", "gy", None, None), P(), P(), P()),
        check_vma=False,
    )
```

```python
import functools

import jax
import jax.numpy as jnp
from jax import lax
from jax.experimental import pallas as pl
from jax.experimental.pallas import tpu as pltpu
from jax.sharding import PartitionSpec as P

EPS = 1e-05
LANE = 128
WIDE = 256
F32 = jnp.float32
BF16 = jnp.bfloat16


def level_masks(slots, side, masks_ref):
    level = lax.broadcasted_iota(jnp.int32, slots.shape, 1)
    at_x = lax.broadcasted_iota(jnp.int32, slots.shape, 2) - lax.axis_index("gx")
    at_y = lax.broadcasted_iota(jnp.int32, slots.shape, 0) - lax.axis_index("gy")
    place = jnp.where(slots >= 0, level + 1, 0).astype(F32)

    def near(off_x, off_y):
        found = jnp.where((at_x == off_x) & (at_y == off_y), place, 0.0)
        found = jnp.sum(jnp.sum(found, axis=0), axis=0, keepdims=True)
        return jnp.sum(found, axis=1, keepdims=True)

    own = near(0, 0)

    def difference(off_x, off_y):
        found = near(off_x, off_y)
        return jnp.where(found > 0.0, found - own, 9.0)

    rows = masks_ref.shape[1]
    row = lax.broadcasted_iota(jnp.int32, (rows, LANE), 0)
    for edge in range(4):
        high = 1 if edge % 2 else -1
        if edge < 2:
            d = jnp.broadcast_to(difference(high, 0), (rows, LANE))
        else:
            corner, middle, other = (difference(off, high) for off in (-1, 0, 1))
            d = jnp.where(row == 0, corner, jnp.where(row == side + 1, other, middle))
        for i, want in enumerate((0.0, -1.0, 1.0)):
            masks_ref[3 * edge + i] = jnp.where(d == want, 1.0, 0.0)


def plane_tiles(load, total, masks):
    low = lax.broadcasted_iota(jnp.int32, load(0).shape, 1) < LANE // 2
    zero = jnp.zeros(load(0).shape, F32)
    aligned = [load(k) for k in range(total)]
    turned = [pltpu.roll(t, LANE // 2, 1) for t in aligned]
    between = [jnp.where(low, turned[j - 1], turned[j]) for j in range(1, total)]
    if masks is None:
        return aligned + [jnp.where(low, zero, turned[0])] + between + [jnp.where(low, turned[-1], zero)]
    same, below, above = masks
    first = jnp.where(low, turned[-1] * below, turned[0] * same)
    last = jnp.where(low, turned[-1] * same, turned[0] * above)
    return [t * same for t in aligned] + [first] + [t * same for t in between] + [last]


def loader(rows):
    return lambda k: rows[:, k * LANE:(k + 1) * LANE].astype(F32)


def column_starts(side, shift):
    pitch = side + 8
    for start in range(0, side + 2, 8):
        size = min(8, side + 2 - start)
        yield start, size, pl.ds(start * pitch + shift, size, stride=pitch)


def own_part(own_ref, field, weights, sums, flip):
    side = own_ref.shape[0]
    tiles = own_ref.shape[2] // LANE
    pitch = side + 8

    def own_plane(x, _):
        base = pl.multiple_of((x + 1) * pitch + 8, 8)
        for i, t in enumerate(plane_tiles(loader(own_ref[x]), tiles, None)):
            field[i, pl.ds(base, side), :] = t
        return 0

    lax.fori_loop(0, side, own_plane, 0)
    for i in range(2 * tiles + 1):
        for shift in (7, pitch):
            for _, size, at in column_starts(side, shift):
                field[i, at, :] = jnp.zeros((size, LANE), F32)

    def tile(k, _):
        taps = [weights[26 - t if flip else t] for t in range(27)]
        for half in range(side // 8):
            part = {}
            for plane in range(1, side + 1):
                near = shifted(field, tiles, k, plane, half, pitch)
                for off_x in range(3):
                    x = plane - off_x
                    if not 0 <= x < side:
                        continue
                    for (off_y, off_z), value in near.items():
                        term = value * taps[9 * off_x + 3 * off_y + off_z]
                        part[x] = part[x] + term if x in part else term
                done = plane - 2
                for x in [done, done + 1] if plane == side else [done]:
                    if x >= 0:
                        sums[k, x * side + 8 * half:x * side + 8 * half + 8, :] = part.pop(x)
        return 0

    lax.fori_loop(0, tiles, tile, 0)


def halo_part(xlo_ref, xhi_ref, ylo_ref, yhi_ref, masks_ref, field, weights, sums, flip):
    side, lanes = xlo_ref.shape
    tiles = lanes // LANE
    pitch = side + 8

    def place(i, ref):
        rows = ref.shape[0]
        masks = tuple(masks_ref[3 * i + m, :rows, :] for m in range(3))
        return plane_tiles(loader(ref[...]), tiles, masks)

    for i, ref, plane in ((0, xlo_ref, 0), (1, xhi_ref, side + 1)):
        for j, t in enumerate(place(i, ref)):
            field[j, plane * pitch + 8:plane * pitch + 8 + side, :] = t

    def x_tile(k, _):
        for plane, off_x, x in ((0, 0, 0), (side + 1, 2, side - 1)):
            for half in range(side // 8):
                row = x * side + 8 * half
                total = sums[k, row:row + 8, :]
                for (off_y, off_z), value in shifted(field, tiles, k, plane, half, pitch).items():
                    tap = 9 * off_x + 3 * off_y + off_z
                    total = total + value * weights[26 - tap if flip else tap]
                sums[k, row:row + 8, :] = total
        return 0

    lax.fori_loop(0, tiles, x_tile, 0)

    for i, ref, shift in ((2, ylo_ref, 7), (3, yhi_ref, pitch)):
        for j, t in enumerate(place(i, ref)):
            for start, size, at in column_starts(side, shift):
                field[j, at, :] = t[start:start + size]

    def y_tile(k, _):
        for shift, off_y, y in ((7, 0, 0), (pitch, 2, side - 1)):
            for x in range(0, side, 8):
                at = pl.ds(x * side + y, 8, stride=side)
                total = sums[k, at, :]
                for off_x in range(3):
                    for off_z in range(3):
                        i = (tiles + k, k, tiles + k + 1)[off_z]
                        tap = 9 * off_x + 3 * off_y + off_z
                        value = field[i, pl.ds((x + off_x) * pitch + shift, 8, stride=pitch), :]
                        total = total + value * weights[26 - tap if flip else tap]
                sums[k, at, :] = total
        return 0

    lax.fori_loop(0, tiles, y_tile, 0)


def shifted(field, tiles, k, plane, half, pitch):
    found = {}
    for off_y in range(3):
        row = plane * pitch + 7 + 8 * half + off_y
        for off_z in range(3):
            i = (tiles + k, k, tiles + k + 1)[off_z]
            found[off_y, off_z] = field[i, row:row + 8, :]
    return found


def edges_of(cells_ref, xa_ref, xb_ref, ylo_ref, yhi_ref):
    side, _, lanes = cells_ref.shape
    odd = lax.axis_index("gx") % 2
    xa_ref[...] = cells_ref[jnp.where(odd == 1, 0, side - 1)]
    xb_ref[...] = cells_ref[jnp.where(odd == 1, side - 1, 0)]
    row = lax.broadcasted_iota(jnp.int32, (2 * side, side * side), 0)
    col = lax.broadcasted_iota(jnp.int32, (2 * side, side * side), 1)
    wanted = jnp.where(row < side, row * side, (row - side) * side + side - 1)
    pick = jnp.where(col == wanted, 1.0, 0.0).astype(BF16)
    flat = cells_ref[...].reshape(side * side, lanes)
    found = jnp.dot(pick, flat, preferred_element_type=F32).astype(BF16)
    ylo_ref[...] = found[:side]
    yhi_ref[...] = found[side:]


def params_kernel(
    slots_ref, mix_ref, taps_ref, gain_ref, masks_ref, weights, mean_mat_ref, mix_mat_ref, gain_wide_ref
):
    channels = mix_ref.shape[0]
    level_masks(slots_ref[...], masks_ref.shape[1] - 8, masks_ref)
    wide = jnp.concatenate([taps_ref[...], taps_ref[...]], axis=1)
    for tap in range(27):
        weights[tap] = jnp.broadcast_to(wide[tap:tap + 1], (8, LANE))
    copies = WIDE // channels
    row_id = lax.broadcasted_iota(jnp.int32, (WIDE, WIDE), 0) // channels
    col_id = lax.broadcasted_iota(jnp.int32, (WIDE, WIDE), 1) // channels
    block = row_id == col_id
    mean_mat_ref[...] = jnp.where(block, 1.0 / channels, 0.0).astype(BF16)
    mix = mix_ref[...].astype(F32)
    mix_row = jnp.concatenate([mix] * copies, axis=1)
    mix_mat_ref[...] = jnp.where(block, jnp.concatenate([mix_row] * copies, axis=0), 0.0).astype(BF16)
    gain_wide_ref[...] = jnp.concatenate([gain_ref[...]] * copies, axis=1)


def own_kernel(flip, own_ref, weights, field, sums):
    own_part(own_ref, field, weights, sums, flip)


def forward_kernel(
    field, depth, weights, mean_mat_ref, mix_mat_ref, gain_wide_ref,
    xlo_ref, xhi_ref, ylo_ref, yhi_ref, masks_ref, own_ref, cot_ref,
    field_out_ref, depth_out_ref, mixed_ref, grad_ref, gxa_ref, gxb_ref, gylo_ref, gyhi_ref,
    normed_bf, grads, gain_sum_ref,
):
    side = own_ref.shape[0]
    lanes = own_ref.shape[2]
    cells = side * side
    halo_part(xlo_ref, xhi_ref, ylo_ref, yhi_ref, masks_ref, field, weights, depth, False)

    mean_mat = mean_mat_ref[...]
    mix_mat = mix_mat_ref[...]
    gain = gain_wide_ref[...]
    rows = 128
    xs = rows // side
    gain_sum = jnp.zeros((8, WIDE), F32)
    for part in range(lanes // WIDE):
        cols = slice(part * WIDE, (part + 1) * WIDE)
        for chunk in range(cells // rows):
            at = slice(chunk * rows, (chunk + 1) * rows)
            planes = slice(chunk * xs, (chunk + 1) * xs)
            dep = jnp.concatenate([depth[2 * part, at, :], depth[2 * part + 1, at, :]], axis=1)
            mean_sq = jnp.dot((dep * dep).astype(BF16), mean_mat, preferred_element_type=F32)
            inv = lax.rsqrt(mean_sq + EPS)
            normed = dep * inv
            norm_bf = (normed * gain).astype(BF16)
            normed_bf[at, cols] = norm_bf
            branch = jnp.dot(norm_bf, mix_mat, preferred_element_type=F32)
            feat = own_ref[planes, :, cols].reshape(rows, WIDE).astype(F32)
            mixed_ref[planes, :, cols] = (feat + branch).astype(BF16).reshape(xs, side, WIDE)
            grad_norm = lax.dot_general(
                cot_ref[planes, :, cols].reshape(rows, WIDE), mix_mat,
                (((1,), (1,)), ((), ())), preferred_element_type=F32,
            )
            gain_sum = gain_sum + jnp.sum((grad_norm * normed).reshape(rows // 8, 8, WIDE), axis=0)
            scaled = grad_norm * gain
            mean = jnp.dot((scaled * normed).astype(BF16), mean_mat, preferred_element_type=F32)
            grad = (inv * (scaled - normed * mean)).astype(BF16)
            grad_ref[planes, :, cols] = grad.reshape(xs, side, WIDE)
            wide_grad = grad.astype(F32)
            grads[2 * part, at, :] = wide_grad[:, :LANE]
            grads[2 * part + 1, at, :] = wide_grad[:, LANE:]
    gain_sum_ref[...] = gain_sum
    edges_of(grad_ref, gxa_ref, gxb_ref, gylo_ref, gyhi_ref)


def sums_kernel(field, normed_bf, grads, gain_sum_ref, cot_ref, packed_ref):
    side, _, lanes = cot_ref.shape
    tiles = lanes // LANE
    channels = packed_ref.shape[1] // 2
    pitch = side + 8
    cells = side * side
    copies = WIDE // channels
    mix_sum = jnp.zeros((WIDE, WIDE), F32)
    for part in range(lanes // WIDE):
        cols = slice(part * WIDE, (part + 1) * WIDE)
        mix_sum = mix_sum + lax.dot_general(
            normed_bf[:, cols],
            cot_ref[:, :, cols].reshape(cells, WIDE),
            (((0,), (0,)), ((), ())),
            preferred_element_type=F32,
        )
    grad_mix = mix_sum[:channels, :channels]
    for i in range(1, copies):
        span = slice(i * channels, (i + 1) * channels)
        grad_mix = grad_mix + mix_sum[span, span]
    packed_ref[0:32, :] = jnp.concatenate([grad_mix[:32], grad_mix[32:]], axis=1)

    def tap_tile(k, sums):
        sums = list(sums)
        for half in range(side // 8):
            near_grads = {}
            for plane in range(side + 2):
                if plane < side:
                    row = plane * side + 8 * half
                    near_grads[plane] = grads[k, row:row + 8, :]
                near = shifted(field, tiles, k, plane, half, pitch)
                for (off_y, off_z), value in near.items():
                    for off_x in range(3):
                        x = plane - off_x
                        if 0 <= x < side:
                            tap = 9 * off_x + 3 * off_y + off_z
                            sums[tap] = sums[tap] + value * near_grads[x]
                near_grads.pop(plane - 2, None)
        return tuple(sums)

    sums = lax.fori_loop(0, tiles, tap_tile, tuple(jnp.zeros((8, LANE), F32) for _ in range(27)))
    gain_row = jnp.sum(gain_sum_ref[...], axis=0, keepdims=True)
    rows = [jnp.sum(t, axis=0, keepdims=True) for t in sums] + [gain_row[:, :LANE] + gain_row[:, LANE:]]
    rows = jnp.concatenate(rows + [jnp.zeros((4, LANE), F32)], axis=0)
    rows = rows[:, :channels] + rows[:, channels:]
    packed_ref[32:48, :] = jnp.concatenate([rows[:16], rows[16:]], axis=1)


def backward_kernel(
    field, sums, weights, xlo_ref, xhi_ref, ylo_ref, yhi_ref, masks_ref, cot_ref,
    field_out_ref, sums_out_ref, out_ref,
):
    side = cot_ref.shape[0]
    halo_part(xlo_ref, xhi_ref, ylo_ref, yhi_ref, masks_ref, field, weights, sums, True)
    for x in range(side):
        for k in range(sums.shape[0]):
            cols = slice(k * LANE, (k + 1) * LANE)
            cot = cot_ref[x, :, cols].astype(F32)
            out_ref[x, :, cols] = (cot + sums[k, x * side:(x + 1) * side, :]).astype(BF16)


def unpack_kernel(mine_ref, theirs_ref, taps_hbm, gain_hbm, mix_hbm, taps_ref, gain_ref, mix_ref, done):
    total = mine_ref[...] + theirs_ref[...]
    channels = mix_ref.shape[0]
    mix_ref[0:32, :] = total[:32, :channels]
    mix_ref[32:64, :] = total[:32, channels:]
    taps_ref[0:16, :] = total[32:48, :channels]
    taps_ref[16:27, :] = total[32:43, channels:]
    gain_ref[...] = total[43:44, channels:]
    copies = [
        pltpu.make_async_copy(src, dst, done.at[i])
        for i, (src, dst) in enumerate(((taps_ref, taps_hbm), (gain_ref, gain_hbm), (mix_ref, mix_hbm)))
    ]
    for copy in copies:
        copy.start()
    for copy in copies:
        copy.wait()


def swap(to_first, to_second, axis):
    count = lax.axis_size(axis)
    first = [(i, i ^ 1) for i in range(count)]
    second = [(i, (((i + 1) ^ 1) - 1) % count) for i in range(count)]
    from_second = lax.ppermute(to_second, axis, second)
    return lax.ppermute(to_first, axis, first), from_second


def low_high(from_first, from_second, axis):
    odd = lax.axis_index(axis) % 2 == 1
    return jnp.where(odd, from_first, from_second), jnp.where(odd, from_second, from_first)


def y_messages(xlo, xhi, ylo, yhi):
    low = jnp.concatenate([xlo[:1], ylo, xhi[:1]], axis=0)
    high = jnp.concatenate([xlo[-1:], yhi, xhi[-1:]], axis=0)
    return low_high(low, high, "gy")


def sum_steps():
    steps = []
    for axis in ("gx", "gy"):
        count = lax.axis_size(axis)
        bit = 1
        while bit < count:
            steps.append((axis, [(i, i ^ bit) for i in range(count)]))
            bit *= 2
    return steps


def shards(features, slot_map, tap_weights, gain, mix_weight, cotangent):
    side, _, _, lanes = features.shape
    channels = gain.shape[0]
    tiles = lanes // LANE
    cells = features.reshape(side, side, lanes)
    cot = cotangent.reshape(side, side, lanes)
    vmem = pl.BlockSpec(memory_space=pltpu.VMEM)
    hbm = pl.BlockSpec(memory_space=pltpu.HBM)
    block = jax.ShapeDtypeStruct((side, side, lanes), BF16)
    edge = jax.ShapeDtypeStruct((side, lanes), BF16)
    field_type = jax.ShapeDtypeStruct((2 * tiles + 1, (side + 2) * (side + 8) + 8, LANE), F32)
    sums_type = jax.ShapeDtypeStruct((tiles, side * side, LANE), F32)
    weights_type = jax.ShapeDtypeStruct((27, 8, LANE), F32)
    mat_type = jax.ShapeDtypeStruct((WIDE, WIDE), BF16)

    def call(kernel, name, operands, outs, scratch=(), aliases={}, flops=0, in_specs=None, out_specs=None):
        return pl.pallas_call(
            kernel,
            out_shape=tuple(jax.ShapeDtypeStruct(t.shape, t.dtype) for t in outs),
            in_specs=in_specs or [vmem] * len(operands),
            out_specs=out_specs or (vmem,) * len(outs),
            scratch_shapes=list(scratch),
            input_output_aliases=aliases,
            compiler_params=pltpu.CompilerParams(vmem_limit_bytes=40 * 1024 * 1024),
            cost_estimate=pl.CostEstimate(flops=flops, bytes_accessed=500_000, transcendentals=0),
            name=name,
        )(*operands)

    xa, xb, ylo, yhi = call(edges_of, "edges", (cells,), (edge, edge, edge, edge), flops=100_000_000_000)
    masks, weights, mean_mat, mix_mat, gain_wide = call(
        params_kernel,
        "params",
        (jnp.transpose(slot_map, (1, 2, 0)), mix_weight, tap_weights, gain.reshape(1, channels)),
        (
            jax.ShapeDtypeStruct((12, side + 8, LANE), F32),
            weights_type,
            mat_type,
            mat_type,
            jax.ShapeDtypeStruct((1, WIDE), F32),
        ),
    )
    xlo, xhi = low_high(*swap(xa, xb, "gx"), "gx")
    to_a, to_b = y_messages(xlo, xhi, ylo, yhi)
    to_a, to_b, weights = lax.optimization_barrier((to_a, to_b, weights))
    ylo, yhi = low_high(*swap(to_a, to_b, "gy"), "gy")
    own_field, own_sums = call(
        functools.partial(own_kernel, False), "own_forward", (cells, weights), (field_type, sums_type),
        flops=10_000_000,
    )
    field, _, mixed, grad_depth, gxa, gxb, gylo, gyhi, normed_bf, grads, gain_sum = call(
        forward_kernel,
        "forward",
        (own_field, own_sums, weights, mean_mat, mix_mat, gain_wide, xlo, xhi, ylo, yhi, masks, cells, cot),
        (
            field_type, sums_type, block, block, edge, edge, edge, edge,
            jax.ShapeDtypeStruct((side * side, lanes), BF16), sums_type, jax.ShapeDtypeStruct((8, WIDE), F32),
        ),
        aliases={0: 0, 1: 1},
        flops=10_000_000,
    )
    gxlo, gxhi = low_high(*swap(gxa, gxb, "gx"), "gx")
    (part,) = call(
        sums_kernel,
        "sums",
        (field, normed_bf, grads, gain_sum, cot),
        (jax.ShapeDtypeStruct((48, LANE), F32),),
        flops=10_000_000,
    )

    steps = sum_steps()
    part = part + lax.ppermute(part, *steps[0])
    part, to_a, to_b = lax.optimization_barrier((part, *y_messages(gxlo, gxhi, gylo, gyhi)))
    part = part + lax.ppermute(part, *steps[1])
    gylo, gyhi = low_high(*swap(to_a, to_b, "gy"), "gy")
    part, grad_depth = lax.optimization_barrier((part, grad_depth))
    theirs = lax.ppermute(part, *steps[2])
    own_field, own_sums = call(
        functools.partial(own_kernel, True), "own_backward", (grad_depth, weights), (field_type, sums_type),
        flops=10_000_000,
    )
    part, own_field, own_sums = lax.optimization_barrier((part + theirs, own_field, own_sums))
    _, _, grad_features = call(
        backward_kernel,
        "backward",
        (own_field, own_sums, weights, gxlo, gxhi, gylo, gyhi, masks, cot),
        (field_type, sums_type, block),
        aliases={0: 0, 1: 1},
        flops=2_000_000,
    )
    for index, step in enumerate(steps[3:-1]):
        part = part + lax.ppermute(part, *step)
        if index == 0:
            part, grad_features = lax.optimization_barrier((part, grad_features))
    theirs = lax.ppermute(part, *steps[-1])

    outs = (
        jax.ShapeDtypeStruct((27, channels), F32),
        jax.ShapeDtypeStruct((1, channels), F32),
        jax.ShapeDtypeStruct((channels, channels), F32),
    )
    grad_taps, grad_gain, grad_mix = call(
        unpack_kernel,
        "unpack",
        (part, theirs),
        outs,
        scratch=[pltpu.VMEM(t.shape, F32) for t in outs] + [pltpu.SemaphoreType.DMA((3,))],
        out_specs=(hbm,) * 3,
    )
    shape = features.shape
    return (mixed.reshape(shape), grad_features.reshape(shape), grad_taps, grad_gain.reshape(channels), grad_mix)


def solution(mesh):
    return jax.shard_map(
        shards,
        mesh=mesh,
        in_specs=(P("gx", "gy", None, None), P(), P(), P(), P(), P("gx", "gy", None, None)),
        out_specs=(P("gx", "gy", None, None), P("gx", "gy", None, None), P(), P(), P()),
        check_vma=False,
    )
```

```python
import functools

import jax
import jax.numpy as jnp
from jax import lax
from jax.experimental import pallas as pl
from jax.experimental.pallas import tpu as pltpu
from jax.sharding import PartitionSpec as P

EPS = 1e-05
LANE = 128
WIDE = 256
F32 = jnp.float32
BF16 = jnp.bfloat16


def level_masks(slots, side, masks_ref):
    level = lax.broadcasted_iota(jnp.int32, slots.shape, 1)
    at_x = lax.broadcasted_iota(jnp.int32, slots.shape, 2) - lax.axis_index("gx")
    at_y = lax.broadcasted_iota(jnp.int32, slots.shape, 0) - lax.axis_index("gy")
    place = jnp.where(slots >= 0, level + 1, 0).astype(F32)

    def near(off_x, off_y):
        found = jnp.where((at_x == off_x) & (at_y == off_y), place, 0.0)
        found = jnp.sum(jnp.sum(found, axis=0), axis=0, keepdims=True)
        return jnp.sum(found, axis=1, keepdims=True)

    own = near(0, 0)

    def difference(off_x, off_y):
        found = near(off_x, off_y)
        return jnp.where(found > 0.0, found - own, 9.0)

    rows = masks_ref.shape[1]
    row = lax.broadcasted_iota(jnp.int32, (rows, LANE), 0)
    for edge in range(4):
        high = 1 if edge % 2 else -1
        if edge < 2:
            d = jnp.broadcast_to(difference(high, 0), (rows, LANE))
        else:
            corner, middle, other = (difference(off, high) for off in (-1, 0, 1))
            d = jnp.where(row == 0, corner, jnp.where(row == side + 1, other, middle))
        for i, want in enumerate((0.0, -1.0, 1.0)):
            masks_ref[3 * edge + i] = jnp.where(d == want, 1.0, 0.0)


def plane_tiles(load, total, masks):
    low = lax.broadcasted_iota(jnp.int32, load(0).shape, 1) < LANE // 2
    zero = jnp.zeros(load(0).shape, F32)
    aligned = [load(k) for k in range(total)]
    turned = [pltpu.roll(t, LANE // 2, 1) for t in aligned]
    between = [jnp.where(low, turned[j - 1], turned[j]) for j in range(1, total)]
    if masks is None:
        return aligned + [jnp.where(low, zero, turned[0])] + between + [jnp.where(low, turned[-1], zero)]
    same, below, above = masks
    first = jnp.where(low, turned[-1] * below, turned[0] * same)
    last = jnp.where(low, turned[-1] * same, turned[0] * above)
    return [t * same for t in aligned] + [first] + [t * same for t in between] + [last]


def loader(rows):
    return lambda k: rows[:, k * LANE:(k + 1) * LANE].astype(F32)


def column_starts(side, shift):
    pitch = side + 8
    for start in range(0, side + 2, 8):
        size = min(8, side + 2 - start)
        yield start, size, pl.ds(start * pitch + shift, size, stride=pitch)


def own_part(own_ref, field, weights, sums, flip):
    side = own_ref.shape[0]
    tiles = own_ref.shape[2] // LANE
    pitch = side + 8

    def own_plane(x, _):
        base = pl.multiple_of((x + 1) * pitch + 8, 8)
        for i, t in enumerate(plane_tiles(loader(own_ref[x]), tiles, None)):
            field[i, pl.ds(base, side), :] = t
        return 0

    lax.fori_loop(0, side, own_plane, 0)
    for i in range(2 * tiles + 1):
        for shift in (7, pitch):
            for _, size, at in column_starts(side, shift):
                field[i, at, :] = jnp.zeros((size, LANE), F32)

    def tile(k, _):
        taps = [weights[26 - t if flip else t] for t in range(27)]
        for half in range(side // 8):
            part = {}
            for plane in range(1, side + 1):
                near = shifted(field, tiles, k, plane, half, pitch)
                for off_x in range(3):
                    x = plane - off_x
                    if not 0 <= x < side:
                        continue
                    for (off_y, off_z), value in near.items():
                        term = value * taps[9 * off_x + 3 * off_y + off_z]
                        part[x] = part[x] + term if x in part else term
                done = plane - 2
                for x in [done, done + 1] if plane == side else [done]:
                    if x >= 0:
                        sums[k, x * side + 8 * half:x * side + 8 * half + 8, :] = part.pop(x)
        return 0

    lax.fori_loop(0, tiles, tile, 0)


def halo_part(xlo_ref, xhi_ref, ylo_ref, yhi_ref, masks_ref, field, weights, sums, flip):
    side, lanes = xlo_ref.shape
    tiles = lanes // LANE
    pitch = side + 8

    def place(i, ref):
        rows = ref.shape[0]
        masks = tuple(masks_ref[3 * i + m, :rows, :] for m in range(3))
        return plane_tiles(loader(ref[...]), tiles, masks)

    for i, ref, plane in ((0, xlo_ref, 0), (1, xhi_ref, side + 1)):
        for j, t in enumerate(place(i, ref)):
            field[j, plane * pitch + 8:plane * pitch + 8 + side, :] = t

    def x_tile(k, _):
        for plane, off_x, x in ((0, 0, 0), (side + 1, 2, side - 1)):
            for half in range(side // 8):
                row = x * side + 8 * half
                total = sums[k, row:row + 8, :]
                for (off_y, off_z), value in shifted(field, tiles, k, plane, half, pitch).items():
                    tap = 9 * off_x + 3 * off_y + off_z
                    total = total + value * weights[26 - tap if flip else tap]
                sums[k, row:row + 8, :] = total
        return 0

    lax.fori_loop(0, tiles, x_tile, 0)

    for i, ref, shift in ((2, ylo_ref, 7), (3, yhi_ref, pitch)):
        for j, t in enumerate(place(i, ref)):
            for start, size, at in column_starts(side, shift):
                field[j, at, :] = t[start:start + size]

    def y_tile(k, _):
        for shift, off_y, y in ((7, 0, 0), (pitch, 2, side - 1)):
            for x in range(0, side, 8):
                at = pl.ds(x * side + y, 8, stride=side)
                total = sums[k, at, :]
                for off_x in range(3):
                    for off_z in range(3):
                        i = (tiles + k, k, tiles + k + 1)[off_z]
                        tap = 9 * off_x + 3 * off_y + off_z
                        value = field[i, pl.ds((x + off_x) * pitch + shift, 8, stride=pitch), :]
                        total = total + value * weights[26 - tap if flip else tap]
                sums[k, at, :] = total
        return 0

    lax.fori_loop(0, tiles, y_tile, 0)


def shifted(field, tiles, k, plane, half, pitch):
    found = {}
    for off_y in range(3):
        row = plane * pitch + 7 + 8 * half + off_y
        for off_z in range(3):
            i = (tiles + k, k, tiles + k + 1)[off_z]
            found[off_y, off_z] = field[i, row:row + 8, :]
    return found


def edges_of(cells_ref, xa_ref, xb_ref, ylo_ref, yhi_ref):
    side, _, lanes = cells_ref.shape
    odd = lax.axis_index("gx") % 2
    xa_ref[...] = cells_ref[jnp.where(odd == 1, 0, side - 1)]
    xb_ref[...] = cells_ref[jnp.where(odd == 1, side - 1, 0)]
    row = lax.broadcasted_iota(jnp.int32, (2 * side, side * side), 0)
    col = lax.broadcasted_iota(jnp.int32, (2 * side, side * side), 1)
    wanted = jnp.where(row < side, row * side, (row - side) * side + side - 1)
    pick = jnp.where(col == wanted, 1.0, 0.0).astype(BF16)
    flat = cells_ref[...].reshape(side * side, lanes)
    found = jnp.dot(pick, flat, preferred_element_type=F32).astype(BF16)
    ylo_ref[...] = found[:side]
    yhi_ref[...] = found[side:]


def params_kernel(
    slots_ref, mix_ref, taps_ref, gain_ref, masks_ref, weights, mean_mat_ref, mix_mat_ref, gain_wide_ref
):
    channels = mix_ref.shape[0]
    level_masks(slots_ref[...], masks_ref.shape[1] - 8, masks_ref)
    wide = jnp.concatenate([taps_ref[...], taps_ref[...]], axis=1)
    for tap in range(27):
        weights[tap] = jnp.broadcast_to(wide[tap:tap + 1], (8, LANE))
    copies = WIDE // channels
    row_id = lax.broadcasted_iota(jnp.int32, (WIDE, WIDE), 0) // channels
    col_id = lax.broadcasted_iota(jnp.int32, (WIDE, WIDE), 1) // channels
    block = row_id == col_id
    mean_mat_ref[...] = jnp.where(block, 1.0 / channels, 0.0).astype(BF16)
    mix = mix_ref[...].astype(F32)
    mix_row = jnp.concatenate([mix] * copies, axis=1)
    mix_mat_ref[...] = jnp.where(block, jnp.concatenate([mix_row] * copies, axis=0), 0.0).astype(BF16)
    gain_wide_ref[...] = jnp.concatenate([gain_ref[...]] * copies, axis=1)


def own_kernel(flip, own_ref, weights, field, sums):
    own_part(own_ref, field, weights, sums, flip)


def forward_kernel(
    field, depth, weights, mean_mat_ref, mix_mat_ref, gain_wide_ref,
    xlo_ref, xhi_ref, ylo_ref, yhi_ref, masks_ref, own_ref, cot_ref,
    field_out_ref, depth_out_ref, mixed_ref, grad_ref, gxa_ref, gxb_ref, gylo_ref, gyhi_ref,
    normed_bf, grads, gain_sum_ref,
):
    side = own_ref.shape[0]
    lanes = own_ref.shape[2]
    cells = side * side
    halo_part(xlo_ref, xhi_ref, ylo_ref, yhi_ref, masks_ref, field, weights, depth, False)

    mean_mat = mean_mat_ref[...]
    mix_mat = mix_mat_ref[...]
    gain = gain_wide_ref[...]
    rows = 128
    xs = rows // side
    gain_sum = jnp.zeros((8, WIDE), F32)
    for part in range(lanes // WIDE):
        cols = slice(part * WIDE, (part + 1) * WIDE)
        for chunk in range(cells // rows):
            at = slice(chunk * rows, (chunk + 1) * rows)
            planes = slice(chunk * xs, (chunk + 1) * xs)
            dep = jnp.concatenate([depth[2 * part, at, :], depth[2 * part + 1, at, :]], axis=1)
            mean_sq = jnp.dot((dep * dep).astype(BF16), mean_mat, preferred_element_type=F32)
            inv = lax.rsqrt(mean_sq + EPS)
            normed = dep * inv
            norm_bf = (normed * gain).astype(BF16)
            normed_bf[at, cols] = norm_bf
            branch = jnp.dot(norm_bf, mix_mat, preferred_element_type=F32)
            feat = own_ref[planes, :, cols].reshape(rows, WIDE).astype(F32)
            mixed_ref[planes, :, cols] = (feat + branch).astype(BF16).reshape(xs, side, WIDE)
            grad_norm = lax.dot_general(
                cot_ref[planes, :, cols].reshape(rows, WIDE), mix_mat,
                (((1,), (1,)), ((), ())), preferred_element_type=F32,
            )
            gain_sum = gain_sum + jnp.sum((grad_norm * normed).reshape(rows // 8, 8, WIDE), axis=0)
            scaled = grad_norm * gain
            mean = jnp.dot((scaled * normed).astype(BF16), mean_mat, preferred_element_type=F32)
            grad = (inv * (scaled - normed * mean)).astype(BF16)
            grad_ref[planes, :, cols] = grad.reshape(xs, side, WIDE)
            wide_grad = grad.astype(F32)
            grads[2 * part, at, :] = wide_grad[:, :LANE]
            grads[2 * part + 1, at, :] = wide_grad[:, LANE:]
    gain_sum_ref[...] = gain_sum
    edges_of(grad_ref, gxa_ref, gxb_ref, gylo_ref, gyhi_ref)


def sums_kernel(field, normed_bf, grads, gain_sum_ref, cot_ref, packed_ref):
    side, _, lanes = cot_ref.shape
    tiles = lanes // LANE
    channels = packed_ref.shape[1] // 2
    pitch = side + 8
    cells = side * side
    copies = WIDE // channels
    mix_sum = jnp.zeros((WIDE, WIDE), F32)
    for part in range(lanes // WIDE):
        cols = slice(part * WIDE, (part + 1) * WIDE)
        mix_sum = mix_sum + lax.dot_general(
            normed_bf[:, cols],
            cot_ref[:, :, cols].reshape(cells, WIDE),
            (((0,), (0,)), ((), ())),
            preferred_element_type=F32,
        )
    grad_mix = mix_sum[:channels, :channels]
    for i in range(1, copies):
        span = slice(i * channels, (i + 1) * channels)
        grad_mix = grad_mix + mix_sum[span, span]
    packed_ref[0:32, :] = jnp.concatenate([grad_mix[:32], grad_mix[32:]], axis=1)

    def tap_tile(k, sums):
        sums = list(sums)
        for half in range(side // 8):
            near_grads = {}
            for plane in range(side + 2):
                if plane < side:
                    row = plane * side + 8 * half
                    near_grads[plane] = grads[k, row:row + 8, :]
                near = shifted(field, tiles, k, plane, half, pitch)
                for (off_y, off_z), value in near.items():
                    for off_x in range(3):
                        x = plane - off_x
                        if 0 <= x < side:
                            tap = 9 * off_x + 3 * off_y + off_z
                            sums[tap] = sums[tap] + value * near_grads[x]
                near_grads.pop(plane - 2, None)
        return tuple(sums)

    sums = lax.fori_loop(0, tiles, tap_tile, tuple(jnp.zeros((8, LANE), F32) for _ in range(27)))
    gain_row = jnp.sum(gain_sum_ref[...], axis=0, keepdims=True)
    rows = [jnp.sum(t, axis=0, keepdims=True) for t in sums] + [gain_row[:, :LANE] + gain_row[:, LANE:]]
    rows = jnp.concatenate(rows + [jnp.zeros((4, LANE), F32)], axis=0)
    rows = rows[:, :channels] + rows[:, channels:]
    packed_ref[32:48, :] = jnp.concatenate([rows[:16], rows[16:]], axis=1)


def backward_kernel(
    field, sums, weights, xlo_ref, xhi_ref, ylo_ref, yhi_ref, masks_ref, cot_ref,
    field_out_ref, sums_out_ref, out_ref,
):
    side = cot_ref.shape[0]
    halo_part(xlo_ref, xhi_ref, ylo_ref, yhi_ref, masks_ref, field, weights, sums, True)
    for x in range(side):
        for k in range(sums.shape[0]):
            cols = slice(k * LANE, (k + 1) * LANE)
            cot = cot_ref[x, :, cols].astype(F32)
            out_ref[x, :, cols] = (cot + sums[k, x * side:(x + 1) * side, :]).astype(BF16)


def unpack_kernel(mine_ref, theirs_ref, taps_hbm, gain_hbm, mix_hbm, taps_ref, gain_ref, mix_ref, done):
    total = mine_ref[...] + theirs_ref[...]
    channels = mix_ref.shape[0]
    mix_ref[0:32, :] = total[:32, :channels]
    mix_ref[32:64, :] = total[:32, channels:]
    taps_ref[0:16, :] = total[32:48, :channels]
    taps_ref[16:27, :] = total[32:43, channels:]
    gain_ref[...] = total[43:44, channels:]
    copies = [
        pltpu.make_async_copy(src, dst, done.at[i])
        for i, (src, dst) in enumerate(((taps_ref, taps_hbm), (gain_ref, gain_hbm), (mix_ref, mix_hbm)))
    ]
    for copy in copies:
        copy.start()
    for copy in copies:
        copy.wait()


def swap(to_first, to_second, axis):
    sizes = {name: lax.axis_size(name) for name in ("gx", "gy")}
    count = sizes[axis]

    def second(place):
        other = "gy" if axis == "gx" else "gx"
        if 0 < place[axis] < count - 1:
            return {**place, axis: ((place[axis] + 1) ^ 1) - 1}
        return {**place, other: place[other] ^ 1}

    def index(place):
        return place["gx"] * sizes["gy"] + place["gy"]

    places = [{"gx": i, "gy": j} for i in range(sizes["gx"]) for j in range(sizes["gy"])]
    from_second = lax.ppermute(to_second, ("gx", "gy"), [(index(p), index(second(p))) for p in places])
    return lax.ppermute(to_first, axis, [(i, i ^ 1) for i in range(count)]), from_second


def low_high(from_first, from_second, axis):
    even = lax.axis_index(axis) % 2 == 0
    return jnp.where(even, from_second, from_first), jnp.where(even, from_first, from_second)


def y_messages(xlo, xhi, ylo, yhi):
    low = jnp.concatenate([xlo[:1], ylo, xhi[:1]], axis=0)
    high = jnp.concatenate([xlo[-1:], yhi, xhi[-1:]], axis=0)
    return low_high(low, high, "gy")


def sum_steps():
    steps = []
    for axis in ("gx", "gy"):
        count = lax.axis_size(axis)
        bit = 1
        while bit < count:
            steps.append((axis, [(i, i ^ bit) for i in range(count)]))
            bit *= 2
    return steps


def shards(features, slot_map, tap_weights, gain, mix_weight, cotangent):
    side, _, _, lanes = features.shape
    channels = gain.shape[0]
    tiles = lanes // LANE
    cells = features.reshape(side, side, lanes)
    cot = cotangent.reshape(side, side, lanes)
    vmem = pl.BlockSpec(memory_space=pltpu.VMEM)
    hbm = pl.BlockSpec(memory_space=pltpu.HBM)
    block = jax.ShapeDtypeStruct((side, side, lanes), BF16)
    edge = jax.ShapeDtypeStruct((side, lanes), BF16)
    field_type = jax.ShapeDtypeStruct((2 * tiles + 1, (side + 2) * (side + 8) + 8, LANE), F32)
    sums_type = jax.ShapeDtypeStruct((tiles, side * side, LANE), F32)
    weights_type = jax.ShapeDtypeStruct((27, 8, LANE), F32)
    mat_type = jax.ShapeDtypeStruct((WIDE, WIDE), BF16)

    def call(kernel, name, operands, outs, scratch=(), aliases={}, flops=0, in_specs=None, out_specs=None):
        return pl.pallas_call(
            kernel,
            out_shape=tuple(jax.ShapeDtypeStruct(t.shape, t.dtype) for t in outs),
            in_specs=in_specs or [vmem] * len(operands),
            out_specs=out_specs or (vmem,) * len(outs),
            scratch_shapes=list(scratch),
            input_output_aliases=aliases,
            compiler_params=pltpu.CompilerParams(vmem_limit_bytes=40 * 1024 * 1024),
            cost_estimate=pl.CostEstimate(flops=flops, bytes_accessed=500_000, transcendentals=0),
            name=name,
        )(*operands)

    xa, xb, ylo, yhi = call(edges_of, "edges", (cells,), (edge, edge, edge, edge), flops=100_000_000_000)
    masks, weights, mean_mat, mix_mat, gain_wide = call(
        params_kernel,
        "params",
        (jnp.transpose(slot_map, (1, 2, 0)), mix_weight, tap_weights, gain.reshape(1, channels)),
        (
            jax.ShapeDtypeStruct((12, side + 8, LANE), F32),
            weights_type,
            mat_type,
            mat_type,
            jax.ShapeDtypeStruct((1, WIDE), F32),
        ),
    )
    xlo, xhi = low_high(*swap(xa, xb, "gx"), "gx")
    to_a, to_b = y_messages(xlo, xhi, ylo, yhi)
    to_a, to_b, weights = lax.optimization_barrier((to_a, to_b, weights))
    ylo, yhi = low_high(*swap(to_a, to_b, "gy"), "gy")
    own_field, own_sums = call(
        functools.partial(own_kernel, False), "own_forward", (cells, weights), (field_type, sums_type),
        flops=10_000_000,
    )
    field, _, mixed, grad_depth, gxa, gxb, gylo, gyhi, normed_bf, grads, gain_sum = call(
        forward_kernel,
        "forward",
        (own_field, own_sums, weights, mean_mat, mix_mat, gain_wide, xlo, xhi, ylo, yhi, masks, cells, cot),
        (
            field_type, sums_type, block, block, edge, edge, edge, edge,
            jax.ShapeDtypeStruct((side * side, lanes), BF16), sums_type, jax.ShapeDtypeStruct((8, WIDE), F32),
        ),
        aliases={0: 0, 1: 1},
        flops=10_000_000,
    )
    gxlo, gxhi = low_high(*swap(gxa, gxb, "gx"), "gx")
    (part,) = call(
        sums_kernel,
        "sums",
        (field, normed_bf, grads, gain_sum, cot),
        (jax.ShapeDtypeStruct((48, LANE), F32),),
        flops=10_000_000,
    )

    steps = sum_steps()
    part = part + lax.ppermute(part, *steps[0])
    part, to_a, to_b = lax.optimization_barrier((part, *y_messages(gxlo, gxhi, gylo, gyhi)))
    part = part + lax.ppermute(part, *steps[1])
    gylo, gyhi = low_high(*swap(to_a, to_b, "gy"), "gy")
    part, grad_depth = lax.optimization_barrier((part, grad_depth))
    theirs = lax.ppermute(part, *steps[2])
    own_field, own_sums = call(
        functools.partial(own_kernel, True), "own_backward", (grad_depth, weights), (field_type, sums_type),
        flops=10_000_000,
    )
    part, own_field, own_sums = lax.optimization_barrier((part + theirs, own_field, own_sums))
    _, _, grad_features = call(
        backward_kernel,
        "backward",
        (own_field, own_sums, weights, gxlo, gxhi, gylo, gyhi, masks, cot),
        (field_type, sums_type, block),
        aliases={0: 0, 1: 1},
        flops=2_000_000,
    )
    for index, step in enumerate(steps[3:-1]):
        part = part + lax.ppermute(part, *step)
        if index == 0:
            part, grad_features = lax.optimization_barrier((part, grad_features))
    theirs = lax.ppermute(part, *steps[-1])

    outs = (
        jax.ShapeDtypeStruct((27, channels), F32),
        jax.ShapeDtypeStruct((1, channels), F32),
        jax.ShapeDtypeStruct((channels, channels), F32),
    )
    grad_taps, grad_gain, grad_mix = call(
        unpack_kernel,
        "unpack",
        (part, theirs),
        outs,
        scratch=[pltpu.VMEM(t.shape, F32) for t in outs] + [pltpu.SemaphoreType.DMA((3,))],
        out_specs=(hbm,) * 3,
    )
    shape = features.shape
    return (mixed.reshape(shape), grad_features.reshape(shape), grad_taps, grad_gain.reshape(channels), grad_mix)


def solution(mesh):
    return jax.shard_map(
        shards,
        mesh=mesh,
        in_specs=(P("gx", "gy", None, None), P(), P(), P(), P(), P("gx", "gy", None, None)),
        out_specs=(P("gx", "gy", None, None), P("gx", "gy", None, None), P(), P(), P()),
        check_vma=False,
    )
```

```python
import functools

import jax
import jax.numpy as jnp
from jax import lax
from jax.experimental import pallas as pl
from jax.experimental.pallas import tpu as pltpu
from jax.sharding import PartitionSpec as P

EPS = 1e-05
LANE = 128
WIDE = 256
PLANES = 4
F32 = jnp.float32
BF16 = jnp.bfloat16


def level_masks(slots, side, masks_ref):
    level = lax.broadcasted_iota(jnp.int32, slots.shape, 1)
    at_x = lax.broadcasted_iota(jnp.int32, slots.shape, 2) - lax.axis_index("gx")
    at_y = lax.broadcasted_iota(jnp.int32, slots.shape, 0) - lax.axis_index("gy")
    place = jnp.where(slots >= 0, level + 1, 0).astype(F32)

    def near(off_x, off_y):
        found = jnp.where((at_x == off_x) & (at_y == off_y), place, 0.0)
        found = jnp.sum(jnp.sum(found, axis=0), axis=0, keepdims=True)
        return jnp.sum(found, axis=1, keepdims=True)

    own = near(0, 0)

    def difference(off_x, off_y):
        found = near(off_x, off_y)
        return jnp.where(found > 0.0, found - own, 9.0)

    rows = masks_ref.shape[1]
    row = lax.broadcasted_iota(jnp.int32, (rows, LANE), 0)
    for edge in range(4):
        high = 1 if edge % 2 else -1
        if edge < 2:
            d = jnp.broadcast_to(difference(high, 0), (rows, LANE))
        else:
            corner, middle, other = (difference(off, high) for off in (-1, 0, 1))
            d = jnp.where(row == 0, corner, jnp.where(row == side + 1, other, middle))
        for i, want in enumerate((0.0, -1.0, 1.0)):
            masks_ref[3 * edge + i] = jnp.where(d == want, 1.0, 0.0)


def plane_tiles(load, total, masks):
    low = lax.broadcasted_iota(jnp.int32, load(0).shape, 1) < LANE // 2
    zero = jnp.zeros(load(0).shape, F32)
    aligned = [load(k) for k in range(total)]
    turned = [pltpu.roll(t, LANE // 2, 1) for t in aligned]
    between = [jnp.where(low, turned[j - 1], turned[j]) for j in range(1, total)]
    if masks is None:
        return aligned + [jnp.where(low, zero, turned[0])] + between + [jnp.where(low, turned[-1], zero)]
    same, below, above = masks
    first = jnp.where(low, turned[-1] * below, turned[0] * same)
    last = jnp.where(low, turned[-1] * same, turned[0] * above)
    return [t * same for t in aligned] + [first] + [t * same for t in between] + [last]


def loader(rows):
    return lambda k: rows[:, k * LANE:(k + 1) * LANE].astype(F32)


def column_starts(side, shift):
    pitch = side + 8
    for start in range(0, side + 2, 8):
        size = min(8, side + 2 - start)
        yield start, size, pl.ds(start * pitch + shift, size, stride=pitch)


def own_part(own_ref, field, weights, sums, flip):
    side = own_ref.shape[0]
    tiles = own_ref.shape[2] // LANE
    pitch = side + 8

    def own_planes(step, _):
        for x in range(PLANES):
            x = step * PLANES + x
            base = pl.multiple_of((x + 1) * pitch + 8, 8)
            for i, t in enumerate(plane_tiles(loader(own_ref[x]), tiles, None)):
                field[i, pl.ds(base, side), :] = t
        return 0

    lax.fori_loop(0, side // PLANES, own_planes, 0)
    for i in range(2 * tiles + 1):
        for shift in (7, pitch):
            for _, size, at in column_starts(side, shift):
                field[i, at, :] = jnp.zeros((size, LANE), F32)

    def tile(k, _):
        taps = [weights[26 - t if flip else t] for t in range(27)]
        for half in range(side // 8):
            part = {}
            for plane in range(1, side + 1):
                near = shifted(field, tiles, k, plane, half, pitch)
                for off_x in range(3):
                    x = plane - off_x
                    if not 0 <= x < side:
                        continue
                    for (off_y, off_z), value in near.items():
                        term = value * taps[9 * off_x + 3 * off_y + off_z]
                        part[x] = part[x] + term if x in part else term
                done = plane - 2
                for x in [done, done + 1] if plane == side else [done]:
                    if x >= 0:
                        sums[k, x * side + 8 * half:x * side + 8 * half + 8, :] = part.pop(x)
        return 0

    lax.fori_loop(0, tiles, tile, 0)


def halo_part(xlo_ref, xhi_ref, ylo_ref, yhi_ref, masks_ref, field, weights, sums, flip):
    side, lanes = xlo_ref.shape
    tiles = lanes // LANE
    pitch = side + 8

    def place(i, ref):
        rows = ref.shape[0]
        masks = tuple(masks_ref[3 * i + m, :rows, :] for m in range(3))
        return plane_tiles(loader(ref[...]), tiles, masks)

    for i, ref, plane in ((0, xlo_ref, 0), (1, xhi_ref, side + 1)):
        for j, t in enumerate(place(i, ref)):
            field[j, plane * pitch + 8:plane * pitch + 8 + side, :] = t

    def x_tile(k):
        for plane, off_x, x in ((0, 0, 0), (side + 1, 2, side - 1)):
            for half in range(side // 8):
                row = x * side + 8 * half
                total = sums[k, row:row + 8, :]
                for (off_y, off_z), value in shifted(field, tiles, k, plane, half, pitch).items():
                    tap = 9 * off_x + 3 * off_y + off_z
                    total = total + value * weights[26 - tap if flip else tap]
                sums[k, row:row + 8, :] = total

    for k in range(tiles):
        x_tile(k)

    for i, ref, shift in ((2, ylo_ref, 7), (3, yhi_ref, pitch)):
        for j, t in enumerate(place(i, ref)):
            for start, size, at in column_starts(side, shift):
                field[j, at, :] = t[start:start + size]

    def y_tile(k):
        for shift, off_y, y in ((7, 0, 0), (pitch, 2, side - 1)):
            for x in range(0, side, 8):
                at = pl.ds(x * side + y, 8, stride=side)
                total = sums[k, at, :]
                for off_x in range(3):
                    for off_z in range(3):
                        i = (tiles + k, k, tiles + k + 1)[off_z]
                        tap = 9 * off_x + 3 * off_y + off_z
                        value = field[i, pl.ds((x + off_x) * pitch + shift, 8, stride=pitch), :]
                        total = total + value * weights[26 - tap if flip else tap]
                sums[k, at, :] = total

    for k in range(tiles):
        y_tile(k)


def shifted(field, tiles, k, plane, half, pitch):
    found = {}
    for off_y in range(3):
        row = plane * pitch + 7 + 8 * half + off_y
        for off_z in range(3):
            i = (tiles + k, k, tiles + k + 1)[off_z]
            found[off_y, off_z] = field[i, row:row + 8, :]
    return found


def edges_of(cells_ref, xa_ref, xb_ref, ylo_ref, yhi_ref):
    side, _, lanes = cells_ref.shape
    odd = lax.axis_index("gx") % 2
    xa_ref[...] = cells_ref[jnp.where(odd == 1, 0, side - 1)]
    xb_ref[...] = cells_ref[jnp.where(odd == 1, side - 1, 0)]
    row = lax.broadcasted_iota(jnp.int32, (2 * side, side * side), 0)
    col = lax.broadcasted_iota(jnp.int32, (2 * side, side * side), 1)
    wanted = jnp.where(row < side, row * side, (row - side) * side + side - 1)
    pick = jnp.where(col == wanted, 1.0, 0.0).astype(BF16)
    flat = cells_ref[...].reshape(side * side, lanes)
    found = jnp.dot(pick, flat, preferred_element_type=F32).astype(BF16)
    ylo_ref[...] = found[:side]
    yhi_ref[...] = found[side:]


def params_kernel(
    slots_ref, mix_ref, taps_ref, gain_ref, masks_ref, weights, mean_mat_ref, mix_mat_ref, gain_wide_ref
):
    channels = mix_ref.shape[0]
    level_masks(slots_ref[...], masks_ref.shape[1] - 8, masks_ref)
    wide = jnp.concatenate([taps_ref[...], taps_ref[...]], axis=1)
    for tap in range(27):
        weights[tap] = jnp.broadcast_to(wide[tap:tap + 1], (8, LANE))
    copies = WIDE // channels
    row_id = lax.broadcasted_iota(jnp.int32, (WIDE, WIDE), 0) // channels
    col_id = lax.broadcasted_iota(jnp.int32, (WIDE, WIDE), 1) // channels
    block = row_id == col_id
    mean_mat_ref[...] = jnp.where(block, 1.0 / channels, 0.0).astype(BF16)
    mix = mix_ref[...].astype(F32)
    mix_row = jnp.concatenate([mix] * copies, axis=1)
    mix_mat_ref[...] = jnp.where(block, jnp.concatenate([mix_row] * copies, axis=0), 0.0).astype(BF16)
    gain_wide_ref[...] = jnp.concatenate([gain_ref[...]] * copies, axis=1)


def own_kernel(flip, own_ref, weights, field, sums):
    own_part(own_ref, field, weights, sums, flip)


def forward_kernel(
    field, depth, weights, mean_mat_ref, mix_mat_ref, gain_wide_ref,
    xlo_ref, xhi_ref, ylo_ref, yhi_ref, masks_ref, cot_ref,
    field_out_ref, depth_out_ref, grad_ref, gxa_ref, gxb_ref, gylo_ref, gyhi_ref,
    normed_bf, grads, gain_sum_ref,
):
    side, _, lanes = cot_ref.shape
    cells = side * side
    halo_part(xlo_ref, xhi_ref, ylo_ref, yhi_ref, masks_ref, field, weights, depth, False)

    mean_mat = mean_mat_ref[...]
    mix_mat = mix_mat_ref[...]
    gain = gain_wide_ref[...]
    rows = 128
    xs = rows // side
    gain_sum = jnp.zeros((8, WIDE), F32)
    for part in range(lanes // WIDE):
        cols = slice(part * WIDE, (part + 1) * WIDE)
        for chunk in range(cells // rows):
            at = slice(chunk * rows, (chunk + 1) * rows)
            planes = slice(chunk * xs, (chunk + 1) * xs)
            dep = jnp.concatenate([depth[2 * part, at, :], depth[2 * part + 1, at, :]], axis=1)
            mean_sq = jnp.dot((dep * dep).astype(BF16), mean_mat, preferred_element_type=F32)
            inv = lax.rsqrt(mean_sq + EPS)
            normed = dep * inv
            norm_bf = (normed * gain).astype(BF16)
            normed_bf[at, cols] = norm_bf
            grad_norm = lax.dot_general(
                cot_ref[planes, :, cols].reshape(rows, WIDE), mix_mat,
                (((1,), (1,)), ((), ())), preferred_element_type=F32,
            )
            gain_sum = gain_sum + jnp.sum((grad_norm * normed).reshape(rows // 8, 8, WIDE), axis=0)
            scaled = grad_norm * gain
            mean = jnp.dot((scaled * normed).astype(BF16), mean_mat, preferred_element_type=F32)
            grad = (inv * (scaled - normed * mean)).astype(BF16)
            grad_ref[planes, :, cols] = grad.reshape(xs, side, WIDE)
            wide_grad = grad.astype(F32)
            grads[2 * part, at, :] = wide_grad[:, :LANE]
            grads[2 * part + 1, at, :] = wide_grad[:, LANE:]
    gain_sum_ref[...] = gain_sum
    edges_of(grad_ref, gxa_ref, gxb_ref, gylo_ref, gyhi_ref)


def mixed_kernel(own_ref, normed_bf, mix_mat_ref, mixed_ref):
    side, _, lanes = own_ref.shape
    mix_mat = mix_mat_ref[...]
    rows = 128
    xs = rows // side
    for part in range(lanes // WIDE):
        cols = slice(part * WIDE, (part + 1) * WIDE)
        for chunk in range(side // xs):
            planes = slice(chunk * xs, (chunk + 1) * xs)
            norm_bf = normed_bf[chunk * rows:(chunk + 1) * rows, cols]
            branch = jnp.dot(norm_bf, mix_mat, preferred_element_type=F32)
            feat = own_ref[planes, :, cols].reshape(rows, WIDE).astype(F32)
            mixed_ref[planes, :, cols] = (feat + branch).astype(BF16).reshape(xs, side, WIDE)


def sums_kernel(field, normed_bf, grads, gain_sum_ref, cot_ref, packed_ref, mix_sum):
    side, _, lanes = cot_ref.shape
    tiles = lanes // LANE
    channels = packed_ref.shape[1] // 2
    pitch = side + 8
    cells = side * side
    mix_sum[...] = jnp.zeros(mix_sum.shape, F32)

    def tap_tile(k, sums):
        sums = list(sums)
        cols = pl.ds(pl.multiple_of(k * LANE, LANE), LANE)
        mix_sum[...] += lax.dot_general(
            normed_bf[:, cols],
            cot_ref[:, :, cols].reshape(cells, LANE),
            (((0,), (0,)), ((), ())),
            preferred_element_type=F32,
        )
        for half in range(side // 8):
            near_grads = {}
            for plane in range(side + 2):
                if plane < side:
                    row = plane * side + 8 * half
                    near_grads[plane] = grads[k, row:row + 8, :]
                near = shifted(field, tiles, k, plane, half, pitch)
                for (off_y, off_z), value in near.items():
                    for off_x in range(3):
                        x = plane - off_x
                        if 0 <= x < side:
                            tap = 9 * off_x + 3 * off_y + off_z
                            sums[tap] = sums[tap] + value * near_grads[x]
                near_grads.pop(plane - 2, None)
        return tuple(sums)

    sums = lax.fori_loop(0, tiles, tap_tile, tuple(jnp.zeros((8, LANE), F32) for _ in range(27)))
    grad_mix = mix_sum[:channels, :channels] + mix_sum[channels:, channels:]
    packed_ref[0:32, :] = jnp.concatenate([grad_mix[:32], grad_mix[32:]], axis=1)
    gain_row = jnp.sum(gain_sum_ref[...], axis=0, keepdims=True)
    rows = [jnp.sum(t, axis=0, keepdims=True) for t in sums] + [gain_row[:, :LANE] + gain_row[:, LANE:]]
    rows = jnp.concatenate(rows + [jnp.zeros((4, LANE), F32)], axis=0)
    rows = rows[:, :channels] + rows[:, channels:]
    packed_ref[32:48, :] = jnp.concatenate([rows[:16], rows[16:]], axis=1)


def backward_kernel(
    field, sums, weights, xlo_ref, xhi_ref, ylo_ref, yhi_ref, masks_ref, cot_ref,
    field_out_ref, sums_out_ref, out_ref,
):
    side = cot_ref.shape[0]
    halo_part(xlo_ref, xhi_ref, ylo_ref, yhi_ref, masks_ref, field, weights, sums, True)
    for x in range(side):
        for k in range(sums.shape[0]):
            cols = slice(k * LANE, (k + 1) * LANE)
            cot = cot_ref[x, :, cols].astype(F32)
            out_ref[x, :, cols] = (cot + sums[k, x * side:(x + 1) * side, :]).astype(BF16)


def unpack_kernel(mine_ref, theirs_ref, taps_hbm, gain_hbm, mix_hbm, taps_ref, gain_ref, mix_ref, done):
    total = mine_ref[...] + theirs_ref[...]
    channels = mix_ref.shape[0]
    mix_ref[0:32, :] = total[:32, :channels]
    mix_ref[32:64, :] = total[:32, channels:]
    taps_ref[0:16, :] = total[32:48, :channels]
    taps_ref[16:27, :] = total[32:43, channels:]
    gain_ref[...] = total[43:44, channels:]
    copies = [
        pltpu.make_async_copy(src, dst, done.at[i])
        for i, (src, dst) in enumerate(((taps_ref, taps_hbm), (gain_ref, gain_hbm), (mix_ref, mix_hbm)))
    ]
    for copy in copies:
        copy.start()
    for copy in copies:
        copy.wait()


def swap(to_first, to_second, axis):
    sizes = {name: lax.axis_size(name) for name in ("gx", "gy")}
    count = sizes[axis]

    def second(place):
        other = "gy" if axis == "gx" else "gx"
        if 0 < place[axis] < count - 1:
            return {**place, axis: ((place[axis] + 1) ^ 1) - 1}
        return {**place, other: place[other] ^ 1}

    def index(place):
        return place["gx"] * sizes["gy"] + place["gy"]

    places = [{"gx": i, "gy": j} for i in range(sizes["gx"]) for j in range(sizes["gy"])]
    from_second = lax.ppermute(to_second, ("gx", "gy"), [(index(p), index(second(p))) for p in places])
    return lax.ppermute(to_first, axis, [(i, i ^ 1) for i in range(count)]), from_second


def low_high(from_first, from_second, axis):
    even = lax.axis_index(axis) % 2 == 0
    return jnp.where(even, from_second, from_first), jnp.where(even, from_first, from_second)


def y_messages(xlo, xhi, ylo, yhi):
    low = jnp.concatenate([xlo[:1], ylo, xhi[:1]], axis=0)
    high = jnp.concatenate([xlo[-1:], yhi, xhi[-1:]], axis=0)
    return low_high(low, high, "gy")


def sum_steps():
    steps = []
    for axis in ("gx", "gy"):
        count = lax.axis_size(axis)
        bit = 1
        while bit < count:
            steps.append((axis, [(i, i ^ bit) for i in range(count)]))
            bit *= 2
    return steps


def shards(features, slot_map, tap_weights, gain, mix_weight, cotangent):
    side, _, _, lanes = features.shape
    channels = gain.shape[0]
    tiles = lanes // LANE
    cells = features.reshape(side, side, lanes)
    cot = cotangent.reshape(side, side, lanes)
    vmem = pl.BlockSpec(memory_space=pltpu.VMEM)
    hbm = pl.BlockSpec(memory_space=pltpu.HBM)
    block = jax.ShapeDtypeStruct((side, side, lanes), BF16)
    edge = jax.ShapeDtypeStruct((side, lanes), BF16)
    field_type = jax.ShapeDtypeStruct((2 * tiles + 1, (side + 2) * (side + 8) + 8, LANE), F32)
    sums_type = jax.ShapeDtypeStruct((tiles, side * side, LANE), F32)
    weights_type = jax.ShapeDtypeStruct((27, 8, LANE), F32)
    mat_type = jax.ShapeDtypeStruct((WIDE, WIDE), BF16)

    def call(kernel, name, operands, outs, scratch=(), aliases={}, flops=0, in_specs=None, out_specs=None):
        return pl.pallas_call(
            kernel,
            out_shape=tuple(jax.ShapeDtypeStruct(t.shape, t.dtype) for t in outs),
            in_specs=in_specs or [vmem] * len(operands),
            out_specs=out_specs or (vmem,) * len(outs),
            scratch_shapes=list(scratch),
            input_output_aliases=aliases,
            compiler_params=pltpu.CompilerParams(vmem_limit_bytes=40 * 1024 * 1024),
            cost_estimate=pl.CostEstimate(flops=flops, bytes_accessed=500_000, transcendentals=0),
            name=name,
        )(*operands)

    xa, xb, ylo, yhi = call(edges_of, "edges", (cells,), (edge, edge, edge, edge), flops=100_000_000_000)
    masks, weights, mean_mat, mix_mat, gain_wide = call(
        params_kernel,
        "params",
        (jnp.transpose(slot_map, (1, 2, 0)), mix_weight, tap_weights, gain.reshape(1, channels)),
        (
            jax.ShapeDtypeStruct((12, side + 8, LANE), F32),
            weights_type,
            mat_type,
            mat_type,
            jax.ShapeDtypeStruct((1, WIDE), F32),
        ),
    )
    xlo, xhi = low_high(*swap(xa, xb, "gx"), "gx")
    to_a, to_b = y_messages(xlo, xhi, ylo, yhi)
    to_a, to_b, weights = lax.optimization_barrier((to_a, to_b, weights))
    ylo, yhi = low_high(*swap(to_a, to_b, "gy"), "gy")
    own_field, own_sums = call(
        functools.partial(own_kernel, False), "own_forward", (cells, weights), (field_type, sums_type),
        flops=10_000_000,
    )
    field, _, grad_depth, gxa, gxb, gylo, gyhi, normed_bf, grads, gain_sum = call(
        forward_kernel,
        "forward",
        (own_field, own_sums, weights, mean_mat, mix_mat, gain_wide, xlo, xhi, ylo, yhi, masks, cot),
        (
            field_type, sums_type, block, edge, edge, edge, edge,
            jax.ShapeDtypeStruct((side * side, lanes), BF16), sums_type, jax.ShapeDtypeStruct((8, WIDE), F32),
        ),
        aliases={0: 0, 1: 1},
        flops=10_000_000,
    )
    gxlo, gxhi = low_high(*swap(gxa, gxb, "gx"), "gx")
    (part,) = call(
        sums_kernel,
        "sums",
        (field, normed_bf, grads, gain_sum, cot),
        (jax.ShapeDtypeStruct((48, LANE), F32),),
        scratch=(pltpu.VMEM((LANE, LANE), F32),),
        flops=10_000_000,
    )

    steps = sum_steps()
    part = part + lax.ppermute(part, *steps[0])
    part, to_a, to_b = lax.optimization_barrier((part, *y_messages(gxlo, gxhi, gylo, gyhi)))
    part = part + lax.ppermute(part, *steps[1])
    gylo, gyhi = low_high(*swap(to_a, to_b, "gy"), "gy")
    part, grad_depth = lax.optimization_barrier((part, grad_depth))
    theirs = lax.ppermute(part, *steps[2])
    own_field, own_sums = call(
        functools.partial(own_kernel, True), "own_backward", (grad_depth, weights), (field_type, sums_type),
        flops=10_000_000,
    )
    part, own_field, own_sums = lax.optimization_barrier((part + theirs, own_field, own_sums))
    _, _, grad_features = call(
        backward_kernel,
        "backward",
        (own_field, own_sums, weights, gxlo, gxhi, gylo, gyhi, masks, cot),
        (field_type, sums_type, block),
        aliases={0: 0, 1: 1},
        flops=2_000_000,
    )
    for index, step in enumerate(steps[3:-1]):
        part = part + lax.ppermute(part, *step)
        if index == 0:
            part, grad_features = lax.optimization_barrier((part, grad_features))
    part, normed_bf = lax.optimization_barrier((part, normed_bf))
    theirs = lax.ppermute(part, *steps[-1])
    (mixed,) = call(mixed_kernel, "mixed", (cells, normed_bf, mix_mat), (block,), flops=10_000_000)

    outs = (
        jax.ShapeDtypeStruct((27, channels), F32),
        jax.ShapeDtypeStruct((1, channels), F32),
        jax.ShapeDtypeStruct((channels, channels), F32),
    )
    grad_taps, grad_gain, grad_mix = call(
        unpack_kernel,
        "unpack",
        (part, theirs),
        outs,
        scratch=[pltpu.VMEM(t.shape, F32) for t in outs] + [pltpu.SemaphoreType.DMA((3,))],
        out_specs=(hbm,) * 3,
    )
    shape = features.shape
    return (mixed.reshape(shape), grad_features.reshape(shape), grad_taps, grad_gain.reshape(channels), grad_mix)


def solution(mesh):
    return jax.shard_map(
        shards,
        mesh=mesh,
        in_specs=(P("gx", "gy", None, None), P(), P(), P(), P(), P("gx", "gy", None, None)),
        out_specs=(P("gx", "gy", None, None), P("gx", "gy", None, None), P(), P(), P()),
        check_vma=False,
    )
```

```python
import functools
import math

import jax
import jax.numpy as jnp
from jax import lax
from jax.experimental import pallas as pl
from jax.experimental.pallas import tpu as pltpu
from jax.sharding import PartitionSpec as P

EPS = 1e-05
LANE = 128
WIDE = 256
PLANES = 4
F32 = jnp.float32
BF16 = jnp.bfloat16


def level_masks(slots, side, masks_ref):
    level = lax.broadcasted_iota(jnp.int32, slots.shape, 1)
    at_x = lax.broadcasted_iota(jnp.int32, slots.shape, 2) - lax.axis_index("gx")
    at_y = lax.broadcasted_iota(jnp.int32, slots.shape, 0) - lax.axis_index("gy")
    place = jnp.where(slots >= 0, level + 1, 0).astype(F32)

    def near(off_x, off_y):
        found = jnp.where((at_x == off_x) & (at_y == off_y), place, 0.0)
        found = jnp.sum(jnp.sum(found, axis=0), axis=0, keepdims=True)
        return jnp.sum(found, axis=1, keepdims=True)

    own = near(0, 0)

    def difference(off_x, off_y):
        found = near(off_x, off_y)
        return jnp.where(found > 0.0, found - own, 9.0)

    rows = masks_ref.shape[1]
    row = lax.broadcasted_iota(jnp.int32, (rows, LANE), 0)
    for edge in range(4):
        high = 1 if edge % 2 else -1
        if edge < 2:
            d = jnp.broadcast_to(difference(high, 0), (rows, LANE))
        else:
            corner, middle, other = (difference(off, high) for off in (-1, 0, 1))
            d = jnp.where(row == 0, corner, jnp.where(row == side + 1, other, middle))
        for i, want in enumerate((0.0, -1.0, 1.0)):
            masks_ref[3 * edge + i] = jnp.where(d == want, 1.0, 0.0)


def plane_tiles(load, total, masks):
    low = lax.broadcasted_iota(jnp.int32, load(0).shape, 1) < LANE // 2
    zero = jnp.zeros(load(0).shape, F32)
    aligned = [load(k) for k in range(total)]
    turned = [pltpu.roll(t, LANE // 2, 1) for t in aligned]
    between = [jnp.where(low, turned[j - 1], turned[j]) for j in range(1, total)]
    if masks is None:
        return aligned + [jnp.where(low, zero, turned[0])] + between + [jnp.where(low, turned[-1], zero)]
    same, below, above = masks
    first = jnp.where(low, turned[-1] * below, turned[0] * same)
    last = jnp.where(low, turned[-1] * same, turned[0] * above)
    return [t * same for t in aligned] + [first] + [t * same for t in between] + [last]


def loader(rows):
    return lambda k: rows[:, k * LANE:(k + 1) * LANE].astype(F32)


def column_starts(side, shift):
    pitch = side + 8
    for start in range(0, side + 2, 8):
        size = min(8, side + 2 - start)
        yield start, size, pl.ds(start * pitch + shift, size, stride=pitch)


def own_part(own_ref, field, weights, sums, flip):
    side = own_ref.shape[0]
    tiles = own_ref.shape[2] // LANE
    pitch = side + 8

    def own_planes(step, _):
        for x in range(PLANES):
            x = step * PLANES + x
            base = pl.multiple_of((x + 1) * pitch + 8, 8)
            for i, t in enumerate(plane_tiles(loader(own_ref[x]), tiles, None)):
                field[i, pl.ds(base, side), :] = t
        return 0

    lax.fori_loop(0, side // PLANES, own_planes, 0)
    for i in range(2 * tiles + 1):
        for shift in (7, pitch):
            for _, size, at in column_starts(side, shift):
                field[i, at, :] = jnp.zeros((size, LANE), F32)

    def tile(k, _):
        taps = [weights[26 - t if flip else t] for t in range(27)]
        for half in range(side // 8):
            part = {}
            for plane in range(1, side + 1):
                near = shifted(field, tiles, k, plane, half, pitch)
                for off_x in range(3):
                    x = plane - off_x
                    if not 0 <= x < side:
                        continue
                    for (off_y, off_z), value in near.items():
                        term = value * taps[9 * off_x + 3 * off_y + off_z]
                        part[x] = part[x] + term if x in part else term
                done = plane - 2
                for x in [done, done + 1] if plane == side else [done]:
                    if x >= 0:
                        sums[k, x * side + 8 * half:x * side + 8 * half + 8, :] = part.pop(x)
        return 0

    lax.fori_loop(0, tiles, tile, 0)


def halo_part(xlo_ref, xhi_ref, ylo_ref, yhi_ref, masks_ref, field, weights, sums, flip):
    side, lanes = xlo_ref.shape
    tiles = lanes // LANE
    pitch = side + 8

    def place(i, ref):
        rows = ref.shape[0]
        masks = tuple(masks_ref[3 * i + m, :rows, :] for m in range(3))
        return plane_tiles(loader(ref[...]), tiles, masks)

    for i, ref, plane in ((0, xlo_ref, 0), (1, xhi_ref, side + 1)):
        for j, t in enumerate(place(i, ref)):
            field[j, plane * pitch + 8:plane * pitch + 8 + side, :] = t

    def x_tile(k):
        for plane, off_x, x in ((0, 0, 0), (side + 1, 2, side - 1)):
            for half in range(side // 8):
                row = x * side + 8 * half
                total = sums[k, row:row + 8, :]
                for (off_y, off_z), value in shifted(field, tiles, k, plane, half, pitch).items():
                    tap = 9 * off_x + 3 * off_y + off_z
                    total = total + value * weights[26 - tap if flip else tap]
                sums[k, row:row + 8, :] = total

    for k in range(tiles):
        x_tile(k)

    for i, ref, shift in ((2, ylo_ref, 7), (3, yhi_ref, pitch)):
        for j, t in enumerate(place(i, ref)):
            for start, size, at in column_starts(side, shift):
                field[j, at, :] = t[start:start + size]

    def y_tile(k):
        for shift, off_y, y in ((7, 0, 0), (pitch, 2, side - 1)):
            for x in range(0, side, 8):
                at = pl.ds(x * side + y, 8, stride=side)
                total = sums[k, at, :]
                for off_x in range(3):
                    for off_z in range(3):
                        i = (tiles + k, k, tiles + k + 1)[off_z]
                        tap = 9 * off_x + 3 * off_y + off_z
                        value = field[i, pl.ds((x + off_x) * pitch + shift, 8, stride=pitch), :]
                        total = total + value * weights[26 - tap if flip else tap]
                sums[k, at, :] = total

    for k in range(tiles):
        y_tile(k)


def shifted(field, tiles, k, plane, half, pitch):
    found = {}
    for off_y in range(3):
        row = plane * pitch + 7 + 8 * half + off_y
        for off_z in range(3):
            i = (tiles + k, k, tiles + k + 1)[off_z]
            found[off_y, off_z] = field[i, row:row + 8, :]
    return found


def x_edges(cells):
    odd = lax.axis_index("gx") % 2 == 1
    return jnp.where(odd, cells[0], cells[-1]), jnp.where(odd, cells[-1], cells[0])


def y_edges_kernel(cells_ref, ylo_ref, yhi_ref):
    side, _, lanes = cells_ref.shape
    row = lax.broadcasted_iota(jnp.int32, (2 * side, side * side), 0)
    col = lax.broadcasted_iota(jnp.int32, (2 * side, side * side), 1)
    wanted = jnp.where(row < side, row * side, (row - side) * side + side - 1)
    pick = jnp.where(col == wanted, 1.0, 0.0).astype(BF16)
    flat = cells_ref[...].reshape(side * side, lanes)
    found = jnp.dot(pick, flat, preferred_element_type=F32).astype(BF16)
    ylo_ref[...] = found[:side]
    yhi_ref[...] = found[side:]


def params_kernel(
    slots_ref, mix_ref, taps_ref, gain_ref, masks_ref, weights, mean_mat_ref, mix_mat_ref, gain_wide_ref
):
    channels = mix_ref.shape[0]
    level_masks(slots_ref[...], masks_ref.shape[1] - 8, masks_ref)
    wide = jnp.concatenate([taps_ref[...], taps_ref[...]], axis=1)
    for tap in range(27):
        weights[tap] = jnp.broadcast_to(wide[tap:tap + 1], (8, LANE))
    copies = WIDE // channels
    row_id = lax.broadcasted_iota(jnp.int32, (WIDE, WIDE), 0) // channels
    col_id = lax.broadcasted_iota(jnp.int32, (WIDE, WIDE), 1) // channels
    block = row_id == col_id
    mean_mat_ref[...] = jnp.where(block, 1.0 / channels, 0.0).astype(BF16)
    mix = mix_ref[...].astype(F32)
    mix_row = jnp.concatenate([mix] * copies, axis=1)
    mix_mat_ref[...] = jnp.where(block, jnp.concatenate([mix_row] * copies, axis=0), 0.0).astype(BF16)
    gain_wide_ref[...] = jnp.concatenate([gain_ref[...]] * copies, axis=1)


def own_kernel(flip, own_ref, weights, field, sums):
    own_part(own_ref, field, weights, sums, flip)


def forward_kernel(
    field, depth, weights, mean_mat_ref, mix_mat_ref, gain_wide_ref,
    xlo_ref, xhi_ref, ylo_ref, yhi_ref, masks_ref, cot_ref,
    field_out_ref, depth_out_ref, grad_ref, gxa_ref, gxb_ref, normed_bf, grads, gain_sum_ref, grad_mix_ref,
):
    side, _, lanes = cot_ref.shape
    cells = side * side
    halo_part(xlo_ref, xhi_ref, ylo_ref, yhi_ref, masks_ref, field, weights, depth, False)

    mean_mat = mean_mat_ref[...]
    mix_mat = mix_mat_ref[...]
    gain = gain_wide_ref[...]
    rows = 128
    xs = rows // side
    gain_sum = jnp.zeros((8, WIDE), F32)
    mix_sum = jnp.zeros((WIDE, WIDE), F32)
    for part in range(lanes // WIDE):
        cols = slice(part * WIDE, (part + 1) * WIDE)
        for chunk in range(cells // rows):
            at = slice(chunk * rows, (chunk + 1) * rows)
            planes = slice(chunk * xs, (chunk + 1) * xs)
            dep = jnp.concatenate([depth[2 * part, at, :], depth[2 * part + 1, at, :]], axis=1)
            mean_sq = jnp.dot((dep * dep).astype(BF16), mean_mat, preferred_element_type=F32)
            inv = lax.rsqrt(mean_sq + EPS)
            normed = dep * inv
            norm_bf = (normed * gain).astype(BF16)
            normed_bf[at, cols] = norm_bf
            grad_norm = lax.dot_general(
                cot_ref[planes, :, cols].reshape(rows, WIDE), mix_mat,
                (((1,), (1,)), ((), ())), preferred_element_type=F32,
            )
            gain_sum = gain_sum + jnp.sum((grad_norm * normed).reshape(rows // 8, 8, WIDE), axis=0)
            scaled = grad_norm * gain
            mean = jnp.dot((scaled * normed).astype(BF16), mean_mat, preferred_element_type=F32)
            grad = (inv * (scaled - normed * mean)).astype(BF16)
            grad_ref[planes, :, cols] = grad.reshape(xs, side, WIDE)
            wide_grad = grad.astype(F32)
            grads[2 * part, at, :] = wide_grad[:, :LANE]
            grads[2 * part + 1, at, :] = wide_grad[:, LANE:]
        mix_sum = mix_sum + lax.dot_general(
            normed_bf[:, cols],
            cot_ref[:, :, cols].reshape(cells, WIDE),
            (((0,), (0,)), ((), ())),
            preferred_element_type=F32,
        )
    gain_sum_ref[...] = gain_sum
    channels = grad_mix_ref.shape[1] // 2
    grad_mix = mix_sum[:channels, :channels]
    for i in range(1, WIDE // channels):
        span = slice(i * channels, (i + 1) * channels)
        grad_mix = grad_mix + mix_sum[span, span]
    grad_mix_ref[...] = jnp.concatenate([grad_mix[:32], grad_mix[32:]], axis=1)
    odd = lax.axis_index("gx") % 2
    gxa_ref[...] = grad_ref[jnp.where(odd == 1, 0, side - 1)]
    gxb_ref[...] = grad_ref[jnp.where(odd == 1, side - 1, 0)]


def mixed_kernel(own_ref, normed_bf, mix_mat_ref, mixed_ref):
    side, _, lanes = own_ref.shape
    mix_mat = mix_mat_ref[...]
    rows = 128
    xs = rows // side
    for part in range(lanes // WIDE):
        cols = slice(part * WIDE, (part + 1) * WIDE)
        for chunk in range(side // xs):
            planes = slice(chunk * xs, (chunk + 1) * xs)
            norm_bf = normed_bf[chunk * rows:(chunk + 1) * rows, cols]
            branch = jnp.dot(norm_bf, mix_mat, preferred_element_type=F32)
            feat = own_ref[planes, :, cols].reshape(rows, WIDE).astype(F32)
            mixed_ref[planes, :, cols] = (feat + branch).astype(BF16).reshape(xs, side, WIDE)


def sums_kernel(field, grads, gain_sum_ref, grad_mix_ref, packed_ref):
    tiles, cells, _ = grads.shape
    side = math.isqrt(cells)
    channels = packed_ref.shape[1] // 2
    pitch = side + 8
    def tap_tile(k, sums):
        sums = list(sums)
        for half in range(side // 8):
            near_grads = {}
            for plane in range(side + 2):
                if plane < side:
                    row = plane * side + 8 * half
                    near_grads[plane] = grads[k, row:row + 8, :]
                near = shifted(field, tiles, k, plane, half, pitch)
                for (off_y, off_z), value in near.items():
                    for off_x in range(3):
                        x = plane - off_x
                        if 0 <= x < side:
                            tap = 9 * off_x + 3 * off_y + off_z
                            sums[tap] = sums[tap] + value * near_grads[x]
                near_grads.pop(plane - 2, None)
        return tuple(sums)

    sums = lax.fori_loop(0, tiles, tap_tile, tuple(jnp.zeros((8, LANE), F32) for _ in range(27)))
    packed_ref[0:32, :] = grad_mix_ref[...]
    gain_row = jnp.sum(gain_sum_ref[...], axis=0, keepdims=True)
    rows = [jnp.sum(t, axis=0, keepdims=True) for t in sums] + [gain_row[:, :LANE] + gain_row[:, LANE:]]
    rows = jnp.concatenate(rows + [jnp.zeros((4, LANE), F32)], axis=0)
    rows = rows[:, :channels] + rows[:, channels:]
    packed_ref[32:48, :] = jnp.concatenate([rows[:16], rows[16:]], axis=1)


def backward_kernel(
    field, sums, weights, xlo_ref, xhi_ref, ylo_ref, yhi_ref, masks_ref, cot_ref,
    field_out_ref, sums_out_ref, out_ref,
):
    side = cot_ref.shape[0]
    halo_part(xlo_ref, xhi_ref, ylo_ref, yhi_ref, masks_ref, field, weights, sums, True)
    for x in range(side):
        for k in range(sums.shape[0]):
            cols = slice(k * LANE, (k + 1) * LANE)
            cot = cot_ref[x, :, cols].astype(F32)
            out_ref[x, :, cols] = (cot + sums[k, x * side:(x + 1) * side, :]).astype(BF16)


def unpack_kernel(mine_ref, theirs_ref, taps_hbm, gain_hbm, mix_hbm, taps_ref, gain_ref, mix_ref, done):
    total = mine_ref[...] + theirs_ref[...]
    channels = mix_ref.shape[0]
    mix_ref[0:32, :] = total[:32, :channels]
    mix_ref[32:64, :] = total[:32, channels:]
    taps_ref[0:16, :] = total[32:48, :channels]
    taps_ref[16:27, :] = total[32:43, channels:]
    gain_ref[...] = total[43:44, channels:]
    copies = [
        pltpu.make_async_copy(src, dst, done.at[i])
        for i, (src, dst) in enumerate(((taps_ref, taps_hbm), (gain_ref, gain_hbm), (mix_ref, mix_hbm)))
    ]
    for copy in copies:
        copy.start()
    for copy in copies:
        copy.wait()


def swap(to_first, to_second, axis):
    sizes = {name: lax.axis_size(name) for name in ("gx", "gy")}
    count = sizes[axis]

    def second(place):
        other = "gy" if axis == "gx" else "gx"
        if 0 < place[axis] < count - 1:
            return {**place, axis: ((place[axis] + 1) ^ 1) - 1}
        return {**place, other: place[other] ^ 1}

    def index(place):
        return place["gx"] * sizes["gy"] + place["gy"]

    places = [{"gx": i, "gy": j} for i in range(sizes["gx"]) for j in range(sizes["gy"])]
    from_second = lax.ppermute(to_second, ("gx", "gy"), [(index(p), index(second(p))) for p in places])
    return lax.ppermute(to_first, axis, [(i, i ^ 1) for i in range(count)]), from_second


def low_high(from_first, from_second, axis):
    even = lax.axis_index(axis) % 2 == 0
    return jnp.where(even, from_second, from_first), jnp.where(even, from_first, from_second)


def y_messages(xlo, xhi, ylo, yhi):
    low = jnp.concatenate([xlo[:1], ylo, xhi[:1]], axis=0)
    high = jnp.concatenate([xlo[-1:], yhi, xhi[-1:]], axis=0)
    return low_high(low, high, "gy")


def sum_steps():
    steps = []
    for axis in ("gx", "gy"):
        count = lax.axis_size(axis)
        bit = 1
        while bit < count:
            steps.append((axis, [(i, i ^ bit) for i in range(count)]))
            bit *= 2
    return steps


def shards(features, slot_map, tap_weights, gain, mix_weight, cotangent):
    side, _, _, lanes = features.shape
    channels = gain.shape[0]
    tiles = lanes // LANE
    cells = features.reshape(side, side, lanes)
    cot = cotangent.reshape(side, side, lanes)
    vmem = pl.BlockSpec(memory_space=pltpu.VMEM)
    hbm = pl.BlockSpec(memory_space=pltpu.HBM)
    block = jax.ShapeDtypeStruct((side, side, lanes), BF16)
    edge = jax.ShapeDtypeStruct((side, lanes), BF16)
    field_type = jax.ShapeDtypeStruct((2 * tiles + 1, (side + 2) * (side + 8) + 8, LANE), F32)
    sums_type = jax.ShapeDtypeStruct((tiles, side * side, LANE), F32)
    weights_type = jax.ShapeDtypeStruct((27, 8, LANE), F32)
    mat_type = jax.ShapeDtypeStruct((WIDE, WIDE), BF16)

    def call(kernel, name, operands, outs, scratch=(), aliases={}, flops=0, in_specs=None, out_specs=None):
        return pl.pallas_call(
            kernel,
            out_shape=tuple(jax.ShapeDtypeStruct(t.shape, t.dtype) for t in outs),
            in_specs=in_specs or [vmem] * len(operands),
            out_specs=out_specs or (vmem,) * len(outs),
            scratch_shapes=list(scratch),
            input_output_aliases=aliases,
            compiler_params=pltpu.CompilerParams(vmem_limit_bytes=40 * 1024 * 1024),
            cost_estimate=pl.CostEstimate(flops=flops, bytes_accessed=500_000, transcendentals=0),
            name=name,
        )(*operands)

    ylo, yhi = call(y_edges_kernel, "y_edges", (cells,), (edge, edge), flops=100_000_000_000)
    masks, weights, mean_mat, mix_mat, gain_wide = call(
        params_kernel,
        "params",
        (jnp.transpose(slot_map, (1, 2, 0)), mix_weight, tap_weights, gain.reshape(1, channels)),
        (
            jax.ShapeDtypeStruct((12, side + 8, LANE), F32),
            weights_type,
            mat_type,
            mat_type,
            jax.ShapeDtypeStruct((1, WIDE), F32),
        ),
    )
    xlo, xhi = low_high(*swap(*x_edges(cells), "gx"), "gx")
    to_a, to_b = y_messages(xlo, xhi, ylo, yhi)
    to_a, to_b, weights = lax.optimization_barrier((to_a, to_b, weights))
    ylo, yhi = low_high(*swap(to_a, to_b, "gy"), "gy")
    own_field, own_sums = call(
        functools.partial(own_kernel, False), "own_forward", (cells, weights), (field_type, sums_type),
        flops=10_000_000,
    )
    field, _, grad_depth, gxa, gxb, normed_bf, grads, gain_sum, grad_mix = call(
        forward_kernel,
        "forward",
        (own_field, own_sums, weights, mean_mat, mix_mat, gain_wide, xlo, xhi, ylo, yhi, masks, cot),
        (
            field_type, sums_type, block, edge, edge,
            jax.ShapeDtypeStruct((side * side, lanes), BF16), sums_type, jax.ShapeDtypeStruct((8, WIDE), F32),
            jax.ShapeDtypeStruct((32, LANE), F32),
        ),
        aliases={0: 0, 1: 1},
        flops=10_000_000,
    )
    gxlo, gxhi = low_high(*swap(gxa, gxb, "gx"), "gx")
    (part,) = call(
        sums_kernel,
        "sums",
        (field, grads, gain_sum, grad_mix),
        (jax.ShapeDtypeStruct((48, LANE), F32),),
        flops=10_000_000,
    )

    steps = sum_steps()
    part, y_cells = lax.optimization_barrier((part, grad_depth))
    part = part + lax.ppermute(part, *steps[0])
    gylo, gyhi = call(y_edges_kernel, "grad_y_edges", (y_cells,), (edge, edge), flops=1_000_000)
    part, to_a, to_b = lax.optimization_barrier((part, *y_messages(gxlo, gxhi, gylo, gyhi)))
    part = part + lax.ppermute(part, *steps[1])
    gylo, gyhi = low_high(*swap(to_a, to_b, "gy"), "gy")
    part, grad_depth = lax.optimization_barrier((part, grad_depth))
    theirs = lax.ppermute(part, *steps[2])
    own_field, own_sums = call(
        functools.partial(own_kernel, True), "own_backward", (grad_depth, weights), (field_type, sums_type),
        flops=10_000_000,
    )
    part, own_field, own_sums = lax.optimization_barrier((part + theirs, own_field, own_sums))
    _, _, grad_features = call(
        backward_kernel,
        "backward",
        (own_field, own_sums, weights, gxlo, gxhi, gylo, gyhi, masks, cot),
        (field_type, sums_type, block),
        aliases={0: 0, 1: 1},
        flops=2_000_000,
    )
    for index, step in enumerate(steps[3:-1]):
        part = part + lax.ppermute(part, *step)
        if index == 0:
            part, grad_features = lax.optimization_barrier((part, grad_features))
    part, normed_bf = lax.optimization_barrier((part, normed_bf))
    theirs = lax.ppermute(part, *steps[-1])
    (mixed,) = call(mixed_kernel, "mixed", (cells, normed_bf, mix_mat), (block,), flops=10_000_000)

    outs = (
        jax.ShapeDtypeStruct((27, channels), F32),
        jax.ShapeDtypeStruct((1, channels), F32),
        jax.ShapeDtypeStruct((channels, channels), F32),
    )
    grad_taps, grad_gain, grad_mix = call(
        unpack_kernel,
        "unpack",
        (part, theirs),
        outs,
        scratch=[pltpu.VMEM(t.shape, F32) for t in outs] + [pltpu.SemaphoreType.DMA((3,))],
        out_specs=(hbm,) * 3,
    )
    shape = features.shape
    return (mixed.reshape(shape), grad_features.reshape(shape), grad_taps, grad_gain.reshape(channels), grad_mix)


def solution(mesh):
    return jax.shard_map(
        shards,
        mesh=mesh,
        in_specs=(P("gx", "gy", None, None), P(), P(), P(), P(), P("gx", "gy", None, None)),
        out_specs=(P("gx", "gy", None, None), P("gx", "gy", None, None), P(), P(), P()),
        check_vma=False,
    )
```

```python
import functools
import math

import jax
import jax.numpy as jnp
from jax import lax
from jax.experimental import pallas as pl
from jax.experimental.pallas import tpu as pltpu
from jax.sharding import PartitionSpec as P

EPS = 1e-05
LANE = 128
WIDE = 256
PLANES = 4
F32 = jnp.float32
BF16 = jnp.bfloat16


def level_masks(slots, side, masks_ref):
    level = lax.broadcasted_iota(jnp.int32, slots.shape, 1)
    at_x = lax.broadcasted_iota(jnp.int32, slots.shape, 2) - lax.axis_index("gx")
    at_y = lax.broadcasted_iota(jnp.int32, slots.shape, 0) - lax.axis_index("gy")
    place = jnp.where(slots >= 0, level + 1, 0).astype(F32)

    def near(off_x, off_y):
        found = jnp.where((at_x == off_x) & (at_y == off_y), place, 0.0)
        found = jnp.sum(jnp.sum(found, axis=0), axis=0, keepdims=True)
        return jnp.sum(found, axis=1, keepdims=True)

    own = near(0, 0)

    def difference(off_x, off_y):
        found = near(off_x, off_y)
        return jnp.where(found > 0.0, found - own, 9.0)

    rows = masks_ref.shape[1]
    row = lax.broadcasted_iota(jnp.int32, (rows, LANE), 0)
    for edge in range(4):
        high = 1 if edge % 2 else -1
        if edge < 2:
            d = jnp.broadcast_to(difference(high, 0), (rows, LANE))
        else:
            corner, middle, other = (difference(off, high) for off in (-1, 0, 1))
            d = jnp.where(row == 0, corner, jnp.where(row == side + 1, other, middle))
        for i, want in enumerate((0.0, -1.0, 1.0)):
            masks_ref[3 * edge + i] = jnp.where(d == want, 1.0, 0.0)


def plane_tiles(load, total, masks):
    low = lax.broadcasted_iota(jnp.int32, load(0).shape, 1) < LANE // 2
    zero = jnp.zeros(load(0).shape, F32)
    aligned = [load(k) for k in range(total)]
    turned = [pltpu.roll(t, LANE // 2, 1) for t in aligned]
    between = [jnp.where(low, turned[j - 1], turned[j]) for j in range(1, total)]
    if masks is None:
        return aligned + [jnp.where(low, zero, turned[0])] + between + [jnp.where(low, turned[-1], zero)]
    same, below, above = masks
    first = jnp.where(low, turned[-1] * below, turned[0] * same)
    last = jnp.where(low, turned[-1] * same, turned[0] * above)
    return [t * same for t in aligned] + [first] + [t * same for t in between] + [last]


def loader(rows):
    return lambda k: rows[:, k * LANE:(k + 1) * LANE].astype(F32)


def column_starts(side, shift):
    pitch = side + 8
    for start in range(0, side + 2, 8):
        size = min(8, side + 2 - start)
        yield start, size, pl.ds(start * pitch + shift, size, stride=pitch)


def placed_tiles(edge, ref, masks_ref):
    rows, lanes = ref.shape
    masks = tuple(masks_ref[3 * edge + m, :rows, :] for m in range(3))
    return plane_tiles(loader(ref[...]), lanes // LANE, masks)


def x_part(own_ref, xlo_ref, xhi_ref, masks_ref, field, weights, sums, flip):
    side = own_ref.shape[0]
    tiles = own_ref.shape[2] // LANE
    pitch = side + 8

    def own_planes(step, _):
        for x in range(PLANES):
            x = step * PLANES + x
            base = pl.multiple_of((x + 1) * pitch + 8, 8)
            for i, t in enumerate(plane_tiles(loader(own_ref[x]), tiles, None)):
                field[i, pl.ds(base, side), :] = t
        return 0

    lax.fori_loop(0, side // PLANES, own_planes, 0)
    for edge, ref, plane in ((0, xlo_ref, 0), (1, xhi_ref, side + 1)):
        for i, t in enumerate(placed_tiles(edge, ref, masks_ref)):
            field[i, plane * pitch + 8:plane * pitch + 8 + side, :] = t
    for i in range(2 * tiles + 1):
        for shift in (7, pitch):
            for _, size, at in column_starts(side, shift):
                field[i, at, :] = jnp.zeros((size, LANE), F32)

    def tile(k, _):
        taps = [weights[26 - t if flip else t] for t in range(27)]
        for half in range(side // 8):
            part = {}
            for plane in range(side + 2):
                near = shifted(field, tiles, k, plane, half, pitch)
                for off_x in range(3):
                    x = plane - off_x
                    if not 0 <= x < side:
                        continue
                    for (off_y, off_z), value in near.items():
                        term = value * taps[9 * off_x + 3 * off_y + off_z]
                        part[x] = part[x] + term if x in part else term
                done = plane - 2
                if done >= 0:
                    row = done * side + 8 * half
                    sums[k, row:row + 8, :] = part.pop(done)
        return 0

    lax.fori_loop(0, tiles, tile, 0)


def y_part(ylo_ref, yhi_ref, masks_ref, field, weights, sums, flip):
    tiles, cells, _ = sums.shape
    side = math.isqrt(cells)
    pitch = side + 8
    for edge, ref, shift in ((2, ylo_ref, 7), (3, yhi_ref, pitch)):
        for j, t in enumerate(placed_tiles(edge, ref, masks_ref)):
            for start, size, at in column_starts(side, shift):
                field[j, at, :] = t[start:start + size]
    for k in range(tiles):
        for shift, off_y, y in ((7, 0, 0), (pitch, 2, side - 1)):
            for x in range(0, side, 8):
                at = pl.ds(x * side + y, 8, stride=side)
                total = sums[k, at, :]
                for off_x in range(3):
                    for off_z in range(3):
                        i = (tiles + k, k, tiles + k + 1)[off_z]
                        tap = 9 * off_x + 3 * off_y + off_z
                        value = field[i, pl.ds((x + off_x) * pitch + shift, 8, stride=pitch), :]
                        total = total + value * weights[26 - tap if flip else tap]
                sums[k, at, :] = total


def shifted(field, tiles, k, plane, half, pitch):
    found = {}
    for off_y in range(3):
        row = plane * pitch + 7 + 8 * half + off_y
        for off_z in range(3):
            i = (tiles + k, k, tiles + k + 1)[off_z]
            found[off_y, off_z] = field[i, row:row + 8, :]
    return found


def x_edges(cells):
    odd = lax.axis_index("gx") % 2 == 1
    return jnp.where(odd, cells[0], cells[-1]), jnp.where(odd, cells[-1], cells[0])


def y_edges_kernel(cells_ref, ylo_ref, yhi_ref):
    side, _, lanes = cells_ref.shape
    row = lax.broadcasted_iota(jnp.int32, (2 * side, side * side), 0)
    col = lax.broadcasted_iota(jnp.int32, (2 * side, side * side), 1)
    wanted = jnp.where(row < side, row * side, (row - side) * side + side - 1)
    pick = jnp.where(col == wanted, 1.0, 0.0).astype(BF16)
    flat = cells_ref[...].reshape(side * side, lanes)
    found = jnp.dot(pick, flat, preferred_element_type=F32).astype(BF16)
    ylo_ref[...] = found[:side]
    yhi_ref[...] = found[side:]


def params_kernel(
    slots_ref, mix_ref, taps_ref, gain_ref, masks_ref, weights, mean_mat_ref, mix_mat_ref, gain_wide_ref
):
    channels = mix_ref.shape[0]
    level_masks(slots_ref[...], masks_ref.shape[1] - 8, masks_ref)
    wide = jnp.concatenate([taps_ref[...], taps_ref[...]], axis=1)
    for tap in range(27):
        weights[tap] = jnp.broadcast_to(wide[tap:tap + 1], (8, LANE))
    copies = WIDE // channels
    row_id = lax.broadcasted_iota(jnp.int32, (WIDE, WIDE), 0) // channels
    col_id = lax.broadcasted_iota(jnp.int32, (WIDE, WIDE), 1) // channels
    block = row_id == col_id
    mean_mat_ref[...] = jnp.where(block, 1.0 / channels, 0.0).astype(BF16)
    mix = mix_ref[...].astype(F32)
    mix_row = jnp.concatenate([mix] * copies, axis=1)
    mix_mat_ref[...] = jnp.where(block, jnp.concatenate([mix_row] * copies, axis=0), 0.0).astype(BF16)
    gain_wide_ref[...] = jnp.concatenate([gain_ref[...]] * copies, axis=1)


def own_kernel(flip, own_ref, xlo_ref, xhi_ref, masks_ref, weights, field, sums):
    x_part(own_ref, xlo_ref, xhi_ref, masks_ref, field, weights, sums, flip)


def forward_kernel(
    field, depth, weights, mean_mat_ref, mix_mat_ref, gain_wide_ref,
    ylo_ref, yhi_ref, masks_ref, cot_ref,
    field_out_ref, depth_out_ref, grad_ref, gxa_ref, gxb_ref, normed_bf, grads, gain_sum_ref, grad_mix_ref,
):
    side, _, lanes = cot_ref.shape
    cells = side * side
    y_part(ylo_ref, yhi_ref, masks_ref, field, weights, depth, False)

    mean_mat = mean_mat_ref[...]
    mix_mat = mix_mat_ref[...]
    gain = gain_wide_ref[...]
    rows = 128
    xs = rows // side
    gain_sum = jnp.zeros((8, WIDE), F32)
    mix_sum = jnp.zeros((WIDE, WIDE), F32)
    for part in range(lanes // WIDE):
        cols = slice(part * WIDE, (part + 1) * WIDE)
        for chunk in range(cells // rows):
            at = slice(chunk * rows, (chunk + 1) * rows)
            planes = slice(chunk * xs, (chunk + 1) * xs)
            dep = jnp.concatenate([depth[2 * part, at, :], depth[2 * part + 1, at, :]], axis=1)
            mean_sq = jnp.dot((dep * dep).astype(BF16), mean_mat, preferred_element_type=F32)
            inv = lax.rsqrt(mean_sq + EPS)
            normed = dep * inv
            norm_bf = (normed * gain).astype(BF16)
            normed_bf[at, cols] = norm_bf
            grad_norm = lax.dot_general(
                cot_ref[planes, :, cols].reshape(rows, WIDE), mix_mat,
                (((1,), (1,)), ((), ())), preferred_element_type=F32,
            )
            gain_sum = gain_sum + jnp.sum((grad_norm * normed).reshape(rows // 8, 8, WIDE), axis=0)
            scaled = grad_norm * gain
            mean = jnp.dot((scaled * normed).astype(BF16), mean_mat, preferred_element_type=F32)
            grad = (inv * (scaled - normed * mean)).astype(BF16)
            grad_ref[planes, :, cols] = grad.reshape(xs, side, WIDE)
            wide_grad = grad.astype(F32)
            grads[2 * part, at, :] = wide_grad[:, :LANE]
            grads[2 * part + 1, at, :] = wide_grad[:, LANE:]
        mix_sum = mix_sum + lax.dot_general(
            normed_bf[:, cols],
            cot_ref[:, :, cols].reshape(cells, WIDE),
            (((0,), (0,)), ((), ())),
            preferred_element_type=F32,
        )
    gain_sum_ref[...] = gain_sum
    channels = grad_mix_ref.shape[1] // 2
    grad_mix = mix_sum[:channels, :channels]
    for i in range(1, WIDE // channels):
        span = slice(i * channels, (i + 1) * channels)
        grad_mix = grad_mix + mix_sum[span, span]
    grad_mix_ref[...] = jnp.concatenate([grad_mix[:32], grad_mix[32:]], axis=1)
    odd = lax.axis_index("gx") % 2
    gxa_ref[...] = grad_ref[jnp.where(odd == 1, 0, side - 1)]
    gxb_ref[...] = grad_ref[jnp.where(odd == 1, side - 1, 0)]


def mixed_kernel(own_ref, normed_bf, mix_mat_ref, mixed_ref):
    side, _, lanes = own_ref.shape
    mix_mat = mix_mat_ref[...]
    rows = 128
    xs = rows // side
    for part in range(lanes // WIDE):
        cols = slice(part * WIDE, (part + 1) * WIDE)
        for chunk in range(side // xs):
            planes = slice(chunk * xs, (chunk + 1) * xs)
            norm_bf = normed_bf[chunk * rows:(chunk + 1) * rows, cols]
            branch = jnp.dot(norm_bf, mix_mat, preferred_element_type=F32)
            feat = own_ref[planes, :, cols].reshape(rows, WIDE).astype(F32)
            mixed_ref[planes, :, cols] = (feat + branch).astype(BF16).reshape(xs, side, WIDE)


def sums_kernel(field, grads, gain_sum_ref, grad_mix_ref, packed_ref):
    tiles, cells, _ = grads.shape
    side = math.isqrt(cells)
    channels = packed_ref.shape[1] // 2
    pitch = side + 8
    def tap_tile(k, sums):
        sums = list(sums)
        for half in range(side // 8):
            near_grads = {}
            for plane in range(side + 2):
                if plane < side:
                    row = plane * side + 8 * half
                    near_grads[plane] = grads[k, row:row + 8, :]
                near = shifted(field, tiles, k, plane, half, pitch)
                for (off_y, off_z), value in near.items():
                    for off_x in range(3):
                        x = plane - off_x
                        if 0 <= x < side:
                            tap = 9 * off_x + 3 * off_y + off_z
                            sums[tap] = sums[tap] + value * near_grads[x]
                near_grads.pop(plane - 2, None)
        return tuple(sums)

    sums = lax.fori_loop(0, tiles, tap_tile, tuple(jnp.zeros((8, LANE), F32) for _ in range(27)))
    packed_ref[0:32, :] = grad_mix_ref[...]
    gain_row = jnp.sum(gain_sum_ref[...], axis=0, keepdims=True)
    rows = [jnp.sum(t, axis=0, keepdims=True) for t in sums] + [gain_row[:, :LANE] + gain_row[:, LANE:]]
    rows = jnp.concatenate(rows + [jnp.zeros((4, LANE), F32)], axis=0)
    rows = rows[:, :channels] + rows[:, channels:]
    packed_ref[32:48, :] = jnp.concatenate([rows[:16], rows[16:]], axis=1)


def backward_kernel(
    field, sums, weights, ylo_ref, yhi_ref, masks_ref, cot_ref,
    field_out_ref, sums_out_ref, out_ref,
):
    side = cot_ref.shape[0]
    y_part(ylo_ref, yhi_ref, masks_ref, field, weights, sums, True)
    for x in range(side):
        for k in range(sums.shape[0]):
            cols = slice(k * LANE, (k + 1) * LANE)
            cot = cot_ref[x, :, cols].astype(F32)
            out_ref[x, :, cols] = (cot + sums[k, x * side:(x + 1) * side, :]).astype(BF16)


def unpack_kernel(mine_ref, theirs_ref, taps_hbm, gain_hbm, mix_hbm, taps_ref, gain_ref, mix_ref, done):
    total = mine_ref[...] + theirs_ref[...]
    channels = mix_ref.shape[0]
    mix_ref[0:32, :] = total[:32, :channels]
    mix_ref[32:64, :] = total[:32, channels:]
    taps_ref[0:16, :] = total[32:48, :channels]
    taps_ref[16:27, :] = total[32:43, channels:]
    gain_ref[...] = total[43:44, channels:]
    copies = [
        pltpu.make_async_copy(src, dst, done.at[i])
        for i, (src, dst) in enumerate(((taps_ref, taps_hbm), (gain_ref, gain_hbm), (mix_ref, mix_hbm)))
    ]
    for copy in copies:
        copy.start()
    for copy in copies:
        copy.wait()


def swap(to_first, to_second, axis):
    sizes = {name: lax.axis_size(name) for name in ("gx", "gy")}
    count = sizes[axis]

    def second(place):
        other = "gy" if axis == "gx" else "gx"
        if 0 < place[axis] < count - 1:
            return {**place, axis: ((place[axis] + 1) ^ 1) - 1}
        return {**place, other: place[other] ^ 1}

    def index(place):
        return place["gx"] * sizes["gy"] + place["gy"]

    places = [{"gx": i, "gy": j} for i in range(sizes["gx"]) for j in range(sizes["gy"])]
    from_second = lax.ppermute(to_second, ("gx", "gy"), [(index(p), index(second(p))) for p in places])
    return lax.ppermute(to_first, axis, [(i, i ^ 1) for i in range(count)]), from_second


def low_high(from_first, from_second, axis, even_form=False):
    place = lax.axis_index(axis) % 2
    if even_form:
        return jnp.where(place == 0, from_second, from_first), jnp.where(place == 0, from_first, from_second)
    return jnp.where(place == 1, from_first, from_second), jnp.where(place == 1, from_second, from_first)


def y_messages(xlo, xhi, ylo, yhi):
    low = jnp.concatenate([xlo[:1], ylo, xhi[:1]], axis=0)
    high = jnp.concatenate([xlo[-1:], yhi, xhi[-1:]], axis=0)
    return low_high(low, high, "gy")


def sum_steps():
    steps = []
    for axis in ("gx", "gy"):
        count = lax.axis_size(axis)
        bit = 1
        while bit < count:
            steps.append((axis, [(i, i ^ bit) for i in range(count)]))
            bit *= 2
    return steps


def shards(features, slot_map, tap_weights, gain, mix_weight, cotangent):
    side, _, _, lanes = features.shape
    channels = gain.shape[0]
    tiles = lanes // LANE
    cells = features.reshape(side, side, lanes)
    cot = cotangent.reshape(side, side, lanes)
    vmem = pl.BlockSpec(memory_space=pltpu.VMEM)
    hbm = pl.BlockSpec(memory_space=pltpu.HBM)
    block = jax.ShapeDtypeStruct((side, side, lanes), BF16)
    edge = jax.ShapeDtypeStruct((side, lanes), BF16)
    field_type = jax.ShapeDtypeStruct((2 * tiles + 1, (side + 2) * (side + 8) + 8, LANE), F32)
    sums_type = jax.ShapeDtypeStruct((tiles, side * side, LANE), F32)
    weights_type = jax.ShapeDtypeStruct((27, 8, LANE), F32)
    mat_type = jax.ShapeDtypeStruct((WIDE, WIDE), BF16)

    def call(kernel, name, operands, outs, scratch=(), aliases={}, flops=0, in_specs=None, out_specs=None):
        return pl.pallas_call(
            kernel,
            out_shape=tuple(jax.ShapeDtypeStruct(t.shape, t.dtype) for t in outs),
            in_specs=in_specs or [vmem] * len(operands),
            out_specs=out_specs or (vmem,) * len(outs),
            scratch_shapes=list(scratch),
            input_output_aliases=aliases,
            compiler_params=pltpu.CompilerParams(vmem_limit_bytes=40 * 1024 * 1024),
            cost_estimate=pl.CostEstimate(flops=flops, bytes_accessed=500_000, transcendentals=0),
            name=name,
        )(*operands)

    ylo, yhi = call(y_edges_kernel, "y_edges", (cells,), (edge, edge), flops=100_000_000_000)
    masks, weights, mean_mat, mix_mat, gain_wide = call(
        params_kernel,
        "params",
        (jnp.transpose(slot_map, (1, 2, 0)), mix_weight, tap_weights, gain.reshape(1, channels)),
        (
            jax.ShapeDtypeStruct((12, side + 8, LANE), F32),
            weights_type,
            mat_type,
            mat_type,
            jax.ShapeDtypeStruct((1, WIDE), F32),
        ),
    )
    xlo, xhi = low_high(*swap(*x_edges(cells), "gx"), "gx")
    to_a, to_b = y_messages(xlo, xhi, ylo, yhi)
    to_a, to_b, weights = lax.optimization_barrier((to_a, to_b, weights))
    ylo, yhi = low_high(*swap(to_a, to_b, "gy"), "gy")
    own_field, own_sums = call(
        functools.partial(own_kernel, False), "own_forward", (cells, xlo, xhi, masks, weights), (field_type, sums_type),
        flops=10_000_000,
    )
    field, _, grad_depth, gxa, gxb, normed_bf, grads, gain_sum, grad_mix = call(
        forward_kernel,
        "forward",
        (own_field, own_sums, weights, mean_mat, mix_mat, gain_wide, ylo, yhi, masks, cot),
        (
            field_type, sums_type, block, edge, edge,
            jax.ShapeDtypeStruct((side * side, lanes), BF16), sums_type, jax.ShapeDtypeStruct((8, WIDE), F32),
            jax.ShapeDtypeStruct((32, LANE), F32),
        ),
        aliases={0: 0, 1: 1},
        flops=10_000_000,
    )
    gxlo, gxhi = low_high(*swap(gxa, gxb, "gx"), "gx", even_form=True)
    (part,) = call(
        sums_kernel,
        "sums",
        (field, grads, gain_sum, grad_mix),
        (jax.ShapeDtypeStruct((48, LANE), F32),),
        flops=10_000_000,
    )

    steps = sum_steps()
    part, y_cells = lax.optimization_barrier((part, grad_depth))
    part = part + lax.ppermute(part, *steps[0])
    gylo, gyhi = call(y_edges_kernel, "grad_y_edges", (y_cells,), (edge, edge), flops=1_000_000)
    part, to_a, to_b = lax.optimization_barrier((part, *y_messages(gxlo, gxhi, gylo, gyhi)))
    part = part + lax.ppermute(part, *steps[1])
    gylo, gyhi = low_high(*swap(to_a, to_b, "gy"), "gy")
    part, grad_depth = lax.optimization_barrier((part, grad_depth))
    theirs = lax.ppermute(part, *steps[2])
    own_field, own_sums = call(
        functools.partial(own_kernel, True), "own_backward", (grad_depth, gxlo, gxhi, masks, weights),
        (field_type, sums_type),
        flops=10_000_000,
    )
    part, own_field, own_sums = lax.optimization_barrier((part + theirs, own_field, own_sums))
    _, _, grad_features = call(
        backward_kernel,
        "backward",
        (own_field, own_sums, weights, gylo, gyhi, masks, cot),
        (field_type, sums_type, block),
        aliases={0: 0, 1: 1},
        flops=2_000_000,
    )
    for index, step in enumerate(steps[3:-1]):
        part = part + lax.ppermute(part, *step)
        if index == 0:
            part, grad_features = lax.optimization_barrier((part, grad_features))
    part, normed_bf = lax.optimization_barrier((part, normed_bf))
    theirs = lax.ppermute(part, *steps[-1])
    (mixed,) = call(mixed_kernel, "mixed", (cells, normed_bf, mix_mat), (block,), flops=10_000_000)

    outs = (
        jax.ShapeDtypeStruct((27, channels), F32),
        jax.ShapeDtypeStruct((1, channels), F32),
        jax.ShapeDtypeStruct((channels, channels), F32),
    )
    grad_taps, grad_gain, grad_mix = call(
        unpack_kernel,
        "unpack",
        (part, theirs),
        outs,
        scratch=[pltpu.VMEM(t.shape, F32) for t in outs] + [pltpu.SemaphoreType.DMA((3,))],
        out_specs=(hbm,) * 3,
    )
    shape = features.shape
    return (mixed.reshape(shape), grad_features.reshape(shape), grad_taps, grad_gain.reshape(channels), grad_mix)


def solution(mesh):
    return jax.shard_map(
        shards,
        mesh=mesh,
        in_specs=(P("gx", "gy", None, None), P(), P(), P(), P(), P("gx", "gy", None, None)),
        out_specs=(P("gx", "gy", None, None), P("gx", "gy", None, None), P(), P(), P()),
        check_vma=False,
    )
```

```python
import functools
import math

import jax
import jax.numpy as jnp
from jax import lax
from jax.experimental import pallas as pl
from jax.experimental.pallas import tpu as pltpu
from jax.sharding import PartitionSpec as P

EPS = 1e-05
LANE = 128
WIDE = 256
PLANES = 4
F32 = jnp.float32
BF16 = jnp.bfloat16


def level_masks(slots, side, masks_ref):
    level = lax.broadcasted_iota(jnp.int32, slots.shape, 1)
    at_x = lax.broadcasted_iota(jnp.int32, slots.shape, 2) - lax.axis_index("gx")
    at_y = lax.broadcasted_iota(jnp.int32, slots.shape, 0) - lax.axis_index("gy")
    place = jnp.where(slots >= 0, level + 1, 0).astype(F32)

    def near(off_x, off_y):
        found = jnp.where((at_x == off_x) & (at_y == off_y), place, 0.0)
        found = jnp.sum(jnp.sum(found, axis=0), axis=0, keepdims=True)
        return jnp.sum(found, axis=1, keepdims=True)

    own = near(0, 0)

    def difference(off_x, off_y):
        found = near(off_x, off_y)
        return jnp.where(found > 0.0, found - own, 9.0)

    rows = masks_ref.shape[1]
    row = lax.broadcasted_iota(jnp.int32, (rows, LANE), 0)
    for edge in range(4):
        high = 1 if edge % 2 else -1
        if edge < 2:
            d = jnp.broadcast_to(difference(high, 0), (rows, LANE))
        else:
            corner, middle, other = (difference(off, high) for off in (-1, 0, 1))
            d = jnp.where(row == 0, corner, jnp.where(row == side + 1, other, middle))
        for i, want in enumerate((0.0, -1.0, 1.0)):
            masks_ref[3 * edge + i] = jnp.where(d == want, 1.0, 0.0)


def plane_tiles(load, total, masks):
    low = lax.broadcasted_iota(jnp.int32, load(0).shape, 1) < LANE // 2
    zero = jnp.zeros(load(0).shape, F32)
    aligned = [load(k) for k in range(total)]
    turned = [pltpu.roll(t, LANE // 2, 1) for t in aligned]
    between = [jnp.where(low, turned[j - 1], turned[j]) for j in range(1, total)]
    if masks is None:
        return aligned + [jnp.where(low, zero, turned[0])] + between + [jnp.where(low, turned[-1], zero)]
    same, below, above = masks
    first = jnp.where(low, turned[-1] * below, turned[0] * same)
    last = jnp.where(low, turned[-1] * same, turned[0] * above)
    return [t * same for t in aligned] + [first] + [t * same for t in between] + [last]


def loader(rows):
    return lambda k: rows[:, k * LANE:(k + 1) * LANE].astype(F32)


def column_starts(side, shift):
    pitch = side + 8
    for start in range(0, side + 2, 8):
        size = min(8, side + 2 - start)
        yield start, size, pl.ds(start * pitch + shift, size, stride=pitch)


def own_part(own_ref, field, weights, sums, flip):
    side = own_ref.shape[0]
    tiles = own_ref.shape[2] // LANE
    pitch = side + 8

    def own_planes(step, _):
        for x in range(PLANES):
            x = step * PLANES + x
            base = pl.multiple_of((x + 1) * pitch + 8, 8)
            for i, t in enumerate(plane_tiles(loader(own_ref[x]), tiles, None)):
                field[i, pl.ds(base, side), :] = t
        return 0

    lax.fori_loop(0, side // PLANES, own_planes, 0)
    for i in range(2 * tiles + 1):
        for shift in (7, pitch):
            for _, size, at in column_starts(side, shift):
                field[i, at, :] = jnp.zeros((size, LANE), F32)

    def tile(k, _):
        taps = [weights[26 - t if flip else t] for t in range(27)]
        for half in range(side // 8):
            part = {}
            for plane in range(1, side + 1):
                near = shifted(field, tiles, k, plane, half, pitch)
                for off_x in range(3):
                    x = plane - off_x
                    if not 0 <= x < side:
                        continue
                    for (off_y, off_z), value in near.items():
                        term = value * taps[9 * off_x + 3 * off_y + off_z]
                        part[x] = part[x] + term if x in part else term
                done = plane - 2
                for x in [done, done + 1] if plane == side else [done]:
                    if x >= 0:
                        sums[k, x * side + 8 * half:x * side + 8 * half + 8, :] = part.pop(x)
        return 0

    lax.fori_loop(0, tiles, tile, 0)


def halo_part(xlo_ref, xhi_ref, ylo_ref, yhi_ref, masks_ref, field, weights, sums, flip):
    side, lanes = xlo_ref.shape
    tiles = lanes // LANE
    pitch = side + 8

    def place(i, ref):
        rows = ref.shape[0]
        masks = tuple(masks_ref[3 * i + m, :rows, :] for m in range(3))
        return plane_tiles(loader(ref[...]), tiles, masks)

    for i, ref, plane in ((0, xlo_ref, 0), (1, xhi_ref, side + 1)):
        for j, t in enumerate(place(i, ref)):
            field[j, plane * pitch + 8:plane * pitch + 8 + side, :] = t

    totals = []

    def x_tile(k):
        for plane, off_x, x in ((0, 0, 0), (side + 1, 2, side - 1)):
            for half in range(side // 8):
                row = x * side + 8 * half
                total = sums[k, row:row + 8, :]
                for (off_y, off_z), value in shifted(field, tiles, k, plane, half, pitch).items():
                    tap = 9 * off_x + 3 * off_y + off_z
                    total = total + value * weights[26 - tap if flip else tap]
                totals.append((k, slice(row, row + 8), total))

    for k in range(tiles):
        x_tile(k)
    for k, at, total in totals:
        sums[k, at, :] = total

    for i, ref, shift in ((2, ylo_ref, 7), (3, yhi_ref, pitch)):
        for j, t in enumerate(place(i, ref)):
            for start, size, at in column_starts(side, shift):
                field[j, at, :] = t[start:start + size]

    totals = []

    def y_tile(k):
        for shift, off_y, y in ((7, 0, 0), (pitch, 2, side - 1)):
            for x in range(0, side, 8):
                at = pl.ds(x * side + y, 8, stride=side)
                total = sums[k, at, :]
                for off_x in range(3):
                    for off_z in range(3):
                        i = (tiles + k, k, tiles + k + 1)[off_z]
                        tap = 9 * off_x + 3 * off_y + off_z
                        value = field[i, pl.ds((x + off_x) * pitch + shift, 8, stride=pitch), :]
                        total = total + value * weights[26 - tap if flip else tap]
                totals.append((k, at, total))

    for k in range(tiles):
        y_tile(k)
    for k, at, total in totals:
        sums[k, at, :] = total


def shifted(field, tiles, k, plane, half, pitch):
    found = {}
    for off_y in range(3):
        row = plane * pitch + 7 + 8 * half + off_y
        for off_z in range(3):
            i = (tiles + k, k, tiles + k + 1)[off_z]
            found[off_y, off_z] = field[i, row:row + 8, :]
    return found


def x_edges(cells):
    odd = lax.axis_index("gx") % 2 == 1
    return jnp.where(odd, cells[0], cells[-1]), jnp.where(odd, cells[-1], cells[0])


def y_edges_kernel(cells_ref, ylo_ref, yhi_ref):
    side, _, lanes = cells_ref.shape
    row = lax.broadcasted_iota(jnp.int32, (2 * side, side * side), 0)
    col = lax.broadcasted_iota(jnp.int32, (2 * side, side * side), 1)
    wanted = jnp.where(row < side, row * side, (row - side) * side + side - 1)
    pick = jnp.where(col == wanted, 1.0, 0.0).astype(BF16)
    flat = cells_ref[...].reshape(side * side, lanes)
    found = jnp.dot(pick, flat, preferred_element_type=F32).astype(BF16)
    ylo_ref[...] = found[:side]
    yhi_ref[...] = found[side:]


def params_kernel(
    slots_ref, mix_ref, taps_ref, gain_ref, masks_ref, weights, mean_mat_ref, mix_mat_ref, gain_wide_ref
):
    channels = mix_ref.shape[0]
    level_masks(slots_ref[...], masks_ref.shape[1] - 8, masks_ref)
    wide = jnp.concatenate([taps_ref[...], taps_ref[...]], axis=1)
    for tap in range(27):
        weights[tap] = jnp.broadcast_to(wide[tap:tap + 1], (8, LANE))
    copies = WIDE // channels
    row_id = lax.broadcasted_iota(jnp.int32, (WIDE, WIDE), 0) // channels
    col_id = lax.broadcasted_iota(jnp.int32, (WIDE, WIDE), 1) // channels
    block = row_id == col_id
    mean_mat_ref[...] = jnp.where(block, 1.0 / channels, 0.0).astype(BF16)
    mix = mix_ref[...].astype(F32)
    mix_row = jnp.concatenate([mix] * copies, axis=1)
    mix_mat_ref[...] = jnp.where(block, jnp.concatenate([mix_row] * copies, axis=0), 0.0).astype(BF16)
    gain_wide_ref[...] = jnp.concatenate([gain_ref[...]] * copies, axis=1)


def own_kernel(flip, own_ref, weights, field, sums):
    own_part(own_ref, field, weights, sums, flip)


def forward_kernel(
    field, depth, weights, mean_mat_ref, mix_mat_ref, gain_wide_ref,
    xlo_ref, xhi_ref, ylo_ref, yhi_ref, masks_ref, cot_ref,
    field_out_ref, depth_out_ref, grad_ref, gxa_ref, gxb_ref, normed_bf, grads, gain_sum_ref, grad_mix_ref,
):
    side, _, lanes = cot_ref.shape
    cells = side * side
    halo_part(xlo_ref, xhi_ref, ylo_ref, yhi_ref, masks_ref, field, weights, depth, False)

    mean_mat = mean_mat_ref[...]
    mix_mat = mix_mat_ref[...]
    gain = gain_wide_ref[...]
    gain_sum = jnp.zeros((8, WIDE), F32)
    mix_sum = jnp.zeros((WIDE, WIDE), F32)
    for part in range(lanes // WIDE):
        cols = slice(part * WIDE, (part + 1) * WIDE)
        dep = jnp.concatenate([depth[2 * part], depth[2 * part + 1]], axis=1)
        cot = cot_ref[:, :, cols].reshape(cells, WIDE)
        mean_sq = jnp.dot((dep * dep).astype(BF16), mean_mat, preferred_element_type=F32)
        grad_norm = lax.dot_general(cot, mix_mat, (((1,), (1,)), ((), ())), preferred_element_type=F32)
        inv = lax.rsqrt(mean_sq + EPS)
        normed = dep * inv
        norm_bf = (normed * gain).astype(BF16)
        scaled = grad_norm * gain
        mean = jnp.dot((scaled * normed).astype(BF16), mean_mat, preferred_element_type=F32)
        mix_sum = mix_sum + lax.dot_general(
            norm_bf, cot, (((0,), (0,)), ((), ())), preferred_element_type=F32
        )
        gain_sum = gain_sum + jnp.sum((grad_norm * normed).reshape(cells // 8, 8, WIDE), axis=0)
        grad = (inv * (scaled - normed * mean)).astype(BF16)
        wide_grad = grad.astype(F32)
        normed_bf[:, cols] = norm_bf
        grad_ref[:, :, cols] = grad.reshape(side, side, WIDE)
        grads[2 * part] = wide_grad[:, :LANE]
        grads[2 * part + 1] = wide_grad[:, LANE:]
    gain_sum_ref[...] = gain_sum
    channels = grad_mix_ref.shape[1] // 2
    grad_mix = mix_sum[:channels, :channels]
    for i in range(1, WIDE // channels):
        span = slice(i * channels, (i + 1) * channels)
        grad_mix = grad_mix + mix_sum[span, span]
    grad_mix_ref[...] = jnp.concatenate([grad_mix[:32], grad_mix[32:]], axis=1)
    odd = lax.axis_index("gx") % 2
    gxa_ref[...] = grad_ref[jnp.where(odd == 1, 0, side - 1)]
    gxb_ref[...] = grad_ref[jnp.where(odd == 1, side - 1, 0)]


def mixed_kernel(own_ref, normed_bf, mix_mat_ref, mixed_ref):
    side, _, lanes = own_ref.shape
    mix_mat = mix_mat_ref[...]
    rows = 128
    xs = rows // side
    for part in range(lanes // WIDE):
        cols = slice(part * WIDE, (part + 1) * WIDE)
        for chunk in range(side // xs):
            planes = slice(chunk * xs, (chunk + 1) * xs)
            norm_bf = normed_bf[chunk * rows:(chunk + 1) * rows, cols]
            branch = jnp.dot(norm_bf, mix_mat, preferred_element_type=F32)
            feat = own_ref[planes, :, cols].reshape(rows, WIDE).astype(F32)
            mixed_ref[planes, :, cols] = (feat + branch).astype(BF16).reshape(xs, side, WIDE)


def sums_kernel(field, grads, gain_sum_ref, grad_mix_ref, packed_ref):
    tiles, cells, _ = grads.shape
    side = math.isqrt(cells)
    channels = packed_ref.shape[1] // 2
    pitch = side + 8
    def tap_tile(k, sums):
        sums = list(sums)
        for half in range(side // 8):
            near_grads = {}
            for plane in range(side + 2):
                if plane < side:
                    row = plane * side + 8 * half
                    near_grads[plane] = grads[k, row:row + 8, :]
                near = shifted(field, tiles, k, plane, half, pitch)
                for (off_y, off_z), value in near.items():
                    for off_x in range(3):
                        x = plane - off_x
                        if 0 <= x < side:
                            tap = 9 * off_x + 3 * off_y + off_z
                            sums[tap] = sums[tap] + value * near_grads[x]
                near_grads.pop(plane - 2, None)
        return tuple(sums)

    sums = lax.fori_loop(0, tiles, tap_tile, tuple(jnp.zeros((8, LANE), F32) for _ in range(27)))
    packed_ref[0:32, :] = grad_mix_ref[...]
    gain_row = jnp.sum(gain_sum_ref[...], axis=0, keepdims=True)
    rows = [jnp.sum(t, axis=0, keepdims=True) for t in sums] + [gain_row[:, :LANE] + gain_row[:, LANE:]]
    rows = jnp.concatenate(rows + [jnp.zeros((4, LANE), F32)], axis=0)
    rows = rows[:, :channels] + rows[:, channels:]
    packed_ref[32:48, :] = jnp.concatenate([rows[:16], rows[16:]], axis=1)


def backward_kernel(
    field, sums, weights, xlo_ref, xhi_ref, ylo_ref, yhi_ref, masks_ref, cot_ref,
    field_out_ref, sums_out_ref, out_ref,
):
    side = cot_ref.shape[0]
    halo_part(xlo_ref, xhi_ref, ylo_ref, yhi_ref, masks_ref, field, weights, sums, True)
    for x in range(side):
        for k in range(sums.shape[0]):
            cols = slice(k * LANE, (k + 1) * LANE)
            cot = cot_ref[x, :, cols].astype(F32)
            out_ref[x, :, cols] = (cot + sums[k, x * side:(x + 1) * side, :]).astype(BF16)


def unpack_kernel(mine_ref, theirs_ref, taps_hbm, gain_hbm, mix_hbm, taps_ref, gain_ref, mix_ref, done):
    total = mine_ref[...] + theirs_ref[...]
    channels = mix_ref.shape[0]
    mix_ref[0:32, :] = total[:32, :channels]
    mix_ref[32:64, :] = total[:32, channels:]
    taps_ref[0:16, :] = total[32:48, :channels]
    taps_ref[16:27, :] = total[32:43, channels:]
    gain_ref[...] = total[43:44, channels:]
    copies = [
        pltpu.make_async_copy(src, dst, done.at[i])
        for i, (src, dst) in enumerate(((taps_ref, taps_hbm), (gain_ref, gain_hbm), (mix_ref, mix_hbm)))
    ]
    for copy in copies:
        copy.start()
    for copy in copies:
        copy.wait()


def swap(to_first, to_second, axis):
    sizes = {name: lax.axis_size(name) for name in ("gx", "gy")}
    count = sizes[axis]

    def second(place):
        other = "gy" if axis == "gx" else "gx"
        if 0 < place[axis] < count - 1:
            return {**place, axis: ((place[axis] + 1) ^ 1) - 1}
        return {**place, other: place[other] ^ 1}

    def index(place):
        return place["gx"] * sizes["gy"] + place["gy"]

    places = [{"gx": i, "gy": j} for i in range(sizes["gx"]) for j in range(sizes["gy"])]
    from_second = lax.ppermute(to_second, ("gx", "gy"), [(index(p), index(second(p))) for p in places])
    return lax.ppermute(to_first, axis, [(i, i ^ 1) for i in range(count)]), from_second


def low_high(from_first, from_second, axis):
    even = lax.axis_index(axis) % 2 == 0
    return jnp.where(even, from_second, from_first), jnp.where(even, from_first, from_second)


def y_messages(xlo, xhi, ylo, yhi):
    low = jnp.concatenate([xlo[:1], ylo, xhi[:1]], axis=0)
    high = jnp.concatenate([xlo[-1:], yhi, xhi[-1:]], axis=0)
    return low_high(low, high, "gy")


def sum_steps():
    steps = []
    for axis in ("gx", "gy"):
        count = lax.axis_size(axis)
        bit = 1
        while bit < count:
            steps.append((axis, [(i, i ^ bit) for i in range(count)]))
            bit *= 2
    return steps


def shards(features, slot_map, tap_weights, gain, mix_weight, cotangent):
    side, _, _, lanes = features.shape
    channels = gain.shape[0]
    tiles = lanes // LANE
    cells = features.reshape(side, side, lanes)
    cot = cotangent.reshape(side, side, lanes)
    vmem = pl.BlockSpec(memory_space=pltpu.VMEM)
    hbm = pl.BlockSpec(memory_space=pltpu.HBM)
    block = jax.ShapeDtypeStruct((side, side, lanes), BF16)
    edge = jax.ShapeDtypeStruct((side, lanes), BF16)
    field_type = jax.ShapeDtypeStruct((2 * tiles + 1, (side + 2) * (side + 8) + 8, LANE), F32)
    sums_type = jax.ShapeDtypeStruct((tiles, side * side, LANE), F32)
    weights_type = jax.ShapeDtypeStruct((27, 8, LANE), F32)
    mat_type = jax.ShapeDtypeStruct((WIDE, WIDE), BF16)

    def call(kernel, name, operands, outs, scratch=(), aliases={}, flops=0, in_specs=None, out_specs=None):
        return pl.pallas_call(
            kernel,
            out_shape=tuple(jax.ShapeDtypeStruct(t.shape, t.dtype) for t in outs),
            in_specs=in_specs or [vmem] * len(operands),
            out_specs=out_specs or (vmem,) * len(outs),
            scratch_shapes=list(scratch),
            input_output_aliases=aliases,
            compiler_params=pltpu.CompilerParams(vmem_limit_bytes=40 * 1024 * 1024),
            cost_estimate=pl.CostEstimate(flops=flops, bytes_accessed=500_000, transcendentals=0),
            name=name,
        )(*operands)

    ylo, yhi = call(y_edges_kernel, "y_edges", (cells,), (edge, edge), flops=100_000_000_000)
    masks, weights, mean_mat, mix_mat, gain_wide = call(
        params_kernel,
        "params",
        (jnp.transpose(slot_map, (1, 2, 0)), mix_weight, tap_weights, gain.reshape(1, channels)),
        (
            jax.ShapeDtypeStruct((12, side + 8, LANE), F32),
            weights_type,
            mat_type,
            mat_type,
            jax.ShapeDtypeStruct((1, WIDE), F32),
        ),
    )
    xlo, xhi = low_high(*swap(*x_edges(cells), "gx"), "gx")
    to_a, to_b = y_messages(xlo, xhi, ylo, yhi)
    to_a, to_b, weights = lax.optimization_barrier((to_a, to_b, weights))
    ylo, yhi = low_high(*swap(to_a, to_b, "gy"), "gy")
    own_field, own_sums = call(
        functools.partial(own_kernel, False), "own_forward", (cells, weights), (field_type, sums_type),
        flops=10_000_000,
    )
    field, _, grad_depth, gxa, gxb, normed_bf, grads, gain_sum, grad_mix = call(
        forward_kernel,
        "forward",
        (own_field, own_sums, weights, mean_mat, mix_mat, gain_wide, xlo, xhi, ylo, yhi, masks, cot),
        (
            field_type, sums_type, block, edge, edge,
            jax.ShapeDtypeStruct((side * side, lanes), BF16), sums_type, jax.ShapeDtypeStruct((8, WIDE), F32),
            jax.ShapeDtypeStruct((32, LANE), F32),
        ),
        aliases={0: 0, 1: 1},
        flops=10_000_000,
    )
    gxlo, gxhi = low_high(*swap(gxa, gxb, "gx"), "gx")
    (part,) = call(
        sums_kernel,
        "sums",
        (field, grads, gain_sum, grad_mix),
        (jax.ShapeDtypeStruct((48, LANE), F32),),
        flops=10_000_000,
    )

    steps = sum_steps()
    part, y_cells = lax.optimization_barrier((part, grad_depth))
    part = part + lax.ppermute(part, *steps[0])
    gylo, gyhi = call(y_edges_kernel, "grad_y_edges", (y_cells,), (edge, edge), flops=1_000_000)
    part, to_a, to_b = lax.optimization_barrier((part, *y_messages(gxlo, gxhi, gylo, gyhi)))
    part = part + lax.ppermute(part, *steps[1])
    gylo, gyhi = low_high(*swap(to_a, to_b, "gy"), "gy")
    part, grad_depth = lax.optimization_barrier((part, grad_depth))
    theirs = lax.ppermute(part, *steps[2])
    own_field, own_sums = call(
        functools.partial(own_kernel, True), "own_backward", (grad_depth, weights), (field_type, sums_type),
        flops=10_000_000,
    )
    part, own_field, own_sums = lax.optimization_barrier((part + theirs, own_field, own_sums))
    _, _, grad_features = call(
        backward_kernel,
        "backward",
        (own_field, own_sums, weights, gxlo, gxhi, gylo, gyhi, masks, cot),
        (field_type, sums_type, block),
        aliases={0: 0, 1: 1},
        flops=2_000_000,
    )
    for index, step in enumerate(steps[3:-1]):
        part = part + lax.ppermute(part, *step)
        if index == 0:
            part, grad_features = lax.optimization_barrier((part, grad_features))
    part, normed_bf = lax.optimization_barrier((part, normed_bf))
    theirs = lax.ppermute(part, *steps[-1])
    (mixed,) = call(mixed_kernel, "mixed", (cells, normed_bf, mix_mat), (block,), flops=10_000_000)

    outs = (
        jax.ShapeDtypeStruct((27, channels), F32),
        jax.ShapeDtypeStruct((1, channels), F32),
        jax.ShapeDtypeStruct((channels, channels), F32),
    )
    grad_taps, grad_gain, grad_mix = call(
        unpack_kernel,
        "unpack",
        (part, theirs),
        outs,
        scratch=[pltpu.VMEM(t.shape, F32) for t in outs] + [pltpu.SemaphoreType.DMA((3,))],
        out_specs=(hbm,) * 3,
    )
    shape = features.shape
    return (mixed.reshape(shape), grad_features.reshape(shape), grad_taps, grad_gain.reshape(channels), grad_mix)


def solution(mesh):
    return jax.shard_map(
        shards,
        mesh=mesh,
        in_specs=(P("gx", "gy", None, None), P(), P(), P(), P(), P("gx", "gy", None, None)),
        out_specs=(P("gx", "gy", None, None), P("gx", "gy", None, None), P(), P(), P()),
        check_vma=False,
    )
```

```python
import functools
import math

import jax
import jax.numpy as jnp
from jax import lax
from jax.experimental import pallas as pl
from jax.experimental.pallas import tpu as pltpu
from jax.sharding import PartitionSpec as P

EPS = 1e-05
LANE = 128
WIDE = 256
PLANES = 4
F32 = jnp.float32
BF16 = jnp.bfloat16


def level_masks(slots, side, masks_ref):
    level = lax.broadcasted_iota(jnp.int32, slots.shape, 1)
    at_x = lax.broadcasted_iota(jnp.int32, slots.shape, 2) - lax.axis_index("gx")
    at_y = lax.broadcasted_iota(jnp.int32, slots.shape, 0) - lax.axis_index("gy")
    place = jnp.where(slots >= 0, level + 1, 0).astype(F32)

    def near(off_x, off_y):
        found = jnp.where((at_x == off_x) & (at_y == off_y), place, 0.0)
        found = jnp.sum(jnp.sum(found, axis=0), axis=0, keepdims=True)
        return jnp.sum(found, axis=1, keepdims=True)

    own = near(0, 0)

    def difference(off_x, off_y):
        found = near(off_x, off_y)
        return jnp.where(found > 0.0, found - own, 9.0)

    rows = masks_ref.shape[1]
    row = lax.broadcasted_iota(jnp.int32, (rows, LANE), 0)
    for edge in range(4):
        high = 1 if edge % 2 else -1
        if edge < 2:
            d = jnp.broadcast_to(difference(high, 0), (rows, LANE))
        else:
            corner, middle, other = (difference(off, high) for off in (-1, 0, 1))
            d = jnp.where(row == 0, corner, jnp.where(row == side + 1, other, middle))
        for i, want in enumerate((0.0, -1.0, 1.0)):
            masks_ref[3 * edge + i] = jnp.where(d == want, 1.0, 0.0)


def plane_tiles(load, total, masks):
    low = lax.broadcasted_iota(jnp.int32, load(0).shape, 1) < LANE // 2
    zero = jnp.zeros(load(0).shape, F32)
    aligned = [load(k) for k in range(total)]
    turned = [pltpu.roll(t, LANE // 2, 1) for t in aligned]
    between = [jnp.where(low, turned[j - 1], turned[j]) for j in range(1, total)]
    if masks is None:
        return aligned + [jnp.where(low, zero, turned[0])] + between + [jnp.where(low, turned[-1], zero)]
    same, below, above = masks
    first = jnp.where(low, turned[-1] * below, turned[0] * same)
    last = jnp.where(low, turned[-1] * same, turned[0] * above)
    return [t * same for t in aligned] + [first] + [t * same for t in between] + [last]


def loader(rows):
    return lambda k: rows[:, k * LANE:(k + 1) * LANE].astype(F32)


def column_starts(side, shift):
    pitch = side + 8
    for start in range(0, side + 2, 8):
        size = min(8, side + 2 - start)
        yield start, size, pl.ds(start * pitch + shift, size, stride=pitch)


def own_part(own_ref, field, weights, sums, flip):
    side = own_ref.shape[0]
    tiles = own_ref.shape[2] // LANE
    pitch = side + 8

    def own_planes(step, _):
        for x in range(PLANES):
            x = step * PLANES + x
            base = pl.multiple_of((x + 1) * pitch + 8, 8)
            for i, t in enumerate(plane_tiles(loader(own_ref[x]), tiles, None)):
                field[i, pl.ds(base, side), :] = t
        return 0

    lax.fori_loop(0, side // PLANES, own_planes, 0)
    for i in range(2 * tiles + 1):
        for shift in (7, pitch):
            for _, size, at in column_starts(side, shift):
                field[i, at, :] = jnp.zeros((size, LANE), F32)

    def tile(k, _):
        taps = [weights[26 - t if flip else t] for t in range(27)]
        for half in range(side // 8):
            part = {}
            for plane in range(1, side + 1):
                near = shifted(field, tiles, k, plane, half, pitch)
                for off_x in range(3):
                    x = plane - off_x
                    if not 0 <= x < side:
                        continue
                    for (off_y, off_z), value in near.items():
                        term = value * taps[9 * off_x + 3 * off_y + off_z]
                        part[x] = part[x] + term if x in part else term
                done = plane - 2
                for x in [done, done + 1] if plane == side else [done]:
                    if x >= 0:
                        sums[k, x * side + 8 * half:x * side + 8 * half + 8, :] = part.pop(x)
        return 0

    lax.fori_loop(0, tiles, tile, 0)


def halo_part(xlo_ref, xhi_ref, ylo_ref, yhi_ref, masks_ref, field, weights, sums, flip):
    side, lanes = xlo_ref.shape
    tiles = lanes // LANE
    pitch = side + 8

    def place(i, ref):
        rows = ref.shape[0]
        masks = tuple(masks_ref[3 * i + m, :rows, :] for m in range(3))
        return plane_tiles(loader(ref[...]), tiles, masks)

    for i, ref, plane in ((0, xlo_ref, 0), (1, xhi_ref, side + 1)):
        for j, t in enumerate(place(i, ref)):
            field[j, plane * pitch + 8:plane * pitch + 8 + side, :] = t

    totals = []

    def x_tile(k):
        for plane, off_x, x in ((0, 0, 0), (side + 1, 2, side - 1)):
            for half in range(side // 8):
                row = x * side + 8 * half
                total = sums[k, row:row + 8, :]
                for (off_y, off_z), value in shifted(field, tiles, k, plane, half, pitch).items():
                    tap = 9 * off_x + 3 * off_y + off_z
                    total = total + value * weights[26 - tap if flip else tap]
                totals.append((k, slice(row, row + 8), total))

    for k in range(tiles):
        x_tile(k)
    for k, at, total in totals:
        sums[k, at, :] = total

    for i, ref, shift in ((2, ylo_ref, 7), (3, yhi_ref, pitch)):
        for j, t in enumerate(place(i, ref)):
            for start, size, at in column_starts(side, shift):
                field[j, at, :] = t[start:start + size]

    totals = []

    def y_tile(k):
        for shift, off_y, y in ((7, 0, 0), (pitch, 2, side - 1)):
            for x in range(0, side, 8):
                at = pl.ds(x * side + y, 8, stride=side)
                total = sums[k, at, :]
                for off_x in range(3):
                    for off_z in range(3):
                        i = (tiles + k, k, tiles + k + 1)[off_z]
                        tap = 9 * off_x + 3 * off_y + off_z
                        value = field[i, pl.ds((x + off_x) * pitch + shift, 8, stride=pitch), :]
                        total = total + value * weights[26 - tap if flip else tap]
                totals.append((k, at, total))

    for k in range(tiles):
        y_tile(k)
    for k, at, total in totals:
        sums[k, at, :] = total


def shifted(field, tiles, k, plane, half, pitch):
    found = {}
    for off_y in range(3):
        row = plane * pitch + 7 + 8 * half + off_y
        for off_z in range(3):
            i = (tiles + k, k, tiles + k + 1)[off_z]
            found[off_y, off_z] = field[i, row:row + 8, :]
    return found


def x_edges(cells):
    odd = lax.axis_index("gx") % 2 == 1
    return jnp.where(odd, cells[0], cells[-1]), jnp.where(odd, cells[-1], cells[0])


def y_edges_kernel(cells_ref, ylo_ref, yhi_ref):
    side, _, lanes = cells_ref.shape
    row = lax.broadcasted_iota(jnp.int32, (2 * side, side * side), 0)
    col = lax.broadcasted_iota(jnp.int32, (2 * side, side * side), 1)
    wanted = jnp.where(row < side, row * side, (row - side) * side + side - 1)
    pick = jnp.where(col == wanted, 1.0, 0.0).astype(BF16)
    flat = cells_ref[...].reshape(side * side, lanes)
    found = jnp.dot(pick, flat, preferred_element_type=F32).astype(BF16)
    ylo_ref[...] = found[:side]
    yhi_ref[...] = found[side:]


def params_kernel(
    slots_ref, mix_ref, taps_ref, gain_ref, masks_ref, weights, mean_mat_ref, mix_mat_ref, gain_wide_ref
):
    channels = mix_ref.shape[0]
    level_masks(slots_ref[...], masks_ref.shape[1] - 8, masks_ref)
    wide = jnp.concatenate([taps_ref[...], taps_ref[...]], axis=1)
    for tap in range(27):
        weights[tap] = jnp.broadcast_to(wide[tap:tap + 1], (8, LANE))
    copies = WIDE // channels
    row_id = lax.broadcasted_iota(jnp.int32, (WIDE, WIDE), 0) // channels
    col_id = lax.broadcasted_iota(jnp.int32, (WIDE, WIDE), 1) // channels
    block = row_id == col_id
    mean_mat_ref[...] = jnp.where(block, 1.0 / channels, 0.0).astype(BF16)
    mix = mix_ref[...].astype(F32)
    mix_row = jnp.concatenate([mix] * copies, axis=1)
    mix_mat_ref[...] = jnp.where(block, jnp.concatenate([mix_row] * copies, axis=0), 0.0).astype(BF16)
    gain_wide_ref[...] = jnp.concatenate([gain_ref[...]] * copies, axis=1)


def own_kernel(flip, own_ref, weights, field, sums):
    own_part(own_ref, field, weights, sums, flip)


def forward_kernel(
    field, depth, weights, mean_mat_ref, mix_mat_ref, gain_wide_ref,
    xlo_ref, xhi_ref, ylo_ref, yhi_ref, masks_ref, cot_ref,
    field_out_ref, depth_out_ref, grad_ref, gxa_ref, gxb_ref, normed_bf, grads, gain_sum_ref, grad_mix_ref,
):
    side, _, lanes = cot_ref.shape
    cells = side * side
    halo_part(xlo_ref, xhi_ref, ylo_ref, yhi_ref, masks_ref, field, weights, depth, False)

    mean_mat = mean_mat_ref[...]
    mix_mat = mix_mat_ref[...]
    gain = gain_wide_ref[...]
    gain_sum = jnp.zeros((8, WIDE), F32)
    mix_sum = jnp.zeros((WIDE, WIDE), F32)
    for part in range(lanes // WIDE):
        cols = slice(part * WIDE, (part + 1) * WIDE)
        dep = jnp.concatenate([depth[2 * part], depth[2 * part + 1]], axis=1)
        cot = cot_ref[:, :, cols].reshape(cells, WIDE)
        mean_sq = jnp.dot((dep * dep).astype(BF16), mean_mat, preferred_element_type=F32)
        grad_norm = lax.dot_general(cot, mix_mat, (((1,), (1,)), ((), ())), preferred_element_type=F32)
        inv = lax.rsqrt(mean_sq + EPS)
        normed = dep * inv
        norm_bf = (normed * gain).astype(BF16)
        scaled = grad_norm * gain
        mean = jnp.dot((scaled * normed).astype(BF16), mean_mat, preferred_element_type=F32)
        mix_sum = mix_sum + lax.dot_general(
            norm_bf, cot, (((0,), (0,)), ((), ())), preferred_element_type=F32
        )
        gain_sum = gain_sum + jnp.sum((grad_norm * normed).reshape(cells // 8, 8, WIDE), axis=0)
        grad = (inv * (scaled - normed * mean)).astype(BF16)
        wide_grad = grad.astype(F32)
        normed_bf[:, cols] = norm_bf
        grad_ref[:, :, cols] = grad.reshape(side, side, WIDE)
        grads[2 * part] = wide_grad[:, :LANE]
        grads[2 * part + 1] = wide_grad[:, LANE:]
    gain_sum_ref[...] = gain_sum
    channels = grad_mix_ref.shape[1] // 2
    grad_mix = mix_sum[:channels, :channels]
    for i in range(1, WIDE // channels):
        span = slice(i * channels, (i + 1) * channels)
        grad_mix = grad_mix + mix_sum[span, span]
    grad_mix_ref[...] = jnp.concatenate([grad_mix[:32], grad_mix[32:]], axis=1)
    odd = lax.axis_index("gx") % 2
    gxa_ref[...] = grad_ref[jnp.where(odd == 1, 0, side - 1)]
    gxb_ref[...] = grad_ref[jnp.where(odd == 1, side - 1, 0)]


def mixed_kernel(own_ref, normed_bf, mix_mat_ref, mixed_ref):
    side, _, lanes = own_ref.shape
    mix_mat = mix_mat_ref[...]
    rows = 128
    xs = rows // side
    for part in range(lanes // WIDE):
        cols = slice(part * WIDE, (part + 1) * WIDE)
        for chunk in range(side // xs):
            planes = slice(chunk * xs, (chunk + 1) * xs)
            norm_bf = normed_bf[chunk * rows:(chunk + 1) * rows, cols]
            branch = jnp.dot(norm_bf, mix_mat, preferred_element_type=F32)
            feat = own_ref[planes, :, cols].reshape(rows, WIDE).astype(F32)
            mixed_ref[planes, :, cols] = (feat + branch).astype(BF16).reshape(xs, side, WIDE)


def sums_kernel(field, grads, gain_sum_ref, grad_mix_ref, packed_ref):
    tiles, cells, _ = grads.shape
    side = math.isqrt(cells)
    channels = packed_ref.shape[1] // 2
    pitch = side + 8
    def tap_tile(k, sums):
        sums = list(sums)
        for half in range(side // 8):
            near_grads = {}
            for plane in range(side + 2):
                if plane < side:
                    row = plane * side + 8 * half
                    near_grads[plane] = grads[k, row:row + 8, :]
                near = shifted(field, tiles, k, plane, half, pitch)
                for (off_y, off_z), value in near.items():
                    for off_x in range(3):
                        x = plane - off_x
                        if 0 <= x < side:
                            tap = 9 * off_x + 3 * off_y + off_z
                            sums[tap] = sums[tap] + value * near_grads[x]
                near_grads.pop(plane - 2, None)
        return tuple(sums)

    sums = lax.fori_loop(0, tiles, tap_tile, tuple(jnp.zeros((8, LANE), F32) for _ in range(27)))
    packed_ref[0:32, :] = grad_mix_ref[...]
    gain_row = jnp.sum(gain_sum_ref[...], axis=0, keepdims=True)
    rows = [jnp.sum(t, axis=0, keepdims=True) for t in sums] + [gain_row[:, :LANE] + gain_row[:, LANE:]]
    rows = jnp.concatenate(rows + [jnp.zeros((4, LANE), F32)], axis=0)
    rows = rows[:, :channels] + rows[:, channels:]
    packed_ref[32:48, :] = jnp.concatenate([rows[:16], rows[16:]], axis=1)


def backward_kernel(
    field, sums, weights, xlo_ref, xhi_ref, ylo_ref, yhi_ref, masks_ref, cot_ref,
    field_out_ref, sums_out_ref, out_ref,
):
    side = cot_ref.shape[0]
    halo_part(xlo_ref, xhi_ref, ylo_ref, yhi_ref, masks_ref, field, weights, sums, True)
    for x in range(side):
        for k in range(sums.shape[0]):
            cols = slice(k * LANE, (k + 1) * LANE)
            cot = cot_ref[x, :, cols].astype(F32)
            out_ref[x, :, cols] = (cot + sums[k, x * side:(x + 1) * side, :]).astype(BF16)


def unpack_kernel(mine_ref, other_ref, one_ref, both_ref, taps_hbm, gain_hbm, mix_hbm, taps_ref, gain_ref, mix_ref, done):
    total = (mine_ref[...] + one_ref[...]) + (other_ref[...] + both_ref[...])
    channels = mix_ref.shape[0]
    mix_ref[0:32, :] = total[:32, :channels]
    mix_ref[32:64, :] = total[:32, channels:]
    taps_ref[0:16, :] = total[32:48, :channels]
    taps_ref[16:27, :] = total[32:43, channels:]
    gain_ref[...] = total[43:44, channels:]
    copies = [
        pltpu.make_async_copy(src, dst, done.at[i])
        for i, (src, dst) in enumerate(((taps_ref, taps_hbm), (gain_ref, gain_hbm), (mix_ref, mix_hbm)))
    ]
    for copy in copies:
        copy.start()
    for copy in copies:
        copy.wait()


def swap(to_first, to_second, axis):
    sizes = {name: lax.axis_size(name) for name in ("gx", "gy")}
    count = sizes[axis]

    def second(place):
        other = "gy" if axis == "gx" else "gx"
        if 0 < place[axis] < count - 1:
            return {**place, axis: ((place[axis] + 1) ^ 1) - 1}
        return {**place, other: place[other] ^ 1}

    def index(place):
        return place["gx"] * sizes["gy"] + place["gy"]

    places = [{"gx": i, "gy": j} for i in range(sizes["gx"]) for j in range(sizes["gy"])]
    from_second = lax.ppermute(to_second, ("gx", "gy"), [(index(p), index(second(p))) for p in places])
    return lax.ppermute(to_first, axis, [(i, i ^ 1) for i in range(count)]), from_second


def low_high(from_first, from_second, axis):
    even = lax.axis_index(axis) % 2 == 0
    return jnp.where(even, from_second, from_first), jnp.where(even, from_first, from_second)


def y_messages(xlo, xhi, ylo, yhi):
    low = jnp.concatenate([xlo[:1], ylo, xhi[:1]], axis=0)
    high = jnp.concatenate([xlo[-1:], yhi, xhi[-1:]], axis=0)
    return low_high(low, high, "gy")


def sum_steps():
    steps = []
    for axis in ("gx", "gy"):
        count = lax.axis_size(axis)
        bit = 1
        while bit < count:
            steps.append((axis, [(i, i ^ bit) for i in range(count)]))
            bit *= 2
    return steps


def both_steps(one, other):
    index = {name: i for i, name in enumerate(("gx", "gy"))}
    sizes = [lax.axis_size("gx"), lax.axis_size("gy")]
    moves = [(index[axis], dict(pairs)) for axis, pairs in (one, other)]
    pairs = []
    for start in range(sizes[0] * sizes[1]):
        place = [start // sizes[1], start % sizes[1]]
        for at, move in moves:
            place[at] = move[place[at]]
        pairs.append((start, place[0] * sizes[1] + place[1]))
    return ("gx", "gy"), pairs


def shards(features, slot_map, tap_weights, gain, mix_weight, cotangent):
    side, _, _, lanes = features.shape
    channels = gain.shape[0]
    tiles = lanes // LANE
    cells = features.reshape(side, side, lanes)
    cot = cotangent.reshape(side, side, lanes)
    vmem = pl.BlockSpec(memory_space=pltpu.VMEM)
    hbm = pl.BlockSpec(memory_space=pltpu.HBM)
    block = jax.ShapeDtypeStruct((side, side, lanes), BF16)
    edge = jax.ShapeDtypeStruct((side, lanes), BF16)
    field_type = jax.ShapeDtypeStruct((2 * tiles + 1, (side + 2) * (side + 8) + 8, LANE), F32)
    sums_type = jax.ShapeDtypeStruct((tiles, side * side, LANE), F32)
    weights_type = jax.ShapeDtypeStruct((27, 8, LANE), F32)
    mat_type = jax.ShapeDtypeStruct((WIDE, WIDE), BF16)

    def call(kernel, name, operands, outs, scratch=(), aliases={}, flops=0, in_specs=None, out_specs=None):
        return pl.pallas_call(
            kernel,
            out_shape=tuple(jax.ShapeDtypeStruct(t.shape, t.dtype) for t in outs),
            in_specs=in_specs or [vmem] * len(operands),
            out_specs=out_specs or (vmem,) * len(outs),
            scratch_shapes=list(scratch),
            input_output_aliases=aliases,
            compiler_params=pltpu.CompilerParams(vmem_limit_bytes=40 * 1024 * 1024),
            cost_estimate=pl.CostEstimate(flops=flops, bytes_accessed=500_000, transcendentals=0),
            name=name,
        )(*operands)

    ylo, yhi = call(y_edges_kernel, "y_edges", (cells,), (edge, edge), flops=100_000_000_000)
    masks, weights, mean_mat, mix_mat, gain_wide = call(
        params_kernel,
        "params",
        (jnp.transpose(slot_map, (1, 2, 0)), mix_weight, tap_weights, gain.reshape(1, channels)),
        (
            jax.ShapeDtypeStruct((12, side + 8, LANE), F32),
            weights_type,
            mat_type,
            mat_type,
            jax.ShapeDtypeStruct((1, WIDE), F32),
        ),
    )
    xlo, xhi = low_high(*swap(*x_edges(cells), "gx"), "gx")
    to_a, to_b = y_messages(xlo, xhi, ylo, yhi)
    to_a, to_b, weights = lax.optimization_barrier((to_a, to_b, weights))
    ylo, yhi = low_high(*swap(to_a, to_b, "gy"), "gy")
    own_field, own_sums = call(
        functools.partial(own_kernel, False), "own_forward", (cells, weights), (field_type, sums_type),
        flops=10_000_000,
    )
    field, _, grad_depth, gxa, gxb, normed_bf, grads, gain_sum, grad_mix = call(
        forward_kernel,
        "forward",
        (own_field, own_sums, weights, mean_mat, mix_mat, gain_wide, xlo, xhi, ylo, yhi, masks, cot),
        (
            field_type, sums_type, block, edge, edge,
            jax.ShapeDtypeStruct((side * side, lanes), BF16), sums_type, jax.ShapeDtypeStruct((8, WIDE), F32),
            jax.ShapeDtypeStruct((32, LANE), F32),
        ),
        aliases={0: 0, 1: 1},
        flops=10_000_000,
    )
    gxlo, gxhi = low_high(*swap(gxa, gxb, "gx"), "gx")
    (part,) = call(
        sums_kernel,
        "sums",
        (field, grads, gain_sum, grad_mix),
        (jax.ShapeDtypeStruct((48, LANE), F32),),
        flops=10_000_000,
    )

    steps = sum_steps()
    part, y_cells = lax.optimization_barrier((part, grad_depth))
    part = part + lax.ppermute(part, *steps[0])
    gylo, gyhi = call(y_edges_kernel, "grad_y_edges", (y_cells,), (edge, edge), flops=1_000_000)
    part, to_a, to_b = lax.optimization_barrier((part, *y_messages(gxlo, gxhi, gylo, gyhi)))
    part = part + lax.ppermute(part, *steps[1])
    gylo, gyhi = low_high(*swap(to_a, to_b, "gy"), "gy")
    part, grad_depth = lax.optimization_barrier((part, grad_depth))
    theirs = lax.ppermute(part, *steps[2])
    own_field, own_sums = call(
        functools.partial(own_kernel, True), "own_backward", (grad_depth, weights), (field_type, sums_type),
        flops=10_000_000,
    )
    part, own_field, own_sums, normed_bf = lax.optimization_barrier(
        (part + theirs, own_field, own_sums, normed_bf)
    )
    for step in steps[3:-2]:
        part = part + lax.ppermute(part, *step)
    theirs = [lax.ppermute(part, *step) for step in (steps[-1], steps[-2], both_steps(*steps[-2:]))]
    _, _, grad_features = call(
        backward_kernel,
        "backward",
        (own_field, own_sums, weights, gxlo, gxhi, gylo, gyhi, masks, cot),
        (field_type, sums_type, block),
        aliases={0: 0, 1: 1},
        flops=2_000_000,
    )
    (mixed,) = call(mixed_kernel, "mixed", (cells, normed_bf, mix_mat), (block,), flops=10_000_000)

    outs = (
        jax.ShapeDtypeStruct((27, channels), F32),
        jax.ShapeDtypeStruct((1, channels), F32),
        jax.ShapeDtypeStruct((channels, channels), F32),
    )
    grad_taps, grad_gain, grad_mix = call(
        unpack_kernel,
        "unpack",
        (part, *theirs),
        outs,
        scratch=[pltpu.VMEM(t.shape, F32) for t in outs] + [pltpu.SemaphoreType.DMA((3,))],
        out_specs=(hbm,) * 3,
    )
    shape = features.shape
    return (mixed.reshape(shape), grad_features.reshape(shape), grad_taps, grad_gain.reshape(channels), grad_mix)


def solution(mesh):
    return jax.shard_map(
        shards,
        mesh=mesh,
        in_specs=(P("gx", "gy", None, None), P(), P(), P(), P(), P("gx", "gy", None, None)),
        out_specs=(P("gx", "gy", None, None), P("gx", "gy", None, None), P(), P(), P()),
        check_vma=False,
    )
```

```python
import functools
import math

import jax
import jax.numpy as jnp
from jax import lax
from jax.experimental import pallas as pl
from jax.experimental.pallas import tpu as pltpu
from jax.sharding import PartitionSpec as P

EPS = 1e-05
LANE = 128
WIDE = 256
PLANES = 8
F32 = jnp.float32
BF16 = jnp.bfloat16


def level_masks(slots, side, masks_ref):
    level = lax.broadcasted_iota(jnp.int32, slots.shape, 1)
    at_x = lax.broadcasted_iota(jnp.int32, slots.shape, 2) - lax.axis_index("gx")
    at_y = lax.broadcasted_iota(jnp.int32, slots.shape, 0) - lax.axis_index("gy")
    place = jnp.where(slots >= 0, level + 1, 0).astype(F32)

    def near(off_x, off_y):
        found = jnp.where((at_x == off_x) & (at_y == off_y), place, 0.0)
        found = jnp.sum(jnp.sum(found, axis=0), axis=0, keepdims=True)
        return jnp.sum(found, axis=1, keepdims=True)

    own = near(0, 0)

    def difference(off_x, off_y):
        found = near(off_x, off_y)
        return jnp.where(found > 0.0, found - own, 9.0)

    rows = masks_ref.shape[1]
    row = lax.broadcasted_iota(jnp.int32, (rows, LANE), 0)
    for edge in range(4):
        high = 1 if edge % 2 else -1
        if edge < 2:
            d = jnp.broadcast_to(difference(high, 0), (rows, LANE))
        else:
            corner, middle, other = (difference(off, high) for off in (-1, 0, 1))
            d = jnp.where(row == 0, corner, jnp.where(row == side + 1, other, middle))
        for i, want in enumerate((0.0, -1.0, 1.0)):
            masks_ref[3 * edge + i] = jnp.where(d == want, 1.0, 0.0)


def plane_tiles(load, total, masks):
    low = lax.broadcasted_iota(jnp.int32, load(0).shape, 1) < LANE // 2
    zero = jnp.zeros(load(0).shape, F32)
    aligned = [load(k) for k in range(total)]
    turned = [pltpu.roll(t, LANE // 2, 1) for t in aligned]
    between = [jnp.where(low, turned[j - 1], turned[j]) for j in range(1, total)]
    if masks is None:
        return aligned + [jnp.where(low, zero, turned[0])] + between + [jnp.where(low, turned[-1], zero)]
    same, below, above = masks
    first = jnp.where(low, turned[-1] * below, turned[0] * same)
    last = jnp.where(low, turned[-1] * same, turned[0] * above)
    return [t * same for t in aligned] + [first] + [t * same for t in between] + [last]


def loader(rows):
    return lambda k: rows[:, k * LANE:(k + 1) * LANE].astype(F32)


def column_starts(side, shift):
    pitch = side + 8
    for start in range(0, side + 2, 8):
        size = min(8, side + 2 - start)
        yield start, size, pl.ds(start * pitch + shift, size, stride=pitch)


def own_part(own_ref, field, weights, sums, flip):
    side = own_ref.shape[0]
    tiles = own_ref.shape[2] // LANE
    pitch = side + 8

    def own_planes(step, _):
        for x in range(PLANES):
            x = step * PLANES + x
            base = pl.multiple_of((x + 1) * pitch + 8, 8)
            for i, t in enumerate(plane_tiles(loader(own_ref[x]), tiles, None)):
                field[i, pl.ds(base, side), :] = t
        return 0

    lax.fori_loop(0, side // PLANES, own_planes, 0)
    for i in range(2 * tiles + 1):
        for shift in (7, pitch):
            for _, size, at in column_starts(side, shift):
                field[i, at, :] = jnp.zeros((size, LANE), F32)

    def tile(k, _):
        taps = [weights[26 - t if flip else t] for t in range(27)]
        for half in range(side // 8):
            part = {}
            for plane in range(1, side + 1):
                near = shifted(field, tiles, k, plane, half, pitch)
                for off_x in range(3):
                    x = plane - off_x
                    if not 0 <= x < side:
                        continue
                    for (off_y, off_z), value in near.items():
                        term = value * taps[9 * off_x + 3 * off_y + off_z]
                        part[x] = part[x] + term if x in part else term
                done = plane - 2
                for x in [done, done + 1] if plane == side else [done]:
                    if x >= 0:
                        sums[k, x * side + 8 * half:x * side + 8 * half + 8, :] = part.pop(x)
        return 0

    lax.fori_loop(0, tiles, tile, 0)


def halo_part(xlo_ref, xhi_ref, ylo_ref, yhi_ref, masks_ref, field, weights, sums, flip):
    side, lanes = xlo_ref.shape
    tiles = lanes // LANE
    pitch = side + 8

    def place(i, ref):
        rows = ref.shape[0]
        masks = tuple(masks_ref[3 * i + m, :rows, :] for m in range(3))
        return plane_tiles(loader(ref[...]), tiles, masks)

    for i, ref, plane in ((0, xlo_ref, 0), (1, xhi_ref, side + 1)):
        for j, t in enumerate(place(i, ref)):
            field[j, plane * pitch + 8:plane * pitch + 8 + side, :] = t

    totals = []

    def x_tile(k):
        for plane, off_x, x in ((0, 0, 0), (side + 1, 2, side - 1)):
            for half in range(side // 8):
                row = x * side + 8 * half
                total = sums[k, row:row + 8, :]
                for (off_y, off_z), value in shifted(field, tiles, k, plane, half, pitch).items():
                    tap = 9 * off_x + 3 * off_y + off_z
                    total = total + value * weights[26 - tap if flip else tap]
                totals.append((k, slice(row, row + 8), total))

    for k in range(tiles):
        x_tile(k)
    for k, at, total in totals:
        sums[k, at, :] = total

    for i, ref, shift in ((2, ylo_ref, 7), (3, yhi_ref, pitch)):
        for j, t in enumerate(place(i, ref)):
            for start, size, at in column_starts(side, shift):
                field[j, at, :] = t[start:start + size]

    totals = []

    def y_tile(k):
        for shift, off_y, y in ((7, 0, 0), (pitch, 2, side - 1)):
            for x in range(0, side, 8):
                at = pl.ds(x * side + y, 8, stride=side)
                total = sums[k, at, :]
                for off_x in range(3):
                    for off_z in range(3):
                        i = (tiles + k, k, tiles + k + 1)[off_z]
                        tap = 9 * off_x + 3 * off_y + off_z
                        value = field[i, pl.ds((x + off_x) * pitch + shift, 8, stride=pitch), :]
                        total = total + value * weights[26 - tap if flip else tap]
                totals.append((k, at, total))

    for k in range(tiles):
        y_tile(k)
    for k, at, total in totals:
        sums[k, at, :] = total


def shifted(field, tiles, k, plane, half, pitch):
    found = {}
    for off_y in range(3):
        row = plane * pitch + 7 + 8 * half + off_y
        for off_z in range(3):
            i = (tiles + k, k, tiles + k + 1)[off_z]
            found[off_y, off_z] = field[i, row:row + 8, :]
    return found


def x_edges(cells):
    odd = lax.axis_index("gx") % 2 == 1
    return jnp.where(odd, cells[0], cells[-1]), jnp.where(odd, cells[-1], cells[0])


def y_edges_kernel(cells_ref, ylo_ref, yhi_ref):
    side, _, lanes = cells_ref.shape
    row = lax.broadcasted_iota(jnp.int32, (2 * side, side * side), 0)
    col = lax.broadcasted_iota(jnp.int32, (2 * side, side * side), 1)
    wanted = jnp.where(row < side, row * side, (row - side) * side + side - 1)
    pick = jnp.where(col == wanted, 1.0, 0.0).astype(BF16)
    flat = cells_ref[...].reshape(side * side, lanes)
    found = jnp.dot(pick, flat, preferred_element_type=F32).astype(BF16)
    ylo_ref[...] = found[:side]
    yhi_ref[...] = found[side:]


def params_kernel(
    slots_ref, mix_ref, taps_ref, gain_ref, masks_ref, weights, mean_mat_ref, mix_mat_ref, gain_wide_ref
):
    channels = mix_ref.shape[0]
    level_masks(slots_ref[...], masks_ref.shape[1] - 8, masks_ref)
    wide = jnp.concatenate([taps_ref[...], taps_ref[...]], axis=1)
    for tap in range(27):
        weights[tap] = jnp.broadcast_to(wide[tap:tap + 1], (8, LANE))
    copies = WIDE // channels
    row_id = lax.broadcasted_iota(jnp.int32, (WIDE, WIDE), 0) // channels
    col_id = lax.broadcasted_iota(jnp.int32, (WIDE, WIDE), 1) // channels
    block = row_id == col_id
    mean_mat_ref[...] = jnp.where(block, 1.0 / channels, 0.0).astype(BF16)
    mix = mix_ref[...].astype(F32)
    mix_row = jnp.concatenate([mix] * copies, axis=1)
    mix_mat_ref[...] = jnp.where(block, jnp.concatenate([mix_row] * copies, axis=0), 0.0).astype(BF16)
    gain_wide_ref[...] = jnp.concatenate([gain_ref[...]] * copies, axis=1)


def own_kernel(flip, own_ref, weights, field, sums):
    own_part(own_ref, field, weights, sums, flip)


def forward_kernel(
    field, depth, weights, mean_mat_ref, mix_mat_ref, gain_wide_ref,
    xlo_ref, xhi_ref, ylo_ref, yhi_ref, masks_ref, cot_ref,
    field_out_ref, depth_out_ref, grad_ref, gxa_ref, gxb_ref, normed_bf, grads, gain_sum_ref, grad_mix_ref,
):
    side, _, lanes = cot_ref.shape
    cells = side * side
    halo_part(xlo_ref, xhi_ref, ylo_ref, yhi_ref, masks_ref, field, weights, depth, False)

    mean_mat = mean_mat_ref[...]
    mix_mat = mix_mat_ref[...]
    gain = gain_wide_ref[...]
    gain_sum = jnp.zeros((8, WIDE), F32)
    mix_sum = jnp.zeros((WIDE, WIDE), F32)
    for first in range(0, lanes // WIDE, 2):
        parts = range(first, first + 2)
        spans = [slice(part * WIDE, (part + 1) * WIDE) for part in parts]
        deps = [jnp.concatenate([depth[2 * part], depth[2 * part + 1]], axis=1) for part in parts]
        cots = [cot_ref[:, :, cols].reshape(cells, WIDE) for cols in spans]
        mean_sqs = [jnp.dot((dep * dep).astype(BF16), mean_mat, preferred_element_type=F32) for dep in deps]
        grad_norms = [
            lax.dot_general(cot, mix_mat, (((1,), (1,)), ((), ())), preferred_element_type=F32) for cot in cots
        ]
        invs = [lax.rsqrt(mean_sq + EPS) for mean_sq in mean_sqs]
        normeds = [dep * inv for dep, inv in zip(deps, invs)]
        norm_bfs = [(normed * gain).astype(BF16) for normed in normeds]
        scaleds = [grad_norm * gain for grad_norm in grad_norms]
        means = [
            jnp.dot((scaled * normed).astype(BF16), mean_mat, preferred_element_type=F32)
            for scaled, normed in zip(scaleds, normeds)
        ]
        for norm_bf, cot, grad_norm, normed in zip(norm_bfs, cots, grad_norms, normeds):
            mix_sum = mix_sum + lax.dot_general(
                norm_bf, cot, (((0,), (0,)), ((), ())), preferred_element_type=F32
            )
            gain_sum = gain_sum + jnp.sum((grad_norm * normed).reshape(cells // 8, 8, WIDE), axis=0)
        outs = [
            (inv * (scaled - normed * mean)).astype(BF16)
            for inv, scaled, normed, mean in zip(invs, scaleds, normeds, means)
        ]
        for part, cols, norm_bf, grad in zip(parts, spans, norm_bfs, outs):
            wide_grad = grad.astype(F32)
            normed_bf[:, cols] = norm_bf
            grad_ref[:, :, cols] = grad.reshape(side, side, WIDE)
            grads[2 * part] = wide_grad[:, :LANE]
            grads[2 * part + 1] = wide_grad[:, LANE:]
    gain_sum_ref[...] = gain_sum
    channels = grad_mix_ref.shape[1] // 2
    grad_mix = mix_sum[:channels, :channels]
    for i in range(1, WIDE // channels):
        span = slice(i * channels, (i + 1) * channels)
        grad_mix = grad_mix + mix_sum[span, span]
    grad_mix_ref[...] = jnp.concatenate([grad_mix[:32], grad_mix[32:]], axis=1)
    odd = lax.axis_index("gx") % 2
    gxa_ref[...] = grad_ref[jnp.where(odd == 1, 0, side - 1)]
    gxb_ref[...] = grad_ref[jnp.where(odd == 1, side - 1, 0)]


def mixed_kernel(own_ref, normed_bf, mix_mat_ref, mixed_ref):
    side, _, lanes = own_ref.shape
    mix_mat = mix_mat_ref[...]
    rows = 128
    xs = rows // side
    for part in range(lanes // WIDE):
        cols = slice(part * WIDE, (part + 1) * WIDE)
        for chunk in range(side // xs):
            planes = slice(chunk * xs, (chunk + 1) * xs)
            norm_bf = normed_bf[chunk * rows:(chunk + 1) * rows, cols]
            branch = jnp.dot(norm_bf, mix_mat, preferred_element_type=F32)
            feat = own_ref[planes, :, cols].reshape(rows, WIDE).astype(F32)
            mixed_ref[planes, :, cols] = (feat + branch).astype(BF16).reshape(xs, side, WIDE)


def sums_kernel(field, grads, gain_sum_ref, grad_mix_ref, packed_ref):
    tiles, cells, _ = grads.shape
    side = math.isqrt(cells)
    channels = packed_ref.shape[1] // 2
    pitch = side + 8
    def tap_tile(k, sums):
        sums = list(sums)
        for half in range(side // 8):
            near_grads = {}
            for plane in range(side + 2):
                if plane < side:
                    row = plane * side + 8 * half
                    near_grads[plane] = grads[k, row:row + 8, :]
                near = shifted(field, tiles, k, plane, half, pitch)
                for (off_y, off_z), value in near.items():
                    for off_x in range(3):
                        x = plane - off_x
                        if 0 <= x < side:
                            tap = 9 * off_x + 3 * off_y + off_z
                            sums[tap] = sums[tap] + value * near_grads[x]
                near_grads.pop(plane - 2, None)
        return tuple(sums)

    sums = lax.fori_loop(0, tiles, tap_tile, tuple(jnp.zeros((8, LANE), F32) for _ in range(27)))
    packed_ref[0:32, :] = grad_mix_ref[...]
    gain_row = jnp.sum(gain_sum_ref[...], axis=0, keepdims=True)
    rows = [jnp.sum(t, axis=0, keepdims=True) for t in sums] + [gain_row[:, :LANE] + gain_row[:, LANE:]]
    rows = jnp.concatenate(rows + [jnp.zeros((4, LANE), F32)], axis=0)
    rows = rows[:, :channels] + rows[:, channels:]
    packed_ref[32:48, :] = jnp.concatenate([rows[:16], rows[16:]], axis=1)


def backward_kernel(
    field, sums, weights, xlo_ref, xhi_ref, ylo_ref, yhi_ref, masks_ref, cot_ref,
    field_out_ref, sums_out_ref, out_ref,
):
    side = cot_ref.shape[0]
    halo_part(xlo_ref, xhi_ref, ylo_ref, yhi_ref, masks_ref, field, weights, sums, True)
    for x in range(side):
        for k in range(sums.shape[0]):
            cols = slice(k * LANE, (k + 1) * LANE)
            cot = cot_ref[x, :, cols].astype(F32)
            out_ref[x, :, cols] = (cot + sums[k, x * side:(x + 1) * side, :]).astype(BF16)


def unpack_kernel(mine_ref, other_ref, one_ref, both_ref, taps_hbm, gain_hbm, mix_hbm, taps_ref, gain_ref, mix_ref, done):
    total = (mine_ref[...] + one_ref[...]) + (other_ref[...] + both_ref[...])
    channels = mix_ref.shape[0]
    mix_ref[0:32, :] = total[:32, :channels]
    mix_ref[32:64, :] = total[:32, channels:]
    taps_ref[0:16, :] = total[32:48, :channels]
    taps_ref[16:27, :] = total[32:43, channels:]
    gain_ref[...] = total[43:44, channels:]
    copies = [
        pltpu.make_async_copy(src, dst, done.at[i])
        for i, (src, dst) in enumerate(((taps_ref, taps_hbm), (gain_ref, gain_hbm), (mix_ref, mix_hbm)))
    ]
    for copy in copies:
        copy.start()
    for copy in copies:
        copy.wait()


def swap(to_first, to_second, axis):
    sizes = {name: lax.axis_size(name) for name in ("gx", "gy")}
    count = sizes[axis]

    def second(place):
        other = "gy" if axis == "gx" else "gx"
        if 0 < place[axis] < count - 1:
            return {**place, axis: ((place[axis] + 1) ^ 1) - 1}
        return {**place, other: place[other] ^ 1}

    def index(place):
        return place["gx"] * sizes["gy"] + place["gy"]

    places = [{"gx": i, "gy": j} for i in range(sizes["gx"]) for j in range(sizes["gy"])]
    from_second = lax.ppermute(to_second, ("gx", "gy"), [(index(p), index(second(p))) for p in places])
    return lax.ppermute(to_first, axis, [(i, i ^ 1) for i in range(count)]), from_second


def low_high(from_first, from_second, axis):
    even = lax.axis_index(axis) % 2 == 0
    return jnp.where(even, from_second, from_first), jnp.where(even, from_first, from_second)


def y_messages(xlo, xhi, ylo, yhi):
    low = jnp.concatenate([xlo[:1], ylo, xhi[:1]], axis=0)
    high = jnp.concatenate([xlo[-1:], yhi, xhi[-1:]], axis=0)
    return low_high(low, high, "gy")


def sum_steps():
    steps = []
    for axis in ("gx", "gy"):
        count = lax.axis_size(axis)
        bit = 1
        while bit < count:
            steps.append((axis, [(i, i ^ bit) for i in range(count)]))
            bit *= 2
    return steps


def both_steps(one, other):
    index = {name: i for i, name in enumerate(("gx", "gy"))}
    sizes = [lax.axis_size("gx"), lax.axis_size("gy")]
    moves = [(index[axis], dict(pairs)) for axis, pairs in (one, other)]
    pairs = []
    for start in range(sizes[0] * sizes[1]):
        place = [start // sizes[1], start % sizes[1]]
        for at, move in moves:
            place[at] = move[place[at]]
        pairs.append((start, place[0] * sizes[1] + place[1]))
    return ("gx", "gy"), pairs


def shards(features, slot_map, tap_weights, gain, mix_weight, cotangent):
    side, _, _, lanes = features.shape
    channels = gain.shape[0]
    tiles = lanes // LANE
    cells = features.reshape(side, side, lanes)
    cot = cotangent.reshape(side, side, lanes)
    vmem = pl.BlockSpec(memory_space=pltpu.VMEM)
    hbm = pl.BlockSpec(memory_space=pltpu.HBM)
    block = jax.ShapeDtypeStruct((side, side, lanes), BF16)
    edge = jax.ShapeDtypeStruct((side, lanes), BF16)
    field_type = jax.ShapeDtypeStruct((2 * tiles + 1, (side + 2) * (side + 8) + 8, LANE), F32)
    sums_type = jax.ShapeDtypeStruct((tiles, side * side, LANE), F32)
    weights_type = jax.ShapeDtypeStruct((27, 8, LANE), F32)
    mat_type = jax.ShapeDtypeStruct((WIDE, WIDE), BF16)

    def call(kernel, name, operands, outs, scratch=(), aliases={}, flops=0, in_specs=None, out_specs=None):
        return pl.pallas_call(
            kernel,
            out_shape=tuple(jax.ShapeDtypeStruct(t.shape, t.dtype) for t in outs),
            in_specs=in_specs or [vmem] * len(operands),
            out_specs=out_specs or (vmem,) * len(outs),
            scratch_shapes=list(scratch),
            input_output_aliases=aliases,
            compiler_params=pltpu.CompilerParams(vmem_limit_bytes=40 * 1024 * 1024),
            cost_estimate=pl.CostEstimate(flops=flops, bytes_accessed=500_000, transcendentals=0),
            name=name,
        )(*operands)

    ylo, yhi = call(y_edges_kernel, "y_edges", (cells,), (edge, edge), flops=100_000_000_000)
    masks, weights, mean_mat, mix_mat, gain_wide = call(
        params_kernel,
        "params",
        (jnp.transpose(slot_map, (1, 2, 0)), mix_weight, tap_weights, gain.reshape(1, channels)),
        (
            jax.ShapeDtypeStruct((12, side + 8, LANE), F32),
            weights_type,
            mat_type,
            mat_type,
            jax.ShapeDtypeStruct((1, WIDE), F32),
        ),
    )
    xlo, xhi = low_high(*swap(*x_edges(cells), "gx"), "gx")
    to_a, to_b = y_messages(xlo, xhi, ylo, yhi)
    to_a, to_b, weights = lax.optimization_barrier((to_a, to_b, weights))
    ylo, yhi = low_high(*swap(to_a, to_b, "gy"), "gy")
    own_field, own_sums = call(
        functools.partial(own_kernel, False), "own_forward", (cells, weights), (field_type, sums_type),
        flops=10_000_000,
    )
    field, _, grad_depth, gxa, gxb, normed_bf, grads, gain_sum, grad_mix = call(
        forward_kernel,
        "forward",
        (own_field, own_sums, weights, mean_mat, mix_mat, gain_wide, xlo, xhi, ylo, yhi, masks, cot),
        (
            field_type, sums_type, block, edge, edge,
            jax.ShapeDtypeStruct((side * side, lanes), BF16), sums_type, jax.ShapeDtypeStruct((8, WIDE), F32),
            jax.ShapeDtypeStruct((32, LANE), F32),
        ),
        aliases={0: 0, 1: 1},
        flops=10_000_000,
    )
    gxlo, gxhi = low_high(*swap(gxa, gxb, "gx"), "gx")
    (part,) = call(
        sums_kernel,
        "sums",
        (field, grads, gain_sum, grad_mix),
        (jax.ShapeDtypeStruct((48, LANE), F32),),
        flops=10_000_000,
    )

    steps = sum_steps()
    part, y_cells = lax.optimization_barrier((part, grad_depth))
    part = part + lax.ppermute(part, *steps[0])
    gylo, gyhi = call(y_edges_kernel, "grad_y_edges", (y_cells,), (edge, edge), flops=1_000_000)
    part, to_a, to_b = lax.optimization_barrier((part, *y_messages(gxlo, gxhi, gylo, gyhi)))
    part = part + lax.ppermute(part, *steps[1])
    gylo, gyhi = low_high(*swap(to_a, to_b, "gy"), "gy")
    part, grad_depth = lax.optimization_barrier((part, grad_depth))
    theirs = lax.ppermute(part, *steps[2])
    own_field, own_sums = call(
        functools.partial(own_kernel, True), "own_backward", (grad_depth, weights), (field_type, sums_type),
        flops=10_000_000,
    )
    part, own_field, own_sums, normed_bf = lax.optimization_barrier(
        (part + theirs, own_field, own_sums, normed_bf)
    )
    for step in steps[3:-2]:
        part = part + lax.ppermute(part, *step)
    theirs = [lax.ppermute(part, *step) for step in (steps[-1], steps[-2], both_steps(*steps[-2:]))]
    _, _, grad_features = call(
        backward_kernel,
        "backward",
        (own_field, own_sums, weights, gxlo, gxhi, gylo, gyhi, masks, cot),
        (field_type, sums_type, block),
        aliases={0: 0, 1: 1},
        flops=2_000_000,
    )
    (mixed,) = call(mixed_kernel, "mixed", (cells, normed_bf, mix_mat), (block,), flops=10_000_000)

    outs = (
        jax.ShapeDtypeStruct((27, channels), F32),
        jax.ShapeDtypeStruct((1, channels), F32),
        jax.ShapeDtypeStruct((channels, channels), F32),
    )
    grad_taps, grad_gain, grad_mix = call(
        unpack_kernel,
        "unpack",
        (part, *theirs),
        outs,
        scratch=[pltpu.VMEM(t.shape, F32) for t in outs] + [pltpu.SemaphoreType.DMA((3,))],
        out_specs=(hbm,) * 3,
    )
    shape = features.shape
    return (mixed.reshape(shape), grad_features.reshape(shape), grad_taps, grad_gain.reshape(channels), grad_mix)


def solution(mesh):
    return jax.shard_map(
        shards,
        mesh=mesh,
        in_specs=(P("gx", "gy", None, None), P(), P(), P(), P(), P("gx", "gy", None, None)),
        out_specs=(P("gx", "gy", None, None), P("gx", "gy", None, None), P(), P(), P()),
        check_vma=False,
    )
```

```python
import functools
import math

import jax
import jax.numpy as jnp
from jax import lax
from jax.experimental import pallas as pl
from jax.experimental.pallas import tpu as pltpu
from jax.sharding import PartitionSpec as P

EPS = 1e-05
LANE = 128
WIDE = 256
PLANES = 4
F32 = jnp.float32
BF16 = jnp.bfloat16


def level_masks(slots, side, masks_ref):
    level = lax.broadcasted_iota(jnp.int32, slots.shape, 1)
    at_x = lax.broadcasted_iota(jnp.int32, slots.shape, 2) - lax.axis_index("gx")
    at_y = lax.broadcasted_iota(jnp.int32, slots.shape, 0) - lax.axis_index("gy")
    place = jnp.where(slots >= 0, level + 1, 0).astype(F32)

    def near(off_x, off_y):
        found = jnp.where((at_x == off_x) & (at_y == off_y), place, 0.0)
        found = jnp.sum(jnp.sum(found, axis=0), axis=0, keepdims=True)
        return jnp.sum(found, axis=1, keepdims=True)

    own = near(0, 0)

    def difference(off_x, off_y):
        found = near(off_x, off_y)
        return jnp.where(found > 0.0, found - own, 9.0)

    rows = masks_ref.shape[1]
    row = lax.broadcasted_iota(jnp.int32, (rows, LANE), 0)
    for edge in range(4):
        high = 1 if edge % 2 else -1
        if edge < 2:
            d = jnp.broadcast_to(difference(high, 0), (rows, LANE))
        else:
            corner, middle, other = (difference(off, high) for off in (-1, 0, 1))
            d = jnp.where(row == 0, corner, jnp.where(row == side + 1, other, middle))
        for i, want in enumerate((0.0, -1.0, 1.0)):
            masks_ref[3 * edge + i] = jnp.where(d == want, 1.0, 0.0)


def plane_tiles(load, total, masks):
    low = lax.broadcasted_iota(jnp.int32, load(0).shape, 1) < LANE // 2
    zero = jnp.zeros(load(0).shape, F32)
    aligned = [load(k) for k in range(total)]
    turned = [pltpu.roll(t, LANE // 2, 1) for t in aligned]
    between = [jnp.where(low, turned[j - 1], turned[j]) for j in range(1, total)]
    if masks is None:
        return aligned + [jnp.where(low, zero, turned[0])] + between + [jnp.where(low, turned[-1], zero)]
    same, below, above = masks
    first = jnp.where(low, turned[-1] * below, turned[0] * same)
    last = jnp.where(low, turned[-1] * same, turned[0] * above)
    return [t * same for t in aligned] + [first] + [t * same for t in between] + [last]


def loader(rows):
    return lambda k: rows[:, k * LANE:(k + 1) * LANE].astype(F32)


def column_starts(side, shift):
    pitch = side + 8
    for start in range(0, side + 2, 8):
        size = min(8, side + 2 - start)
        yield start, size, pl.ds(start * pitch + shift, size, stride=pitch)


def own_part(own_ref, field, weights, sums, flip):
    side = own_ref.shape[0]
    tiles = own_ref.shape[2] // LANE
    pitch = side + 8

    def own_planes(step, _):
        for x in range(PLANES):
            x = step * PLANES + x
            base = pl.multiple_of((x + 1) * pitch + 8, 8)
            for i, t in enumerate(plane_tiles(loader(own_ref[x]), tiles, None)):
                field[i, pl.ds(base, side), :] = t
        return 0

    lax.fori_loop(0, side // PLANES, own_planes, 0)
    for i in range(2 * tiles + 1):
        for shift in (7, pitch):
            for _, size, at in column_starts(side, shift):
                field[i, at, :] = jnp.zeros((size, LANE), F32)

    def tile(k, _):
        taps = [weights[26 - t if flip else t] for t in range(27)]
        for half in range(side // 8):
            part = {}
            for plane in range(1, side + 1):
                near = shifted(field, tiles, k, plane, half, pitch)
                for off_x in range(3):
                    x = plane - off_x
                    if not 0 <= x < side:
                        continue
                    for (off_y, off_z), value in near.items():
                        term = value * taps[9 * off_x + 3 * off_y + off_z]
                        part[x] = part[x] + term if x in part else term
                done = plane - 2
                for x in [done, done + 1] if plane == side else [done]:
                    if x >= 0:
                        sums[k, x * side + 8 * half:x * side + 8 * half + 8, :] = part.pop(x)
        return 0

    lax.fori_loop(0, tiles, tile, 0)


def halo_part(xlo_ref, xhi_ref, ylo_ref, yhi_ref, masks_ref, field, weights, sums, flip):
    side, lanes = xlo_ref.shape
    tiles = lanes // LANE
    pitch = side + 8

    def place(i, ref):
        rows = ref.shape[0]
        masks = tuple(masks_ref[3 * i + m, :rows, :] for m in range(3))
        return plane_tiles(loader(ref[...]), tiles, masks)

    for i, ref, plane in ((0, xlo_ref, 0), (1, xhi_ref, side + 1)):
        for j, t in enumerate(place(i, ref)):
            field[j, plane * pitch + 8:plane * pitch + 8 + side, :] = t

    totals = []

    def x_tile(k):
        for plane, off_x, x in ((0, 0, 0), (side + 1, 2, side - 1)):
            for half in range(side // 8):
                row = x * side + 8 * half
                total = sums[k, row:row + 8, :]
                for (off_y, off_z), value in shifted(field, tiles, k, plane, half, pitch).items():
                    tap = 9 * off_x + 3 * off_y + off_z
                    total = total + value * weights[26 - tap if flip else tap]
                totals.append((k, slice(row, row + 8), total))

    for k in range(tiles):
        x_tile(k)
    for k, at, total in totals:
        sums[k, at, :] = total

    for i, ref, shift in ((2, ylo_ref, 7), (3, yhi_ref, pitch)):
        for j, t in enumerate(place(i, ref)):
            for start, size, at in column_starts(side, shift):
                field[j, at, :] = t[start:start + size]

    totals = []

    def y_tile(k):
        for shift, off_y, y in ((7, 0, 0), (pitch, 2, side - 1)):
            for x in range(0, side, 8):
                at = pl.ds(x * side + y, 8, stride=side)
                total = sums[k, at, :]
                for off_x in range(3):
                    for off_z in range(3):
                        i = (tiles + k, k, tiles + k + 1)[off_z]
                        tap = 9 * off_x + 3 * off_y + off_z
                        value = field[i, pl.ds((x + off_x) * pitch + shift, 8, stride=pitch), :]
                        total = total + value * weights[26 - tap if flip else tap]
                totals.append((k, at, total))

    for k in range(tiles):
        y_tile(k)
    for k, at, total in totals:
        sums[k, at, :] = total


def shifted(field, tiles, k, plane, half, pitch):
    found = {}
    for off_y in range(3):
        row = plane * pitch + 7 + 8 * half + off_y
        for off_z in range(3):
            i = (tiles + k, k, tiles + k + 1)[off_z]
            found[off_y, off_z] = field[i, row:row + 8, :]
    return found


def x_edges(cells):
    odd = lax.axis_index("gx") % 2 == 1
    return jnp.where(odd, cells[0], cells[-1]), jnp.where(odd, cells[-1], cells[0])


def y_edges_kernel(cells_ref, ylo_ref, yhi_ref):
    side, _, lanes = cells_ref.shape
    row = lax.broadcasted_iota(jnp.int32, (2 * side, side * side), 0)
    col = lax.broadcasted_iota(jnp.int32, (2 * side, side * side), 1)
    wanted = jnp.where(row < side, row * side, (row - side) * side + side - 1)
    pick = jnp.where(col == wanted, 1.0, 0.0).astype(BF16)
    flat = cells_ref[...].reshape(side * side, lanes)
    found = jnp.dot(pick, flat, preferred_element_type=F32).astype(BF16)
    ylo_ref[...] = found[:side]
    yhi_ref[...] = found[side:]


def params_kernel(
    slots_ref, mix_ref, taps_ref, gain_ref, masks_ref, weights, mean_mat_ref, mix_mat_ref, gain_wide_ref
):
    channels = mix_ref.shape[0]
    level_masks(slots_ref[...], masks_ref.shape[1] - 8, masks_ref)
    wide = jnp.concatenate([taps_ref[...], taps_ref[...]], axis=1)
    for tap in range(27):
        weights[tap] = jnp.broadcast_to(wide[tap:tap + 1], (8, LANE))
    copies = WIDE // channels
    row_id = lax.broadcasted_iota(jnp.int32, (WIDE, WIDE), 0) // channels
    col_id = lax.broadcasted_iota(jnp.int32, (WIDE, WIDE), 1) // channels
    block = row_id == col_id
    mean_mat_ref[...] = jnp.where(block, 1.0 / channels, 0.0).astype(BF16)
    mix = mix_ref[...].astype(F32)
    mix_row = jnp.concatenate([mix] * copies, axis=1)
    mix_mat_ref[...] = jnp.where(block, jnp.concatenate([mix_row] * copies, axis=0), 0.0).astype(BF16)
    gain_wide_ref[...] = jnp.concatenate([gain_ref[...]] * copies, axis=1)


def own_kernel(flip, own_ref, weights, field, sums):
    own_part(own_ref, field, weights, sums, flip)


def forward_kernel(
    field, depth, weights, mean_mat_ref, mix_mat_ref, gain_wide_ref,
    xlo_ref, xhi_ref, ylo_ref, yhi_ref, masks_ref, cot_ref,
    field_out_ref, depth_out_ref, grad_ref, gxa_ref, gxb_ref, normed_bf, grads, gain_sum_ref, grad_mix_ref,
):
    side, _, lanes = cot_ref.shape
    cells = side * side
    halo_part(xlo_ref, xhi_ref, ylo_ref, yhi_ref, masks_ref, field, weights, depth, False)

    mean_mat = mean_mat_ref[...]
    mix_mat = mix_mat_ref[...]
    gain = gain_wide_ref[...]
    gain_sum = jnp.zeros((8, WIDE), F32)
    mix_sum = jnp.zeros((WIDE, WIDE), F32)
    for part in range(lanes // WIDE):
        cols = slice(part * WIDE, (part + 1) * WIDE)
        dep = jnp.concatenate([depth[2 * part], depth[2 * part + 1]], axis=1)
        cot = cot_ref[:, :, cols].reshape(cells, WIDE)
        mean_sq = jnp.dot((dep * dep).astype(BF16), mean_mat, preferred_element_type=F32)
        grad_norm = lax.dot_general(cot, mix_mat, (((1,), (1,)), ((), ())), preferred_element_type=F32)
        inv = lax.rsqrt(mean_sq + EPS)
        normed = dep * inv
        norm_bf = (normed * gain).astype(BF16)
        scaled = grad_norm * gain
        mean = jnp.dot((scaled * normed).astype(BF16), mean_mat, preferred_element_type=F32)
        mix_sum = mix_sum + lax.dot_general(
            norm_bf, cot, (((0,), (0,)), ((), ())), preferred_element_type=F32
        )
        gain_sum = gain_sum + jnp.sum((grad_norm * normed).reshape(cells // 8, 8, WIDE), axis=0)
        grad = (inv * (scaled - normed * mean)).astype(BF16)
        wide_grad = grad.astype(F32)
        normed_bf[:, cols] = norm_bf
        grad_ref[:, :, cols] = grad.reshape(side, side, WIDE)
        grads[2 * part] = wide_grad[:, :LANE]
        grads[2 * part + 1] = wide_grad[:, LANE:]
    gain_sum_ref[...] = gain_sum
    channels = grad_mix_ref.shape[1] // 2
    grad_mix = mix_sum[:channels, :channels]
    for i in range(1, WIDE // channels):
        span = slice(i * channels, (i + 1) * channels)
        grad_mix = grad_mix + mix_sum[span, span]
    grad_mix_ref[...] = jnp.concatenate([grad_mix[:32], grad_mix[32:]], axis=1)
    odd = lax.axis_index("gx") % 2
    gxa_ref[...] = grad_ref[jnp.where(odd == 1, 0, side - 1)]
    gxb_ref[...] = grad_ref[jnp.where(odd == 1, side - 1, 0)]


def mixed_kernel(own_ref, normed_bf, mix_mat_ref, mixed_ref):
    side, _, lanes = own_ref.shape
    mix_mat = mix_mat_ref[...]
    rows = 128
    xs = rows // side
    for part in range(lanes // WIDE):
        cols = slice(part * WIDE, (part + 1) * WIDE)
        for chunk in range(side // xs):
            planes = slice(chunk * xs, (chunk + 1) * xs)
            norm_bf = normed_bf[chunk * rows:(chunk + 1) * rows, cols]
            branch = jnp.dot(norm_bf, mix_mat, preferred_element_type=F32)
            feat = own_ref[planes, :, cols].reshape(rows, WIDE).astype(F32)
            mixed_ref[planes, :, cols] = (feat + branch).astype(BF16).reshape(xs, side, WIDE)


def sums_kernel(field, grads, gain_sum_ref, grad_mix_ref, packed_ref):
    tiles, cells, _ = grads.shape
    side = math.isqrt(cells)
    channels = packed_ref.shape[1] // 2
    pitch = side + 8
    def tap_tile(k, sums):
        sums = list(sums)
        for half in range(side // 8):
            near_grads = {}
            for plane in range(side + 2):
                if plane < side:
                    row = plane * side + 8 * half
                    near_grads[plane] = grads[k, row:row + 8, :]
                near = shifted(field, tiles, k, plane, half, pitch)
                for (off_y, off_z), value in near.items():
                    for off_x in range(3):
                        x = plane - off_x
                        if 0 <= x < side:
                            tap = 9 * off_x + 3 * off_y + off_z
                            sums[tap] = sums[tap] + value * near_grads[x]
                near_grads.pop(plane - 2, None)
        return tuple(sums)

    sums = lax.fori_loop(0, tiles, tap_tile, tuple(jnp.zeros((8, LANE), F32) for _ in range(27)))
    packed_ref[0:32, :] = grad_mix_ref[...]
    gain_row = jnp.sum(gain_sum_ref[...], axis=0, keepdims=True)
    rows = [jnp.sum(t, axis=0, keepdims=True) for t in sums] + [gain_row[:, :LANE] + gain_row[:, LANE:]]
    rows = jnp.concatenate(rows + [jnp.zeros((4, LANE), F32)], axis=0)
    rows = rows[:, :channels] + rows[:, channels:]
    packed_ref[32:48, :] = jnp.concatenate([rows[:16], rows[16:]], axis=1)


def backward_kernel(
    field, sums, weights, xlo_ref, xhi_ref, ylo_ref, yhi_ref, masks_ref, cot_ref,
    field_out_ref, sums_out_ref, out_ref,
):
    side = cot_ref.shape[0]
    halo_part(xlo_ref, xhi_ref, ylo_ref, yhi_ref, masks_ref, field, weights, sums, True)
    for x in range(side):
        for k in range(sums.shape[0]):
            cols = slice(k * LANE, (k + 1) * LANE)
            cot = cot_ref[x, :, cols].astype(F32)
            out_ref[x, :, cols] = (cot + sums[k, x * side:(x + 1) * side, :]).astype(BF16)


def unpack_kernel(mine_ref, other_ref, one_ref, both_ref, taps_hbm, gain_hbm, mix_hbm, taps_ref, gain_ref, mix_ref, done):
    total = (mine_ref[...] + one_ref[...]) + (other_ref[...] + both_ref[...])
    channels = mix_ref.shape[0]
    mix_ref[0:32, :] = total[:32, :channels]
    mix_ref[32:64, :] = total[:32, channels:]
    taps_ref[0:16, :] = total[32:48, :channels]
    taps_ref[16:27, :] = total[32:43, channels:]
    gain_ref[...] = total[43:44, channels:]
    copies = [
        pltpu.make_async_copy(src, dst, done.at[i])
        for i, (src, dst) in enumerate(((taps_ref, taps_hbm), (gain_ref, gain_hbm), (mix_ref, mix_hbm)))
    ]
    for copy in copies:
        copy.start()
    for copy in copies:
        copy.wait()


def swap(to_first, to_second, axis):
    sizes = {name: lax.axis_size(name) for name in ("gx", "gy")}
    count = sizes[axis]

    def second(place):
        other = "gy" if axis == "gx" else "gx"
        if 0 < place[axis] < count - 1:
            return {**place, axis: ((place[axis] + 1) ^ 1) - 1}
        return {**place, other: place[other] ^ 1}

    def index(place):
        return place["gx"] * sizes["gy"] + place["gy"]

    places = [{"gx": i, "gy": j} for i in range(sizes["gx"]) for j in range(sizes["gy"])]
    from_second = lax.ppermute(to_second, ("gx", "gy"), [(index(p), index(second(p))) for p in places])
    return lax.ppermute(to_first, axis, [(i, i ^ 1) for i in range(count)]), from_second


def low_high(from_first, from_second, axis):
    even = lax.axis_index(axis) % 2 == 0
    return jnp.where(even, from_second, from_first), jnp.where(even, from_first, from_second)


def y_messages(xlo, xhi, ylo, yhi):
    low = jnp.concatenate([xlo[:1], ylo, xhi[:1]], axis=0)
    high = jnp.concatenate([xlo[-1:], yhi, xhi[-1:]], axis=0)
    return low_high(low, high, "gy")


def sum_steps():
    steps = []
    for axis in ("gx", "gy"):
        count = lax.axis_size(axis)
        bit = 1
        while bit < count:
            steps.append((axis, [(i, i ^ bit) for i in range(count)]))
            bit *= 2
    return steps


def both_steps(one, other):
    index = {name: i for i, name in enumerate(("gx", "gy"))}
    sizes = [lax.axis_size("gx"), lax.axis_size("gy")]
    moves = [(index[axis], dict(pairs)) for axis, pairs in (one, other)]
    pairs = []
    for start in range(sizes[0] * sizes[1]):
        place = [start // sizes[1], start % sizes[1]]
        for at, move in moves:
            place[at] = move[place[at]]
        pairs.append((start, place[0] * sizes[1] + place[1]))
    return ("gx", "gy"), pairs


def shards(features, slot_map, tap_weights, gain, mix_weight, cotangent):
    side, _, _, lanes = features.shape
    channels = gain.shape[0]
    tiles = lanes // LANE
    cells = features.reshape(side, side, lanes)
    cot = cotangent.reshape(side, side, lanes)
    vmem = pl.BlockSpec(memory_space=pltpu.VMEM)
    hbm = pl.BlockSpec(memory_space=pltpu.HBM)
    block = jax.ShapeDtypeStruct((side, side, lanes), BF16)
    edge = jax.ShapeDtypeStruct((side, lanes), BF16)
    field_type = jax.ShapeDtypeStruct((2 * tiles + 1, (side + 2) * (side + 8) + 8, LANE), F32)
    sums_type = jax.ShapeDtypeStruct((tiles, side * side, LANE), F32)
    weights_type = jax.ShapeDtypeStruct((27, 8, LANE), F32)
    mat_type = jax.ShapeDtypeStruct((WIDE, WIDE), BF16)

    def call(kernel, name, operands, outs, scratch=(), aliases={}, flops=0, in_specs=None, out_specs=None):
        return pl.pallas_call(
            kernel,
            out_shape=tuple(jax.ShapeDtypeStruct(t.shape, t.dtype) for t in outs),
            in_specs=in_specs or [vmem] * len(operands),
            out_specs=out_specs or (vmem,) * len(outs),
            scratch_shapes=list(scratch),
            input_output_aliases=aliases,
            compiler_params=pltpu.CompilerParams(vmem_limit_bytes=40 * 1024 * 1024),
            cost_estimate=pl.CostEstimate(flops=flops, bytes_accessed=500_000, transcendentals=0),
            name=name,
        )(*operands)

    ylo, yhi = call(y_edges_kernel, "y_edges", (cells,), (edge, edge), flops=100_000_000_000)
    masks, weights, mean_mat, mix_mat, gain_wide = call(
        params_kernel,
        "params",
        (jnp.transpose(slot_map, (1, 2, 0)), mix_weight, tap_weights, gain.reshape(1, channels)),
        (
            jax.ShapeDtypeStruct((12, side + 8, LANE), F32),
            weights_type,
            mat_type,
            mat_type,
            jax.ShapeDtypeStruct((1, WIDE), F32),
        ),
    )
    xlo, xhi = low_high(*swap(*x_edges(cells), "gx"), "gx")
    to_a, to_b = y_messages(xlo, xhi, ylo, yhi)
    to_a, to_b, weights = lax.optimization_barrier((to_a, to_b, weights))
    ylo, yhi = low_high(*swap(to_a, to_b, "gy"), "gy")
    own_field, own_sums = call(
        functools.partial(own_kernel, False), "own_forward", (cells, weights), (field_type, sums_type),
        flops=10_000_000,
    )
    field, _, grad_depth, gxa, gxb, normed_bf, grads, gain_sum, grad_mix = call(
        forward_kernel,
        "forward",
        (own_field, own_sums, weights, mean_mat, mix_mat, gain_wide, xlo, xhi, ylo, yhi, masks, cot),
        (
            field_type, sums_type, block, edge, edge,
            jax.ShapeDtypeStruct((side * side, lanes), BF16), sums_type, jax.ShapeDtypeStruct((8, WIDE), F32),
            jax.ShapeDtypeStruct((32, LANE), F32),
        ),
        aliases={0: 0, 1: 1},
        flops=10_000_000,
    )
    gxlo, gxhi = low_high(*swap(gxa, gxb, "gx"), "gx")
    (part,) = call(
        sums_kernel,
        "sums",
        (field, grads, gain_sum, grad_mix),
        (jax.ShapeDtypeStruct((48, LANE), F32),),
        flops=10_000_000,
    )

    steps = sum_steps()
    gylo, gyhi = call(y_edges_kernel, "grad_y_edges", (grad_depth,), (edge, edge), flops=1_000_000)
    part, to_a, to_b = lax.optimization_barrier((part, *y_messages(gxlo, gxhi, gylo, gyhi)))
    core, across, both = [lax.ppermute(part, *step) for step in (steps[0], steps[1], both_steps(*steps[:2]))]
    part = (part + core) + (across + both)
    gylo, gyhi = low_high(*swap(to_a, to_b, "gy"), "gy")
    part, grad_depth = lax.optimization_barrier((part, grad_depth))
    theirs = lax.ppermute(part, *steps[2])
    own_field, own_sums = call(
        functools.partial(own_kernel, True), "own_backward", (grad_depth, weights), (field_type, sums_type),
        flops=10_000_000,
    )
    part, own_field, own_sums, normed_bf = lax.optimization_barrier(
        (part + theirs, own_field, own_sums, normed_bf)
    )
    for step in steps[3:-2]:
        part = part + lax.ppermute(part, *step)
    theirs = [lax.ppermute(part, *step) for step in (steps[-1], steps[-2], both_steps(*steps[-2:]))]
    _, _, grad_features = call(
        backward_kernel,
        "backward",
        (own_field, own_sums, weights, gxlo, gxhi, gylo, gyhi, masks, cot),
        (field_type, sums_type, block),
        aliases={0: 0, 1: 1},
        flops=2_000_000,
    )
    (mixed,) = call(mixed_kernel, "mixed", (cells, normed_bf, mix_mat), (block,), flops=10_000_000)

    outs = (
        jax.ShapeDtypeStruct((27, channels), F32),
        jax.ShapeDtypeStruct((1, channels), F32),
        jax.ShapeDtypeStruct((channels, channels), F32),
    )
    grad_taps, grad_gain, grad_mix = call(
        unpack_kernel,
        "unpack",
        (part, *theirs),
        outs,
        scratch=[pltpu.VMEM(t.shape, F32) for t in outs] + [pltpu.SemaphoreType.DMA((3,))],
        out_specs=(hbm,) * 3,
    )
    shape = features.shape
    return (mixed.reshape(shape), grad_features.reshape(shape), grad_taps, grad_gain.reshape(channels), grad_mix)


def solution(mesh):
    return jax.shard_map(
        shards,
        mesh=mesh,
        in_specs=(P("gx", "gy", None, None), P(), P(), P(), P(), P("gx", "gy", None, None)),
        out_specs=(P("gx", "gy", None, None), P("gx", "gy", None, None), P(), P(), P()),
        check_vma=False,
    )
```

```python
import functools
import math

import jax
import jax.numpy as jnp
from jax import lax
from jax.experimental import pallas as pl
from jax.experimental.pallas import tpu as pltpu
from jax.sharding import PartitionSpec as P

EPS = 1e-05
LANE = 128
WIDE = 256
PLANES = 4
F32 = jnp.float32
BF16 = jnp.bfloat16


def level_masks(slots, side, masks_ref):
    level = lax.broadcasted_iota(jnp.int32, slots.shape, 1)
    at_x = lax.broadcasted_iota(jnp.int32, slots.shape, 2) - lax.axis_index("gx")
    at_y = lax.broadcasted_iota(jnp.int32, slots.shape, 0) - lax.axis_index("gy")
    place = jnp.where(slots >= 0, level + 1, 0).astype(F32)

    def near(off_x, off_y):
        found = jnp.where((at_x == off_x) & (at_y == off_y), place, 0.0)
        found = jnp.sum(jnp.sum(found, axis=0), axis=0, keepdims=True)
        return jnp.sum(found, axis=1, keepdims=True)

    own = near(0, 0)

    def difference(off_x, off_y):
        found = near(off_x, off_y)
        return jnp.where(found > 0.0, found - own, 9.0)

    rows = masks_ref.shape[1]
    row = lax.broadcasted_iota(jnp.int32, (rows, LANE), 0)
    for edge in range(4):
        high = 1 if edge % 2 else -1
        if edge < 2:
            d = jnp.broadcast_to(difference(high, 0), (rows, LANE))
        else:
            corner, middle, other = (difference(off, high) for off in (-1, 0, 1))
            d = jnp.where(row == 0, corner, jnp.where(row == side + 1, other, middle))
        for i, want in enumerate((0.0, -1.0, 1.0)):
            masks_ref[3 * edge + i] = jnp.where(d == want, 1.0, 0.0)


def plane_tiles(load, total, masks):
    low = lax.broadcasted_iota(jnp.int32, load(0).shape, 1) < LANE // 2
    zero = jnp.zeros(load(0).shape, F32)
    aligned = [load(k) for k in range(total)]
    turned = [pltpu.roll(t, LANE // 2, 1) for t in aligned]
    between = [jnp.where(low, turned[j - 1], turned[j]) for j in range(1, total)]
    if masks is None:
        return aligned + [jnp.where(low, zero, turned[0])] + between + [jnp.where(low, turned[-1], zero)]
    same, below, above = masks
    first = jnp.where(low, turned[-1] * below, turned[0] * same)
    last = jnp.where(low, turned[-1] * same, turned[0] * above)
    return [t * same for t in aligned] + [first] + [t * same for t in between] + [last]


def loader(rows):
    return lambda k: rows[:, k * LANE:(k + 1) * LANE].astype(F32)


def column_starts(side, shift):
    pitch = side + 8
    for start in range(0, side + 2, 8):
        size = min(8, side + 2 - start)
        yield start, size, pl.ds(start * pitch + shift, size, stride=pitch)


def own_part(own_ref, field, weights, sums, flip):
    side = own_ref.shape[0]
    tiles = own_ref.shape[2] // LANE
    pitch = side + 8

    def own_planes(step, _):
        for x in range(PLANES):
            x = step * PLANES + x
            base = pl.multiple_of((x + 1) * pitch + 8, 8)
            for i, t in enumerate(plane_tiles(loader(own_ref[x]), tiles, None)):
                field[i, pl.ds(base, side), :] = t
        return 0

    lax.fori_loop(0, side // PLANES, own_planes, 0)
    for i in range(2 * tiles + 1):
        for shift in (7, pitch):
            for _, size, at in column_starts(side, shift):
                field[i, at, :] = jnp.zeros((size, LANE), F32)

    def tile(k, _):
        taps = [weights[26 - t if flip else t] for t in range(27)]
        for half in range(side // 8):
            part = {}
            for plane in range(1, side + 1):
                near = shifted(field, tiles, k, plane, half, pitch)
                for off_x in range(3):
                    x = plane - off_x
                    if not 0 <= x < side:
                        continue
                    for (off_y, off_z), value in near.items():
                        term = value * taps[9 * off_x + 3 * off_y + off_z]
                        part[x] = part[x] + term if x in part else term
                done = plane - 2
                for x in [done, done + 1] if plane == side else [done]:
                    if x >= 0:
                        sums[k, x * side + 8 * half:x * side + 8 * half + 8, :] = part.pop(x)
        return 0

    lax.fori_loop(0, tiles, tile, 0)


def halo_part(xlo_ref, xhi_ref, ylo_ref, yhi_ref, masks_ref, field, weights, sums, flip):
    side, lanes = xlo_ref.shape
    tiles = lanes // LANE
    pitch = side + 8

    def place(i, ref):
        rows = ref.shape[0]
        masks = tuple(masks_ref[3 * i + m, :rows, :] for m in range(3))
        return plane_tiles(loader(ref[...]), tiles, masks)

    for i, ref, plane in ((0, xlo_ref, 0), (1, xhi_ref, side + 1)):
        for j, t in enumerate(place(i, ref)):
            field[j, plane * pitch + 8:plane * pitch + 8 + side, :] = t

    totals = []

    def x_tile(k):
        for plane, off_x, x in ((0, 0, 0), (side + 1, 2, side - 1)):
            for half in range(side // 8):
                row = x * side + 8 * half
                total = sums[k, row:row + 8, :]
                for (off_y, off_z), value in shifted(field, tiles, k, plane, half, pitch).items():
                    tap = 9 * off_x + 3 * off_y + off_z
                    total = total + value * weights[26 - tap if flip else tap]
                totals.append((k, slice(row, row + 8), total))

    for k in range(tiles):
        x_tile(k)
    for k, at, total in totals:
        sums[k, at, :] = total

    for i, ref, shift in ((2, ylo_ref, 7), (3, yhi_ref, pitch)):
        for j, t in enumerate(place(i, ref)):
            for start, size, at in column_starts(side, shift):
                field[j, at, :] = t[start:start + size]

    totals = []

    def y_tile(k):
        for shift, off_y, y in ((7, 0, 0), (pitch, 2, side - 1)):
            for x in range(0, side, 8):
                at = pl.ds(x * side + y, 8, stride=side)
                total = sums[k, at, :]
                for off_x in range(3):
                    for off_z in range(3):
                        i = (tiles + k, k, tiles + k + 1)[off_z]
                        tap = 9 * off_x + 3 * off_y + off_z
                        value = field[i, pl.ds((x + off_x) * pitch + shift, 8, stride=pitch), :]
                        total = total + value * weights[26 - tap if flip else tap]
                totals.append((k, at, total))

    for k in range(tiles):
        y_tile(k)
    for k, at, total in totals:
        sums[k, at, :] = total


def shifted(field, tiles, k, plane, half, pitch):
    found = {}
    for off_y in range(3):
        row = plane * pitch + 7 + 8 * half + off_y
        for off_z in range(3):
            i = (tiles + k, k, tiles + k + 1)[off_z]
            found[off_y, off_z] = field[i, row:row + 8, :]
    return found


def x_edges(cells):
    odd = lax.axis_index("gx") % 2 == 1
    return jnp.where(odd, cells[0], cells[-1]), jnp.where(odd, cells[-1], cells[0])


def y_edges_kernel(cells_ref, ylo_ref, yhi_ref):
    side, _, lanes = cells_ref.shape
    row = lax.broadcasted_iota(jnp.int32, (2 * side, side * side), 0)
    col = lax.broadcasted_iota(jnp.int32, (2 * side, side * side), 1)
    wanted = jnp.where(row < side, row * side, (row - side) * side + side - 1)
    pick = jnp.where(col == wanted, 1.0, 0.0).astype(BF16)
    flat = cells_ref[...].reshape(side * side, lanes)
    found = jnp.dot(pick, flat, preferred_element_type=F32).astype(BF16)
    ylo_ref[...] = found[:side]
    yhi_ref[...] = found[side:]


def params_kernel(
    slots_ref, mix_ref, taps_ref, gain_ref, masks_ref, weights, mean_mat_ref, mix_mat_ref, gain_wide_ref
):
    channels = mix_ref.shape[0]
    level_masks(slots_ref[...], masks_ref.shape[1] - 8, masks_ref)
    wide = jnp.concatenate([taps_ref[...], taps_ref[...]], axis=1)
    for tap in range(27):
        weights[tap] = jnp.broadcast_to(wide[tap:tap + 1], (8, LANE))
    copies = WIDE // channels
    row_id = lax.broadcasted_iota(jnp.int32, (WIDE, WIDE), 0) // channels
    col_id = lax.broadcasted_iota(jnp.int32, (WIDE, WIDE), 1) // channels
    block = row_id == col_id
    mean_mat_ref[...] = jnp.where(block, 1.0 / channels, 0.0).astype(BF16)
    mix = mix_ref[...].astype(F32)
    mix_row = jnp.concatenate([mix] * copies, axis=1)
    mix_mat_ref[...] = jnp.where(block, jnp.concatenate([mix_row] * copies, axis=0), 0.0).astype(BF16)
    gain_wide_ref[...] = jnp.concatenate([gain_ref[...]] * copies, axis=1)


def own_kernel(flip, own_ref, weights, field, sums):
    own_part(own_ref, field, weights, sums, flip)


def forward_kernel(
    field, depth, weights, mean_mat_ref, mix_mat_ref, gain_wide_ref,
    xlo_ref, xhi_ref, ylo_ref, yhi_ref, masks_ref, cot_ref,
    field_out_ref, depth_out_ref, grad_ref, gxa_ref, gxb_ref, normed_bf, grads, gain_sum_ref, grad_mix_ref,
):
    side, _, lanes = cot_ref.shape
    cells = side * side
    halo_part(xlo_ref, xhi_ref, ylo_ref, yhi_ref, masks_ref, field, weights, depth, False)

    mean_mat = mean_mat_ref[...]
    mix_mat = mix_mat_ref[...]
    gain = gain_wide_ref[...]
    gain_sum = jnp.zeros((8, WIDE), F32)
    mix_sum = jnp.zeros((WIDE, WIDE), F32)
    for part in range(lanes // WIDE):
        cols = slice(part * WIDE, (part + 1) * WIDE)
        dep = jnp.concatenate([depth[2 * part], depth[2 * part + 1]], axis=1)
        cot = cot_ref[:, :, cols].reshape(cells, WIDE)
        mean_sq = jnp.dot((dep * dep).astype(BF16), mean_mat, preferred_element_type=F32)
        grad_norm = lax.dot_general(cot, mix_mat, (((1,), (1,)), ((), ())), preferred_element_type=F32)
        inv = lax.rsqrt(mean_sq + EPS)
        normed = dep * inv
        norm_bf = (normed * gain).astype(BF16)
        scaled = grad_norm * gain
        mean = jnp.dot((scaled * normed).astype(BF16), mean_mat, preferred_element_type=F32)
        mix_sum = mix_sum + lax.dot_general(
            norm_bf, cot, (((0,), (0,)), ((), ())), preferred_element_type=F32
        )
        gain_sum = gain_sum + jnp.sum((grad_norm * normed).reshape(cells // 8, 8, WIDE), axis=0)
        grad = (inv * (scaled - normed * mean)).astype(BF16)
        wide_grad = grad.astype(F32)
        normed_bf[:, cols] = norm_bf
        grad_ref[:, :, cols] = grad.reshape(side, side, WIDE)
        grads[2 * part] = wide_grad[:, :LANE]
        grads[2 * part + 1] = wide_grad[:, LANE:]
    gain_sum_ref[...] = gain_sum
    channels = grad_mix_ref.shape[1] // 2
    grad_mix = mix_sum[:channels, :channels]
    for i in range(1, WIDE // channels):
        span = slice(i * channels, (i + 1) * channels)
        grad_mix = grad_mix + mix_sum[span, span]
    grad_mix_ref[...] = jnp.concatenate([grad_mix[:32], grad_mix[32:]], axis=1)
    odd = lax.axis_index("gx") % 2
    gxa_ref[...] = grad_ref[jnp.where(odd == 1, 0, side - 1)]
    gxb_ref[...] = grad_ref[jnp.where(odd == 1, side - 1, 0)]


def mixed_kernel(own_ref, normed_bf, mix_mat_ref, mixed_ref):
    side, _, lanes = own_ref.shape
    mix_mat = mix_mat_ref[...]
    rows = 128
    xs = rows // side
    for part in range(lanes // WIDE):
        cols = slice(part * WIDE, (part + 1) * WIDE)
        for chunk in range(side // xs):
            planes = slice(chunk * xs, (chunk + 1) * xs)
            norm_bf = normed_bf[chunk * rows:(chunk + 1) * rows, cols]
            branch = jnp.dot(norm_bf, mix_mat, preferred_element_type=F32)
            feat = own_ref[planes, :, cols].reshape(rows, WIDE).astype(F32)
            mixed_ref[planes, :, cols] = (feat + branch).astype(BF16).reshape(xs, side, WIDE)


def sums_kernel(field, grads, gain_sum_ref, grad_mix_ref, packed_ref):
    tiles, cells, _ = grads.shape
    side = math.isqrt(cells)
    channels = packed_ref.shape[1] // 2
    pitch = side + 8
    def tap_tile(k, sums):
        sums = list(sums)
        for half in range(side // 8):
            near_grads = {}
            for plane in range(side + 2):
                if plane < side:
                    row = plane * side + 8 * half
                    near_grads[plane] = grads[k, row:row + 8, :]
                near = shifted(field, tiles, k, plane, half, pitch)
                for (off_y, off_z), value in near.items():
                    for off_x in range(3):
                        x = plane - off_x
                        if 0 <= x < side:
                            tap = 9 * off_x + 3 * off_y + off_z
                            sums[tap] = sums[tap] + value * near_grads[x]
                near_grads.pop(plane - 2, None)
        return tuple(sums)

    sums = lax.fori_loop(0, tiles, tap_tile, tuple(jnp.zeros((8, LANE), F32) for _ in range(27)))
    packed_ref[0:32, :] = grad_mix_ref[...]
    gain_row = jnp.sum(gain_sum_ref[...], axis=0, keepdims=True)
    rows = [jnp.sum(t, axis=0, keepdims=True) for t in sums] + [gain_row[:, :LANE] + gain_row[:, LANE:]]
    rows = jnp.concatenate(rows + [jnp.zeros((4, LANE), F32)], axis=0)
    rows = rows[:, :channels] + rows[:, channels:]
    packed_ref[32:48, :] = jnp.concatenate([rows[:16], rows[16:]], axis=1)


def backward_kernel(
    field, sums, weights, xlo_ref, xhi_ref, ylo_ref, yhi_ref, masks_ref, cot_ref,
    field_out_ref, sums_out_ref, out_ref,
):
    side = cot_ref.shape[0]
    halo_part(xlo_ref, xhi_ref, ylo_ref, yhi_ref, masks_ref, field, weights, sums, True)
    for x in range(side):
        for k in range(sums.shape[0]):
            cols = slice(k * LANE, (k + 1) * LANE)
            cot = cot_ref[x, :, cols].astype(F32)
            out_ref[x, :, cols] = (cot + sums[k, x * side:(x + 1) * side, :]).astype(BF16)


def unpack_kernel(mine_ref, other_ref, one_ref, both_ref, taps_hbm, gain_hbm, mix_hbm, taps_ref, gain_ref, mix_ref, done):
    total = (mine_ref[...] + one_ref[...]) + (other_ref[...] + both_ref[...])
    channels = mix_ref.shape[0]
    mix_ref[0:32, :] = total[:32, :channels]
    mix_ref[32:64, :] = total[:32, channels:]
    taps_ref[0:16, :] = total[32:48, :channels]
    taps_ref[16:27, :] = total[32:43, channels:]
    gain_ref[...] = total[43:44, channels:]
    copies = [
        pltpu.make_async_copy(src, dst, done.at[i])
        for i, (src, dst) in enumerate(((taps_ref, taps_hbm), (gain_ref, gain_hbm), (mix_ref, mix_hbm)))
    ]
    for copy in copies:
        copy.start()
    for copy in copies:
        copy.wait()


def swap(to_first, to_second, axis):
    sizes = {name: lax.axis_size(name) for name in ("gx", "gy")}
    count = sizes[axis]

    def second(place):
        other = "gy" if axis == "gx" else "gx"
        if 0 < place[axis] < count - 1:
            return {**place, axis: ((place[axis] + 1) ^ 1) - 1}
        return {**place, other: place[other] ^ 1}

    def index(place):
        return place["gx"] * sizes["gy"] + place["gy"]

    places = [{"gx": i, "gy": j} for i in range(sizes["gx"]) for j in range(sizes["gy"])]
    from_second = lax.ppermute(to_second, ("gx", "gy"), [(index(p), index(second(p))) for p in places])
    return lax.ppermute(to_first, axis, [(i, i ^ 1) for i in range(count)]), from_second


def low_high(from_first, from_second, axis):
    even = lax.axis_index(axis) % 2 == 0
    return jnp.where(even, from_second, from_first), jnp.where(even, from_first, from_second)


def y_messages(xlo, xhi, ylo, yhi):
    low = jnp.concatenate([xlo[:1], ylo, xhi[:1]], axis=0)
    high = jnp.concatenate([xlo[-1:], yhi, xhi[-1:]], axis=0)
    return low_high(low, high, "gy")


def sum_steps():
    steps = []
    for axis in ("gx", "gy"):
        count = lax.axis_size(axis)
        bit = 1
        while bit < count:
            steps.append((axis, [(i, i ^ bit) for i in range(count)]))
            bit *= 2
    return steps


def both_steps(one, other):
    index = {name: i for i, name in enumerate(("gx", "gy"))}
    sizes = [lax.axis_size("gx"), lax.axis_size("gy")]
    moves = [(index[axis], dict(pairs)) for axis, pairs in (one, other)]
    pairs = []
    for start in range(sizes[0] * sizes[1]):
        place = [start // sizes[1], start % sizes[1]]
        for at, move in moves:
            place[at] = move[place[at]]
        pairs.append((start, place[0] * sizes[1] + place[1]))
    return ("gx", "gy"), pairs


def shards(features, slot_map, tap_weights, gain, mix_weight, cotangent):
    side, _, _, lanes = features.shape
    channels = gain.shape[0]
    tiles = lanes // LANE
    cells = features.reshape(side, side, lanes)
    cot = cotangent.reshape(side, side, lanes)
    vmem = pl.BlockSpec(memory_space=pltpu.VMEM)
    hbm = pl.BlockSpec(memory_space=pltpu.HBM)
    block = jax.ShapeDtypeStruct((side, side, lanes), BF16)
    edge = jax.ShapeDtypeStruct((side, lanes), BF16)
    field_type = jax.ShapeDtypeStruct((2 * tiles + 1, (side + 2) * (side + 8) + 8, LANE), F32)
    sums_type = jax.ShapeDtypeStruct((tiles, side * side, LANE), F32)
    weights_type = jax.ShapeDtypeStruct((27, 8, LANE), F32)
    mat_type = jax.ShapeDtypeStruct((WIDE, WIDE), BF16)

    def call(kernel, name, operands, outs, scratch=(), aliases={}, flops=0, in_specs=None, out_specs=None):
        return pl.pallas_call(
            kernel,
            out_shape=tuple(jax.ShapeDtypeStruct(t.shape, t.dtype) for t in outs),
            in_specs=in_specs or [vmem] * len(operands),
            out_specs=out_specs or (vmem,) * len(outs),
            scratch_shapes=list(scratch),
            input_output_aliases=aliases,
            compiler_params=pltpu.CompilerParams(vmem_limit_bytes=40 * 1024 * 1024),
            cost_estimate=pl.CostEstimate(flops=flops, bytes_accessed=500_000, transcendentals=0),
            name=name,
        )(*operands)

    ylo, yhi = call(y_edges_kernel, "y_edges", (cells,), (edge, edge), flops=100_000_000_000)
    masks, weights, mean_mat, mix_mat, gain_wide = call(
        params_kernel,
        "params",
        (jnp.transpose(slot_map, (1, 2, 0)), mix_weight, tap_weights, gain.reshape(1, channels)),
        (
            jax.ShapeDtypeStruct((12, side + 8, LANE), F32),
            weights_type,
            mat_type,
            mat_type,
            jax.ShapeDtypeStruct((1, WIDE), F32),
        ),
    )
    xlo, xhi = low_high(*swap(*x_edges(cells), "gx"), "gx")
    to_a, to_b = y_messages(xlo, xhi, ylo, yhi)
    to_a, to_b, weights = lax.optimization_barrier((to_a, to_b, weights))
    ylo, yhi = low_high(*swap(to_a, to_b, "gy"), "gy")
    own_field, own_sums = call(
        functools.partial(own_kernel, False), "own_forward", (cells, weights), (field_type, sums_type),
        flops=10_000_000,
    )
    field, _, grad_depth, gxa, gxb, normed_bf, grads, gain_sum, grad_mix = call(
        forward_kernel,
        "forward",
        (own_field, own_sums, weights, mean_mat, mix_mat, gain_wide, xlo, xhi, ylo, yhi, masks, cot),
        (
            field_type, sums_type, block, edge, edge,
            jax.ShapeDtypeStruct((side * side, lanes), BF16), sums_type, jax.ShapeDtypeStruct((8, WIDE), F32),
            jax.ShapeDtypeStruct((32, LANE), F32),
        ),
        aliases={0: 0, 1: 1},
        flops=10_000_000,
    )
    gxlo, gxhi = low_high(*swap(gxa, gxb, "gx"), "gx")
    (part,) = call(
        sums_kernel,
        "sums",
        (field, grads, gain_sum, grad_mix),
        (jax.ShapeDtypeStruct((48, LANE), F32),),
        flops=10_000_000,
    )

    steps = sum_steps()
    part, y_cells = lax.optimization_barrier((part, grad_depth))
    core, across, both = [lax.ppermute(part, *step) for step in (steps[0], steps[1], both_steps(*steps[:2]))]
    gylo, gyhi = call(y_edges_kernel, "grad_y_edges", (y_cells,), (edge, edge), flops=1_000_000)
    to_a, to_b = y_messages(gxlo, gxhi, gylo, gyhi)
    part = (part + core) + (across + both)
    gylo, gyhi = low_high(*swap(to_a, to_b, "gy"), "gy")
    part, grad_depth = lax.optimization_barrier((part, grad_depth))
    theirs = lax.ppermute(part, *steps[2])
    own_field, own_sums = call(
        functools.partial(own_kernel, True), "own_backward", (grad_depth, weights), (field_type, sums_type),
        flops=10_000_000,
    )
    part, own_field, own_sums, normed_bf = lax.optimization_barrier(
        (part + theirs, own_field, own_sums, normed_bf)
    )
    for step in steps[3:-2]:
        part = part + lax.ppermute(part, *step)
    theirs = [lax.ppermute(part, *step) for step in (steps[-1], steps[-2], both_steps(*steps[-2:]))]
    _, _, grad_features = call(
        backward_kernel,
        "backward",
        (own_field, own_sums, weights, gxlo, gxhi, gylo, gyhi, masks, cot),
        (field_type, sums_type, block),
        aliases={0: 0, 1: 1},
        flops=2_000_000,
    )
    (mixed,) = call(mixed_kernel, "mixed", (cells, normed_bf, mix_mat), (block,), flops=10_000_000)

    outs = (
        jax.ShapeDtypeStruct((27, channels), F32),
        jax.ShapeDtypeStruct((1, channels), F32),
        jax.ShapeDtypeStruct((channels, channels), F32),
    )
    grad_taps, grad_gain, grad_mix = call(
        unpack_kernel,
        "unpack",
        (part, *theirs),
        outs,
        scratch=[pltpu.VMEM(t.shape, F32) for t in outs] + [pltpu.SemaphoreType.DMA((3,))],
        out_specs=(hbm,) * 3,
    )
    shape = features.shape
    return (mixed.reshape(shape), grad_features.reshape(shape), grad_taps, grad_gain.reshape(channels), grad_mix)


def solution(mesh):
    return jax.shard_map(
        shards,
        mesh=mesh,
        in_specs=(P("gx", "gy", None, None), P(), P(), P(), P(), P("gx", "gy", None, None)),
        out_specs=(P("gx", "gy", None, None), P("gx", "gy", None, None), P(), P(), P()),
        check_vma=False,
    )
```
